32 devices in a mesh: dp: 16 (over z, y, x), tensor: 2 (over core).
Axes of the slice: x: 2, y: 2, z: 4, core: 2. Of those that a mesh axis runs over, the one named last changes fastest.
Arguments:
- tokens: bfloat16 [16, 960, 768], P('dp'), may hold values from -6 to 6
- cotangent: bfloat16 [16, 960, 768], P('dp'), may hold values from -24 to 24
- inclusion: int32 [16], P('dp'), may hold values 0 or 1
- attn_weights: float32 [768, 4, 768], P('dp', None, 'tensor'), may hold values from -1.2577882 to 1.2577882
- mlp_weights: float32 [768, 2, 3072], P('dp', None, 'tensor'), may hold values from -0.3247595 to 0.3247595
- attn_momentum: float32 [768, 4, 768], P('dp', None, 'tensor'), may hold values from -6 to 6
- mlp_momentum: float32 [768, 2, 3072], P('dp', None, 'tensor'), may hold values from -20 to 20
- attn_noise: float32 [768, 4, 768], P('dp', None, 'tensor'), may hold values from -6 to 6
- mlp_noise: float32 [768, 2, 3072], P('dp', None, 'tensor'), may hold values from -6 to 6
- vectors: float32 [9216], replicated, may hold values from -0.8 to 1.25
- vector_momentum: float32 [9216], replicated, may hold values from -24 to 24
- vector_noise: float32 [9216], replicated, may hold values from -6 to 6
Outputs:
- out_act: bfloat16 [16, 960, 768], P('dp')
- input_grad: bfloat16 [16, 960, 768], P('dp')
- attn_momentum_new: float32 [768, 4, 768], P('dp', None, 'tensor')
- mlp_momentum_new: float32 [768, 2, 3072], P('dp', None, 'tensor')
- attn_new: float32 [768, 4, 768], P('dp', None, 'tensor')
- mlp_new: float32 [768, 2, 3072], P('dp', None, 'tensor')
- vector_momentum_new: float32 [9216], replicated
- vectors_new: float32 [9216], replicated
The draws below stay inside these ranges and needn't reach their ends.
All inputs are finite; a program needn't handle non-finite values. No bound on the sum of `inclusion` on one device may be relied on, other than what follows from the above.
Results may differ from the reference program's by a relative error of at most 0.017.
Values may be sent and summed in bfloat16 or wider, within the bound.
A program may use at most 192 MiB of HBM per device.

```python
import math
import jax
import jax.numpy as jnp
from jax import lax

D = 768
H = 12
HD = 64
FF = 3072
LEN = 960
NS_ITERS = 5
EXAMPLES = 16
VEC = 9216
N_DP = 16
N_TENSOR = 2


def draw_cotangent(key, part):
    key = jax.random.fold_in(key, 11)
    scale_key, value_key = jax.random.split(key)
    scales = jnp.exp(jax.random.uniform(scale_key, (EXAMPLES, 1, 1), jnp.float32, math.log(0.25), math.log(4.0)))
    values = jax.random.truncated_normal(value_key, -6.0, 6.0, (EXAMPLES, LEN, D), jnp.float32)
    return (values * scales).astype(jnp.bfloat16)


def draw_attn_weights(key, part):
    key = jax.random.fold_in(key, 23)
    rise_ratio = 3.0
    normal_draw = jax.random.truncated_normal(key, -4.0, 4.0, (D, 4, D), jnp.float32)
    column = jnp.arange(D, dtype=jnp.float32) / (D - 1)
    column_ramp = jnp.power(rise_ratio, 0.5 * column)
    unit_row = jnp.ones((D,), jnp.float32)
    out_scale = max(1.0, math.sqrt(LEN) / 8.0)
    slot_scales = jnp.stack([unit_row, unit_row, column_ramp, out_scale * unit_row], axis=0)
    return normal_draw * slot_scales[None, :, :] / math.sqrt(D)


def draw_mlp_weights(key, part):
    key = jax.random.fold_in(key, 29)
    rise_ratio = 3.0
    normal_draw = jax.random.truncated_normal(key, -4.0, 4.0, (D, 2, FF), jnp.float32)
    column = jnp.arange(FF, dtype=jnp.float32) / (FF - 1)
    column_ramp = jnp.power(rise_ratio, 0.5 * column)
    unit_row = jnp.ones((FF,), jnp.float32)
    slot_scales = jnp.stack([column_ramp / math.sqrt(D), unit_row / math.sqrt(FF)], axis=0)
    return normal_draw * slot_scales[None, :, :]


def draw_vectors(key, part):
    key = jax.random.fold_in(key, 37)
    gain_key, bias_key = jax.random.split(key)
    gain_rows = 1.0 + 0.1 * jax.random.truncated_normal(gain_key, -2.5, 2.5, (2, D), jnp.float32)
    biases = 0.2 * jax.random.truncated_normal(bias_key, -4.0, 4.0, (6 * D + FF,), jnp.float32)
    return jnp.concatenate([gain_rows[0], biases[0:D], gain_rows[1], biases[D:]])


def touch_ends(drawn, key, low, high):
    index_at = [jax.random.randint(jax.random.fold_in(key, axis), (), 0, length) for axis, length in enumerate(drawn.shape)]
    widest = drawn.shape.index(max(drawn.shape))
    next_to = index_at[:widest] + [(index_at[widest] + 1) % drawn.shape[widest]] + index_at[widest + 1:]
    return drawn.at[tuple(index_at)].set(low).at[tuple(next_to)].set(high)


def levels(key, shape, cuts, least, top_value):
    gain = 1.0
    for axis_at, blocks in cuts:
        heights = jax.random.uniform(jax.random.fold_in(jax.random.fold_in(key, 6), axis_at), (blocks,), jnp.float32, least / len(cuts), top_value / len(cuts))
        gain = gain * jnp.repeat(jnp.exp(heights), shape[axis_at] // blocks).reshape((-1,) + (1,) * (len(shape) - 1 - axis_at))
    return gain


def scatter_about(rng, extent, width, most, cuts=(), kind=jnp.bfloat16):
    result = jax.random.normal(rng, extent, jnp.float32) * width
    if len(cuts) > 0:
        result = levels(rng, extent, cuts, -0.22, 0.18) * result
    return jnp.clip(result, min=-most, max=most).astype(kind)


def setup_inputs(seed: int = 0) -> dict:
    keys = jax.random.split(jax.random.key(seed), 13)
    tokens = scatter_about(keys[0], (EXAMPLES, LEN, D), 1.0, 6.0, ((0, 16),))
    cotangent = draw_cotangent(jax.random.fold_in(keys[12], 71), 0)
    inclusion = touch_ends((jax.random.randint(keys[2], (EXAMPLES,), 0, 4) < 3).astype(jnp.int32), jax.random.fold_in(keys[2], 1), 0, 1)
    attn_weights = draw_attn_weights(jax.random.fold_in(keys[12], 71), 0)
    mlp_weights = draw_mlp_weights(jax.random.fold_in(keys[12], 71), 0)
    attn_momentum = scatter_about(keys[5], (D, 4, D), (0.25 * (LEN / N_DP) ** 0.5), 6.0, ((0, 16), (2, 2)), jnp.float32)
    mlp_momentum = scatter_about(keys[6], (D, 2, FF), (0.45 * (LEN / N_DP) ** 0.5), 20.0, ((0, 16), (2, 2)), jnp.float32)
    attn_noise = scatter_about(keys[7], (D, 4, D), 1.0, 6.0, ((0, 16), (2, 2)), jnp.float32)
    mlp_noise = scatter_about(keys[8], (D, 2, FF), 1.0, 6.0, ((0, 16), (2, 2)), jnp.float32)
    vectors = draw_vectors(jax.random.fold_in(keys[12], 71), 0)
    vector_momentum = scatter_about(keys[10], (VEC,), (0.5 * (LEN / N_DP) ** 0.5), 24.0, (), jnp.float32)
    vector_noise = scatter_about(keys[11], (VEC,), 1.0, 6.0, (), jnp.float32)
    return {"tokens": tokens, "cotangent": cotangent, "inclusion": inclusion, "attn_weights": attn_weights, "mlp_weights": mlp_weights, "attn_momentum": attn_momentum, "mlp_momentum": mlp_momentum, "attn_noise": attn_noise, "mlp_noise": mlp_noise, "vectors": vectors, "vector_momentum": vector_momentum, "vector_noise": vector_noise}


@jax.custom_vjp
def low(v):
    return lax.optimization_barrier(v.astype(jnp.bfloat16)).astype(jnp.float32)

@jax.custom_vjp
def low_back(v):
    return v

def low_keep(v):
    return (low(v), None)

def low_pass(kept, grad):
    return (grad,)

def back_keep(v):
    return (v, None)

def back_low(kept, grad):
    return (low(grad),)
low.defvjp(low_keep, low_pass)
low_back.defvjp(back_keep, back_low)
COEF_A = 3.4445
COEF_B = -4.775
COEF_C = 2.0315

def product(left, right):
    return jnp.dot(left, right, precision=lax.Precision.HIGHEST)

def layer_norm(values, norm_gain, norm_bias):
    centered = values - lax.optimization_barrier(jnp.mean(values, axis=-1, keepdims=True))
    inverse = lax.rsqrt(lax.optimization_barrier(jnp.mean(centered * centered, axis=-1, keepdims=True)) + 1e-05)
    return centered * inverse * norm_gain + norm_bias

def attend(head_inputs):
    queries, key_rows, value_rows = head_inputs
    length = queries.shape[0]
    scores = low_back(product(queries, key_rows.T))
    causal = lax.broadcasted_iota(jnp.int32, (length, length), 0) >= lax.broadcasted_iota(jnp.int32, (length, length), 1)
    masked = jnp.where(causal, scores, -1e+30)
    row_peak = lax.optimization_barrier(jnp.max(masked, axis=1, keepdims=True))
    logsum = row_peak + jnp.log(lax.optimization_barrier(jnp.sum(jnp.exp(masked - row_peak), axis=1, keepdims=True)))
    probability = low(jnp.exp(masked - logsum))
    return product(probability, value_rows)

def forward(inputs, attn_weights, mlp_weights, vectors):
    attn_low = low(attn_weights)
    mlp_low = low(mlp_weights)
    length = inputs.shape[0]
    head_width = D // N_TENSOR
    hidden_width = FF // N_TENSOR
    query_scale = 1.0 / math.sqrt(HD)
    first = low(layer_norm(inputs, vectors[0:D], vectors[D:2 * D]))
    queries = low(low_back((product(first, attn_low[:, 0, :]) + vectors[4 * D:5 * D]) * query_scale))
    key_rows = low(low_back(product(first, attn_low[:, 1, :])))
    value_rows = low(low_back(product(first, attn_low[:, 2, :]) + vectors[5 * D:6 * D]))

    def to_heads(matrix):
        return matrix.reshape(length, H, HD).transpose(1, 0, 2)
    attended = lax.map(jax.checkpoint(attend), (to_heads(queries), to_heads(key_rows), to_heads(value_rows)))
    attended = low(low_back(attended.transpose(1, 0, 2).reshape(length, D)))
    attn_total = jnp.zeros((length, D), jnp.float32)
    for group_index in range(N_TENSOR):
        lower = group_index * head_width
        attn_total = attn_total + low(low_back(product(attended[:, lower:lower + head_width], attn_low[:, 3, lower:lower + head_width].T)))
    middle = inputs + attn_total + vectors[6 * D:7 * D]
    second = low(layer_norm(middle, vectors[2 * D:3 * D], vectors[3 * D:4 * D]))
    pre_act = low_back(product(second, mlp_low[:, 0, :]) + vectors[8 * D:8 * D + FF])
    activation = low(jax.nn.gelu(pre_act, approximate=True))
    mlp_total = jnp.zeros((length, D), jnp.float32)
    for group_index in range(N_TENSOR):
        lower = group_index * hidden_width
        mlp_total = mlp_total + low(low_back(product(activation[:, lower:lower + hidden_width], mlp_low[:, 1, lower:lower + hidden_width].T)))
    return middle + mlp_total + vectors[7 * D:8 * D]

def newton(matrix):
    current = matrix / (jnp.sqrt(jnp.sum(matrix * matrix)) + 1e-07)
    for iteration in range(NS_ITERS):
        gram_matrix = product(current, current.T)
        polynomial = COEF_B * gram_matrix + COEF_C * product(gram_matrix, gram_matrix)
        current = COEF_A * current + product(polynomial, current)
    return current

def reference(tokens, cotangent, inclusion, attn_weights, mlp_weights, attn_momentum, mlp_momentum, attn_noise, mlp_noise, vectors, vector_momentum, vector_noise):
    clip = 1.5 * D * math.sqrt(LEN)
    sigma = 0.05 * math.sqrt(N_DP) / D
    batch = 0.75 * EXAMPLES

    def example_step(running, example):
        token_rows, cot_rows, included = example
        output, pullback = jax.vjp(forward, token_rows.astype(jnp.float32), attn_weights, mlp_weights, vectors)
        grad_in, grad_attn, grad_mlp, grad_vec = pullback(cot_rows.astype(jnp.float32))
        square = jnp.sum(grad_attn * grad_attn) + jnp.sum(grad_mlp * grad_mlp) + jnp.sum(grad_vec * grad_vec)
        factor = included.astype(jnp.float32) * jnp.minimum(1.0, clip / (jnp.sqrt(square) + 1e-06))
        running = (running[0] + factor * grad_attn, running[1] + factor * grad_mlp, running[2] + factor * grad_vec)
        return (running, (output.astype(jnp.bfloat16), grad_in.astype(jnp.bfloat16)))
    initial = (jnp.zeros_like(attn_weights), jnp.zeros_like(mlp_weights), jnp.zeros_like(vectors))
    sums, outputs = lax.scan(example_step, initial, (tokens, cotangent, inclusion))
    out_act, input_grad = outputs
    noise_scale = sigma * clip
    attn_momentum_new = 0.5 * attn_momentum + (sums[0] + noise_scale * attn_noise) / batch
    mlp_momentum_new = 0.5 * mlp_momentum + (sums[1] + noise_scale * mlp_noise) / batch
    vector_momentum_new = 0.5 * vector_momentum + (sums[2] + noise_scale * vector_noise) / batch
    attn_orth = jnp.stack([newton(attn_momentum_new[:, slot_index, :]) for slot_index in range(4)], axis=1)
    mlp_orth = jnp.stack([newton(mlp_momentum_new[:, slot_index, :]) for slot_index in range(2)], axis=1)
    attn_rates = jnp.array([0.5, 0.5, 0.5, 0.5 * max(1.0, math.sqrt(LEN) / 8.0)], jnp.float32)
    mlp_rates = jnp.array([0.5 * math.sqrt(FF / D), 0.5], jnp.float32)
    attn_new = attn_weights - attn_rates[None, :, None] * attn_orth
    mlp_new = mlp_weights - mlp_rates[None, :, None] * mlp_orth
    vector_rate = 0.2 * math.sqrt(N_DP / LEN)
    vectors_new = vectors - vector_rate * vector_momentum_new
    return (out_act, input_grad, attn_momentum_new, mlp_momentum_new, attn_new, mlp_new, vector_momentum_new, vectors_new)
```

```python
import functools
import math

import jax
import jax.numpy as jnp
from jax import lax
from jax.experimental import pallas as pl
from jax.experimental.pallas import tpu as pltpu
from jax.sharding import PartitionSpec as P

D = 768
HD = 64
FF = 3072
LEN = 960
NS_ITERS = 5


COEF_A = 3.4445
COEF_B = -4.775
COEF_C = 2.0315


def gelu_tanh(values):
    return jax.nn.gelu(values, approximate=True)


def layer_norm(values, norm_gain, norm_bias):
    centered = values - jnp.mean(values, axis=-1, keepdims=True)
    inverse = lax.rsqrt(jnp.mean(centered * centered, axis=-1, keepdims=True) + 1e-05)
    normed = centered * inverse
    return (normed * norm_gain + norm_bias, normed, inverse)


def norm_back(grad_out, norm_gain, normed, inverse):
    scaled = grad_out * norm_gain
    return inverse * (
        scaled
        - jnp.mean(scaled, axis=-1, keepdims=True)
        - normed * jnp.mean(scaled * normed, axis=-1, keepdims=True)
    )


def contract(left, right, left_dim, right_dim):
    return lax.dot_general(
        left, right, (((left_dim,), (right_dim,)), ((), ())), preferred_element_type=jnp.float32
    )


MESH = pl.DeviceIdType.MESH
MIB = 1 << 20
LINE = 4
OWNERS = (7, 8, 6, 9, 4, 11)


def place():
    dp = lax.axis_index("dp")
    core = lax.axis_index("tensor")
    z = dp // 4
    y = dp % 4 // 2
    x = dp % 2
    return dp, core, z, y, x


def remote(src, dst, send, recv, dp, core):
    return pltpu.make_async_remote_copy(
        src_ref=src, dst_ref=dst, send_sem=send, recv_sem=recv, device_id=(dp, core), device_id_type=MESH
    )


def greet(barrier, dp, core):
    pl.semaphore_signal(barrier, inc=1, device_id=(dp, core), device_id_type=MESH)


def greet_all(dp, core, count, with_core):
    barrier = pltpu.get_barrier_semaphore()
    for step in range(1, count):
        greet(barrier, (dp + step) % count, core)
    if with_core:
        greet(barrier, dp, 1 - core)
    pl.semaphore_wait(barrier, count - 1 + int(with_core))


def scatter_kernel(rates, orth, attn, mlp, attn_new, mlp_new, attn_low, mlp_low, send, recv):
    dp, core, z, y, x = place()
    rows = attn.shape[0]
    count = orth.shape[0] // rows
    greet_all(dp, core, count, False)

    def at(ref, block):
        return ref.at[pl.ds(pl.multiple_of(block * rows, rows), rows)]

    def low_of(slot):
        return attn_low.at[slot] if slot < 4 else mlp_low.at[slot - 4]

    def size_of(slot):
        return attn.shape[2] if slot < 4 else mlp.shape[2]

    for slot in range(6):
        owner = OWNERS[slot]

        @pl.when(dp == owner)
        def _():
            for step in range(1, count):
                target = (owner + step) % count
                src = at(orth, target).at[:, 0 : size_of(slot)]
                remote(src, low_of(slot), send.at[target], recv.at[slot], target, core).start()
            pltpu.make_async_copy(
                at(orth, owner).at[:, 0 : size_of(slot)], low_of(slot), recv.at[slot]
            ).start()

    for slot in range(6):
        owner = OWNERS[slot]
        low = low_of(slot)

        @pl.when(dp != owner)
        def _():
            remote(low, low, send.at[0], recv.at[slot], owner, core).wait_recv()

        @pl.when(dp == owner)
        def _():
            pltpu.make_async_copy(low, low, recv.at[slot]).wait()

        @pl.loop(0, rows // 16)
        def _(i):
            part = pl.ds(pl.multiple_of(i * 16, 16), 16)
            step = rates[slot] * low[part, :].astype(jnp.float32)
            if slot < 4:
                attn_new[part, slot, :] = attn[part, slot, :] - step
            else:
                mlp_new[part, slot - 4, :] = mlp[part, slot - 4, :] - step

    for slot in range(6):
        owner = OWNERS[slot]

        @pl.when(dp == owner)
        def _():
            for step in range(1, count):
                target = (owner + step) % count
                src = at(orth, target).at[:, 0 : size_of(slot)]
                remote(src, low_of(slot), send.at[target], recv.at[slot], target, core).wait_send()


def scatter_rows(orth, attn, mlp, rates, collective_id):
    dma = pltpu.SemaphoreType.DMA
    count = lax.axis_size("dp")
    rows = attn.shape[0]
    vmem = pl.BlockSpec(memory_space=pltpu.VMEM)
    return pl.pallas_call(
        functools.partial(scatter_kernel, rates),
        out_shape=[
            jax.ShapeDtypeStruct(attn.shape, jnp.float32),
            jax.ShapeDtypeStruct(mlp.shape, jnp.float32),
        ],
        in_specs=[vmem] * 3,
        out_specs=[vmem] * 2,
        scratch_shapes=[
            pltpu.VMEM((4, rows, attn.shape[2]), jnp.bfloat16),
            pltpu.VMEM((2, rows, mlp.shape[2]), jnp.bfloat16),
            dma((count,)),
            dma((6,)),
        ],
        compiler_params=pltpu.CompilerParams(
            collective_id=collective_id, has_side_effects=True, vmem_limit_bytes=32 * MIB
        ),
        name="scatter_rows",
    )(orth, attn, mlp)


def head_mask(shape):
    return lax.broadcasted_iota(jnp.int32, shape, 1) < HD


def spans(length):
    return [(start, min(256, length - start)) for start in range(0, length, 256)]


def attend_forward(q_ref, k_ref, v_ref, o_ref, lse_ref, turned, value_turned, after=lambda head: None):
    length = q_ref.shape[0]
    value_turned[...] = v_ref[...].astype(jnp.float32).T.astype(jnp.bfloat16)
    keys = k_ref[...]
    for head in range(2):
        mine = head_mask(keys.shape) if head == 0 else ~head_mask(keys.shape)
        head_keys = jnp.where(mine, keys, jnp.zeros_like(keys))
        for start, size in spans(length):
            stop = start + size
            scores = contract(head_keys[0:stop], q_ref[start:stop, :], 1, 1)
            key_at = lax.broadcasted_iota(jnp.int32, (stop, size), 0)
            query_at = lax.broadcasted_iota(jnp.int32, (stop, size), 1) + start
            scores = jnp.where(key_at <= query_at, scores, -1e30)
            peak = jnp.max(scores, axis=0, keepdims=True)
            weights = jnp.exp(scores - peak)
            total = jnp.sum(weights, axis=0, keepdims=True)
            mixed = contract(
                value_turned[head * HD : (head + 1) * HD, 0:stop], weights.astype(jnp.bfloat16), 1, 0
            )
            turned[head * HD : (head + 1) * HD, start:stop] = mixed / total
            lse_ref[head : head + 1, start:stop] = peak + jnp.log(total)
        after(head)
    o_ref[...] = turned[...].T.astype(jnp.bfloat16)


def attend_backward(q_ref, k_ref, v_ref, o_ref, do_ref, lse_ref, dq_ref, dk_ref, dv_ref, turned):
    length = q_ref.shape[0]
    keys, values = k_ref[...], v_ref[...]
    key_turned = keys.astype(jnp.float32).T.astype(jnp.bfloat16)
    inner = (o_ref[...].astype(jnp.float32) * do_ref[...].astype(jnp.float32)).T
    mask = head_mask(keys.shape)
    turned[...] = jnp.zeros_like(turned)
    for start, size in spans(length):
        stop = start + size
        both_k, both_v = [], []
        for head in range(2):
            mine = mask[start:stop] if head == 0 else ~mask[start:stop]
            head_keys = jnp.where(mine, keys[start:stop], 0)
            head_values = jnp.where(mine, values[start:stop], 0)
            head_inner = jnp.sum(inner[head * HD : (head + 1) * HD, start:], axis=0, keepdims=True)
            scores = contract(head_keys, q_ref[start:, :], 1, 1)
            grad_prob = contract(head_values, do_ref[start:, :], 1, 1)
            key_at = lax.broadcasted_iota(jnp.int32, scores.shape, 0)
            query_at = lax.broadcasted_iota(jnp.int32, scores.shape, 1)
            scores = jnp.where(key_at <= query_at, scores, -1e30)
            prob = jnp.exp(scores - lse_ref[head : head + 1, start:])
            grad_scores = (prob * (grad_prob - head_inner)).astype(jnp.bfloat16)
            both_v.append(contract(prob.astype(jnp.bfloat16), do_ref[start:, :], 1, 0))
            both_k.append(contract(grad_scores, q_ref[start:, :], 1, 0))
            turned[head * HD : (head + 1) * HD, start:] += contract(
                key_turned[head * HD : (head + 1) * HD, start:stop], grad_scores, 1, 0
            )
        pick = mask[start:stop]
        dk_ref[start:stop, :] = jnp.where(pick, both_k[0], both_k[1]).astype(jnp.bfloat16)
        dv_ref[start:stop, :] = jnp.where(pick, both_v[0], both_v[1]).astype(jnp.bfloat16)
    dq_ref[...] = (turned[...].T * (1.0 / math.sqrt(HD))).astype(jnp.bfloat16)


def pairs_forward(queries, keys, values):
    length, width = queries.shape
    block = pl.BlockSpec((length, 2 * HD), lambda i: (0, i))
    stat = pl.BlockSpec((None, 2, length), lambda i: (i, 0, 0))
    return pl.pallas_call(
        attend_forward,
        grid=(width // (2 * HD),),
        out_shape=[
            jax.ShapeDtypeStruct((length, width), jnp.bfloat16),
            jax.ShapeDtypeStruct((width // (2 * HD), 2, length), jnp.float32),
        ],
        in_specs=[block] * 3,
        out_specs=[block, stat],
        scratch_shapes=[pltpu.VMEM((2 * HD, length), jnp.float32), pltpu.VMEM((2 * HD, length), jnp.bfloat16)],
        compiler_params=pltpu.CompilerParams(vmem_limit_bytes=48 * MIB),
        name="attend_forward",
    )(queries, keys, values)


def pairs_backward(queries, keys, values, attended, grad_attended, stats):
    length, width = queries.shape
    block = pl.BlockSpec((length, 2 * HD), lambda i: (0, i))
    stat = pl.BlockSpec((None, 2, length), lambda i: (i, 0, 0))
    return pl.pallas_call(
        attend_backward,
        grid=(width // (2 * HD),),
        out_shape=[jax.ShapeDtypeStruct((length, width), jnp.bfloat16)] * 3,
        in_specs=[block] * 5 + [stat],
        out_specs=[block] * 3,
        scratch_shapes=[pltpu.VMEM((2 * HD, length), jnp.float32)],
        compiler_params=pltpu.CompilerParams(vmem_limit_bytes=48 * MIB),
        name="attend_backward",
    )(queries, keys, values, attended, grad_attended, stats)


class Gathering:
    def __init__(self, a_ref, b_ref, a_out, b_out, send, recv, local):
        self.own = (a_ref, b_ref)
        self.outs = (a_out, b_out)
        self.send, self.recv, self.local = send, recv, local
        self.rows = a_ref.shape[0]
        self.dp, self.core, self.z, self.y, self.x = place()
        self.x_peer = self.dp + 1 - 2 * self.x
        self.y_peer = self.dp + 2 - 4 * self.y

    def block(self, side, index):
        return self.outs[side].at[pl.ds(pl.multiple_of(index * self.rows, self.rows), self.rows)]

    def copy(self, kind, side, index, own, target):
        src = self.own[side] if own else self.block(side, index)
        return remote(
            src, self.block(side, index), self.send.at[kind, index // 4], self.recv.at[side, index], target, self.core
        )

    def arrived(self, side, index):
        block = self.block(side, index)
        remote(block, block, self.send.at[0, 0], self.recv.at[side, index], self.dp, self.core).wait_recv()

    def at(self, level, y_off, x_off):
        y = self.y + y_off * (1 - 2 * self.y)
        x = self.x + x_off * (1 - 2 * self.x)
        return level * 4 + y * 2 + x

    def line(self, level, own, action):
        index = self.at(level, 0, 0)

        @pl.when((self.z < LINE - 1) & (level <= self.z))
        def _():
            for side in range(2):
                action(self.copy(side, side, index, own, self.dp + 4))

        @pl.when((self.z > 0) & (level >= self.z))
        def _():
            for side in range(2):
                action(self.copy(2 + side, side, index, own, self.dp - 4))

        for side in range(2):
            action(self.copy(4 + side, side, index, own, self.x_peer))
            action(self.copy(6 + side, side, index, own, self.y_peer))

    def relays(self, level):
        return (
            (0, self.at(level, 0, 1), self.copy(8, 0, self.at(level, 0, 1), False, self.y_peer)),
            (1, self.at(level, 1, 0), self.copy(9, 1, self.at(level, 1, 0), False, self.x_peer)),
        )

    def by_distance(self, distance, action):
        if distance == 0:
            action(self.z)
            return

        @pl.when(self.z >= distance)
        def _():
            action(self.z - distance)

        @pl.when(self.z + distance < LINE)
        def _():
            action(self.z + distance)

    def local_copies(self):
        return [
            pltpu.make_async_copy(self.own[side], self.block(side, self.dp), self.local.at[side]) for side in range(2)
        ]

    def begin(self):
        self.line(self.z, True, lambda copy: copy.start())
        for copy in self.local_copies():
            copy.start()

    def onward(self, distance):
        def action(level):
            for side in range(2):
                self.arrived(side, self.at(level, 0, 0))
            self.line(level, False, lambda copy: copy.start())

        self.by_distance(distance, action)

    def relay(self, distance):
        def action(level):
            for side, index, copy in self.relays(level):
                self.arrived(side, index)
                copy.start()

        self.by_distance(distance, action)

    def finish(self):
        for level in range(LINE):
            self.arrived(1, self.at(level, 0, 1))
            self.arrived(0, self.at(level, 1, 0))
            for side in range(2):
                self.arrived(side, self.at(level, 1, 1))
        for copy in self.local_copies():
            copy.wait()

    def drain(self):
        for level in range(LINE):
            self.line(level, False, lambda copy: copy.wait_send())
            for _, _, copy in self.relays(level):
                copy.wait_send()


def norm_tile(values, gain, bias):
    centered = values - jnp.mean(values, axis=-1, keepdims=True)
    inverse = lax.rsqrt(jnp.mean(centered * centered, axis=-1, keepdims=True) + 1e-05)
    return centered * inverse * gain + bias


def tiles(count, rows, action):
    @pl.loop(0, count // rows)
    def _(i):
        action(pl.ds(pl.multiple_of(i * rows, rows), rows))


def front_kernel(
    tokens, vec, qk_shard, vo_shard, f0_shard, f1_shard, p0_shard, p1_shard,
    qk_all, vo_all, f0, f1, p0, p1, first, q, k, v, o, lse, middle, second, act, slope,
    turned, mixed, partial, partial_other, pre,
    send, recv, local, swap_send, swap_recv,
):
    dp, core, z, y, x = place()
    length = tokens.shape[0]
    width = q.shape[1]
    chunk = length // 4
    barrier = pltpu.get_barrier_semaphore()
    greet(barrier, dp + 1 - 2 * x, core)
    greet(barrier, dp + 2 - 4 * y, core)
    greet(barrier, dp, 1 - core)

    @pl.when(z > 0)
    def _():
        greet(barrier, dp - 4, core)

    @pl.when(z < LINE - 1)
    def _():
        greet(barrier, dp + 4, core)

    pl.semaphore_wait(barrier, 3 + (z + 2) // 3 + (5 - z) // 3)

    rounds = [
        Gathering(a, b, a_out, b_out, send.at[i], recv.at[i], local.at[i])
        for i, (a, b, a_out, b_out) in enumerate(
            ((qk_shard, vo_shard, qk_all, vo_all), (f0_shard, f1_shard, f0, f1), (p0_shard, p1_shard, p0, p1))
        )
    ]
    rounds[0].begin()

    def norm_one(part):
        tile = norm_tile(tokens[part, :].astype(jnp.float32), vec[0:1, :], vec[1:2, :])
        first[part, :] = tile.astype(jnp.bfloat16)

    tiles(length, 16, norm_one)
    rounds[0].onward(1)
    rounds[0].relay(0)
    rounds[0].onward(2)
    rounds[0].relay(1)
    rounds[0].onward(3)
    rounds[0].relay(2)
    rounds[0].relay(3)
    rounds[1].begin()
    rounds[0].finish()

    mine = pl.ds(pl.multiple_of(core * width, width), width)
    scale = 1.0 / math.sqrt(HD)
    q[...] = ((contract(first[...], qk_all[:, 0:width], 1, 0) + vec[4:5, mine]) * scale).astype(jnp.bfloat16)
    k[...] = contract(first[...], qk_all[:, width:], 1, 0).astype(jnp.bfloat16)
    v[...] = (contract(first[...], vo_all[:, 0:width], 1, 0) + vec[5:6, mine]).astype(jnp.bfloat16)

    def step(index):
        if index == 1:
            rounds[1].onward(1)
            rounds[1].relay(0)
        if index == 2:
            rounds[1].onward(2)
            rounds[1].relay(1)
        if index == 3:
            rounds[1].onward(3)
            rounds[1].relay(2)
        if index == 4:
            rounds[1].relay(3)
            rounds[2].begin()
        if index == 6:
            rounds[2].onward(1)
            rounds[2].relay(0)
        if index == 7:
            rounds[2].onward(2)
            rounds[2].relay(1)
        if index == 8:
            rounds[2].onward(3)
            rounds[2].relay(2)
        if index == 9:
            rounds[2].relay(3)

    for pair in range(width // (2 * HD)):
        lanes = pl.ds(pair * 2 * HD, 2 * HD)
        attend_forward(
            q.at[:, lanes], k.at[:, lanes], v.at[:, lanes], o.at[:, lanes], lse.at[pair], turned, mixed,
            lambda head: step(2 * pair + head),
        )

    def swap_copy(i):
        part = pl.ds(i * chunk, chunk)
        return remote(partial.at[part], partial_other.at[part], swap_send.at[i], swap_recv.at[i], dp, 1 - core)

    for i in range(4):
        part = pl.ds(i * chunk, chunk)
        partial[part, :] = contract(o[part, :], vo_all[:, width:], 1, 1).astype(jnp.bfloat16)
        swap_copy(i).start()
    step(6)
    rounds[1].finish()
    for i in range(4):
        swap_copy(i).wait_recv()

        def norm_two(part):
            rows = pl.ds(pl.multiple_of(i * chunk + part.start, 16), part.size)
            total = partial[rows, :].astype(jnp.float32) + partial_other[rows, :].astype(jnp.float32)
            tile = tokens[rows, :].astype(jnp.float32) + total + vec[6:7, :]
            middle[rows, :] = tile
            second[rows, :] = norm_tile(tile, vec[2:3, :], vec[3:4, :]).astype(jnp.bfloat16)

        tiles(chunk, 16, norm_two)
        rows = pl.ds(i * chunk, chunk)
        for side, weight in enumerate((f0, f1)):
            pre[:, side * D : (side + 1) * D] = contract(second[rows, :], weight[...], 1, 0)

        def curve(part):
            rows = pl.ds(pl.multiple_of(i * chunk + part.start, 16), part.size)
            for side in range(2):
                columns = pl.ds(side * D, D)
                value = pre[part, columns] + vec[pl.ds(8 + 2 * core + side, 1), :]
                square = value * value
                root = math.sqrt(2.0 / math.pi)
                bent = jnp.tanh(value * (root + root * 0.044715 * square))
                half = 0.5 + 0.5 * bent
                act[rows, columns] = (value * half).astype(jnp.bfloat16)
                inner = root + (3.0 * root * 0.044715) * square
                slope[rows, columns] = (half + (0.5 * value) * (1.0 - bent * bent) * inner).astype(jnp.bfloat16)

        tiles(chunk, 16, curve)
        step(7 + i)
    rounds[2].finish()
    for i in range(4):
        swap_copy(i).wait_send()
    for gathering in rounds:
        gathering.drain()


def front(tokens, vec, shards, collective_id):
    dma = pltpu.SemaphoreType.DMA
    low = jnp.bfloat16
    count = lax.axis_size("dp")
    length = tokens.shape[0]
    width = shards[0].shape[1] // 2
    hidden = 2 * D
    shape = jax.ShapeDtypeStruct
    vmem = pl.BlockSpec(memory_space=pltpu.VMEM)
    return pl.pallas_call(
        front_kernel,
        out_shape=[shape((count * shard.shape[0], shard.shape[1]), low) for shard in shards]
        + [shape((length, D), low)]
        + [shape((length, width), low)] * 4
        + [
            shape((width // (2 * HD), 2, length), jnp.float32),
            shape((length, D), jnp.float32),
            shape((length, D), low),
            shape((length, hidden), low),
            shape((length, hidden), low),
        ],
        in_specs=[vmem] * 8,
        out_specs=[vmem] * 16,
        scratch_shapes=[
            pltpu.VMEM((2 * HD, length), jnp.float32),
            pltpu.VMEM((2 * HD, length), low),
            pltpu.VMEM((length, D), low),
            pltpu.VMEM((length, D), low),
            pltpu.VMEM((length // 4, hidden), jnp.float32),
            dma((3, 10, LINE)),
            dma((3, 2, count)),
            dma((3, 2)),
            dma((4,)),
            dma((4,)),
        ],
        compiler_params=pltpu.CompilerParams(
            collective_id=collective_id, has_side_effects=True, vmem_limit_bytes=56 * MIB
        ),
        name="front",
    )(tokens, vec, *shards)


def norm_back_tile(grad, gain, values):
    centered = values - jnp.mean(values, axis=-1, keepdims=True)
    inverse = lax.rsqrt(jnp.mean(centered * centered, axis=-1, keepdims=True) + 1e-05)
    normed = centered * inverse
    scaled = grad * gain
    back = inverse * (
        scaled
        - jnp.mean(scaled, axis=-1, keepdims=True)
        - normed * jnp.mean(scaled * normed, axis=-1, keepdims=True)
    )
    return back, normed


def shifted(part, start):
    return pl.ds(pl.multiple_of(start + part.start, 16), part.size)


def column_sum(value):
    return jnp.sum(value, axis=0, keepdims=True)


def mlp_back_kernel(
    cot, vec, f0, f1, p0, p1, vo, o, middle, second, act, slope,
    out, grad_mid, do, ga, gb, sums,
    du, partial, other, m_partial, m_other, low, turned, acc, swap_send, swap_recv,
):
    dp = lax.axis_index("dp")
    core = lax.axis_index("tensor")
    length = cot.shape[0]
    width = o.shape[1]
    chunk = length // 4
    barrier = pltpu.get_barrier_semaphore()
    greet(barrier, dp, 1 - core)
    pl.semaphore_wait(barrier, 1)
    acc[...] = jnp.zeros_like(acc)
    sums[...] = jnp.zeros_like(sums)

    def swap_copy(kind, i):
        part = pl.ds(i * chunk, chunk)
        src, dst = ((partial, other), (m_partial, m_other))[kind]
        return remote(src.at[part], dst.at[part], swap_send.at[kind, i], swap_recv.at[kind, i], dp, 1 - core)

    sides = ((0, f0, p0), (1, f1, p1))
    for i in range(4):
        rows = pl.ds(i * chunk, chunk)
        for side, _, weight in sides:
            columns = pl.ds(side * D, D)
            value = contract(cot[rows, :], weight[...], 1, 0) * slope[rows, columns].astype(jnp.float32)
            value = value.astype(jnp.bfloat16)
            du[rows, columns] = value
            sums[4 + side : 5 + side, :] += column_sum(value.astype(jnp.float32))
        partial[rows, :] = (
            contract(du[rows, 0:D], f0[...], 1, 1) + contract(du[rows, D:], f1[...], 1, 1)
        ).astype(jnp.bfloat16)
        swap_copy(0, i).start()
    for i in range(4):
        rows = pl.ds(i * chunk, chunk)
        m_partial[rows, :] = (
            contract(act[rows, 0:D], p0[...], 1, 1) + contract(act[rows, D:], p1[...], 1, 1)
        ).astype(jnp.bfloat16)
        swap_copy(1, i).start()

    def outer(left, right, target, start):
        size = right.shape[1]
        for block in range(D // 256):
            rows = pl.ds(block * 256, 256)
            value = contract(left[rows, :], right[...], 1, 0)
            target[rows, start : start + size] = value.astype(jnp.bfloat16)
            row = 6 if size == D else 7
            sums[row : row + 1, 0:size] += column_sum(value * value)

    turned[...] = cot[...].T
    for side in range(2):
        outer(turned, act.at[:, side * D : (side + 1) * D], gb, width + side * D)
    for i in range(4):
        swap_copy(0, i).wait_recv()

        def back(part):
            rows = shifted(part, i * chunk)
            grad = partial[rows, :].astype(jnp.float32) + other[rows, :].astype(jnp.float32)
            outgoing = cot[rows, :].astype(jnp.float32)
            value, normed = norm_back_tile(grad, vec[2:3, :], middle[rows, :])
            value = value + outgoing
            grad_mid[rows, :] = value
            low[rows, :] = value.astype(jnp.bfloat16)
            acc[0] += grad * normed
            acc[1] += grad
            acc[2] += value
            acc[3] += outgoing

        tiles(chunk, 16, back)
        rows = pl.ds(i * chunk, chunk)
        do[rows, :] = contract(low[rows, :], vo[:, width:], 1, 0).astype(jnp.bfloat16)
    for row in range(4):
        sums[row : row + 1, :] = column_sum(acc[row])
    turned[...] = low[...].T
    outer(turned, o, gb, 0)
    turned[...] = second[...].T
    for side in range(2):
        outer(turned, du.at[:, side * D : (side + 1) * D], ga, side * D)
    for i in range(4):
        swap_copy(1, i).wait_recv()

        def finish(part):
            rows = shifted(part, i * chunk)
            total = m_partial[rows, :].astype(jnp.float32) + m_other[rows, :].astype(jnp.float32)
            out[rows, :] = (middle[rows, :] + total + vec[7:8, :]).astype(jnp.bfloat16)

        tiles(chunk, 16, finish)
    for kind in range(2):
        for i in range(4):
            swap_copy(kind, i).wait_send()


def mlp_back(cot, vec, f0, f1, p0, p1, vo, o, middle, second, act, slope, collective_id):
    dma = pltpu.SemaphoreType.DMA
    low = jnp.bfloat16
    length, hidden = act.shape
    width = o.shape[1]
    shape = jax.ShapeDtypeStruct
    vmem = pl.BlockSpec(memory_space=pltpu.VMEM)
    return pl.pallas_call(
        mlp_back_kernel,
        out_shape=[
            shape((length, D), low),
            shape((length, D), jnp.float32),
            shape((length, width), low),
            shape((D, hidden), low),
            shape((D, width + hidden), low),
            shape((8, D), jnp.float32),
        ],
        in_specs=[vmem] * 12,
        out_specs=[vmem] * 6,
        scratch_shapes=[pltpu.VMEM((length, hidden), low)]
        + [pltpu.VMEM((length, D), low)] * 5
        + [pltpu.VMEM((D, length), low), pltpu.VMEM((4, 16, D), jnp.float32), dma((2, 4)), dma((2, 4))],
        compiler_params=pltpu.CompilerParams(
            collective_id=collective_id, has_side_effects=True, vmem_limit_bytes=56 * MIB
        ),
        name="mlp_back",
    )(cot, vec, f0, f1, p0, p1, vo, o, middle, second, act, slope)


def attn_back_kernel(
    noise_scale, batch, clip,
    tokens, vec, first, q, k, v, o, do, lse, qk_all, vo_all, grad_mid, ga_early, gb_early, sums, included,
    attn_mom, mlp_mom, attn_noise, mlp_noise,
    grad_in, attn_out, mlp_out, vec_out, owned,
    dqk, dv, ga_late, gb_late, head_turned, turned, partial, other, acc, square, factors,
    diag_a, diag_b, x_a, x_b, y_a, y_b, up_a, up_b, down_a, down_b, attn_low, mlp_low, vec_send, vec_recv,
    send, recv, vec_sems, gather_send, gather_recv, swap_send, swap_recv, small,
):
    dp, core, z, y, x = place()
    rows = attn_mom.shape[0]
    width = attn_mom.shape[2]
    wide = mlp_mom.shape[2]
    length = tokens.shape[0]
    chunk = length // 4
    x_peer, y_peer = dp + 1 - 2 * x, dp + 2 - 4 * y
    count = ga_early.shape[0] // rows
    z_near = dp + 4 - 8 * (z % 2)
    z_far = dp + 8 - 16 * (z // 2)
    late_a, late_b = ga_late.shape[1], gb_late.shape[1]
    owned[...] = jnp.zeros_like(owned)
    greet_all(dp, core, count, True)

    def at(ref, block):
        return ref.at[pl.ds(pl.multiple_of(block * rows, rows), rows)]

    def go(kind, level, src, dst, target):
        return remote(src, dst, send.at[kind, level], recv.at[kind, level], target, core)

    half = z // 2
    order = (3 - 3 * half, 2 - half, 1 - z + 4 * half, z)
    parts_a = ((0, late_a, ga_late), (late_a, ga_early.shape[1], ga_early))
    parts_b = ((0, late_b, gb_late), (late_b, gb_early.shape[1], gb_early))

    def x_block(level):
        return level * 4 + y * 2 + 1 - x

    def y_block(level):
        return level * 4 + (1 - y) * 2 + x

    def diag_copies(level, early):
        block = level * 4 + (1 - y) * 2 + 1 - x
        kind = 0 if early else 10
        start_a, size_a, grad_a = parts_a[early]
        start_b, size_b, grad_b = parts_b[early]
        return (
            go(kind, level, at(grad_a, block), diag_a.at[level, :, pl.ds(start_a, size_a)], y_peer),
            go(kind + 1, level, at(grad_b, block), diag_b.at[level, :, pl.ds(start_b, size_b)], x_peer),
        )

    def own_copies(level, early):
        kind = 2 if early else 12
        start_a, size_a, grad_a = parts_a[early]
        start_b, size_b, grad_b = parts_b[early]
        return (
            go(kind, level, at(grad_b, x_block(level)), x_b.at[level, :, pl.ds(start_b, size_b)], x_peer),
            go(kind + 1, level, at(grad_a, y_block(level)), y_a.at[level, :, pl.ds(start_a, size_a)], y_peer),
        )

    def sum_copies(level):
        return (
            go(4, level, diag_a.at[level], x_a.at[level], x_peer),
            go(5, level, diag_b.at[level], y_b.at[level], y_peer),
        )

    def up_copies(level):
        return (
            go(6, level, x_a.at[level], up_a.at[level], dp + 4),
            go(7, level, x_b.at[level], up_b.at[level], dp + 4),
        )

    def down_copies(level):
        return (
            go(8, level, x_a.at[level], down_a.at[level], dp - 4),
            go(9, level, x_b.at[level], down_b.at[level], dp - 4),
        )

    def small_copy(index):
        src, dst, target = (
            (square.at[0], square.at[1], (dp, 1 - core)),
            (factors.at[0], factors.at[1], (x_peer, core)),
            (factors.at[0], factors.at[2], (y_peer, core)),
        )[index]
        return remote(src, dst, small.at[0, index], small.at[1, index], *target)

    def vec_copy(stage):
        target = ((dp, 1 - core), (x_peer, core), (y_peer, core), (z_near, core), (z_far, core))[stage]
        return remote(vec_send.at[stage], vec_recv.at[stage], vec_sems.at[0, stage], vec_sems.at[1, stage], *target)

    def vec_step(stage):
        vec_copy(stage).wait_recv()
        total = vec_send[stage] + vec_recv[stage]
        if stage < 4:
            vec_send[stage + 1] = total
            vec_copy(stage + 1).start()
        else:
            vec_out[...] = total

    def swap_copy(i):
        part = pl.ds(i * chunk, chunk)
        return remote(partial.at[part], other.at[part], swap_send.at[i], swap_recv.at[i], dp, 1 - core)

    for level in order:
        for copy in diag_copies(level, 1):
            copy.start()
    for level in order:
        for copy in own_copies(level, 1):
            copy.start()

    acc[...] = jnp.zeros_like(acc)
    for pair in range(width // (2 * HD)):
        lanes = pl.ds(pair * 2 * HD, 2 * HD)
        attend_backward(
            q.at[:, lanes], k.at[:, lanes], v.at[:, lanes], o.at[:, lanes], do.at[:, lanes], lse.at[pair],
            dqk.at[:, lanes], dqk.at[:, pl.ds(width + pair * 2 * HD, 2 * HD)], dv.at[:, lanes], head_turned,
        )
    for i in range(4):
        part = pl.ds(i * chunk, chunk)
        partial[part, :] = (
            contract(dqk[part, :], qk_all[...], 1, 1) + contract(dv[part, :], vo_all[:, 0:width], 1, 1)
        ).astype(jnp.bfloat16)
        swap_copy(i).start()
    turned[...] = first[...].T
    squares = jnp.zeros((1, 1), jnp.float32)
    for right, target in ((dqk, ga_late), (dv, gb_late)):
        for block in range(D // 256):
            part = pl.ds(block * 256, 256)
            value = contract(turned[part, :], right[...], 1, 0)
            target[part, :] = value.astype(jnp.bfloat16)
            squares = squares + jnp.sum(column_sum(value * value), axis=1, keepdims=True)
    for level in order:
        for copy in diag_copies(level, 0):
            copy.start()
    for level in order:
        for copy in own_copies(level, 0):
            copy.start()
    bias_q = column_sum(dqk[:, 0:width].astype(jnp.float32))
    bias_v = column_sum(dv[...].astype(jnp.float32))
    for value in (sums[6:7, :], sums[7:8, :]):
        squares = squares + jnp.sum(value, axis=1, keepdims=True)
    for value in (bias_q, bias_v, sums[4:5, :], sums[5:6, :]):
        squares = squares + jnp.sum(value * value, axis=1, keepdims=True)
    square[0] = jnp.broadcast_to(squares, square.shape[1:])
    small_copy(0).start()

    for i in range(4):
        swap_copy(i).wait_recv()

        def back(part):
            here = shifted(part, i * chunk)
            grad = partial[here, :].astype(jnp.float32) + other[here, :].astype(jnp.float32)
            value, normed = norm_back_tile(grad, vec[0:1, :], tokens[here, :].astype(jnp.float32))
            grad_in[here, :] = (grad_mid[here, :] + value).astype(jnp.bfloat16)
            acc[0] += grad * normed
            acc[1] += grad

        tiles(chunk, 16, back)
    gain_one, bias_one = column_sum(acc[0]), column_sum(acc[1])
    shared = jnp.zeros((1, 1), jnp.float32)
    for value in (gain_one, bias_one, sums[0:1, :], sums[1:2, :], sums[2:3, :], sums[3:4, :]):
        shared = shared + jnp.sum(value * value, axis=1, keepdims=True)
    small_copy(0).wait_recv()
    norm = jnp.sqrt(square[0, 0:1, 0:1] + square[1, 0:1, 0:1] + shared)
    factor = included[0:1, 0:1] * jnp.minimum(1.0, clip / (norm + 1e-06))
    factors[0] = jnp.broadcast_to(factor, factors.shape[1:])
    small_copy(1).start()
    small_copy(2).start()
    leading = factor * (1 - core).astype(jnp.float32)
    vec_send[0] = jnp.zeros(vec_send.shape[1:], jnp.float32)
    mine = pl.ds(pl.multiple_of(core * width, width), width)
    for row, value in ((0, gain_one), (1, bias_one), (2, sums[0:1, :]), (3, sums[1:2, :]), (6, sums[2:3, :]), (7, sums[3:4, :])):
        vec_send[0, row : row + 1, :] = leading * value
    vec_send[0, 4:5, mine] = factor * bias_q
    vec_send[0, 5:6, mine] = factor * bias_v
    vec_send[0, pl.ds(8 + 2 * core, 1), :] = factor * sums[4:5, :]
    vec_send[0, pl.ds(9 + 2 * core, 1), :] = factor * sums[5:6, :]
    vec_copy(0).start()
    small_copy(1).wait_recv()
    small_copy(2).wait_recv()
    factor_x, factor_y = factors[1, 0:1, 0:1], factors[2, 0:1, 0:1]

    def weigh(dst, parts, block, scale_dst, terms):
        @pl.loop(0, rows // 16)
        def _(i):
            part = pl.ds(pl.multiple_of(i * 16, 16), 16)
            for start, size, grad in parts:
                columns = pl.ds(start, size)
                own = grad[pl.ds(pl.multiple_of(block * rows + i * 16, 16), 16), :].astype(jnp.float32)
                total = factor * own
                for scale, ref in ((scale_dst, dst),) + terms:
                    value = ref[part, columns].astype(jnp.float32)
                    total = total + (value if scale is None else scale * value)
                dst[part, columns] = total.astype(dst.dtype)

    vec_step(0)
    for level in order:
        to_x, to_y = sum_copies(level)
        for early in range(2):
            wait_a, wait_b = diag_copies(level, early)
            wait_a.wait_recv()
            wait_b.wait_recv()
        weigh(diag_a.at[level], parts_a, x_block(level), factor_y, ())
        to_x.start()
        weigh(diag_b.at[level], parts_b, y_block(level), factor_x, ())
        to_y.start()
    vec_step(1)

    def arrivals(level):
        for copy in own_copies(level, 0) + own_copies(level, 1) + sum_copies(level):
            copy.wait_recv()

    for index in range(3):
        level = order[index]
        block = level * 4 + y * 2 + x
        arrivals(level)

        def combine(extra_a, extra_b):
            weigh(x_a.at[level], parts_a, block, None, ((factor_y, y_a.at[level]),) + extra_a)
            weigh(x_b.at[level], parts_b, block, factor_x, ((None, y_b.at[level]),) + extra_b)

        @pl.when(level > z)
        def _():
            @pl.when(z > 0)
            def _():
                for copy in up_copies(level):
                    copy.wait_recv()
                combine(((None, up_a.at[level]),), ((None, up_b.at[level]),))

            @pl.when(z == 0)
            def _():
                combine((), ())

            for copy in up_copies(level):
                copy.start()

        @pl.when(level < z)
        def _():
            @pl.when(z < LINE - 1)
            def _():
                for copy in down_copies(level):
                    copy.wait_recv()
                combine(((None, down_a.at[level]),), ((None, down_b.at[level]),))

            @pl.when(z == LINE - 1)
            def _():
                combine((), ())

            for copy in down_copies(level):
                copy.start()

        vec_step(2 + index)
    arrivals(z)

    @pl.when(z > 0)
    def _():
        for copy in up_copies(z):
            copy.wait_recv()

    @pl.when(z == 0)
    def _():
        up_a[0] = jnp.zeros(up_a.shape[1:], up_a.dtype)
        up_b[0] = jnp.zeros(up_b.shape[1:], up_b.dtype)

    @pl.when(z < LINE - 1)
    def _():
        for copy in down_copies(z):
            copy.wait_recv()

    @pl.when(z == LINE - 1)
    def _():
        down_a[LINE - 1] = jnp.zeros(down_a.shape[1:], down_a.dtype)
        down_b[LINE - 1] = jnp.zeros(down_b.shape[1:], down_b.dtype)

    side_a = ((None, x_a), (factor_y, y_a), (None, up_a), (None, down_a))
    side_b = ((factor_x, x_b), (None, y_b), (None, up_b), (None, down_b))
    pieces = (
        (4, side_a, 2 * width, ga_early, 0),
        (5, side_b, 2 * width, gb_early, width),
        (0, side_a, 0, ga_late, 0),
        (1, side_a, width, ga_late, width),
        (2, side_b, 0, gb_late, 0),
        (3, side_b, width, gb_early, 0),
    )
    for slot, terms, column, grad, grad_column in pieces:
        size = width if slot < 4 else wide
        columns = pl.ds(column, size)
        low = attn_low.at[slot] if slot < 4 else mlp_low.at[slot - 4]

        @pl.loop(0, rows // 16)
        def _(i):
            part = pl.ds(pl.multiple_of(i * 16, 16), 16)
            own = grad[pl.ds(pl.multiple_of(dp * rows + i * 16, 16), 16), pl.ds(grad_column, size)]
            total = factor * own.astype(jnp.float32)
            for scale, ref in terms:
                value = ref[z, part, columns].astype(jnp.float32)
                total = total + (value if scale is None else scale * value)
            if slot < 4:
                moment = 0.5 * attn_mom[part, slot, :] + (total + noise_scale * attn_noise[part, slot, :]) / batch
                attn_out[part, slot, :] = moment
            else:
                moment = 0.5 * mlp_mom[part, slot - 4, :] + (total + noise_scale * mlp_noise[part, slot - 4, :]) / batch
                mlp_out[part, slot - 4, :] = moment
            low[part, :] = moment.astype(low.dtype)

        owner = OWNERS[slot]
        target = at(owned, dp).at[:, 0:size]

        @pl.when(dp != owner)
        def _():
            remote(low, target, gather_send.at[slot], gather_recv.at[dp], owner, core).start()

        @pl.when(dp == owner)
        def _():
            pltpu.make_async_copy(low, target, gather_send.at[slot]).start()

    for slot in range(6):
        size = width if slot < 4 else wide
        low = attn_low.at[slot] if slot < 4 else mlp_low.at[slot - 4]
        owner = OWNERS[slot]

        @pl.when(dp != owner)
        def _():
            remote(low, low, gather_send.at[slot], gather_recv.at[dp], owner, core).wait_send()

        @pl.when(dp == owner)
        def _():
            pltpu.make_async_copy(low, at(owned, dp).at[:, 0:size], gather_send.at[slot]).wait()
            for source in range(count):
                if source != owner:
                    block = at(owned, source).at[:, 0:size]
                    remote(block, block, gather_send.at[slot], gather_recv.at[source], source, core).wait_recv()

    for index in range(3):
        small_copy(index).wait_send()
    for i in range(4):
        swap_copy(i).wait_send()
    for stage in range(5):
        vec_copy(stage).wait_send()
    for level in range(LINE):
        for early in range(2):
            for copy in diag_copies(level, early) + own_copies(level, early):
                copy.wait_send()
        for copy in sum_copies(level):
            copy.wait_send()

        @pl.when(level > z)
        def _():
            for copy in up_copies(level):
                copy.wait_send()

        @pl.when(level < z)
        def _():
            for copy in down_copies(level):
                copy.wait_send()


def attn_back(
    tokens, vec, first, q, k, v, o, do, lse, qk_all, vo_all, grad_mid, ga_early, gb_early, sums, included,
    attn_mom, mlp_mom, attn_noise, mlp_noise, noise_scale, batch, clip, collective_id,
):
    dma = pltpu.SemaphoreType.DMA
    low = jnp.bfloat16
    count = lax.axis_size("dp")
    length = tokens.shape[0]
    rows, _, width = attn_mom.shape
    wide = mlp_mom.shape[2]
    side = 2 * width + wide
    shape = jax.ShapeDtypeStruct
    vmem = pl.BlockSpec(memory_space=pltpu.VMEM)
    scratch = pltpu.VMEM
    return pl.pallas_call(
        functools.partial(attn_back_kernel, noise_scale, batch, clip),
        out_shape=[
            shape((length, D), low),
            shape(attn_mom.shape, jnp.float32),
            shape(mlp_mom.shape, jnp.float32),
            shape(vec.shape, jnp.float32),
            shape((D, wide), low),
        ],
        in_specs=[vmem] * 20,
        out_specs=[vmem] * 5,
        scratch_shapes=[
            scratch((length, 2 * width), low),
            scratch((length, width), low),
            scratch((D, 2 * width), low),
            scratch((D, width), low),
            scratch((2 * HD, length), jnp.float32),
            scratch((D, length), low),
            scratch((length, D), low),
            scratch((length, D), low),
            scratch((2, 16, D), jnp.float32),
            scratch((2, 8, 128), jnp.float32),
            scratch((3, 8, 128), jnp.float32),
        ]
        + [scratch((LINE, rows, side), low)] * 10
        + [
            scratch((4, rows, width), low),
            scratch((2, rows, wide), low),
            scratch((5,) + vec.shape, jnp.float32),
            scratch((5,) + vec.shape, jnp.float32),
            dma((14, LINE)),
            dma((14, LINE)),
            dma((2, 5)),
            dma((6,)),
            dma((count,)),
            dma((4,)),
            dma((4,)),
            dma((2, 3)),
        ],
        compiler_params=pltpu.CompilerParams(
            collective_id=collective_id, has_side_effects=True, vmem_limit_bytes=60 * MIB
        ),
        name="attn_back",
    )(
        tokens, vec, first, q, k, v, o, do, lse, qk_all, vo_all, grad_mid, ga_early, gb_early, sums, included,
        attn_mom, mlp_mom, attn_noise, mlp_noise,
    )


def placed(piece, start, total_size):
    return lax.dynamic_update_slice_in_dim(jnp.zeros((total_size,), jnp.float32), piece, start, 0)


def other_core(value):
    return lax.ppermute(value, "tensor", [(0, 1), (1, 0)])


def newton(owned):
    gram = contract(owned, owned, 1, 1)
    gram = gram + other_core(gram)
    rows = gram.shape[0]
    diagonal = lax.broadcasted_iota(jnp.int32, (rows, rows), 0) == lax.broadcasted_iota(
        jnp.int32, (rows, rows), 1
    )
    scale = 1.0 / (jnp.sqrt(jnp.sum(jnp.where(diagonal, gram, 0.0))) + 1e-07)
    current = gram * (scale * scale)

    def product(left, right, fine):
        if fine:
            return jnp.dot(left, right, precision=lax.Precision.HIGH)
        return contract(left.astype(jnp.bfloat16), right.astype(jnp.bfloat16), 1, 0)

    factor = None
    for iteration in range(NS_ITERS):
        fine = iteration >= NS_ITERS - 2
        rest = COEF_B * current + COEF_C * product(current, current, fine)
        if factor is None:
            factor = jnp.where(diagonal, COEF_A, 0.0) + rest
        else:
            factor = COEF_A * factor + product(rest, factor, fine)
        if iteration < NS_ITERS - 1:
            once = COEF_A * current + product(rest, current, fine)
            current = COEF_A * once + product(rest, once, fine)
    return contract((factor * scale).astype(jnp.bfloat16), owned, 1, 0).astype(jnp.bfloat16)


def body(
    fast,
    tokens,
    cotangent,
    inclusion,
    attn_weights,
    mlp_weights,
    attn_momentum,
    mlp_momentum,
    attn_noise,
    mlp_noise,
    vectors,
    vector_momentum,
    vector_noise,
):
    dp_count = lax.axis_size("dp")
    dp_index = lax.axis_index("dp")
    halves = lax.axis_size("tensor")
    tensor_index = lax.axis_index("tensor")
    head_width = D // halves
    hidden_width = FF // halves
    query_scale = 1.0 / math.sqrt(HD)
    clip = 1.5 * D * math.sqrt(LEN)
    sigma = 0.05 * math.sqrt(dp_count) / D
    batch = 0.75 * dp_count
    attn_shard = attn_weights.astype(jnp.bfloat16)
    mlp_shard = mlp_weights.astype(jnp.bfloat16)
    rows = attn_shard.shape[0]
    shards = (
        attn_shard[:, 0:2].reshape(rows, 2 * head_width),
        attn_shard[:, 2:4].reshape(rows, 2 * head_width),
        mlp_shard[:, 0, 0:D],
        mlp_shard[:, 0, D:],
        mlp_shard[:, 1, 0:D],
        mlp_shard[:, 1, D:],
    )
    noise_scale = sigma * clip
    if fast:
        vec = vectors.reshape(-1, D)
        (
            query_key, value_out, fc_one, fc_two, pr_one, pr_two,
            first_low, queries, key_rows, value_rows, attended_low, stats, middle, second_low, activation_low, slope,
        ) = front(tokens[0], vec, shards, 0)
        result, grad_mid, grad_attended, early_a, early_b, sums = mlp_back(
            cotangent[0], vec, fc_one, fc_two, pr_one, pr_two, value_out, attended_low, middle, second_low,
            activation_low, slope, 1,
        )
        grad_in, attn_moment, mlp_moment, vector_summed, owned = attn_back(
            tokens[0], vec, first_low, queries, key_rows, value_rows, attended_low, grad_attended, stats,
            query_key, value_out, grad_mid, early_a, early_b, sums,
            jnp.broadcast_to(inclusion[0].astype(jnp.float32), (8, 128)),
            attn_momentum, mlp_momentum, attn_noise, mlp_noise, noise_scale, batch, clip, 2,
        )
        vector_summed = vector_summed.reshape(-1)
    else:
        gain_one = vectors[0:D]
        bias_one = vectors[D : 2 * D]
        gain_two = vectors[2 * D : 3 * D]
        bias_two = vectors[3 * D : 4 * D]
        query_bias = lax.dynamic_slice_in_dim(vectors, 4 * D + tensor_index * head_width, head_width)
        value_bias = lax.dynamic_slice_in_dim(vectors, 5 * D + tensor_index * head_width, head_width)
        attn_bias = vectors[6 * D : 7 * D]
        mlp_bias = vectors[7 * D : 8 * D]
        hidden_bias = lax.dynamic_slice_in_dim(
            vectors, 8 * D + tensor_index * hidden_width, hidden_width
        )
        inputs = tokens[0].astype(jnp.float32)
        length = inputs.shape[0]
        first, normed_one, inverse_one = layer_norm(inputs, gain_one, bias_one)

        def both_cores(partial):
            low = partial.astype(jnp.bfloat16)
            return low.astype(jnp.float32) + other_core(low).astype(jnp.float32)

        query_key, value_out, fc_one, fc_two, pr_one, pr_two = (
            lax.all_gather(shard, "dp", axis=0, tiled=True) for shard in shards
        )
        value_weight, out_weight = value_out[:, 0:head_width], value_out[:, head_width:]
        first_low = first.astype(jnp.bfloat16)
        qk = contract(first_low, query_key, 1, 0)
        queries = ((qk[:, 0:head_width] + query_bias) * query_scale).astype(jnp.bfloat16)
        key_rows = qk[:, head_width:].astype(jnp.bfloat16)
        value_rows = (contract(first_low, value_weight, 1, 0) + value_bias).astype(jnp.bfloat16)
        attended_low, stats = pairs_forward(queries, key_rows, value_rows)
        middle = inputs + both_cores(contract(attended_low, out_weight, 1, 1)) + attn_bias
        second_low = layer_norm(middle, gain_two, bias_two)[0].astype(jnp.bfloat16)
        pre_act = contract(second_low, jnp.concatenate([fc_one, fc_two], axis=1), 1, 0) + hidden_bias
        activation, gelu_back = jax.vjp(gelu_tanh, pre_act)
        activation_low = activation.astype(jnp.bfloat16)
        slope = gelu_back(jnp.ones_like(pre_act))[0]
        _, normed_two, inverse_two = layer_norm(middle, gain_two, bias_two)
        fc_weight = jnp.concatenate([fc_one, fc_two], axis=1)
        pr_weight = jnp.concatenate([pr_one, pr_two], axis=1)
        result = middle + both_cores(contract(activation_low, pr_weight, 1, 1)) + mlp_bias
        cot_low = cotangent[0]
        grad_out = cot_low.astype(jnp.float32)
        d_pr = contract(cot_low, activation_low, 0, 0)
        grad_pre = (contract(cot_low, pr_weight, 1, 0) * slope.astype(jnp.float32)).astype(jnp.bfloat16)
        d_fc = contract(second_low, grad_pre, 0, 0)
        d_hidden_bias = jnp.sum(grad_pre.astype(jnp.float32), axis=0)
        grad_two = both_cores(contract(grad_pre, fc_weight, 1, 1))
        grad_mid = grad_out + norm_back(grad_two, gain_two, normed_two, inverse_two)
        d_gain_two = jnp.sum(grad_two * normed_two, axis=0)
        d_bias_two = jnp.sum(grad_two, axis=0)
        d_attn_bias = jnp.sum(grad_mid, axis=0)
        d_mlp_bias = jnp.sum(grad_out, axis=0)
        mid_low = grad_mid.astype(jnp.bfloat16)
        d_out = contract(mid_low, attended_low, 0, 0)
        grad_attended = contract(mid_low, out_weight, 1, 0).astype(jnp.bfloat16)
        grad_q, grad_k, grad_v = pairs_backward(
            queries, key_rows, value_rows, attended_low, grad_attended, stats
        )
        grad_qk = jnp.concatenate([grad_q, grad_k], axis=1)
        d_query_key = contract(first_low, grad_qk, 0, 0)
        d_value = contract(first_low, grad_v, 0, 0)
        d_query_bias = jnp.sum(grad_q.astype(jnp.float32), axis=0)
        d_value_bias = jnp.sum(grad_v.astype(jnp.float32), axis=0)
        grad_one = both_cores(contract(grad_qk, query_key, 1, 1) + contract(grad_v, value_weight, 1, 1))
        grad_in = grad_mid + norm_back(grad_one, gain_one, normed_one, inverse_one)
        d_gain_one = jnp.sum(grad_one * normed_one, axis=0)
        d_bias_one = jnp.sum(grad_one, axis=0)
        split_square = sum(
            jnp.sum(value * value)
            for value in (d_query_key, d_value, d_out, d_fc, d_pr, d_query_bias, d_value_bias, d_hidden_bias)
        )
        split_tile = jnp.broadcast_to(split_square, (8, 128))
        total_square = (split_tile + other_core(split_tile))[0, 0] + sum(
            jnp.sum(value * value)
            for value in (d_gain_one, d_bias_one, d_gain_two, d_bias_two, d_attn_bias, d_mlp_bias)
        )
        factor = inclusion[0].astype(jnp.float32) * jnp.minimum(
            1.0, clip / (jnp.sqrt(total_square) + 1e-06)
        )
        leading = (tensor_index == 0).astype(jnp.float32)
        vector_grad = (
            jnp.concatenate(
                [
                    leading * d_gain_one,
                    leading * d_bias_one,
                    leading * d_gain_two,
                    leading * d_bias_two,
                    placed(d_query_bias, tensor_index * head_width, D),
                    placed(d_value_bias, tensor_index * head_width, D),
                    leading * d_attn_bias,
                    leading * d_mlp_bias,
                    placed(d_hidden_bias, tensor_index * hidden_width, FF),
                ]
            )
            * factor
        )
        result, grad_in = result.astype(jnp.bfloat16), grad_in.astype(jnp.bfloat16)
        attn_grad = jnp.concatenate([d_query_key, d_value, d_out], axis=1) * factor
        mlp_grad = jnp.stack([d_fc, d_pr], axis=1) * factor
        attn_summed = lax.psum_scatter(attn_grad, "dp", scatter_dimension=0, tiled=True)
        mlp_summed = lax.psum_scatter(mlp_grad, "dp", scatter_dimension=0, tiled=True)
        attn_summed = attn_summed.reshape(rows, 4, head_width)
        vector_summed = lax.psum(vector_grad, ("dp", "tensor"))
        attn_moment = 0.5 * attn_momentum + (attn_summed + noise_scale * attn_noise) / batch
        mlp_moment = 0.5 * mlp_momentum + (mlp_summed + noise_scale * mlp_noise) / batch
        owners = jnp.array([slot * dp_count // 6 for slot in range(6)])
        full_attn = lax.all_gather(attn_moment.astype(jnp.bfloat16), "dp", axis=0, tiled=True)
        full_mlp = lax.all_gather(mlp_moment.astype(jnp.bfloat16), "dp", axis=0, tiled=True)
        attn_pick = (owners[0:4] == dp_index)[None, :, None]
        mlp_pick = (owners[4:6] == dp_index)[None, :, None]
        mine_attn = jnp.sum(jnp.where(attn_pick, full_attn, 0), axis=1)
        mine_mlp = jnp.sum(jnp.where(mlp_pick, full_mlp, 0), axis=1)
        owned = jnp.pad(mine_attn, ((0, 0), (0, hidden_width - head_width))) + mine_mlp
    vector_moment = 0.5 * vector_momentum + (vector_summed + noise_scale * vector_noise) / batch
    vector_rate = 0.2 * math.sqrt(dp_count / LEN)
    vectors_new = vectors - vector_rate * vector_moment
    orthogonal = newton(owned)
    rates = (0.5, 0.5, 0.5, 0.5 * max(1.0, math.sqrt(LEN) / 8.0), 0.5 * math.sqrt(FF / D), 0.5)
    if fast:
        attn_new, mlp_new = scatter_rows(orthogonal, attn_weights, mlp_weights, rates, 3)
    else:
        attn_rows = jnp.where(attn_pick, orthogonal[:, None, 0:head_width], 0)
        mlp_rows = jnp.where(mlp_pick, orthogonal[:, None, :], 0)
        attn_orth = lax.psum_scatter(attn_rows, "dp", scatter_dimension=0, tiled=True)
        mlp_orth = lax.psum_scatter(mlp_rows, "dp", scatter_dimension=0, tiled=True)
        attn_new = attn_weights - jnp.array(rates[0:4])[None, :, None] * attn_orth
        mlp_new = mlp_weights - jnp.array(rates[4:6])[None, :, None] * mlp_orth
    return (
        result[None],
        grad_in[None],
        attn_moment,
        mlp_moment,
        attn_new,
        mlp_new,
        vector_moment,
        vectors_new,
    )


def solution(mesh):
    fast = mesh.shape["dp"] == 16 and mesh.shape["tensor"] == 2
    in_specs = (
        P("dp", None, None),
        P("dp", None, None),
        P("dp"),
        P("dp", None, "tensor"),
        P("dp", None, "tensor"),
        P("dp", None, "tensor"),
        P("dp", None, "tensor"),
        P("dp", None, "tensor"),
        P("dp", None, "tensor"),
        P(),
        P(),
        P(),
    )
    out_specs = (
        P("dp", None, None),
        P("dp", None, None),
        P("dp", None, "tensor"),
        P("dp", None, "tensor"),
        P("dp", None, "tensor"),
        P("dp", None, "tensor"),
        P(),
        P(),
    )
    return jax.shard_map(
        functools.partial(body, fast), mesh=mesh, in_specs=in_specs, out_specs=out_specs, check_vma=False
    )
```

```python
import functools
import math

import jax
import jax.numpy as jnp
from jax import lax
from jax.experimental import pallas as pl
from jax.experimental.pallas import tpu as pltpu
from jax.sharding import PartitionSpec as P

D = 768
HD = 64
FF = 3072
LEN = 960
NS_ITERS = 5


COEF_A = 3.4445
COEF_B = -4.775
COEF_C = 2.0315


def gelu_tanh(values):
    return jax.nn.gelu(values, approximate=True)


def layer_norm(values, norm_gain, norm_bias):
    centered = values - jnp.mean(values, axis=-1, keepdims=True)
    inverse = lax.rsqrt(jnp.mean(centered * centered, axis=-1, keepdims=True) + 1e-05)
    normed = centered * inverse
    return (normed * norm_gain + norm_bias, normed, inverse)


def norm_back(grad_out, norm_gain, normed, inverse):
    scaled = grad_out * norm_gain
    return inverse * (
        scaled
        - jnp.mean(scaled, axis=-1, keepdims=True)
        - normed * jnp.mean(scaled * normed, axis=-1, keepdims=True)
    )


def contract(left, right, left_dim, right_dim):
    return lax.dot_general(
        left, right, (((left_dim,), (right_dim,)), ((), ())), preferred_element_type=jnp.float32
    )


MESH = pl.DeviceIdType.MESH
MIB = 1 << 20
LINE = 4
OWNERS = (7, 8, 6, 9, 4, 11)


def place():
    dp = lax.axis_index("dp")
    core = lax.axis_index("tensor")
    z = dp // 4
    y = dp % 4 // 2
    x = dp % 2
    return dp, core, z, y, x


def remote(src, dst, send, recv, dp, core):
    return pltpu.make_async_remote_copy(
        src_ref=src, dst_ref=dst, send_sem=send, recv_sem=recv, device_id=(dp, core), device_id_type=MESH
    )


def greet(barrier, dp, core):
    pl.semaphore_signal(barrier, inc=1, device_id=(dp, core), device_id_type=MESH)


def greet_all(dp, core, count, with_core):
    barrier = pltpu.get_barrier_semaphore()
    for step in range(1, count):
        greet(barrier, (dp + step) % count, core)
    if with_core:
        greet(barrier, dp, 1 - core)
    pl.semaphore_wait(barrier, count - 1 + int(with_core))


class Staging:
    def __init__(self, sems):
        self.sems = sems
        self.count = 0
        self.waiting = {}
        self.out = []

    def move(self, src, dst):
        copy = pltpu.make_async_copy(src, dst, self.sems.at[self.count])
        self.count += 1
        copy.start()
        return copy

    def fetch(self, name, src, dst):
        self.waiting[name] = self.move(src, dst)

    def need(self, *names):
        for name in names:
            if name in self.waiting:
                self.waiting.pop(name).wait()

    def keep(self, src, dst):
        self.out.append(self.move(src, dst))

    def finish(self):
        for copy in self.out:
            copy.wait()


def gram_kernel(owned_in, *refs):
    results, (gram, scale), kept, held, (own, sems) = refs[:4], refs[4:6], refs[6:10], refs[10:14], refs[14:]
    dp = lax.axis_index("dp")
    stage = Staging(sems)
    stage.fetch("own", owned_in, own)
    for index in range(4):
        stage.fetch(index, results[index], held[index])
    stage.need("own")
    rows = gram.shape[0]

    def fill(size):
        total = contract(own[0, :, 0:size], own[0, :, 0:size], 1, 1) + contract(own[1, :, 0:size], own[1, :, 0:size], 1, 1)
        square = jnp.zeros((1, 1), jnp.float32)
        tile = 256
        here = lax.broadcasted_iota(jnp.int32, (tile, tile), 0) == lax.broadcasted_iota(jnp.int32, (tile, tile), 1)
        for start in range(0, rows, tile):
            corner = jnp.where(here, total[start : start + tile, start : start + tile], 0.0)
            square = square + jnp.sum(jnp.sum(corner, axis=0, keepdims=True), axis=1, keepdims=True)
        inverse = 1.0 / (jnp.sqrt(square) + 1e-07)
        scale[...] = jnp.broadcast_to(inverse, scale.shape)
        gram[...] = total * (inverse * inverse)

    for index in range(4):
        stage.need(index)
        stage.keep(held[index], kept[index])
    narrow = own.shape[2] // 4
    attn = (dp == OWNERS[0]) | (dp == OWNERS[1]) | (dp == OWNERS[2]) | (dp == OWNERS[3])
    mlp = (dp == OWNERS[4]) | (dp == OWNERS[5])

    @pl.when(attn)
    def _():
        fill(narrow)

    @pl.when(mlp)
    def _():
        fill(own.shape[2])

    stage.finish()


def gram_of(owned, results):
    rows = owned.shape[1]
    shape = jax.ShapeDtypeStruct
    vmem = pl.BlockSpec(memory_space=pltpu.VMEM)
    anywhere = pl.BlockSpec(memory_space=pl.ANY)
    return pl.pallas_call(
        gram_kernel,
        out_shape=[shape((rows, rows), jnp.float32), shape((8, 128), jnp.float32)]
        + [shape(value.shape, value.dtype) for value in results],
        in_specs=[anywhere] * 5,
        out_specs=[vmem] * 2 + [anywhere] * 4,
        scratch_shapes=[pltpu.VMEM(value.shape, value.dtype) for value in results]
        + [pltpu.VMEM(owned.shape, owned.dtype), pltpu.SemaphoreType.DMA((9,))],
        compiler_params=pltpu.CompilerParams(vmem_limit_bytes=60 * MIB),
        name="gram",
    )(owned, *results)


def scatter_kernel(
    rates, factor, scale, owned_in, attn_in, mlp_in, attn_new, mlp_new,
    own, attn, mlp, orth, attn_low, mlp_low, relayed, send, recv, relay_send, relay_recv, stage_sems,
):
    dp, core, z, y, x = place()
    rows = attn.shape[0]
    count = orth.shape[0] // rows
    stage = Staging(stage_sems)
    stage.fetch("own", owned_in.at[0], own)
    stage.fetch("attn", attn_in, attn)
    stage.fetch("mlp", mlp_in, mlp)
    greet_all(dp, core, count, False)
    stage.need("own")

    def at(ref, block):
        return ref.at[pl.ds(pl.multiple_of(block * rows, rows), rows)]

    def low_of(slot):
        return attn_low.at[slot] if slot < 4 else mlp_low.at[slot - 4]

    def size_of(slot):
        return attn.shape[2] if slot < 4 else mlp.shape[2]

    def deliver(slot, target):
        owner = OWNERS[slot]
        src = at(orth, target).at[:, 0 : size_of(slot)]
        level = target // 4
        across_x, across_y = target % 2 != owner % 2, target % 4 // 2 != owner % 4 // 2
        if slot >= 4 and level != owner // 4 and across_x != across_y:
            stop = owner // 4 * 4 + target % 4
            return remote(src, relayed.at[level], send.at[target], relay_recv.at[level], stop, core)
        return remote(src, low_of(slot), send.at[target], recv.at[slot], target, core)

    def onward(slot, action):
        owner = OWNERS[slot]
        for stop in range(owner // 4 * 4, owner // 4 * 4 + 4):
            if (stop % 2 != owner % 2) != (stop % 4 // 2 != owner % 4 // 2):

                @pl.when(dp == stop)
                def _():
                    for level in levels_of(owner):
                        action(level, level * 4 + stop % 4)

    def relay_copy(slot, level, target):
        return remote(relayed.at[level], low_of(slot), relay_send.at[level], recv.at[slot], target, core)

    def levels_of(owner):
        return (3, 2, 0) if owner // 4 == 1 else (0, 1, 3)

    def turns(target, owner):
        return (target % 2 != owner % 2) != (target % 4 // 2 != owner % 4 // 2)

    pieces = ((0, 5), (5, 11), (11, 16))
    for slot in range(6):
        owner = OWNERS[slot]
        size = size_of(slot)

        @pl.when(dp == owner)
        def _():
            for first, last in pieces if owner // 4 > 1 else pieces[::-1]:
                part = pl.ds(first * rows, (last - first) * rows)
                value = contract(factor[part, :], own[:, 0:size], 1, 0) * scale[0:1, 0:1]
                orth[part, 0:size] = value.astype(orth.dtype)
                far = [target for target in range(first, last) if target // 4 != owner // 4]
                far.sort(key=lambda target: (levels_of(owner).index(target // 4), not turns(target, owner)))
                for target in far:
                    deliver(slot, target).start()
            pltpu.make_async_copy(at(orth, owner).at[:, 0:size], low_of(slot), recv.at[slot]).start()
            for target in range(owner // 4 * 4, owner // 4 * 4 + 4):
                if target != owner:
                    deliver(slot, target).start()

    for slot in (4, 5):

        def pass_on(level, target):
            block = relayed.at[level]
            remote(block, block, relay_send.at[level], relay_recv.at[level], dp, core).wait_recv()
            relay_copy(slot, level, target).start()

        onward(slot, pass_on)

    stage.need("attn", "mlp")
    for slot in range(6):
        owner = OWNERS[slot]
        low = low_of(slot)

        @pl.when(dp != owner)
        def _():
            remote(low, low, send.at[0], recv.at[slot], owner, core).wait_recv()

        @pl.when(dp == owner)
        def _():
            pltpu.make_async_copy(low, low, recv.at[slot]).wait()

        @pl.loop(0, rows // 16)
        def _(i):
            part = pl.ds(pl.multiple_of(i * 16, 16), 16)
            step = rates[slot] * low[part, :].astype(jnp.float32)
            if slot < 4:
                attn_new[part, slot, :] = attn[part, slot, :] - step
            else:
                mlp_new[part, slot - 4, :] = mlp[part, slot - 4, :] - step

    for slot in range(6):
        owner = OWNERS[slot]

        @pl.when(dp == owner)
        def _():
            for target in range(count):
                if target != owner:
                    deliver(slot, target).wait_send()

    for slot in (4, 5):
        onward(slot, lambda level, target: relay_copy(slot, level, target).wait_send())


def scatter_rows(factor, scale, owned, attn, mlp, rates, collective_id):
    dma = pltpu.SemaphoreType.DMA
    count = lax.axis_size("dp")
    rows = attn.shape[0]
    shape = jax.ShapeDtypeStruct
    vmem = pl.BlockSpec(memory_space=pltpu.VMEM)
    anywhere = pl.BlockSpec(memory_space=pl.ANY)
    return pl.pallas_call(
        functools.partial(scatter_kernel, rates),
        out_shape=[shape(attn.shape, jnp.float32), shape(mlp.shape, jnp.float32)],
        in_specs=[vmem] * 2 + [anywhere] * 3,
        out_specs=[vmem] * 2,
        scratch_shapes=[
            pltpu.VMEM(owned.shape[1:], owned.dtype),
            pltpu.VMEM(attn.shape, attn.dtype),
            pltpu.VMEM(mlp.shape, mlp.dtype),
            pltpu.VMEM(owned.shape[1:], owned.dtype),
            pltpu.VMEM((4, rows, attn.shape[2]), jnp.bfloat16),
            pltpu.VMEM((2, rows, mlp.shape[2]), jnp.bfloat16),
            pltpu.VMEM((LINE, rows, mlp.shape[2]), jnp.bfloat16),
            dma((count,)),
            dma((6,)),
            dma((LINE,)),
            dma((LINE,)),
            dma((3,)),
        ],
        compiler_params=pltpu.CompilerParams(
            collective_id=collective_id, has_side_effects=True, vmem_limit_bytes=32 * MIB
        ),
        name="scatter_rows",
    )(factor, scale, owned, attn, mlp)


def head_mask(shape):
    return lax.broadcasted_iota(jnp.int32, shape, 1) < HD


def spans(length):
    return [(start, min(256, length - start)) for start in range(0, length, 256)]


def attend_forward(q_ref, k_ref, v_ref, o_ref, lse_ref, turned, value_turned, after=lambda head: None):
    length = q_ref.shape[0]
    value_turned[...] = v_ref[...].astype(jnp.float32).T.astype(jnp.bfloat16)
    keys = k_ref[...]
    for head in range(2):
        mine = head_mask(keys.shape) if head == 0 else ~head_mask(keys.shape)
        head_keys = jnp.where(mine, keys, jnp.zeros_like(keys))
        for start, size in spans(length):
            stop = start + size
            scores = contract(head_keys[0:stop], q_ref[start:stop, :], 1, 1)
            key_at = lax.broadcasted_iota(jnp.int32, (stop, size), 0)
            query_at = lax.broadcasted_iota(jnp.int32, (stop, size), 1) + start
            scores = jnp.where(key_at <= query_at, scores, -1e30)
            peak = jnp.max(scores, axis=0, keepdims=True)
            weights = jnp.exp(scores - peak)
            total = jnp.sum(weights, axis=0, keepdims=True)
            mixed = contract(
                value_turned[head * HD : (head + 1) * HD, 0:stop], weights.astype(jnp.bfloat16), 1, 0
            )
            turned[head * HD : (head + 1) * HD, start:stop] = mixed / total
            lse_ref[head : head + 1, start:stop] = peak + jnp.log(total)
        after(head)
    o_ref[...] = turned[...].T.astype(jnp.bfloat16)


def attend_backward(q_ref, k_ref, v_ref, o_ref, do_ref, lse_ref, dq_ref, dk_ref, dv_ref, turned):
    length = q_ref.shape[0]
    keys, values = k_ref[...], v_ref[...]
    key_turned = keys.astype(jnp.float32).T.astype(jnp.bfloat16)
    inner = (o_ref[...].astype(jnp.float32) * do_ref[...].astype(jnp.float32)).T
    mask = head_mask(keys.shape)
    turned[...] = jnp.zeros_like(turned)
    for start, size in spans(length):
        stop = start + size
        both_k, both_v = [], []
        for head in range(2):
            mine = mask[start:stop] if head == 0 else ~mask[start:stop]
            head_keys = jnp.where(mine, keys[start:stop], 0)
            head_values = jnp.where(mine, values[start:stop], 0)
            head_inner = jnp.sum(inner[head * HD : (head + 1) * HD, start:], axis=0, keepdims=True)
            scores = contract(head_keys, q_ref[start:, :], 1, 1)
            grad_prob = contract(head_values, do_ref[start:, :], 1, 1)
            key_at = lax.broadcasted_iota(jnp.int32, scores.shape, 0)
            query_at = lax.broadcasted_iota(jnp.int32, scores.shape, 1)
            scores = jnp.where(key_at <= query_at, scores, -1e30)
            prob = jnp.exp(scores - lse_ref[head : head + 1, start:])
            grad_scores = (prob * (grad_prob - head_inner)).astype(jnp.bfloat16)
            both_v.append(contract(prob.astype(jnp.bfloat16), do_ref[start:, :], 1, 0))
            both_k.append(contract(grad_scores, q_ref[start:, :], 1, 0))
            turned[head * HD : (head + 1) * HD, start:] += contract(
                key_turned[head * HD : (head + 1) * HD, start:stop], grad_scores, 1, 0
            )
        pick = mask[start:stop]
        dk_ref[start:stop, :] = jnp.where(pick, both_k[0], both_k[1]).astype(jnp.bfloat16)
        dv_ref[start:stop, :] = jnp.where(pick, both_v[0], both_v[1]).astype(jnp.bfloat16)
    dq_ref[...] = (turned[...].T * (1.0 / math.sqrt(HD))).astype(jnp.bfloat16)


def pairs_forward(queries, keys, values):
    length, width = queries.shape
    block = pl.BlockSpec((length, 2 * HD), lambda i: (0, i))
    stat = pl.BlockSpec((None, 2, length), lambda i: (i, 0, 0))
    return pl.pallas_call(
        attend_forward,
        grid=(width // (2 * HD),),
        out_shape=[
            jax.ShapeDtypeStruct((length, width), jnp.bfloat16),
            jax.ShapeDtypeStruct((width // (2 * HD), 2, length), jnp.float32),
        ],
        in_specs=[block] * 3,
        out_specs=[block, stat],
        scratch_shapes=[pltpu.VMEM((2 * HD, length), jnp.float32), pltpu.VMEM((2 * HD, length), jnp.bfloat16)],
        compiler_params=pltpu.CompilerParams(vmem_limit_bytes=48 * MIB),
        name="attend_forward",
    )(queries, keys, values)


def pairs_backward(queries, keys, values, attended, grad_attended, stats):
    length, width = queries.shape
    block = pl.BlockSpec((length, 2 * HD), lambda i: (0, i))
    stat = pl.BlockSpec((None, 2, length), lambda i: (i, 0, 0))
    return pl.pallas_call(
        attend_backward,
        grid=(width // (2 * HD),),
        out_shape=[jax.ShapeDtypeStruct((length, width), jnp.bfloat16)] * 3,
        in_specs=[block] * 5 + [stat],
        out_specs=[block] * 3,
        scratch_shapes=[pltpu.VMEM((2 * HD, length), jnp.float32)],
        compiler_params=pltpu.CompilerParams(vmem_limit_bytes=48 * MIB),
        name="attend_backward",
    )(queries, keys, values, attended, grad_attended, stats)


NORM_ROWS = 240


class Gathering:
    def __init__(self, a_ref, b_ref, a_out, b_out, send, recv, local):
        self.own = (a_ref, b_ref)
        self.outs = (a_out, b_out)
        self.send, self.recv, self.local = send, recv, local
        self.rows = a_ref.shape[0]
        self.dp, self.core, self.z, self.y, self.x = place()
        self.x_peer = self.dp + 1 - 2 * self.x
        self.y_peer = self.dp + 2 - 4 * self.y

    def block(self, side, index):
        return self.outs[side].at[pl.ds(pl.multiple_of(index * self.rows, self.rows), self.rows)]

    def copy(self, kind, side, index, own, target):
        src = self.own[side] if own else self.block(side, index)
        return remote(
            src, self.block(side, index), self.send.at[kind, index // 4], self.recv.at[side, index], target, self.core
        )

    def arrived(self, side, index):
        block = self.block(side, index)
        remote(block, block, self.send.at[0, 0], self.recv.at[side, index], self.dp, self.core).wait_recv()

    def at(self, level, y_off, x_off):
        y = self.y + y_off * (1 - 2 * self.y)
        x = self.x + x_off * (1 - 2 * self.x)
        return level * 4 + y * 2 + x

    def line(self, level, own, action):
        index = self.at(level, 0, 0)

        @pl.when((self.z < LINE - 1) & (level <= self.z))
        def _():
            for side in range(2):
                action(self.copy(side, side, index, own, self.dp + 4))

        @pl.when((self.z > 0) & (level >= self.z))
        def _():
            for side in range(2):
                action(self.copy(2 + side, side, index, own, self.dp - 4))

        for side in range(2):
            action(self.copy(4 + side, side, index, own, self.x_peer))
            action(self.copy(6 + side, side, index, own, self.y_peer))

    def relays(self, level):
        return (
            (0, self.at(level, 0, 1), self.copy(8, 0, self.at(level, 0, 1), False, self.y_peer)),
            (1, self.at(level, 1, 0), self.copy(9, 1, self.at(level, 1, 0), False, self.x_peer)),
        )

    def by_distance(self, distance, action):
        if distance == 0:
            action(self.z)
            return

        @pl.when(self.z >= distance)
        def _():
            action(self.z - distance)

        @pl.when(self.z + distance < LINE)
        def _():
            action(self.z + distance)

    def local_copies(self):
        return [
            pltpu.make_async_copy(self.own[side], self.block(side, self.dp), self.local.at[side]) for side in range(2)
        ]

    def begin(self):
        self.line(self.z, True, lambda copy: copy.start())
        for copy in self.local_copies():
            copy.start()

    def onward(self, distance):
        def action(level):
            for side in range(2):
                self.arrived(side, self.at(level, 0, 0))
            self.line(level, False, lambda copy: copy.start())

        self.by_distance(distance, action)

    def relay(self, distance):
        def action(level):
            for side, index, copy in self.relays(level):
                self.arrived(side, index)
                copy.start()

        self.by_distance(distance, action)

    def finish(self):
        for level in range(LINE):
            self.arrived(1, self.at(level, 0, 1))
            self.arrived(0, self.at(level, 1, 0))
            for side in range(2):
                self.arrived(side, self.at(level, 1, 1))
        for copy in self.local_copies():
            copy.wait()

    def drain(self):
        for level in range(LINE):
            self.line(level, False, lambda copy: copy.wait_send())
            for _, _, copy in self.relays(level):
                copy.wait_send()


def norm_tile(values, gain, bias):
    centered = values - jnp.mean(values, axis=-1, keepdims=True)
    inverse = lax.rsqrt(jnp.mean(centered * centered, axis=-1, keepdims=True) + 1e-05)
    return centered * inverse * gain + bias


def tiles(count, rows, action):
    @pl.loop(0, count // rows)
    def _(i):
        action(pl.ds(pl.multiple_of(i * rows, rows), rows))


def front_kernel(
    tokens_in, vec_in, attn_in, mlp_in,
    qk_out, vo_out, f0_out, f1_out, p0, p1, first_out, q_out, k_out, v_out, o_out, lse, middle_out, second_out, act_out,
    slope_out, vec,
    tokens, qk_all, vo_all, f0, f1, first, q, k, v, o, middle, second, act, slope,
    turned, mixed, partial, partial_other, pre, attn, mlp, qk_shard, vo_shard, f0_shard, f1_shard, p0_shard, p1_shard,
    send, recv, local, swap_send, swap_recv, stage_sems,
):
    dp, core, z, y, x = place()
    length = tokens.shape[0]
    width = q.shape[1]
    chunk = length // 4
    stage = Staging(stage_sems)
    stage.fetch("attn", attn_in, attn)
    stage.fetch("tokens", tokens_in, tokens)
    stage.fetch("mlp", mlp_in, mlp)
    for row in range(vec.shape[0]):
        for column in range(D // 128):
            at = row * (D // 128) + column
            vec[row : row + 1, column * 128 : (column + 1) * 128] = vec_in[at : at + 1, :]
    stage.need("attn")
    for slot, shard in enumerate((qk_shard, qk_shard, vo_shard, vo_shard)):
        shard[:, slot % 2 * width : (slot % 2 + 1) * width] = attn[:, slot, :].astype(jnp.bfloat16)
    barrier = pltpu.get_barrier_semaphore()
    greet(barrier, dp + 1 - 2 * x, core)
    greet(barrier, dp + 2 - 4 * y, core)
    greet(barrier, dp, 1 - core)

    @pl.when(z > 0)
    def _():
        greet(barrier, dp - 4, core)

    @pl.when(z < LINE - 1)
    def _():
        greet(barrier, dp + 4, core)

    pl.semaphore_wait(barrier, 3 + (z + 2) // 3 + (5 - z) // 3)

    rounds = [
        Gathering(a, b, a_out, b_out, send.at[i], recv.at[i], local.at[i])
        for i, (a, b, a_out, b_out) in enumerate(
            ((qk_shard, vo_shard, qk_all, vo_all), (f0_shard, f1_shard, f0, f1), (p0_shard, p1_shard, p0, p1))
        )
    ]
    rounds[0].begin()
    stage.need("tokens", "mlp")
    for slot, shard in enumerate((f0_shard, f1_shard, p0_shard, p1_shard)):
        shard[...] = mlp[:, slot // 2, slot % 2 * D : (slot % 2 + 1) * D].astype(jnp.bfloat16)

    def norm_one(part):
        tile = norm_tile(tokens[part, :].astype(jnp.float32), vec[0:1, :], vec[1:2, :])
        first[part, :] = tile.astype(jnp.bfloat16)

    tiles(length, NORM_ROWS, norm_one)
    stage.keep(first, first_out)
    rounds[0].onward(1)
    rounds[0].relay(0)
    rounds[0].onward(2)
    rounds[0].relay(1)
    rounds[0].onward(3)
    rounds[0].relay(2)
    rounds[0].relay(3)
    rounds[1].begin()
    rounds[0].finish()
    stage.keep(qk_all, qk_out)
    stage.keep(vo_all, vo_out)

    mine = pl.ds(pl.multiple_of(core * width, width), width)
    scale = 1.0 / math.sqrt(HD)
    q[...] = ((contract(first[...], qk_all[:, 0:width], 1, 0) + vec[4:5, mine]) * scale).astype(jnp.bfloat16)
    k[...] = contract(first[...], qk_all[:, width:], 1, 0).astype(jnp.bfloat16)
    v[...] = (contract(first[...], vo_all[:, 0:width], 1, 0) + vec[5:6, mine]).astype(jnp.bfloat16)

    for value, target in ((q, q_out), (k, k_out), (v, v_out)):
        stage.keep(value, target)

    def step(index):
        if index == 1:
            rounds[1].onward(1)
            rounds[1].relay(0)
        if index == 2:
            rounds[1].onward(2)
            rounds[1].relay(1)
        if index == 3:
            rounds[1].onward(3)
            rounds[1].relay(2)
        if index == 4:
            rounds[1].relay(3)
            rounds[2].begin()
        if index == 6:
            rounds[2].onward(1)
            rounds[2].relay(0)
        if index == 7:
            rounds[2].onward(2)
            rounds[2].relay(1)
        if index == 8:
            rounds[2].onward(3)
            rounds[2].relay(2)
        if index == 9:
            rounds[2].relay(3)

    for pair in range(width // (2 * HD)):
        lanes = pl.ds(pair * 2 * HD, 2 * HD)
        attend_forward(
            q.at[:, lanes], k.at[:, lanes], v.at[:, lanes], o.at[:, lanes], lse.at[pair], turned, mixed,
            lambda head: step(2 * pair + head),
        )

    stage.keep(o, o_out)

    def swap_copy(i):
        part = pl.ds(i * chunk, chunk)
        return remote(partial.at[part], partial_other.at[part], swap_send.at[i], swap_recv.at[i], dp, 1 - core)

    for i in range(4):
        part = pl.ds(i * chunk, chunk)
        partial[part, :] = contract(o[part, :], vo_all[:, width:], 1, 1).astype(jnp.bfloat16)
        swap_copy(i).start()
    step(6)
    rounds[1].finish()
    stage.keep(f0, f0_out)
    stage.keep(f1, f1_out)
    for i in range(4):
        swap_copy(i).wait_recv()

        def norm_two(part):
            rows = pl.ds(pl.multiple_of(i * chunk + part.start, 16), part.size)
            total = partial[rows, :].astype(jnp.float32) + partial_other[rows, :].astype(jnp.float32)
            tile = tokens[rows, :].astype(jnp.float32) + total + vec[6:7, :]
            middle[rows, :] = tile
            second[rows, :] = norm_tile(tile, vec[2:3, :], vec[3:4, :]).astype(jnp.bfloat16)

        tiles(chunk, NORM_ROWS, norm_two)
        rows = pl.ds(i * chunk, chunk)
        for side, weight in enumerate((f0, f1)):
            pre[:, side * D : (side + 1) * D] = contract(second[rows, :], weight[...], 1, 0)

        def curve(part):
            rows = pl.ds(pl.multiple_of(i * chunk + part.start, 16), part.size)
            for side in range(2):
                columns = pl.ds(side * D, D)
                value = pre[part, columns] + vec[pl.ds(8 + 2 * core + side, 1), :]
                square = value * value
                root = math.sqrt(2.0 / math.pi)
                bent = jnp.tanh(value * (root + root * 0.044715 * square))
                half = 0.5 + 0.5 * bent
                act[rows, columns] = (value * half).astype(jnp.bfloat16)
                inner = root + (3.0 * root * 0.044715) * square
                slope[rows, columns] = (half + (0.5 * value) * (1.0 - bent * bent) * inner).astype(jnp.bfloat16)

        tiles(chunk, 48, curve)
        for value, target in ((middle, middle_out), (second, second_out), (act, act_out), (slope, slope_out)):
            stage.keep(value.at[rows], target.at[rows])
        step(7 + i)
    rounds[2].finish()
    for i in range(4):
        swap_copy(i).wait_send()
    for gathering in rounds:
        gathering.drain()
    stage.finish()


def front(tokens, vec, attn, mlp, collective_id):
    dma = pltpu.SemaphoreType.DMA
    low = jnp.bfloat16
    count = lax.axis_size("dp")
    length = tokens.shape[0]
    rows, _, width = attn.shape
    hidden = 2 * D
    shape = jax.ShapeDtypeStruct
    vmem = pl.BlockSpec(memory_space=pltpu.VMEM)
    anywhere = pl.BlockSpec(memory_space=pl.ANY)
    return pl.pallas_call(
        front_kernel,
        out_shape=[shape((count * rows, D), low)] * 6
        + [shape((length, D), low)]
        + [shape((length, width), low)] * 4
        + [
            shape((width // (2 * HD), 2, length), jnp.float32),
            shape((length, D), jnp.float32),
            shape((length, D), low),
            shape((length, hidden), low),
            shape((length, hidden), low),
            shape((vec.shape[0] * 128 // D, D), jnp.float32),
        ],
        in_specs=[anywhere, vmem] + [anywhere] * 2,
        out_specs=[anywhere] * 11 + [vmem] + [anywhere] * 4 + [vmem],
        scratch_shapes=[
            pltpu.VMEM((length, D), low),
            pltpu.VMEM((D, 2 * width), low),
            pltpu.VMEM((D, 2 * width), low),
            pltpu.VMEM((D, D), low),
            pltpu.VMEM((D, D), low),
            pltpu.VMEM((length, D), low),
            pltpu.VMEM((length, width), low),
            pltpu.VMEM((length, width), low),
            pltpu.VMEM((length, width), low),
            pltpu.VMEM((length, width), low),
            pltpu.VMEM((length, D), jnp.float32),
            pltpu.VMEM((length, D), low),
            pltpu.VMEM((length, hidden), low),
            pltpu.VMEM((length, hidden), low),
            pltpu.VMEM((2 * HD, length), jnp.float32),
            pltpu.VMEM((2 * HD, length), low),
            pltpu.VMEM((length, D), low),
            pltpu.VMEM((length, D), low),
            pltpu.VMEM((length // 4, hidden), jnp.float32),
            pltpu.VMEM(attn.shape, jnp.float32),
            pltpu.VMEM(mlp.shape, jnp.float32),
        ]
        + [pltpu.VMEM((rows, D), low)] * 6
        + [
            dma((3, 10, LINE)),
            dma((3, 2, count)),
            dma((3, 2)),
            dma((4,)),
            dma((4,)),
            dma((32,)),
        ],
        compiler_params=pltpu.CompilerParams(
            collective_id=collective_id, has_side_effects=True, vmem_limit_bytes=56 * MIB
        ),
        name="front",
    )(tokens, vec, attn, mlp)


BACK_ROWS = 80


def fold(value):
    return jnp.sum(value.reshape(-1, 8, value.shape[1]), axis=0)


def norm_back_tile(grad, gain, values):
    centered = values - jnp.mean(values, axis=-1, keepdims=True)
    inverse = lax.rsqrt(jnp.mean(centered * centered, axis=-1, keepdims=True) + 1e-05)
    normed = centered * inverse
    scaled = grad * gain
    back = inverse * (
        scaled
        - jnp.mean(scaled, axis=-1, keepdims=True)
        - normed * jnp.mean(scaled * normed, axis=-1, keepdims=True)
    )
    return back, normed


def shifted(part, start):
    return pl.ds(pl.multiple_of(start + part.start, 16), part.size)


def column_sum(value):
    return jnp.sum(value, axis=0, keepdims=True)


def mlp_back_kernel(
    cot_in, vec, f0_in, f1_in, p0_in, p1_in, vo_in, o_in, middle_in, second_in, act_in, slope_in,
    out_out, grad_mid_out, do_out, ga_out, gb_out, go_out, sums,
    cot, f0, f1, p0, p1, wo, o, middle, second, act, slope, out, grad_mid, do, ga, gb, go,
    du, partial, other, m_partial, m_other, low, turned, acc, swap_send, swap_recv, stage_sems,
):
    dp = lax.axis_index("dp")
    core = lax.axis_index("tensor")
    length = cot.shape[0]
    width = o.shape[1]
    chunk = length // 4
    stage = Staging(stage_sems)
    for name, src, dst in (
        ("cot", cot_in, cot), ("p0", p0_in, p0), ("slope", slope_in, slope), ("p1", p1_in, p1), ("f0", f0_in, f0),
        ("f1", f1_in, f1), ("act", act_in, act), ("middle", middle_in, middle),
        ("wo", vo_in.at[:, pl.ds(width, width)], wo), ("o", o_in, o), ("second", second_in, second),
    ):
        stage.fetch(name, src, dst)
    barrier = pltpu.get_barrier_semaphore()
    greet(barrier, dp, 1 - core)
    pl.semaphore_wait(barrier, 1)
    acc[...] = jnp.zeros_like(acc)
    sums[...] = jnp.zeros_like(sums)

    def swap_copy(kind, i):
        part = pl.ds(i * chunk, chunk)
        src, dst = ((partial, other), (m_partial, m_other))[kind]
        return remote(src.at[part], dst.at[part], swap_send.at[kind, i], swap_recv.at[kind, i], dp, 1 - core)

    sides = ((0, f0, p0), (1, f1, p1))
    for i in range(4):
        rows = pl.ds(i * chunk, chunk)
        for side, _, weight in sides:
            columns = pl.ds(side * D, D)
            stage.need("cot", "slope", ("p0", "p1")[side])
            value = contract(cot[rows, :], weight[...], 1, 0) * slope[rows, columns].astype(jnp.float32)
            value = value.astype(jnp.bfloat16)
            du[rows, columns] = value
            sums[4 + side : 5 + side, :] += column_sum(value.astype(jnp.float32))
        stage.need("f0", "f1")
        partial[rows, :] = (
            contract(du[rows, 0:D], f0[...], 1, 1) + contract(du[rows, D:], f1[...], 1, 1)
        ).astype(jnp.bfloat16)
        swap_copy(0, i).start()
    for i in range(4):
        rows = pl.ds(i * chunk, chunk)
        stage.need("act")
        m_partial[rows, :] = (
            contract(act[rows, 0:D], p0[...], 1, 1) + contract(act[rows, D:], p1[...], 1, 1)
        ).astype(jnp.bfloat16)
        swap_copy(1, i).start()

    def outer(left, right, target, start):
        size = right.shape[1]
        for block in range(D // 256):
            rows = pl.ds(block * 256, 256)
            value = contract(left[rows, :], right[...], 1, 0)
            target[rows, start : start + size] = value.astype(jnp.bfloat16)
            row = 6 if size == D else 7
            sums[row : row + 1, 0:size] += column_sum(value * value)

    turned[...] = cot[...].T
    for side in range(2):
        outer(turned, act.at[:, side * D : (side + 1) * D], gb, side * D)
    stage.keep(gb, gb_out)
    stage.need("middle", "wo")
    for i in range(4):
        swap_copy(0, i).wait_recv()

        def back(part):
            rows = shifted(part, i * chunk)
            grad = partial[rows, :].astype(jnp.float32) + other[rows, :].astype(jnp.float32)
            outgoing = cot[rows, :].astype(jnp.float32)
            value, normed = norm_back_tile(grad, vec[2:3, :], middle[rows, :])
            value = value + outgoing
            grad_mid[rows, :] = value
            low[rows, :] = value.astype(jnp.bfloat16)
            acc[0] += fold(grad * normed)
            acc[1] += fold(grad)
            acc[2] += fold(value)
            acc[3] += fold(outgoing)

        tiles(chunk, BACK_ROWS, back)
        rows = pl.ds(i * chunk, chunk)
        do[rows, :] = contract(low[rows, :], wo[...], 1, 0).astype(jnp.bfloat16)
    for row in range(4):
        sums[row : row + 1, :] = column_sum(acc[row])
    stage.keep(grad_mid, grad_mid_out)
    stage.keep(do, do_out)
    turned[...] = low[...].T
    stage.need("o", "second")
    outer(turned, o, go, 0)
    stage.keep(go, go_out)
    turned[...] = second[...].T
    for side in range(2):
        outer(turned, du.at[:, side * D : (side + 1) * D], ga, side * D)
    stage.keep(ga, ga_out)
    for i in range(4):
        swap_copy(1, i).wait_recv()

        def finish(part):
            rows = shifted(part, i * chunk)
            total = m_partial[rows, :].astype(jnp.float32) + m_other[rows, :].astype(jnp.float32)
            out[rows, :] = (middle[rows, :] + total + vec[7:8, :]).astype(jnp.bfloat16)

        tiles(chunk, 48, finish)
        part = pl.ds(i * chunk, chunk)
        stage.keep(out.at[part], out_out.at[part])
    for kind in range(2):
        for i in range(4):
            swap_copy(kind, i).wait_send()
    stage.finish()


def mlp_back(cot, vec, f0, f1, p0, p1, vo, o, middle, second, act, slope, collective_id):
    dma = pltpu.SemaphoreType.DMA
    low = jnp.bfloat16
    length, hidden = act.shape
    width = o.shape[1]
    shape = jax.ShapeDtypeStruct
    vmem = pl.BlockSpec(memory_space=pltpu.VMEM)
    anywhere = pl.BlockSpec(memory_space=pl.ANY)
    scratch = pltpu.VMEM
    return pl.pallas_call(
        mlp_back_kernel,
        out_shape=[
            shape((length, D), low),
            shape((length, D), jnp.float32),
            shape((length, width), low),
            shape((D, hidden), low),
            shape((D, hidden), low),
            shape((D, width), low),
            shape((8, D), jnp.float32),
        ],
        in_specs=[anywhere, vmem] + [anywhere] * 10,
        out_specs=[anywhere] * 6 + [vmem],
        scratch_shapes=[
            scratch((length, D), low),
            scratch((D, D), low),
            scratch((D, D), low),
            scratch((D, D), low),
            scratch((D, D), low),
            scratch((D, width), low),
            scratch((length, width), low),
            scratch((length, D), jnp.float32),
            scratch((length, D), low),
            scratch((length, hidden), low),
            scratch((length, hidden), low),
            scratch((length, D), low),
            scratch((length, D), jnp.float32),
            scratch((length, width), low),
            scratch((D, hidden), low),
            scratch((D, hidden), low),
            scratch((D, width), low),
        ]
        + [pltpu.VMEM((length, hidden), low)]
        + [pltpu.VMEM((length, D), low)] * 5
        + [pltpu.VMEM((D, length), low), pltpu.VMEM((4, 8, D), jnp.float32), dma((2, 4)), dma((2, 4)), dma((24,))],
        compiler_params=pltpu.CompilerParams(
            collective_id=collective_id, has_side_effects=True, vmem_limit_bytes=60 * MIB
        ),
        name="mlp_back",
    )(cot, vec, f0, f1, p0, p1, vo, o, middle, second, act, slope)


class Reducing:
    def __init__(self, grads, buffers, sources, send, recv, rows):
        self.grads, self.sources = grads, sources
        self.diag, self.from_x, self.from_y, self.up, self.down = buffers[0:2], buffers[2:4], buffers[4:6], buffers[6:8], buffers[8:10]
        self.send, self.recv, self.rows = send, recv, rows
        self.dp, self.core, self.z, self.y, self.x = place()
        self.x_peer = self.dp + 1 - 2 * self.x
        self.y_peer = self.dp + 2 - 4 * self.y
        half = self.z // 2
        self.order = (3 - 3 * half, 2 - half, 1 - self.z + 4 * half, self.z)

    def at(self, ref, block):
        return ref.at[pl.ds(pl.multiple_of(block * self.rows, self.rows), self.rows)]

    def block(self, level, y_off, x_off):
        y = self.y + y_off * (1 - 2 * self.y)
        x = self.x + x_off * (1 - 2 * self.x)
        return level * 4 + y * 2 + x

    def go(self, kind, level, src, dst, target):
        return remote(src, dst, self.send.at[kind, level], self.recv.at[kind, level], target, self.core)

    def diag_copy(self, level, side):
        block = self.at(self.sources[side], self.block(level, 1, 1))
        return self.go(side, level, block, self.diag[side].at[level], (self.y_peer, self.x_peer)[side])

    def own_copy(self, level, side):
        block = self.at(self.sources[side], self.block(level, 1 - side, side))
        target = (self.from_y, self.from_x)[side][side].at[level]
        return self.go(2 + side, level, block, target, (self.y_peer, self.x_peer)[side])

    def sum_copy(self, level, side):
        target = (self.from_x, self.from_y)[side][side].at[level]
        return self.go(4 + side, level, self.diag[side].at[level], target, (self.x_peer, self.y_peer)[side])

    def up_copy(self, level, side):
        return self.go(6 + side, level, self.from_x[side].at[level], self.up[side].at[level], self.dp + 4)

    def down_copy(self, level, side):
        return self.go(8 + side, level, self.from_x[side].at[level], self.down[side].at[level], self.dp - 4)

    def first(self):
        for level in self.order:
            for side in range(2):
                self.diag_copy(level, side).start()
        for level in self.order:
            for side in range(2):
                self.own_copy(level, side).start()

    def scale(self, factor, factor_x, factor_y):
        self.factor, self.factor_x, self.factor_y = factor, factor_x, factor_y

    def weigh(self, side, block, dst, scale_dst, terms):
        grad = self.grads[side]

        @pl.loop(0, self.rows // 16)
        def _(i):
            part = pl.ds(pl.multiple_of(i * 16, 16), 16)
            own = grad[pl.ds(pl.multiple_of(block * self.rows + i * 16, 16), 16), :]
            total = self.factor * own.astype(jnp.float32)
            for scale, ref in ((scale_dst, dst),) + terms:
                value = ref[part, :].astype(jnp.float32)
                total = total + (value if scale is None else scale * value)
            dst[part, :] = total.astype(dst.dtype)

    def sums(self, level):
        for side in range(2):
            self.diag_copy(level, side).wait_recv()
            block = self.block(level, side, 1 - side)
            self.weigh(side, block, self.diag[side].at[level], (self.factor_y, self.factor_x)[side], ())
            self.sum_copy(level, side).start()

    def arrivals(self, level, side):
        self.own_copy(level, side).wait_recv()
        self.sum_copy(level, side).wait_recv()

    def chain(self, index):
        level = self.order[index]
        block = self.block(level, 0, 0)
        for side in range(2):
            self.arrivals(level, side)
            scale_x = None if side == 0 else self.factor_x
            term_y = (self.factor_y if side == 0 else None, self.from_y[side].at[level])

            def combine(*extra):
                self.weigh(side, block, self.from_x[side].at[level], scale_x, (term_y,) + extra)

            @pl.when(level > self.z)
            def _():
                @pl.when(self.z > 0)
                def _():
                    self.up_copy(level, side).wait_recv()
                    combine((None, self.up[side].at[level]))

                @pl.when(self.z == 0)
                def _():
                    combine()

                self.up_copy(level, side).start()

            @pl.when(level < self.z)
            def _():
                @pl.when(self.z < LINE - 1)
                def _():
                    self.down_copy(level, side).wait_recv()
                    combine((None, self.down[side].at[level]))

                @pl.when(self.z == LINE - 1)
                def _():
                    combine()

                self.down_copy(level, side).start()

    def last(self, side):
        self.arrivals(self.z, side)

        @pl.when(self.z > 0)
        def _():
            self.up_copy(self.z, side).wait_recv()

        @pl.when(self.z == 0)
        def _():
            self.up[side][0] = jnp.zeros(self.up[side].shape[1:], self.up[side].dtype)

        @pl.when(self.z < LINE - 1)
        def _():
            self.down_copy(self.z, side).wait_recv()

        @pl.when(self.z == LINE - 1)
        def _():
            self.down[side][LINE - 1] = jnp.zeros(self.down[side].shape[1:], self.down[side].dtype)

    def total(self, side, part, columns):
        here = pl.ds(pl.multiple_of(self.dp * self.rows + part.start, 16), part.size)
        total = self.factor * self.grads[side][here, columns].astype(jnp.float32)
        scales = (None, self.factor_y) if side == 0 else (self.factor_x, None)
        for scale, ref in zip(scales + (None, None), (self.from_x, self.from_y, self.up, self.down)):
            value = ref[side][self.z, part, columns].astype(jnp.float32)
            total = total + (value if scale is None else scale * value)
        return total

    def drain(self):
        for level in range(LINE):
            for side in range(2):
                self.diag_copy(level, side).wait_send()
                self.own_copy(level, side).wait_send()
                self.sum_copy(level, side).wait_send()

            @pl.when(level > self.z)
            def _():
                for side in range(2):
                    self.up_copy(level, side).wait_send()

            @pl.when(level < self.z)
            def _():
                for side in range(2):
                    self.down_copy(level, side).wait_send()


def owner_at(slot):
    return OWNERS[slot] // 4, OWNERS[slot] % 4 // 2, OWNERS[slot] % 2


def attn_back_kernel(
    noise_scale, batch, clip,
    tokens_in, vec, first_in, q_in, k_in, v_in, o_in, do_in, lse, qk_in, vo_in, grad_mid_in, ga_in, gb_in, go_in, sums,
    included, attn_mom_in, mlp_mom_in, attn_noise_in, mlp_noise_in,
    grad_in_out, attn_out, mlp_out, vec_out, owned,
    tokens, first, q, k, v, o, do, qk_all, wv, grad_mid, ga, gb, attn_mom, mlp_mom, attn_noise, mlp_noise, grad_in,
    dqk, dv, ga_late, gb_late, head_turned, turned, partial, other, acc, square, factors,
    diag_a, diag_b, x_a, x_b, y_a, y_b, up_a, up_b, down_a, down_b,
    late_diag_a, late_diag_b, late_x_a, late_x_b, late_y_a, late_y_b, late_up_a, late_up_b, late_down_a, late_down_b,
    attn_low, mlp_low, relayed, vec_send, vec_recv,
    send, recv, late_send, late_recv, vec_sems, gather_send, gather_recv, relay_sems, swap_send, swap_recv, small, pass_send, pass_recv,
    stage_sems,
):
    dp, core, z, y, x = place()
    rows, _, width = attn_mom.shape
    wide = mlp_mom.shape[2]
    length = tokens.shape[0]
    chunk = length // 4
    x_peer, y_peer = dp + 1 - 2 * x, dp + 2 - 4 * y
    count = ga.shape[0] // rows
    z_near = dp + 4 - 8 * (z % 2)
    z_far = dp + 8 - 16 * (z // 2)
    stage = Staging(stage_sems)
    for name, src, dst in (
        ("q", q_in, q), ("k", k_in, k), ("v", v_in, v), ("o", o_in, o), ("do", do_in, do), ("qk_all", qk_in, qk_all),
        ("wv", vo_in.at[:, pl.ds(0, width)], wv), ("first", first_in, first), ("go", go_in, gb_late.at[:, pl.ds(width, width)]),
        ("tokens", tokens_in, tokens), ("grad_mid", grad_mid_in, grad_mid), ("ga", ga_in, ga), ("gb", gb_in, gb),
        ("mlp_mom", mlp_mom_in, mlp_mom), ("mlp_noise", mlp_noise_in, mlp_noise), ("attn_mom", attn_mom_in, attn_mom),
        ("attn_noise", attn_noise_in, attn_noise),
    ):
        stage.fetch(name, src, dst)
    greet_all(dp, core, count, True)

    main = Reducing(
        (ga, gb), (diag_a, diag_b, x_a, x_b, y_a, y_b, up_a, up_b, down_a, down_b), (ga_in, gb_in), send, recv, rows
    )
    late = Reducing(
        (ga_late, gb_late),
        (late_diag_a, late_diag_b, late_x_a, late_x_b, late_y_a, late_y_b, late_up_a, late_up_b, late_down_a, late_down_b),
        (ga_late, gb_late),
        late_send,
        late_recv,
        rows,
    )
    main.first()

    def small_copy(index):
        src, dst, target = (
            (square.at[0], square.at[1], (dp, 1 - core)),
            (factors.at[0], factors.at[1], (x_peer, core)),
            (factors.at[0], factors.at[2], (y_peer, core)),
        )[index]
        return remote(src, dst, small.at[0, index], small.at[1, index], *target)

    def vec_copy(step):
        target = ((dp, 1 - core), (z_near, core), (z_far, core), (x_peer, core), (y_peer, core))[step]
        return remote(vec_send.at[step], vec_recv.at[step], vec_sems.at[0, step], vec_sems.at[1, step], *target)

    def vec_step(step):
        vec_copy(step).wait_recv()
        total = vec_send[step] + vec_recv[step]
        if step < 4:
            vec_send[step + 1] = total
            vec_copy(step + 1).start()
        else:
            vec_out[...] = total

    def swap_copy(i):
        part = pl.ds(i * chunk, chunk)
        return remote(partial.at[part], other.at[part], swap_send.at[i], swap_recv.at[i], dp, 1 - core)

    acc[...] = jnp.zeros_like(acc)
    stage.need("q", "k", "v", "o", "do")
    for pair in range(width // (2 * HD)):
        lanes = pl.ds(pair * 2 * HD, 2 * HD)
        attend_backward(
            q.at[:, lanes], k.at[:, lanes], v.at[:, lanes], o.at[:, lanes], do.at[:, lanes], lse.at[pair],
            dqk.at[:, lanes], dqk.at[:, pl.ds(width + pair * 2 * HD, 2 * HD)], dv.at[:, lanes], head_turned,
        )
    stage.need("qk_all", "wv")
    for i in range(4):
        part = pl.ds(i * chunk, chunk)
        partial[part, :] = (contract(dqk[part, :], qk_all[...], 1, 1) + contract(dv[part, :], wv[...], 1, 1)).astype(
            jnp.bfloat16
        )
        swap_copy(i).start()
    stage.need("first", "go")
    turned[...] = first[...].T
    squares = jnp.zeros((1, 1), jnp.float32)
    for right, target in ((dqk, ga_late), (dv, gb_late)):
        for block in range(D // 256):
            part = pl.ds(block * 256, 256)
            value = contract(turned[part, :], right[...], 1, 0)
            target[part, 0 : right.shape[1]] = value.astype(jnp.bfloat16)
            squares = squares + jnp.sum(column_sum(value * value), axis=1, keepdims=True)
    late.first()
    bias_q = column_sum(dqk[:, 0:width].astype(jnp.float32))
    bias_v = column_sum(dv[...].astype(jnp.float32))
    for value in (sums[6:7, :], sums[7:8, :]):
        squares = squares + jnp.sum(value, axis=1, keepdims=True)
    for value in (bias_q, bias_v, sums[4:5, :], sums[5:6, :]):
        squares = squares + jnp.sum(value * value, axis=1, keepdims=True)
    square[0] = jnp.broadcast_to(squares, square.shape[1:])
    small_copy(0).start()

    stage.need("tokens", "grad_mid")
    for i in range(4):
        swap_copy(i).wait_recv()

        def back(part):
            here = shifted(part, i * chunk)
            grad = partial[here, :].astype(jnp.float32) + other[here, :].astype(jnp.float32)
            value, normed = norm_back_tile(grad, vec[0:1, :], tokens[here, :].astype(jnp.float32))
            grad_in[here, :] = (grad_mid[here, :] + value).astype(jnp.bfloat16)
            acc[0] += fold(grad * normed)
            acc[1] += fold(grad)

        tiles(chunk, BACK_ROWS, back)
    stage.keep(grad_in, grad_in_out)
    gain_one, bias_one = column_sum(acc[0]), column_sum(acc[1])
    shared = jnp.zeros((1, 1), jnp.float32)
    for value in (gain_one, bias_one, sums[0:1, :], sums[1:2, :], sums[2:3, :], sums[3:4, :]):
        shared = shared + jnp.sum(value * value, axis=1, keepdims=True)
    small_copy(0).wait_recv()
    norm = jnp.sqrt(square[0, 0:1, 0:1] + square[1, 0:1, 0:1] + shared)
    factor = included[0].astype(jnp.float32) * jnp.minimum(1.0, clip / (norm + 1e-06))
    factors[0] = jnp.broadcast_to(factor, factors.shape[1:])
    small_copy(1).start()
    small_copy(2).start()
    leading = factor * (1 - core).astype(jnp.float32)
    vec_send[0] = jnp.zeros(vec_send.shape[1:], jnp.float32)
    mine = pl.ds(pl.multiple_of(core * width, width), width)
    for row, value in ((0, gain_one), (1, bias_one), (2, sums[0:1, :]), (3, sums[1:2, :]), (6, sums[2:3, :]), (7, sums[3:4, :])):
        vec_send[0, row : row + 1, :] = leading * value
    vec_send[0, 4:5, mine] = factor * bias_q
    vec_send[0, 5:6, mine] = factor * bias_v
    vec_send[0, pl.ds(8 + 2 * core, 1), :] = factor * sums[4:5, :]
    vec_send[0, pl.ds(9 + 2 * core, 1), :] = factor * sums[5:6, :]
    vec_copy(0).start()
    stage.need("ga", "gb", "mlp_mom", "mlp_noise", "attn_mom", "attn_noise")
    small_copy(1).wait_recv()
    small_copy(2).wait_recv()
    for part in (main, late):
        part.scale(factor, factors[1, 0:1, 0:1], factors[2, 0:1, 0:1])

    def moment(slot, reducing, side, column):
        size = width if slot < 4 else wide
        low = attn_low.at[slot] if slot < 4 else mlp_low.at[slot - 4]
        old, noise, new = (attn_mom, attn_noise, attn_out) if slot < 4 else (mlp_mom, mlp_noise, mlp_out)
        index = slot if slot < 4 else slot - 4

        @pl.loop(0, rows // 16)
        def _(i):
            part = pl.ds(pl.multiple_of(i * 16, 16), 16)
            total = reducing.total(side, part, pl.ds(column, size))
            value = 0.5 * old[part, index, :] + (total + noise_scale * noise[part, index, :]) / batch
            new[part, index, :] = value
            low[part, :] = value.astype(low.dtype)

        for action in sends(slot):
            action(lambda copy: copy.start())

    def landing(slot, source):
        size = width if slot < 4 else wide
        return main.at(owned.at[0], source).at[:, 0:size]

    def sends(slot):
        owner = OWNERS[slot]
        owner_z, owner_y, owner_x = owner_at(slot)
        low = attn_low.at[slot] if slot < 4 else mlp_low.at[slot - 4]
        across = (y != owner_y) & (x != owner_x) & (z != owner_z)

        def keep(action):
            @pl.when(dp == owner)
            def _():
                action(pltpu.make_async_copy(low, landing(slot, dp), gather_send.at[slot]))

        def direct(action):
            away = (dp != owner) & jnp.logical_not(across) if slot >= 4 else dp != owner

            @pl.when(away)
            def _():
                action(remote(low, landing(slot, dp), gather_send.at[slot], gather_recv.at[dp], owner, core))

        def turn(action):
            if slot >= 4:

                @pl.when(across)
                def _():
                    action(remote(low, relayed, gather_send.at[slot], relay_sems.at[0], z * 4 + owner_y * 2 + owner_x, core))

        return keep, direct, turn

    def relay_copy(slot):
        source = z * 4 + (1 - y) * 2 + 1 - x
        return remote(relayed, landing(slot, source), relay_sems.at[1], gather_recv.at[source], OWNERS[slot], core)

    def relays(slot, action):
        owner_z, owner_y, owner_x = owner_at(slot)

        @pl.when((y == owner_y) & (x == owner_x) & (z != owner_z))
        def _():
            action()

    for index, level in enumerate(main.order):
        main.sums(level)
        if index < 3:
            vec_step(index)
    main.chain(0)
    for level in late.order:
        late.sums(level)
    main.chain(1)
    main.chain(2)
    main.last(0)
    moment(4, main, 0, 0)
    main.last(1)
    moment(5, main, 1, 0)
    late.chain(0)
    late.chain(1)
    late.chain(2)
    vec_step(3)
    late.last(0)
    moment(0, late, 0, 0)
    moment(1, late, 0, width)
    late.last(1)
    moment(2, late, 1, 0)
    moment(3, late, 1, width)
    for slot in (4, 5):

        def forward():
            remote(relayed, relayed, relay_sems.at[1], relay_sems.at[0], dp, core).wait_recv()
            relay_copy(slot).start()

        relays(slot, forward)
    vec_step(4)

    def pass_on(slot, source):
        size = width if slot < 4 else wide
        block = landing(slot, source)
        other_half = main.at(owned.at[1], source).at[:, 0:size]
        return remote(block, other_half, pass_send.at[source], pass_recv.at[source], dp, 1 - core)

    for slot in range(6):
        owner = OWNERS[slot]
        low = attn_low.at[slot] if slot < 4 else mlp_low.at[slot - 4]

        @pl.when(dp != owner)
        def _():
            remote(low, low, gather_send.at[slot], gather_recv.at[dp], owner, core).wait_send()

        @pl.when(dp == owner)
        def _():
            pltpu.make_async_copy(low, landing(slot, dp), gather_send.at[slot]).wait()
            pass_on(slot, dp).start()

            @pl.loop(1, count)
            def _(step):
                source = (dp + step) % count
                block = landing(slot, source)
                remote(block, block, gather_send.at[slot], gather_recv.at[source], source, core).wait_recv()
                pass_on(slot, source).start()

            @pl.loop(0, count)
            def _(source):
                pass_on(slot, source).wait()

    for slot in (4, 5):
        relays(slot, lambda: relay_copy(slot).wait_send())
    for index in range(3):
        small_copy(index).wait_send()
    for i in range(4):
        swap_copy(i).wait_send()
    for step in range(5):
        vec_copy(step).wait_send()
    main.drain()
    late.drain()
    stage.finish()


def attn_back(
    tokens, vec, first, q, k, v, o, do, lse, qk_all, vo_all, grad_mid, ga, gb, go, sums, included,
    attn_mom, mlp_mom, attn_noise, mlp_noise, noise_scale, batch, clip, collective_id,
):
    dma = pltpu.SemaphoreType.DMA
    low = jnp.bfloat16
    count = lax.axis_size("dp")
    length = tokens.shape[0]
    rows, _, width = attn_mom.shape
    wide = mlp_mom.shape[2]
    shape = jax.ShapeDtypeStruct
    vmem = pl.BlockSpec(memory_space=pltpu.VMEM)
    anywhere = pl.BlockSpec(memory_space=pl.ANY)
    scratch = pltpu.VMEM
    return pl.pallas_call(
        functools.partial(attn_back_kernel, noise_scale, batch, clip),
        out_shape=[
            shape((length, D), low),
            shape(attn_mom.shape, jnp.float32),
            shape(mlp_mom.shape, jnp.float32),
            shape(vec.shape, jnp.float32),
            shape((2, D, wide), low),
        ],
        in_specs=[anywhere, vmem]
        + [anywhere] * 6
        + [vmem]
        + [anywhere] * 6
        + [vmem, pl.BlockSpec(memory_space=pltpu.SMEM)]
        + [anywhere] * 4,
        out_specs=[anywhere] + [vmem] * 3 + [anywhere],
        scratch_shapes=[
            scratch((length, D), low),
            scratch((length, D), low),
        ]
        + [scratch((length, width), low)] * 5
        + [
            scratch((D, 2 * width), low),
            scratch((D, width), low),
            scratch((length, D), jnp.float32),
            scratch((D, wide), low),
            scratch((D, wide), low),
            scratch(attn_mom.shape, jnp.float32),
            scratch(mlp_mom.shape, jnp.float32),
            scratch(attn_mom.shape, jnp.float32),
            scratch(mlp_mom.shape, jnp.float32),
            scratch((length, D), low),
            scratch((length, 2 * width), low),
            scratch((length, width), low),
            scratch((D, 2 * width), low),
            scratch((D, 2 * width), low),
            scratch((2 * HD, length), jnp.float32),
            scratch((D, length), low),
            scratch((length, D), low),
            scratch((length, D), low),
            scratch((2, 8, D), jnp.float32),
            scratch((2, 8, 128), jnp.float32),
            scratch((3, 8, 128), jnp.float32),
        ]
        + [scratch((LINE, rows, wide), low)] * 10
        + [scratch((LINE, rows, 2 * width), low)] * 10
        + [
            scratch((4, rows, width), low),
            scratch((2, rows, wide), low),
            scratch((rows, wide), low),
            scratch((5,) + vec.shape, jnp.float32),
            scratch((5,) + vec.shape, jnp.float32),
            dma((10, LINE)),
            dma((10, LINE)),
            dma((10, LINE)),
            dma((10, LINE)),
            dma((2, 5)),
            dma((6,)),
            dma((count,)),
            dma((2,)),
            dma((4,)),
            dma((4,)),
            dma((2, 3)),
            dma((count,)),
            dma((count,)),
            dma((20,)),
        ],
        compiler_params=pltpu.CompilerParams(
            collective_id=collective_id, has_side_effects=True, vmem_limit_bytes=62 * MIB
        ),
        name="attn_back",
    )(
        tokens, vec, first, q, k, v, o, do, lse, qk_all, vo_all, grad_mid, ga, gb, go, sums, included,
        attn_mom, mlp_mom, attn_noise, mlp_noise,
    )


def placed(piece, start, total_size):
    return lax.dynamic_update_slice_in_dim(jnp.zeros((total_size,), jnp.float32), piece, start, 0)


def other_core(value):
    return lax.ppermute(value, "tensor", [(0, 1), (1, 0)])


SHIFTS = (0.0, 0.0, 0.0, 0.8, 0.72)


def polynomials(current):
    rows = current.shape[0]
    diagonal = lax.broadcasted_iota(jnp.int32, (rows, rows), 0) == lax.broadcasted_iota(jnp.int32, (rows, rows), 1)

    def less(matrix, shift):
        return matrix - jnp.where(diagonal, shift, 0.0) if shift else matrix

    def product(left, right):
        return contract(left.astype(jnp.bfloat16), right.astype(jnp.bfloat16), 1, 0)

    factor = None
    for iteration in range(NS_ITERS):
        shift = SHIFTS[iteration]
        moved = less(current, shift)
        square = product(moved, moved) + 2.0 * shift * moved
        lead = COEF_B * shift + COEF_C * shift * shift
        rest = lax.optimization_barrier(COEF_B * moved + COEF_C * square)
        whole = COEF_A + lead
        if factor is None:
            factor = jnp.where(diagonal, whole, 0.0) + rest
        else:
            factor = lax.optimization_barrier(whole * factor + product(rest, factor))
        if iteration < NS_ITERS - 1:
            once = lax.optimization_barrier(whole * current + shift * rest + product(rest, moved))
            second = whole * shift
            current = lax.optimization_barrier(whole * once + second * rest + product(rest, less(once, second)))
    return factor.astype(jnp.bfloat16)


def newton(owned):
    gram = contract(owned, owned, 1, 1)
    gram = gram + other_core(gram)
    scale = 1.0 / (jnp.sqrt(jnp.trace(gram)) + 1e-07)
    return (contract(polynomials(gram * (scale * scale)), owned, 1, 0) * scale).astype(jnp.bfloat16)


def body(
    fast,
    tokens,
    cotangent,
    inclusion,
    attn_weights,
    mlp_weights,
    attn_momentum,
    mlp_momentum,
    attn_noise,
    mlp_noise,
    vectors,
    vector_momentum,
    vector_noise,
):
    dp_count = lax.axis_size("dp")
    dp_index = lax.axis_index("dp")
    halves = lax.axis_size("tensor")
    tensor_index = lax.axis_index("tensor")
    head_width = D // halves
    hidden_width = FF // halves
    query_scale = 1.0 / math.sqrt(HD)
    clip = 1.5 * D * math.sqrt(LEN)
    sigma = 0.05 * math.sqrt(dp_count) / D
    batch = 0.75 * dp_count
    noise_scale = sigma * clip
    if fast:
        (
            query_key, value_out, fc_one, fc_two, pr_one, pr_two,
            first_low, queries, key_rows, value_rows, attended_low, stats, middle, second_low, activation_low, slope, vec,
        ) = front(tokens[0], vectors.reshape(-1, 128), attn_weights, mlp_weights, 0)
        result, grad_mid, grad_attended, grad_fc, grad_pr, grad_wo, sums = mlp_back(
            cotangent[0], vec, fc_one, fc_two, pr_one, pr_two, value_out, attended_low, middle, second_low,
            activation_low, slope, 1,
        )
        grad_in, attn_moment, mlp_moment, vector_summed, owned = attn_back(
            tokens[0], vec, first_low, queries, key_rows, value_rows, attended_low, grad_attended, stats,
            query_key, value_out, grad_mid, grad_fc, grad_pr, grad_wo, sums,
            inclusion, attn_momentum, mlp_momentum, attn_noise, mlp_noise, noise_scale, batch, clip, 2,
        )
        vector_summed = vector_summed.reshape(-1)
    else:
        attn_shard = attn_weights.astype(jnp.bfloat16)
        mlp_shard = mlp_weights.astype(jnp.bfloat16)
        rows = attn_shard.shape[0]
        shards = (
            attn_shard[:, 0:2].reshape(rows, 2 * head_width),
            attn_shard[:, 2:4].reshape(rows, 2 * head_width),
            mlp_shard[:, 0, 0:D],
            mlp_shard[:, 0, D:],
            mlp_shard[:, 1, 0:D],
            mlp_shard[:, 1, D:],
        )
        gain_one = vectors[0:D]
        bias_one = vectors[D : 2 * D]
        gain_two = vectors[2 * D : 3 * D]
        bias_two = vectors[3 * D : 4 * D]
        query_bias = lax.dynamic_slice_in_dim(vectors, 4 * D + tensor_index * head_width, head_width)
        value_bias = lax.dynamic_slice_in_dim(vectors, 5 * D + tensor_index * head_width, head_width)
        attn_bias = vectors[6 * D : 7 * D]
        mlp_bias = vectors[7 * D : 8 * D]
        hidden_bias = lax.dynamic_slice_in_dim(
            vectors, 8 * D + tensor_index * hidden_width, hidden_width
        )
        inputs = tokens[0].astype(jnp.float32)
        length = inputs.shape[0]
        first, normed_one, inverse_one = layer_norm(inputs, gain_one, bias_one)

        def both_cores(partial):
            low = partial.astype(jnp.bfloat16)
            return low.astype(jnp.float32) + other_core(low).astype(jnp.float32)

        query_key, value_out, fc_one, fc_two, pr_one, pr_two = (
            lax.all_gather(shard, "dp", axis=0, tiled=True) for shard in shards
        )
        value_weight, out_weight = value_out[:, 0:head_width], value_out[:, head_width:]
        first_low = first.astype(jnp.bfloat16)
        qk = contract(first_low, query_key, 1, 0)
        queries = ((qk[:, 0:head_width] + query_bias) * query_scale).astype(jnp.bfloat16)
        key_rows = qk[:, head_width:].astype(jnp.bfloat16)
        value_rows = (contract(first_low, value_weight, 1, 0) + value_bias).astype(jnp.bfloat16)
        attended_low, stats = pairs_forward(queries, key_rows, value_rows)
        middle = inputs + both_cores(contract(attended_low, out_weight, 1, 1)) + attn_bias
        second_low = layer_norm(middle, gain_two, bias_two)[0].astype(jnp.bfloat16)
        pre_act = contract(second_low, jnp.concatenate([fc_one, fc_two], axis=1), 1, 0) + hidden_bias
        activation, gelu_back = jax.vjp(gelu_tanh, pre_act)
        activation_low = activation.astype(jnp.bfloat16)
        slope = gelu_back(jnp.ones_like(pre_act))[0]
        _, normed_two, inverse_two = layer_norm(middle, gain_two, bias_two)
        fc_weight = jnp.concatenate([fc_one, fc_two], axis=1)
        pr_weight = jnp.concatenate([pr_one, pr_two], axis=1)
        result = middle + both_cores(contract(activation_low, pr_weight, 1, 1)) + mlp_bias
        cot_low = cotangent[0]
        grad_out = cot_low.astype(jnp.float32)
        d_pr = contract(cot_low, activation_low, 0, 0)
        grad_pre = (contract(cot_low, pr_weight, 1, 0) * slope.astype(jnp.float32)).astype(jnp.bfloat16)
        d_fc = contract(second_low, grad_pre, 0, 0)
        d_hidden_bias = jnp.sum(grad_pre.astype(jnp.float32), axis=0)
        grad_two = both_cores(contract(grad_pre, fc_weight, 1, 1))
        grad_mid = grad_out + norm_back(grad_two, gain_two, normed_two, inverse_two)
        d_gain_two = jnp.sum(grad_two * normed_two, axis=0)
        d_bias_two = jnp.sum(grad_two, axis=0)
        d_attn_bias = jnp.sum(grad_mid, axis=0)
        d_mlp_bias = jnp.sum(grad_out, axis=0)
        mid_low = grad_mid.astype(jnp.bfloat16)
        d_out = contract(mid_low, attended_low, 0, 0)
        grad_attended = contract(mid_low, out_weight, 1, 0).astype(jnp.bfloat16)
        grad_q, grad_k, grad_v = pairs_backward(
            queries, key_rows, value_rows, attended_low, grad_attended, stats
        )
        grad_qk = jnp.concatenate([grad_q, grad_k], axis=1)
        d_query_key = contract(first_low, grad_qk, 0, 0)
        d_value = contract(first_low, grad_v, 0, 0)
        d_query_bias = jnp.sum(grad_q.astype(jnp.float32), axis=0)
        d_value_bias = jnp.sum(grad_v.astype(jnp.float32), axis=0)
        grad_one = both_cores(contract(grad_qk, query_key, 1, 1) + contract(grad_v, value_weight, 1, 1))
        grad_in = grad_mid + norm_back(grad_one, gain_one, normed_one, inverse_one)
        d_gain_one = jnp.sum(grad_one * normed_one, axis=0)
        d_bias_one = jnp.sum(grad_one, axis=0)
        split_square = sum(
            jnp.sum(value * value)
            for value in (d_query_key, d_value, d_out, d_fc, d_pr, d_query_bias, d_value_bias, d_hidden_bias)
        )
        split_tile = jnp.broadcast_to(split_square, (8, 128))
        total_square = (split_tile + other_core(split_tile))[0, 0] + sum(
            jnp.sum(value * value)
            for value in (d_gain_one, d_bias_one, d_gain_two, d_bias_two, d_attn_bias, d_mlp_bias)
        )
        factor = inclusion[0].astype(jnp.float32) * jnp.minimum(
            1.0, clip / (jnp.sqrt(total_square) + 1e-06)
        )
        leading = (tensor_index == 0).astype(jnp.float32)
        vector_grad = (
            jnp.concatenate(
                [
                    leading * d_gain_one,
                    leading * d_bias_one,
                    leading * d_gain_two,
                    leading * d_bias_two,
                    placed(d_query_bias, tensor_index * head_width, D),
                    placed(d_value_bias, tensor_index * head_width, D),
                    leading * d_attn_bias,
                    leading * d_mlp_bias,
                    placed(d_hidden_bias, tensor_index * hidden_width, FF),
                ]
            )
            * factor
        )
        result, grad_in = result.astype(jnp.bfloat16), grad_in.astype(jnp.bfloat16)
        attn_grad = jnp.concatenate([d_query_key, d_value, d_out], axis=1) * factor
        mlp_grad = jnp.stack([d_fc, d_pr], axis=1) * factor
        attn_summed = lax.psum_scatter(attn_grad, "dp", scatter_dimension=0, tiled=True)
        mlp_summed = lax.psum_scatter(mlp_grad, "dp", scatter_dimension=0, tiled=True)
        attn_summed = attn_summed.reshape(rows, 4, head_width)
        vector_summed = lax.psum(vector_grad, ("dp", "tensor"))
        attn_moment = 0.5 * attn_momentum + (attn_summed + noise_scale * attn_noise) / batch
        mlp_moment = 0.5 * mlp_momentum + (mlp_summed + noise_scale * mlp_noise) / batch
        owners = jnp.array([slot * dp_count // 6 for slot in range(6)])
        full_attn = lax.all_gather(attn_moment.astype(jnp.bfloat16), "dp", axis=0, tiled=True)
        full_mlp = lax.all_gather(mlp_moment.astype(jnp.bfloat16), "dp", axis=0, tiled=True)
        attn_pick = (owners[0:4] == dp_index)[None, :, None]
        mlp_pick = (owners[4:6] == dp_index)[None, :, None]
        mine_attn = jnp.sum(jnp.where(attn_pick, full_attn, 0), axis=1)
        mine_mlp = jnp.sum(jnp.where(mlp_pick, full_mlp, 0), axis=1)
        owned = jnp.pad(mine_attn, ((0, 0), (0, hidden_width - head_width))) + mine_mlp
    vector_moment = 0.5 * vector_momentum + (vector_summed + noise_scale * vector_noise) / batch
    vector_rate = 0.2 * math.sqrt(dp_count / LEN)
    vectors_new = vectors - vector_rate * vector_moment
    rates = (0.5, 0.5, 0.5, 0.5 * max(1.0, math.sqrt(LEN) / 8.0), 0.5 * math.sqrt(FF / D), 0.5)
    if fast:
        gram, scale, result, grad_in, attn_moment, mlp_moment = gram_of(
            owned, (result, grad_in, attn_moment, mlp_moment)
        )
        attn_new, mlp_new = scatter_rows(
            polynomials(gram), scale, owned, attn_weights, mlp_weights, rates, 3
        )
    else:
        orthogonal = newton(owned)
        attn_rows = jnp.where(attn_pick, orthogonal[:, None, 0:head_width], 0)
        mlp_rows = jnp.where(mlp_pick, orthogonal[:, None, :], 0)
        attn_orth = lax.psum_scatter(attn_rows, "dp", scatter_dimension=0, tiled=True)
        mlp_orth = lax.psum_scatter(mlp_rows, "dp", scatter_dimension=0, tiled=True)
        attn_new = attn_weights - jnp.array(rates[0:4])[None, :, None] * attn_orth
        mlp_new = mlp_weights - jnp.array(rates[4:6])[None, :, None] * mlp_orth
    return (
        result[None],
        grad_in[None],
        attn_moment,
        mlp_moment,
        attn_new,
        mlp_new,
        vector_moment,
        vectors_new,
    )


def solution(mesh):
    fast = mesh.shape["dp"] == 16 and mesh.shape["tensor"] == 2
    in_specs = (
        P("dp", None, None),
        P("dp", None, None),
        P("dp"),
        P("dp", None, "tensor"),
        P("dp", None, "tensor"),
        P("dp", None, "tensor"),
        P("dp", None, "tensor"),
        P("dp", None, "tensor"),
        P("dp", None, "tensor"),
        P(),
        P(),
        P(),
    )
    out_specs = (
        P("dp", None, None),
        P("dp", None, None),
        P("dp", None, "tensor"),
        P("dp", None, "tensor"),
        P("dp", None, "tensor"),
        P("dp", None, "tensor"),
        P(),
        P(),
    )
    return jax.shard_map(
        functools.partial(body, fast), mesh=mesh, in_specs=in_specs, out_specs=out_specs, check_vma=False
    )
```

```python
import functools
import math

import jax
import jax.numpy as jnp
from jax import lax
from jax.experimental import pallas as pl
from jax.experimental.pallas import tpu as pltpu
from jax.sharding import PartitionSpec as P

D = 768
HD = 64
FF = 3072
LEN = 960
NS_ITERS = 5


COEF_A = 3.4445
COEF_B = -4.775
COEF_C = 2.0315


def gelu_tanh(values):
    return jax.nn.gelu(values, approximate=True)


def layer_norm(values, norm_gain, norm_bias):
    centered = values - jnp.mean(values, axis=-1, keepdims=True)
    inverse = lax.rsqrt(jnp.mean(centered * centered, axis=-1, keepdims=True) + 1e-05)
    normed = centered * inverse
    return (normed * norm_gain + norm_bias, normed, inverse)


def norm_back(grad_out, norm_gain, normed, inverse):
    scaled = grad_out * norm_gain
    return inverse * (
        scaled
        - jnp.mean(scaled, axis=-1, keepdims=True)
        - normed * jnp.mean(scaled * normed, axis=-1, keepdims=True)
    )


def contract(left, right, left_dim, right_dim):
    return lax.dot_general(
        left, right, (((left_dim,), (right_dim,)), ((), ())), preferred_element_type=jnp.float32
    )


MESH = pl.DeviceIdType.MESH
MIB = 1 << 20
LINE = 4
OWNERS = (7, 8, 6, 9, 4, 11)


def place():
    dp = lax.axis_index("dp")
    core = lax.axis_index("tensor")
    z = dp // 4
    y = dp % 4 // 2
    x = dp % 2
    return dp, core, z, y, x


def remote(src, dst, send, recv, dp, core):
    return pltpu.make_async_remote_copy(
        src_ref=src, dst_ref=dst, send_sem=send, recv_sem=recv, device_id=(dp, core), device_id_type=MESH
    )


def greet(barrier, dp, core):
    pl.semaphore_signal(barrier, inc=1, device_id=(dp, core), device_id_type=MESH)


def greet_all(dp, core, count):
    barrier = pltpu.get_barrier_semaphore()
    for step in range(1, count):
        greet(barrier, (dp + step) % count, core)
    pl.semaphore_wait(barrier, count - 1)


def greet_plane(dp, core, count, z, y, x):
    barrier = pltpu.get_barrier_semaphore()
    for step in range(1, count):
        greet(barrier, (dp + step) % count, core)
    for step in range(4):
        greet(barrier, z * 4 + (dp + step) % 4, 1 - core)
    return lambda: pl.semaphore_wait(barrier, count + 3)


class Staging:
    def __init__(self, sems):
        self.sems = sems
        self.count = 0
        self.waiting = {}
        self.out = []

    def move(self, src, dst):
        copy = pltpu.make_async_copy(src, dst, self.sems.at[self.count])
        self.count += 1
        copy.start()
        return copy

    def fetch(self, name, src, dst):
        self.waiting[name] = self.move(src, dst)

    def need(self, *names):
        for name in names:
            if name in self.waiting:
                self.waiting.pop(name).wait()

    def keep(self, src, dst):
        self.out.append(self.move(src, dst))

    def finish(self):
        for copy in self.out:
            copy.wait()


def gram_kernel(owned_in, *refs):
    results, (gram, scale), kept, held, (own, sems) = refs[:4], refs[4:6], refs[6:10], refs[10:14], refs[14:]
    dp = lax.axis_index("dp")
    stage = Staging(sems)
    stage.fetch("mine", owned_in.at[0], own.at[0])
    for index in range(4):
        stage.fetch(index, results[index], held[index])
    stage.fetch("other", owned_in.at[1], own.at[1])
    rows = gram.shape[0]
    attn = (dp == OWNERS[0]) | (dp == OWNERS[1]) | (dp == OWNERS[2]) | (dp == OWNERS[3])
    mlp = (dp == OWNERS[4]) | (dp == OWNERS[5])

    def each(action):
        pl.when(attn)(lambda: action(own.shape[2] // 4))
        pl.when(mlp)(lambda: action(own.shape[2]))

    def first(size):
        gram[...] = contract(own[0, :, 0:size], own[0, :, 0:size], 1, 1)

    def second(size):
        total = gram[...] + contract(own[1, :, 0:size], own[1, :, 0:size], 1, 1)
        square = jnp.zeros((1, 1), jnp.float32)
        tile = 256
        here = lax.broadcasted_iota(jnp.int32, (tile, tile), 0) == lax.broadcasted_iota(jnp.int32, (tile, tile), 1)
        for start in range(0, rows, tile):
            corner = jnp.where(here, total[start : start + tile, start : start + tile], 0.0)
            square = square + jnp.sum(jnp.sum(corner, axis=0, keepdims=True), axis=1, keepdims=True)
        inverse = 1.0 / (jnp.sqrt(square) + 1e-07)
        scale[...] = jnp.broadcast_to(inverse, scale.shape)
        gram[...] = total * (inverse * inverse)

    stage.need("mine")
    each(first)
    for index in range(4):
        stage.need(index)
        stage.keep(held[index], kept[index])
    stage.need("other")
    each(second)
    stage.finish()


def gram_of(owned, results):
    rows = owned.shape[1]
    shape = jax.ShapeDtypeStruct
    vmem = pl.BlockSpec(memory_space=pltpu.VMEM)
    anywhere = pl.BlockSpec(memory_space=pl.ANY)
    return pl.pallas_call(
        gram_kernel,
        out_shape=[shape((rows, rows), jnp.float32), shape((8, 128), jnp.float32)]
        + [shape(value.shape, value.dtype) for value in results],
        in_specs=[anywhere] * 5,
        out_specs=[vmem] * 2 + [anywhere] * 4,
        scratch_shapes=[pltpu.VMEM(value.shape, value.dtype) for value in results]
        + [pltpu.VMEM(owned.shape, owned.dtype), pltpu.SemaphoreType.DMA((10,))],
        compiler_params=pltpu.CompilerParams(vmem_limit_bytes=60 * MIB),
        name="gram",
    )(owned, *results)


def scatter_kernel(
    rates, factor, scale, owned_in, attn_in, mlp_in, attn_new, mlp_new,
    own, attn, mlp, orth, attn_low, mlp_low, relayed, send, recv, relay_send, relay_recv, stage_sems,
):
    dp, core, z, y, x = place()
    rows = attn.shape[0]
    count = orth.shape[0] // rows
    stage = Staging(stage_sems)
    stage.fetch("own", owned_in.at[0], own)
    stage.fetch("attn", attn_in, attn)
    stage.fetch("mlp", mlp_in, mlp)
    greet_all(dp, core, count)
    stage.need("own")

    def at(ref, block):
        return ref.at[pl.ds(pl.multiple_of(block * rows, rows), rows)]

    def low_of(slot):
        return attn_low.at[slot] if slot < 4 else mlp_low.at[slot - 4]

    def size_of(slot):
        return attn.shape[2] if slot < 4 else mlp.shape[2]

    def deliver(slot, target):
        owner = OWNERS[slot]
        src = at(orth, target).at[:, 0 : size_of(slot)]
        level = target // 4
        if slot >= 4 and level in stops(owner).get(target % 4, ()):
            stop = owner // 4 * 4 + target % 4
            return remote(src, relayed.at[level], send.at[target], relay_recv.at[level], stop, core)
        return remote(src, low_of(slot), send.at[target], recv.at[slot], target, core)

    def onward(slot, action):
        owner = OWNERS[slot]
        for column, levels in stops(owner).items():

            @pl.when(dp == owner // 4 * 4 + column)
            def _():
                for level in levels:
                    action(level, level * 4 + column)

    def relay_copy(slot, level, target):
        return remote(relayed.at[level], low_of(slot), relay_send.at[level], recv.at[slot], target, core)

    def levels_of(owner):
        return (3, 2, 0) if owner // 4 == 1 else (0, 1, 3)

    def stops(owner):
        far, near, alone = levels_of(owner)
        column = owner % 4
        by_x, by_y = column + 1 - 2 * (column % 2), column + 2 - 4 * (column // 2)
        return {by_x: (far, near), by_y: (far, near, alone)}

    def queue(owner):
        far, near, alone = levels_of(owner)
        home, column = owner // 4, owner % 4
        by_x, by_y, across = column + 1 - 2 * (column % 2), column + 2 - 4 * (column // 2), 3 - column
        links = (
            [far * 4 + by_x, near * 4 + by_x, home * 4 + across, home * 4 + by_x],
            [far * 4 + by_y, near * 4 + by_y, alone * 4 + by_y, home * 4 + by_y],
            [far * 4 + across, far * 4 + column, near * 4 + across, near * 4 + column],
            [alone * 4 + across, alone * 4 + by_x, alone * 4 + column],
        )
        return [link[turn] for turn in range(4) for link in links if turn < len(link)]

    pieces = ((0, 5), (5, 11), (11, 16))
    for slot in range(6):
        owner = OWNERS[slot]
        size = size_of(slot)

        @pl.when(dp == owner)
        def _():
            waiting = queue(owner)
            ready = set()
            for first, last in (pieces[0], pieces[2], pieces[1]):
                part = pl.ds(first * rows, (last - first) * rows)
                value = contract(factor[part, :], own[:, 0:size], 1, 0) * scale[0:1, 0:1]
                orth[part, 0:size] = value.astype(orth.dtype)
                ready.update(range(first, last))
                while waiting and waiting[0] in ready:
                    deliver(slot, waiting.pop(0)).start()
            pltpu.make_async_copy(at(orth, owner).at[:, 0:size], low_of(slot), recv.at[slot]).start()

    for slot in (4, 5):

        def pass_on(level, target):
            block = relayed.at[level]
            remote(block, block, relay_send.at[level], relay_recv.at[level], dp, core).wait_recv()
            relay_copy(slot, level, target).start()

        onward(slot, pass_on)

    stage.need("attn", "mlp")
    for slot in range(6):
        owner = OWNERS[slot]
        low = low_of(slot)

        @pl.when(dp != owner)
        def _():
            remote(low, low, send.at[0], recv.at[slot], owner, core).wait_recv()

        @pl.when(dp == owner)
        def _():
            pltpu.make_async_copy(low, low, recv.at[slot]).wait()

        @pl.loop(0, rows // 16)
        def _(i):
            part = pl.ds(pl.multiple_of(i * 16, 16), 16)
            step = rates[slot] * low[part, :].astype(jnp.float32)
            if slot < 4:
                attn_new[part, slot, :] = attn[part, slot, :] - step
            else:
                mlp_new[part, slot - 4, :] = mlp[part, slot - 4, :] - step

    for slot in range(6):
        owner = OWNERS[slot]

        @pl.when(dp == owner)
        def _():
            for target in range(count):
                if target != owner:
                    deliver(slot, target).wait_send()

    for slot in (4, 5):
        onward(slot, lambda level, target: relay_copy(slot, level, target).wait_send())


def scatter_rows(factor, scale, owned, attn, mlp, rates, collective_id):
    dma = pltpu.SemaphoreType.DMA
    count = lax.axis_size("dp")
    rows = attn.shape[0]
    shape = jax.ShapeDtypeStruct
    vmem = pl.BlockSpec(memory_space=pltpu.VMEM)
    anywhere = pl.BlockSpec(memory_space=pl.ANY)
    return pl.pallas_call(
        functools.partial(scatter_kernel, rates),
        out_shape=[shape(attn.shape, jnp.float32), shape(mlp.shape, jnp.float32)],
        in_specs=[vmem] * 2 + [anywhere] * 3,
        out_specs=[vmem] * 2,
        scratch_shapes=[
            pltpu.VMEM(owned.shape[1:], owned.dtype),
            pltpu.VMEM(attn.shape, attn.dtype),
            pltpu.VMEM(mlp.shape, mlp.dtype),
            pltpu.VMEM(owned.shape[1:], owned.dtype),
            pltpu.VMEM((4, rows, attn.shape[2]), jnp.bfloat16),
            pltpu.VMEM((2, rows, mlp.shape[2]), jnp.bfloat16),
            pltpu.VMEM((LINE, rows, mlp.shape[2]), jnp.bfloat16),
            dma((count,)),
            dma((6,)),
            dma((LINE,)),
            dma((LINE,)),
            dma((3,)),
        ],
        compiler_params=pltpu.CompilerParams(
            collective_id=collective_id, has_side_effects=True, vmem_limit_bytes=32 * MIB
        ),
        name="scatter_rows",
    )(factor, scale, owned, attn, mlp)


def head_mask(shape):
    return lax.broadcasted_iota(jnp.int32, shape, 1) < HD


def spans(length):
    return [(start, min(256, length - start)) for start in range(0, length, 256)]


def attend_forward(q_ref, k_ref, v_ref, o_ref, lse_ref, turned, value_turned, after=lambda head: None):
    length = q_ref.shape[0]
    value_turned[...] = v_ref[...].astype(jnp.float32).T.astype(jnp.bfloat16)
    keys = k_ref[...]
    for head in range(2):
        mine = head_mask(keys.shape) if head == 0 else ~head_mask(keys.shape)
        head_keys = jnp.where(mine, keys, jnp.zeros_like(keys))
        for start, size in spans(length):
            stop = start + size
            scores = contract(head_keys[0:stop], q_ref[start:stop, :], 1, 1)
            key_at = lax.broadcasted_iota(jnp.int32, (stop, size), 0)
            query_at = lax.broadcasted_iota(jnp.int32, (stop, size), 1) + start
            scores = jnp.where(key_at <= query_at, scores, -1e30)
            peak = jnp.max(scores, axis=0, keepdims=True)
            weights = jnp.exp(scores - peak)
            total = jnp.sum(weights, axis=0, keepdims=True)
            mixed = contract(
                value_turned[head * HD : (head + 1) * HD, 0:stop], weights.astype(jnp.bfloat16), 1, 0
            )
            turned[head * HD : (head + 1) * HD, start:stop] = mixed / total
            lse_ref[head : head + 1, start:stop] = peak + jnp.log(total)
        after(head)
    o_ref[...] = turned[...].T.astype(jnp.bfloat16)


def attend_backward(q_ref, k_ref, v_ref, o_ref, do_ref, lse_ref, dq_ref, dk_ref, dv_ref, turned):
    length = q_ref.shape[0]
    keys, values = k_ref[...], v_ref[...]
    key_turned = keys.astype(jnp.float32).T.astype(jnp.bfloat16)
    inner = (o_ref[...].astype(jnp.float32) * do_ref[...].astype(jnp.float32)).T
    mask = head_mask(keys.shape)
    turned[...] = jnp.zeros_like(turned)
    for start, size in spans(length):
        stop = start + size
        both_k, both_v = [], []
        for head in range(2):
            mine = mask[start:stop] if head == 0 else ~mask[start:stop]
            head_keys = jnp.where(mine, keys[start:stop], 0)
            head_values = jnp.where(mine, values[start:stop], 0)
            head_inner = jnp.sum(inner[head * HD : (head + 1) * HD, start:], axis=0, keepdims=True)
            scores = contract(head_keys, q_ref[start:, :], 1, 1)
            grad_prob = contract(head_values, do_ref[start:, :], 1, 1)
            key_at = lax.broadcasted_iota(jnp.int32, scores.shape, 0)
            query_at = lax.broadcasted_iota(jnp.int32, scores.shape, 1)
            scores = jnp.where(key_at <= query_at, scores, -1e30)
            prob = jnp.exp(scores - lse_ref[head : head + 1, start:])
            grad_scores = (prob * (grad_prob - head_inner)).astype(jnp.bfloat16)
            both_v.append(contract(prob.astype(jnp.bfloat16), do_ref[start:, :], 1, 0))
            both_k.append(contract(grad_scores, q_ref[start:, :], 1, 0))
            turned[head * HD : (head + 1) * HD, start:] += contract(
                key_turned[head * HD : (head + 1) * HD, start:stop], grad_scores, 1, 0
            )
        pick = mask[start:stop]
        dk_ref[start:stop, :] = jnp.where(pick, both_k[0], both_k[1]).astype(jnp.bfloat16)
        dv_ref[start:stop, :] = jnp.where(pick, both_v[0], both_v[1]).astype(jnp.bfloat16)
    dq_ref[...] = (turned[...].T * (1.0 / math.sqrt(HD))).astype(jnp.bfloat16)


def pairs_forward(queries, keys, values):
    length, width = queries.shape
    block = pl.BlockSpec((length, 2 * HD), lambda i: (0, i))
    stat = pl.BlockSpec((None, 2, length), lambda i: (i, 0, 0))
    return pl.pallas_call(
        attend_forward,
        grid=(width // (2 * HD),),
        out_shape=[
            jax.ShapeDtypeStruct((length, width), jnp.bfloat16),
            jax.ShapeDtypeStruct((width // (2 * HD), 2, length), jnp.float32),
        ],
        in_specs=[block] * 3,
        out_specs=[block, stat],
        scratch_shapes=[pltpu.VMEM((2 * HD, length), jnp.float32), pltpu.VMEM((2 * HD, length), jnp.bfloat16)],
        compiler_params=pltpu.CompilerParams(vmem_limit_bytes=48 * MIB),
        name="attend_forward",
    )(queries, keys, values)


def pairs_backward(queries, keys, values, attended, grad_attended, stats):
    length, width = queries.shape
    block = pl.BlockSpec((length, 2 * HD), lambda i: (0, i))
    stat = pl.BlockSpec((None, 2, length), lambda i: (i, 0, 0))
    return pl.pallas_call(
        attend_backward,
        grid=(width // (2 * HD),),
        out_shape=[jax.ShapeDtypeStruct((length, width), jnp.bfloat16)] * 3,
        in_specs=[block] * 5 + [stat],
        out_specs=[block] * 3,
        scratch_shapes=[pltpu.VMEM((2 * HD, length), jnp.float32)],
        compiler_params=pltpu.CompilerParams(vmem_limit_bytes=48 * MIB),
        name="attend_backward",
    )(queries, keys, values, attended, grad_attended, stats)


NORM_ROWS = 240


class Gathering:
    def __init__(self, a_ref, b_ref, a_out, b_out, send, recv, local):
        self.own = (a_ref, b_ref)
        self.outs = (a_out, b_out)
        self.send, self.recv, self.local = send, recv, local
        self.rows = a_ref.shape[0]
        self.dp, self.core, self.z, self.y, self.x = place()
        self.x_peer = self.dp + 1 - 2 * self.x
        self.y_peer = self.dp + 2 - 4 * self.y

    def block(self, side, index):
        return self.outs[side].at[pl.ds(pl.multiple_of(index * self.rows, self.rows), self.rows)]

    def copy(self, kind, side, index, own, target):
        src = self.own[side] if own else self.block(side, index)
        return remote(
            src, self.block(side, index), self.send.at[kind, index // 4], self.recv.at[side, index], target, self.core
        )

    def arrived(self, side, index):
        block = self.block(side, index)
        remote(block, block, self.send.at[0, 0], self.recv.at[side, index], self.dp, self.core).wait_recv()

    def at(self, level, y_off, x_off):
        y = self.y + y_off * (1 - 2 * self.y)
        x = self.x + x_off * (1 - 2 * self.x)
        return level * 4 + y * 2 + x

    def line(self, level, own, action):
        index = self.at(level, 0, 0)

        @pl.when((self.z < LINE - 1) & (level <= self.z))
        def _():
            for side in range(2):
                action(self.copy(side, side, index, own, self.dp + 4))

        @pl.when((self.z > 0) & (level >= self.z))
        def _():
            for side in range(2):
                action(self.copy(2 + side, side, index, own, self.dp - 4))

        for side in range(2):
            action(self.copy(4 + side, side, index, own, self.x_peer))
            action(self.copy(6 + side, side, index, own, self.y_peer))

    def relays(self, level):
        return (
            (0, self.at(level, 0, 1), self.copy(8, 0, self.at(level, 0, 1), False, self.y_peer)),
            (1, self.at(level, 1, 0), self.copy(9, 1, self.at(level, 1, 0), False, self.x_peer)),
        )

    def by_distance(self, distance, action):
        if distance == 0:
            action(self.z)
            return

        @pl.when(self.z >= distance)
        def _():
            action(self.z - distance)

        @pl.when(self.z + distance < LINE)
        def _():
            action(self.z + distance)

    def local_copies(self):
        return [
            pltpu.make_async_copy(self.own[side], self.block(side, self.dp), self.local.at[side]) for side in range(2)
        ]

    def begin(self):
        self.line(self.z, True, lambda copy: copy.start())
        for copy in self.local_copies():
            copy.start()

    def onward(self, distance):
        def action(level):
            for side in range(2):
                self.arrived(side, self.at(level, 0, 0))
            self.line(level, False, lambda copy: copy.start())

        self.by_distance(distance, action)

    def relay(self, distance):
        def action(level):
            for side, index, copy in self.relays(level):
                self.arrived(side, index)
                copy.start()

        self.by_distance(distance, action)

    def finish(self):
        for level in range(LINE):
            self.arrived(1, self.at(level, 0, 1))
            self.arrived(0, self.at(level, 1, 0))
            for side in range(2):
                self.arrived(side, self.at(level, 1, 1))
        for copy in self.local_copies():
            copy.wait()

    def drain(self):
        for level in range(LINE):
            self.line(level, False, lambda copy: copy.wait_send())
            for _, _, copy in self.relays(level):
                copy.wait_send()


def norm_tile(values, gain, bias):
    centered = values - jnp.mean(values, axis=-1, keepdims=True)
    inverse = lax.rsqrt(jnp.mean(centered * centered, axis=-1, keepdims=True) + 1e-05)
    return centered * inverse * gain + bias


def tiles(count, rows, action):
    @pl.loop(0, count // rows)
    def _(i):
        action(pl.ds(pl.multiple_of(i * rows, rows), rows))


BACK_ROWS = 80


def fold(value):
    return jnp.sum(value.reshape(-1, 8, value.shape[1]), axis=0)


def norm_back_tile(grad, gain, values):
    centered = values - jnp.mean(values, axis=-1, keepdims=True)
    inverse = lax.rsqrt(jnp.mean(centered * centered, axis=-1, keepdims=True) + 1e-05)
    normed = centered * inverse
    scaled = grad * gain
    back = inverse * (
        scaled
        - jnp.mean(scaled, axis=-1, keepdims=True)
        - normed * jnp.mean(scaled * normed, axis=-1, keepdims=True)
    )
    return back, normed


def shifted(part, start):
    return pl.ds(pl.multiple_of(start + part.start, 16), part.size)


def column_sum(value):
    return jnp.sum(value, axis=0, keepdims=True)


def forward_kernel(
    tokens_in, vec_in, attn_in, mlp_in, cot_in,
    qk_out, vo_out, first_out, q_out, k_out, v_out, o_out, out_out, grad_mid_out, do_out, ga_out, gb_out, go_out,
    x_a, x_b, y_a, y_b, lse, vec, sums,
    tokens, qk_all, vo_all, f0, f1, p0, p1, first, q, k, v, o, middle, second, act, slope,
    turned, mixed, partial, partial_other, pre, attn, mlp, qk_shard, vo_shard, f0_shard, f1_shard, p0_shard, p1_shard,
    cot, out, grad_mid, do, ga, gb, go, du, back_partial, back_other, m_partial, m_other, low, across, acc,
    gather_send, gather_recv, local, swap_send, swap_recv, send, recv, stage_sems,
):
    dp, core, z, y, x = place()
    length = tokens.shape[0]
    width = q.shape[1]
    chunk = length // 4
    x_peer, y_peer = dp + 1 - 2 * x, dp + 2 - 4 * y
    shard_rows = x_a.shape[1]
    stage = Staging(stage_sems)
    stage.fetch("attn", attn_in, attn)
    stage.fetch("tokens", tokens_in, tokens)
    stage.fetch("mlp", mlp_in, mlp)
    stage.fetch("cot", cot_in, cot)
    for row in range(vec.shape[0]):
        for column in range(D // 128):
            at = row * (D // 128) + column
            vec[row : row + 1, column * 128 : (column + 1) * 128] = vec_in[at : at + 1, :]
    stage.need("attn")
    for slot, shard in enumerate((qk_shard, qk_shard, vo_shard, vo_shard)):
        shard[:, slot % 2 * width : (slot % 2 + 1) * width] = attn[:, slot, :].astype(jnp.bfloat16)
    barrier = pltpu.get_barrier_semaphore()
    greet(barrier, dp + 1 - 2 * x, core)
    greet(barrier, dp + 2 - 4 * y, core)
    greet(barrier, dp, 1 - core)

    @pl.when(z > 0)
    def _():
        greet(barrier, dp - 4, core)

    @pl.when(z < LINE - 1)
    def _():
        greet(barrier, dp + 4, core)

    pl.semaphore_wait(barrier, 3 + (z + 2) // 3 + (5 - z) // 3)

    rounds = [
        Gathering(a, b, a_out, b_out, gather_send.at[i], gather_recv.at[i], local.at[i])
        for i, (a, b, a_out, b_out) in enumerate(
            ((qk_shard, vo_shard, qk_all, vo_all), (f0_shard, f1_shard, f0, f1), (p0_shard, p1_shard, p0, p1))
        )
    ]
    rounds[0].begin()
    stage.need("tokens", "mlp")
    for slot, shard in enumerate((f0_shard, f1_shard, p0_shard, p1_shard)):
        shard[...] = mlp[:, slot // 2, slot % 2 * D : (slot % 2 + 1) * D].astype(jnp.bfloat16)

    def norm_one(part):
        tile = norm_tile(tokens[part, :].astype(jnp.float32), vec[0:1, :], vec[1:2, :])
        first[part, :] = tile.astype(jnp.bfloat16)

    tiles(length, NORM_ROWS, norm_one)
    stage.keep(first, first_out)
    rounds[0].onward(1)
    rounds[0].relay(0)
    rounds[0].onward(2)
    rounds[0].relay(1)
    rounds[0].onward(3)
    rounds[0].relay(2)
    rounds[0].relay(3)
    rounds[1].begin()
    rounds[0].finish()
    stage.keep(qk_all, qk_out)
    stage.keep(vo_all, vo_out)

    mine = pl.ds(pl.multiple_of(core * width, width), width)
    scale = 1.0 / math.sqrt(HD)
    q[...] = ((contract(first[...], qk_all[:, 0:width], 1, 0) + vec[4:5, mine]) * scale).astype(jnp.bfloat16)
    k[...] = contract(first[...], qk_all[:, width:], 1, 0).astype(jnp.bfloat16)
    v[...] = (contract(first[...], vo_all[:, 0:width], 1, 0) + vec[5:6, mine]).astype(jnp.bfloat16)

    for value, target in ((q, q_out), (k, k_out), (v, v_out)):
        stage.keep(value, target)

    def step(index):
        if index == 1:
            rounds[1].onward(1)
            rounds[1].relay(0)
        if index == 2:
            rounds[1].onward(2)
            rounds[1].relay(1)
        if index == 3:
            rounds[1].onward(3)
            rounds[1].relay(2)
        if index == 4:
            rounds[1].relay(3)
            rounds[2].begin()
        if index == 6:
            rounds[2].onward(1)
            rounds[2].relay(0)
        if index == 7:
            rounds[2].onward(2)
            rounds[2].relay(1)
        if index == 8:
            rounds[2].onward(3)
            rounds[2].relay(2)
        if index == 9:
            rounds[2].relay(3)

    for pair in range(width // (2 * HD)):
        lanes = pl.ds(pair * 2 * HD, 2 * HD)
        attend_forward(
            q.at[:, lanes], k.at[:, lanes], v.at[:, lanes], o.at[:, lanes], lse.at[pair], turned, mixed,
            lambda head: step(2 * pair + head),
        )

    stage.keep(o, o_out)

    def swap_copy(kind, i):
        part = pl.ds(i * chunk, chunk)
        src, dst = ((back_partial, back_other), (m_partial, m_other), (partial, partial_other))[kind]
        return remote(src.at[part], dst.at[part], swap_send.at[kind, i], swap_recv.at[kind, i], dp, 1 - core)

    for i in range(4):
        part = pl.ds(i * chunk, chunk)
        partial[part, :] = contract(o[part, :], vo_all[:, width:], 1, 1).astype(jnp.bfloat16)
        swap_copy(2, i).start()
    step(6)
    rounds[1].finish()
    for i in range(4):
        swap_copy(2, i).wait_recv()

        def norm_two(part):
            rows = pl.ds(pl.multiple_of(i * chunk + part.start, 16), part.size)
            total = partial[rows, :].astype(jnp.float32) + partial_other[rows, :].astype(jnp.float32)
            tile = tokens[rows, :].astype(jnp.float32) + total + vec[6:7, :]
            middle[rows, :] = tile
            second[rows, :] = norm_tile(tile, vec[2:3, :], vec[3:4, :]).astype(jnp.bfloat16)

        tiles(chunk, NORM_ROWS, norm_two)
        rows = pl.ds(i * chunk, chunk)
        for side, weight in enumerate((f0, f1)):
            pre[:, side * D : (side + 1) * D] = contract(second[rows, :], weight[...], 1, 0)

        def curve(part):
            rows = pl.ds(pl.multiple_of(i * chunk + part.start, 16), part.size)
            for side in range(2):
                columns = pl.ds(side * D, D)
                value = pre[part, columns] + vec[pl.ds(8 + 2 * core + side, 1), :]
                square = value * value
                root = math.sqrt(2.0 / math.pi)
                bent = jnp.tanh(value * (root + root * 0.044715 * square))
                half = 0.5 + 0.5 * bent
                act[rows, columns] = (value * half).astype(jnp.bfloat16)
                inner = root + (3.0 * root * 0.044715) * square
                slope[rows, columns] = (half + (0.5 * value) * (1.0 - bent * bent) * inner).astype(jnp.bfloat16)

        tiles(chunk, 48, curve)
        step(7 + i)

    def early(side, level):
        grad, to_x, to_y = ((ga, x_a, y_a), (gb, x_b, y_b))[side]
        x_block = level * 4 + y * 2 + 1 - x
        y_block = level * 4 + (1 - y) * 2 + x

        def part(block):
            return grad.at[pl.ds(pl.multiple_of(block * shard_rows, shard_rows), shard_rows)]

        return (
            remote(part(x_block), to_x.at[level], send.at[side, level], recv.at[side, level], x_peer, core),
            remote(part(y_block), to_y.at[level], send.at[2 + side, level], recv.at[2 + side, level], y_peer, core),
        )

    def outer(left, right, target, start):
        size = right.shape[1]
        for block in range(D // 256):
            part = pl.ds(block * 256, 256)
            value = contract(left[part, :], right[...], 1, 0)
            target[part, start : start + size] = value.astype(jnp.bfloat16)
            row = 6 if size == D else 7
            sums[row : row + 1, 0:size] += column_sum(value * value)

    stage.need("cot")
    sums[...] = jnp.zeros_like(sums)
    across[...] = cot[...].T
    for side in range(2):
        outer(across, act.at[:, side * D : (side + 1) * D], gb, side * D)
    for level in range(LINE):
        for copy in early(1, level):
            copy.start()
    rounds[2].finish()
    acc[...] = jnp.zeros_like(acc)
    for i in range(4):
        part = pl.ds(i * chunk, chunk)
        for side, weight in enumerate((p0, p1)):
            columns = pl.ds(side * D, D)
            value = contract(cot[part, :], weight[...], 1, 0) * slope[part, columns].astype(jnp.float32)
            value = value.astype(jnp.bfloat16)
            du[part, columns] = value
            sums[4 + side : 5 + side, :] += column_sum(value.astype(jnp.float32))
        back_partial[part, :] = (
            contract(du[part, 0:D], f0[...], 1, 1) + contract(du[part, D:], f1[...], 1, 1)
        ).astype(jnp.bfloat16)
        swap_copy(0, i).start()
    across[...] = second[...].T
    for side in range(2):
        outer(across, du.at[:, side * D : (side + 1) * D], ga, side * D)
    for level in range(LINE):
        for copy in early(0, level):
            copy.start()
    stage.keep(ga, ga_out)
    for i in range(4):
        part = pl.ds(i * chunk, chunk)
        m_partial[part, :] = (
            contract(act[part, 0:D], p0[...], 1, 1) + contract(act[part, D:], p1[...], 1, 1)
        ).astype(jnp.bfloat16)
        swap_copy(1, i).start()
    stage.keep(gb, gb_out)
    for i in range(4):
        swap_copy(0, i).wait_recv()

        def back(part):
            rows = shifted(part, i * chunk)
            grad = back_partial[rows, :].astype(jnp.float32) + back_other[rows, :].astype(jnp.float32)
            outgoing = cot[rows, :].astype(jnp.float32)
            value, normed = norm_back_tile(grad, vec[2:3, :], middle[rows, :])
            value = value + outgoing
            grad_mid[rows, :] = value
            low[rows, :] = value.astype(jnp.bfloat16)
            acc[0] += fold(grad * normed)
            acc[1] += fold(grad)
            acc[2] += fold(value)
            acc[3] += fold(outgoing)

        tiles(chunk, BACK_ROWS, back)
        rows = pl.ds(i * chunk, chunk)
        do[rows, :] = contract(low[rows, :], vo_all[:, width:], 1, 0).astype(jnp.bfloat16)
    for row in range(4):
        sums[row : row + 1, :] = column_sum(acc[row])
    stage.keep(grad_mid, grad_mid_out)
    stage.keep(do, do_out)
    across[...] = low[...].T
    outer(across, o, go, 0)
    stage.keep(go, go_out)
    for i in range(4):
        swap_copy(1, i).wait_recv()

        def finish(part):
            rows = shifted(part, i * chunk)
            total = m_partial[rows, :].astype(jnp.float32) + m_other[rows, :].astype(jnp.float32)
            out[rows, :] = (middle[rows, :] + total + vec[7:8, :]).astype(jnp.bfloat16)

        tiles(chunk, 48, finish)
        part = pl.ds(i * chunk, chunk)
        stage.keep(out.at[part], out_out.at[part])
    for kind in range(3):
        for i in range(4):
            swap_copy(kind, i).wait_send()
    for side in range(2):
        for level in range(LINE):
            for copy in early(side, level):
                copy.wait()
    for gathering in rounds:
        gathering.drain()
    stage.finish()


def forward(tokens, vec, attn, mlp, cot, collective_id):
    dma = pltpu.SemaphoreType.DMA
    low = jnp.bfloat16
    count = lax.axis_size("dp")
    length = tokens.shape[0]
    rows, _, width = attn.shape
    hidden = 2 * D
    shape = jax.ShapeDtypeStruct
    scratch = pltpu.VMEM
    vmem = pl.BlockSpec(memory_space=pltpu.VMEM)
    anywhere = pl.BlockSpec(memory_space=pl.ANY)
    whole, thin, wide = (length, D), (length, width), (length, hidden)
    return pl.pallas_call(
        forward_kernel,
        out_shape=[shape((D, D), low)] * 2
        + [shape(whole, low)]
        + [shape(thin, low)] * 4
        + [
            shape(whole, low),
            shape(whole, jnp.float32),
            shape(thin, low),
            shape((D, hidden), low),
            shape((D, hidden), low),
            shape((D, width), low),
        ]
        + [shape((LINE, rows, hidden), low)] * 4
        + [
            shape((width // (2 * HD), 2, length), jnp.float32),
            shape((vec.shape[0] * 128 // D, D), jnp.float32),
            shape((8, D), jnp.float32),
        ],
        in_specs=[anywhere, vmem] + [anywhere] * 3,
        out_specs=[anywhere] * 17 + [vmem] * 3,
        scratch_shapes=[scratch(whole, low)]
        + [scratch((D, D), low)] * 6
        + [scratch(whole, low)]
        + [scratch(thin, low)] * 4
        + [
            scratch(whole, jnp.float32),
            scratch(whole, low),
            scratch(wide, low),
            scratch(wide, low),
            scratch((2 * HD, length), jnp.float32),
            scratch((2 * HD, length), low),
            scratch(whole, low),
            scratch(whole, low),
            scratch((length // 4, hidden), jnp.float32),
            scratch(attn.shape, jnp.float32),
            scratch(mlp.shape, jnp.float32),
        ]
        + [scratch((rows, D), low)] * 6
        + [
            scratch(whole, low),
            scratch(whole, low),
            scratch(whole, jnp.float32),
            scratch(thin, low),
            scratch((D, hidden), low),
            scratch((D, hidden), low),
            scratch((D, width), low),
            scratch(wide, low),
        ]
        + [scratch(whole, low)] * 5
        + [
            scratch((D, length), low),
            scratch((4, 8, D), jnp.float32),
            dma((3, 10, LINE)),
            dma((3, 2, count)),
            dma((3, 2)),
            dma((3, 4)),
            dma((3, 4)),
            dma((4, LINE)),
            dma((4, LINE)),
            dma((32,)),
        ],
        compiler_params=pltpu.CompilerParams(
            collective_id=collective_id, has_side_effects=True, vmem_limit_bytes=63 * MIB
        ),
        name="forward",
    )(tokens, vec, attn, mlp, cot)


class Reducing:
    def __init__(self, grads, buffers, sources, send, recv, rows, direct):
        self.direct = direct
        self.grads, self.sources = grads, sources
        self.diag, self.from_x, self.from_y, self.up, self.down = buffers[0:2], buffers[2:4], buffers[4:6], buffers[6:8], buffers[8:10]
        self.send, self.recv, self.rows = send, recv, rows
        self.dp, self.core, self.z, self.y, self.x = place()
        self.x_peer = self.dp + 1 - 2 * self.x
        self.y_peer = self.dp + 2 - 4 * self.y
        half = self.z // 2
        self.order = (3 - 3 * half, 2 - half, 1 - self.z + 4 * half, self.z)

    def at(self, ref, block):
        return ref.at[pl.ds(pl.multiple_of(block * self.rows, self.rows), self.rows)]

    def block(self, level, y_off, x_off):
        y = self.y + y_off * (1 - 2 * self.y)
        x = self.x + x_off * (1 - 2 * self.x)
        return level * 4 + y * 2 + x

    def go(self, kind, level, src, dst, target):
        return remote(src, dst, self.send.at[kind, level], self.recv.at[kind, level], target, self.core)

    def diag_copy(self, level, side):
        block = self.at(self.sources[side], self.block(level, 1, 1))
        target = self.block(self.z, 1, 1) if self.direct else (self.y_peer, self.x_peer)[side]
        return self.go(side, level, block, self.diag[side].at[level], target)

    def own_copy(self, level, side):
        block = self.at(self.sources[side], self.block(level, 1 - side, side))
        target = (self.from_y, self.from_x)[side][side].at[level]
        return self.go(2 + side, level, block, target, (self.y_peer, self.x_peer)[side])

    def sum_copy(self, level, side):
        target = (self.from_x, self.from_y)[side][side].at[level]
        return self.go(4 + side, level, self.diag[side].at[level], target, (self.x_peer, self.y_peer)[side])

    def up_copy(self, level, side):
        return self.go(6 + side, level, self.from_x[side].at[level], self.up[side].at[level], self.dp + 4)

    def down_copy(self, level, side):
        return self.go(8 + side, level, self.from_x[side].at[level], self.down[side].at[level], self.dp - 4)

    def first(self, *indices):
        for index in indices:
            level = self.order[index]
            for side in range(2):
                self.diag_copy(level, side).start()
            for side in () if self.direct else range(2):
                self.own_copy(level, side).start()

    def scale(self, factor, factor_x, factor_y, factor_diag):
        self.factor, self.factor_x, self.factor_y, self.factor_diag = factor, factor_x, factor_y, factor_diag

    def weigh(self, side, block, dst, scale_dst, terms):
        grad = self.grads[side]

        @pl.loop(0, self.rows // 16)
        def _(i):
            part = pl.ds(pl.multiple_of(i * 16, 16), 16)
            own = grad[pl.ds(pl.multiple_of(block * self.rows + i * 16, 16), 16), :]
            total = self.factor * own.astype(jnp.float32)
            for scale, ref in ((scale_dst, dst),) + terms:
                value = ref[part, :].astype(jnp.float32)
                total = total + (value if scale is None else scale * value)
            dst[part, :] = total.astype(dst.dtype)

    def sums(self, level):
        for side in range(2):
            self.diag_copy(level, side).wait_recv()
            block = self.block(level, side, 1 - side)
            self.weigh(side, block, self.diag[side].at[level], (self.factor_y, self.factor_x)[side], ())
            self.sum_copy(level, side).start()

    def scales(self, side):
        if self.direct:
            return self.factor_x, self.factor_y
        return (None, self.factor_y) if side == 0 else (self.factor_x, None)

    def arrivals(self, level, side):
        if self.direct:
            self.diag_copy(level, side).wait_recv()
            return
        self.own_copy(level, side).wait_recv()
        self.sum_copy(level, side).wait_recv()

    def chain(self, index):
        level = self.order[index]
        block = self.block(level, 0, 0)
        for side in range(2):
            self.arrivals(level, side)
            scale_x, scale_y = self.scales(side)
            terms = ((scale_y, self.from_y[side].at[level]),)
            if self.direct:
                terms = terms + ((self.factor_diag, self.diag[side].at[level]),)

            def combine(*extra):
                self.weigh(side, block, self.from_x[side].at[level], scale_x, terms + extra)

            @pl.when(level > self.z)
            def _():
                @pl.when(self.z > 0)
                def _():
                    self.up_copy(level, side).wait_recv()
                    combine((None, self.up[side].at[level]))

                @pl.when(self.z == 0)
                def _():
                    combine()

                self.up_copy(level, side).start()

            @pl.when(level < self.z)
            def _():
                @pl.when(self.z < LINE - 1)
                def _():
                    self.down_copy(level, side).wait_recv()
                    combine((None, self.down[side].at[level]))

                @pl.when(self.z == LINE - 1)
                def _():
                    combine()

                self.down_copy(level, side).start()

    def last(self, side):
        self.arrivals(self.z, side)

        @pl.when(self.z > 0)
        def _():
            self.up_copy(self.z, side).wait_recv()

        @pl.when(self.z == 0)
        def _():
            self.up[side][0] = jnp.zeros(self.up[side].shape[1:], self.up[side].dtype)

        @pl.when(self.z < LINE - 1)
        def _():
            self.down_copy(self.z, side).wait_recv()

        @pl.when(self.z == LINE - 1)
        def _():
            self.down[side][LINE - 1] = jnp.zeros(self.down[side].shape[1:], self.down[side].dtype)

    def total(self, side, part, columns):
        here = pl.ds(pl.multiple_of(self.dp * self.rows + part.start, 16), part.size)
        total = self.factor * self.grads[side][here, columns].astype(jnp.float32)
        terms = list(zip(self.scales(side) + (None, None), (self.from_x, self.from_y, self.up, self.down)))
        if self.direct:
            terms.append((self.factor_diag, self.diag))
        for scale, ref in terms:
            value = ref[side][self.z, part, columns].astype(jnp.float32)
            total = total + (value if scale is None else scale * value)
        return total

    def drain(self):
        for level in range(LINE):
            for side in range(2):
                self.diag_copy(level, side).wait_send()
                if not self.direct:
                    self.own_copy(level, side).wait_send()
                    self.sum_copy(level, side).wait_send()

            @pl.when(level > self.z)
            def _():
                for side in range(2):
                    self.up_copy(level, side).wait_send()

            @pl.when(level < self.z)
            def _():
                for side in range(2):
                    self.down_copy(level, side).wait_send()


def owner_at(slot):
    return OWNERS[slot] // 4, OWNERS[slot] % 4 // 2, OWNERS[slot] % 2


def attn_back_kernel(
    noise_scale, batch, clip,
    tokens_in, vec, first_in, q_in, k_in, v_in, o_in, do_in, lse, qk_in, vo_in, grad_mid_in, ga_in, gb_in, go_in,
    x_a_in, x_b_in, y_a_in, y_b_in, sums, included, attn_mom_in, mlp_mom_in, attn_noise_in, mlp_noise_in,
    grad_in_out, attn_out, mlp_out, vec_out, owned,
    tokens, first, q, k, v, o, do, qk_all, wv, grad_mid, ga, gb, attn_mom, mlp_mom, attn_noise, mlp_noise, grad_in,
    dqk, dv, ga_late, gb_late, head_turned, turned, partial, other, acc, square, factors,
    diag_a, diag_b, x_a, x_b, y_a, y_b, up_a, up_b, down_a, down_b,
    late_diag_a, late_diag_b, late_x_a, late_x_b, late_y_a, late_y_b, late_up_a, late_up_b, late_down_a, late_down_b,
    attn_low, mlp_low, relayed, vec_plane, vec_line,
    send, recv, late_send, late_recv, vec_sems, line_sems, gather_send, gather_recv, relay_sems, swap_send, swap_recv, small, pass_send, pass_recv,
    stage_sems,
):
    dp, core, z, y, x = place()
    rows, _, width = attn_mom.shape
    wide = mlp_mom.shape[2]
    length = tokens.shape[0]
    chunk = length // 4
    x_peer, y_peer = dp + 1 - 2 * x, dp + 2 - 4 * y
    count = ga.shape[0] // rows
    stage = Staging(stage_sems)
    for name, src, dst in (
        ("q", q_in, q), ("k", k_in, k), ("v", v_in, v), ("o", o_in, o), ("do", do_in, do), ("qk_all", qk_in, qk_all),
        ("wv", vo_in.at[:, pl.ds(0, width)], wv), ("first", first_in, first), ("go", go_in, gb_late.at[:, pl.ds(width, width)]),
        ("tokens", tokens_in, tokens), ("grad_mid", grad_mid_in, grad_mid), ("ga", ga_in, ga), ("gb", gb_in, gb),
        ("x_a", x_a_in, x_a), ("x_b", x_b_in, x_b), ("y_a", y_a_in, y_a), ("y_b", y_b_in, y_b),
        ("mlp_mom", mlp_mom_in, mlp_mom), ("mlp_noise", mlp_noise_in, mlp_noise), ("attn_mom", attn_mom_in, attn_mom),
        ("attn_noise", attn_noise_in, attn_noise),
    ):
        stage.fetch(name, src, dst)
    greeted = greet_plane(dp, core, count, z, y, x)

    main = Reducing(
        (ga, gb), (diag_a, diag_b, x_a, x_b, y_a, y_b, up_a, up_b, down_a, down_b), (ga_in, gb_in), send, recv, rows, True
    )
    late = Reducing(
        (ga_late, gb_late),
        (late_diag_a, late_diag_b, late_x_a, late_x_b, late_y_a, late_y_b, late_up_a, late_up_b, late_down_a, late_down_b),
        (ga_late, gb_late),
        late_send,
        late_recv,
        rows,
        False,
    )

    def small_copy(index):
        src, dst, target = (
            (square.at[0], square.at[1], (dp, 1 - core)),
            (factors.at[0], factors.at[1], (x_peer, core)),
            (factors.at[0], factors.at[2], (y_peer, core)),
            (factors.at[0], factors.at[3], (main.block(z, 1, 1), core)),
        )[index]
        return remote(src, dst, small.at[0, index], small.at[1, index], *target)

    mine_in_plane = (y * 2 + x) * 2 + core

    def plane_copies():
        copies = []
        for y_off, x_off, core_off in [(i // 4, i // 2 % 2, i % 2) for i in range(1, 8)]:
            target = main.block(z, y_off, x_off)
            target_core = core + core_off * (1 - 2 * core)
            place_there = target % 4 * 2 + target_core
            copies.append(
                remote(
                    vec_plane.at[mine_in_plane], vec_plane.at[mine_in_plane], vec_sems.at[0, place_there],
                    vec_sems.at[1, mine_in_plane], target, target_core,
                )
            )
        return copies

    def plane_arrivals():
        for i in range(1, 8):
            index = (mine_in_plane + i) % 8
            block = vec_plane.at[index]
            remote(block, block, vec_sems.at[0, index], vec_sems.at[1, index], dp, core).wait_recv()

    def line_copies():
        return [
            remote(vec_line.at[z], vec_line.at[z], line_sems.at[0, (z + i) % LINE], line_sems.at[1, z], (dp + 4 * i) % count, core)
            for i in range(1, LINE)
        ]

    def vec_turn():
        plane_arrivals()
        total = vec_plane[0]
        for index in range(1, 8):
            total = total + vec_plane[index]
        vec_line[z] = total
        for copy in line_copies():
            copy.start()

    def vec_finish():
        for i in range(1, LINE):
            index = (z + i) % LINE
            block = vec_line.at[index]
            remote(block, block, line_sems.at[0, index], line_sems.at[1, index], dp, core).wait_recv()
        total = vec_line[0]
        for index in range(1, LINE):
            total = total + vec_line[index]
        per_row = D // 128
        for row in range(vec_out.shape[0]):
            at = row % per_row * 128
            vec_out[row : row + 1, :] = total[row // per_row : row // per_row + 1, at : at + 128]
        for copy in plane_copies() + line_copies():
            copy.wait_send()

    def swap_copy(i):
        part = pl.ds(i * chunk, chunk)
        return remote(partial.at[part], other.at[part], swap_send.at[i], swap_recv.at[i], dp, 1 - core)

    acc[...] = jnp.zeros_like(acc)
    stage.need("q", "k", "v", "o", "do")
    for pair in range(width // (2 * HD)):
        lanes = pl.ds(pair * 2 * HD, 2 * HD)
        attend_backward(
            q.at[:, lanes], k.at[:, lanes], v.at[:, lanes], o.at[:, lanes], do.at[:, lanes], lse.at[pair],
            dqk.at[:, lanes], dqk.at[:, pl.ds(width + pair * 2 * HD, 2 * HD)], dv.at[:, lanes], head_turned,
        )
        if pair == 0:
            greeted()
            main.first(0, 1, 2, 3)
    stage.need("qk_all", "wv")
    for i in range(4):
        part = pl.ds(i * chunk, chunk)
        partial[part, :] = (contract(dqk[part, :], qk_all[...], 1, 1) + contract(dv[part, :], wv[...], 1, 1)).astype(
            jnp.bfloat16
        )
        swap_copy(i).start()
    stage.need("first", "go")
    turned[...] = first[...].T
    squares = jnp.zeros((1, 1), jnp.float32)
    for right, target in ((dqk, ga_late), (dv, gb_late)):
        for block in range(D // 256):
            part = pl.ds(block * 256, 256)
            value = contract(turned[part, :], right[...], 1, 0)
            target[part, 0 : right.shape[1]] = value.astype(jnp.bfloat16)
            squares = squares + jnp.sum(column_sum(value * value), axis=1, keepdims=True)
    late.first(0, 1)
    bias_q = column_sum(dqk[:, 0:width].astype(jnp.float32))
    bias_v = column_sum(dv[...].astype(jnp.float32))
    for value in (sums[6:7, :], sums[7:8, :]):
        squares = squares + jnp.sum(value, axis=1, keepdims=True)
    for value in (bias_q, bias_v, sums[4:5, :], sums[5:6, :]):
        squares = squares + jnp.sum(value * value, axis=1, keepdims=True)
    square[0] = jnp.broadcast_to(squares, square.shape[1:])
    small_copy(0).start()

    stage.need("tokens", "grad_mid")
    for i in range(4):
        swap_copy(i).wait_recv()

        def back(part):
            here = shifted(part, i * chunk)
            grad = partial[here, :].astype(jnp.float32) + other[here, :].astype(jnp.float32)
            value, normed = norm_back_tile(grad, vec[0:1, :], tokens[here, :].astype(jnp.float32))
            grad_in[here, :] = (grad_mid[here, :] + value).astype(jnp.bfloat16)
            acc[0] += fold(grad * normed)
            acc[1] += fold(grad)

        tiles(chunk, BACK_ROWS, back)
    stage.keep(grad_in, grad_in_out)
    gain_one, bias_one = column_sum(acc[0]), column_sum(acc[1])
    shared = jnp.zeros((1, 1), jnp.float32)
    for value in (gain_one, bias_one, sums[0:1, :], sums[1:2, :], sums[2:3, :], sums[3:4, :]):
        shared = shared + jnp.sum(value * value, axis=1, keepdims=True)
    small_copy(0).wait_recv()
    norm = jnp.sqrt(square[0, 0:1, 0:1] + square[1, 0:1, 0:1] + shared)
    factor = included[0].astype(jnp.float32) * jnp.minimum(1.0, clip / (norm + 1e-06))
    factors[0] = jnp.broadcast_to(factor, factors.shape[1:])
    for index in (1, 2, 3):
        small_copy(index).start()
    leading = factor * (1 - core).astype(jnp.float32)
    vec_plane[mine_in_plane] = jnp.zeros(vec_plane.shape[1:], jnp.float32)
    mine = pl.ds(pl.multiple_of(core * width, width), width)
    for row, value in ((0, gain_one), (1, bias_one), (2, sums[0:1, :]), (3, sums[1:2, :]), (6, sums[2:3, :]), (7, sums[3:4, :])):
        vec_plane[mine_in_plane, row : row + 1, :] = leading * value
    vec_plane[mine_in_plane, 4:5, mine] = factor * bias_q
    vec_plane[mine_in_plane, 5:6, mine] = factor * bias_v
    vec_plane[mine_in_plane, pl.ds(8 + 2 * core, 1), :] = factor * sums[4:5, :]
    vec_plane[mine_in_plane, pl.ds(9 + 2 * core, 1), :] = factor * sums[5:6, :]
    stage.need("ga", "gb", "x_a", "x_b", "y_a", "y_b", "mlp_mom", "mlp_noise", "attn_mom", "attn_noise")
    for index in (1, 2, 3):
        small_copy(index).wait_recv()
    for part in (main, late):
        part.scale(factor, factors[1, 0:1, 0:1], factors[2, 0:1, 0:1], factors[3, 0:1, 0:1])

    def moment(slot, reducing, side, column):
        size = width if slot < 4 else wide
        low = attn_low.at[slot] if slot < 4 else mlp_low.at[slot - 4]
        old, noise, new = (attn_mom, attn_noise, attn_out) if slot < 4 else (mlp_mom, mlp_noise, mlp_out)
        index = slot if slot < 4 else slot - 4

        @pl.loop(0, rows // 16)
        def _(i):
            part = pl.ds(pl.multiple_of(i * 16, 16), 16)
            total = reducing.total(side, part, pl.ds(column, size))
            value = 0.5 * old[part, index, :] + (total + noise_scale * noise[part, index, :]) / batch
            new[part, index, :] = value
            low[part, :] = value.astype(low.dtype)

        for action in sends(slot):
            action(lambda copy: copy.start())

    def landing(slot, source):
        size = width if slot < 4 else wide
        return main.at(owned.at[0], source).at[:, 0:size]

    def sends(slot):
        owner = OWNERS[slot]
        owner_z, owner_y, owner_x = owner_at(slot)
        low = attn_low.at[slot] if slot < 4 else mlp_low.at[slot - 4]
        alone = 0 if owner_z == 1 else LINE - 1
        far = (y != owner_y) & (x != owner_x)
        near = (y != owner_y) | (x != owner_x)
        across = (z != owner_z) & (far | ((z == alone) & near))

        def keep(action):
            @pl.when(dp == owner)
            def _():
                action(pltpu.make_async_copy(low, landing(slot, dp), gather_send.at[slot]))

        def direct(action):
            away = (dp != owner) & jnp.logical_not(across) if slot >= 4 else dp != owner

            @pl.when(away)
            def _():
                action(remote(low, landing(slot, dp), gather_send.at[slot], gather_recv.at[dp], owner, core))

        def turn(action):
            if slot >= 4:

                @pl.when(across)
                def _():
                    stop = z * 4 + owner_y * 2 + owner_x
                    action(remote(low, relayed.at[dp % 4], gather_send.at[slot], relay_sems.at[0, dp % 4], stop, core))

        return keep, direct, turn

    def relays(slot, action):
        owner_z, owner_y, owner_x = owner_at(slot)
        alone = 0 if owner_z == 1 else LINE - 1
        column = owner_y * 2 + owner_x
        here = (y == owner_y) & (x == owner_x) & (z != owner_z)

        @pl.when(here)
        def _():
            action(3 - column)

        @pl.when(here & (z == alone))
        def _():
            action(column + 1 - 2 * owner_x)
            action(column + 2 - 4 * owner_y)

    def relay_copy(slot, column):
        source = z * 4 + column
        return remote(
            relayed.at[column], landing(slot, source), relay_sems.at[1, column], gather_recv.at[source], OWNERS[slot], core
        )

    def forward(slot, column):
        block = relayed.at[column]
        remote(block, block, relay_sems.at[1, column], relay_sems.at[0, column], dp, core).wait_recv()
        relay_copy(slot, column).start()

    def pass_on(slot, source):
        size = width if slot < 4 else wide
        block = landing(slot, source)
        other_half = main.at(owned.at[1], source).at[:, 0:size]
        return remote(block, other_half, pass_send.at[source], pass_recv.at[source], dp, 1 - core)

    def turned_off(slot, source):
        owner_z, owner_y, owner_x = owner_at(slot)
        off_x, off_y = source % 2 != owner_x, source % 4 // 2 != owner_y
        alone = 0 if owner_z == 1 else LINE - 1
        return slot >= 4 and source // 4 != owner_z and ((off_x and off_y) or (source // 4 == alone and (off_x or off_y)))

    def collect(slot, late_ones):
        @pl.when(dp == OWNERS[slot])
        def _():
            for step in range(1, count):
                source = (OWNERS[slot] + step) % count
                if turned_off(slot, source) == late_ones:
                    block = landing(slot, source)
                    remote(block, block, gather_send.at[slot], gather_recv.at[source], source, core).wait_recv()
                    pass_on(slot, source).start()

    main.chain(0)
    late.first(2)
    late.sums(late.order[0])
    main.chain(1)
    late.first(3)
    late.sums(late.order[1])
    for copy in plane_copies():
        copy.start()
    main.chain(2)
    late.sums(late.order[2])
    late.sums(late.order[3])
    main.last(0)
    moment(4, main, 0, 0)
    main.last(1)
    moment(5, main, 1, 0)
    late.chain(0)
    vec_turn()
    late.chain(1)
    for slot in (4, 5):
        relays(slot, functools.partial(forward, slot))
    late.chain(2)
    for slot in (4, 5):
        collect(slot, False)
    late.last(0)
    moment(0, late, 0, 0)
    moment(1, late, 0, width)
    late.last(1)
    moment(2, late, 1, 0)
    moment(3, late, 1, width)

    for slot in range(6):
        low = attn_low.at[slot] if slot < 4 else mlp_low.at[slot - 4]

        @pl.when(dp == OWNERS[slot])
        def _():
            pltpu.make_async_copy(low, landing(slot, dp), gather_send.at[slot]).wait()
            pass_on(slot, dp).start()

    for slot in (4, 5):
        collect(slot, True)
    for slot in range(4):
        collect(slot, False)
    for slot in range(6):
        owner = OWNERS[slot]
        low = attn_low.at[slot] if slot < 4 else mlp_low.at[slot - 4]

        @pl.when(dp != owner)
        def _():
            remote(low, low, gather_send.at[slot], gather_recv.at[dp], owner, core).wait_send()

        @pl.when(dp == owner)
        def _():
            @pl.loop(0, count)
            def _(source):
                pass_on(slot, source).wait()

    vec_finish()
    for slot in (4, 5):
        relays(slot, lambda column: relay_copy(slot, column).wait_send())
    for index in range(4):
        small_copy(index).wait_send()
    for i in range(4):
        swap_copy(i).wait_send()
    main.drain()
    late.drain()
    stage.finish()


def attn_back(
    tokens, vec, first, q, k, v, o, do, lse, qk_all, vo_all, grad_mid, ga, gb, go, x_a, x_b, y_a, y_b, sums, included,
    attn_mom, mlp_mom, attn_noise, mlp_noise, noise_scale, batch, clip, collective_id,
):
    dma = pltpu.SemaphoreType.DMA
    low = jnp.bfloat16
    count = lax.axis_size("dp")
    length = tokens.shape[0]
    rows, _, width = attn_mom.shape
    wide = mlp_mom.shape[2]
    shape = jax.ShapeDtypeStruct
    vmem = pl.BlockSpec(memory_space=pltpu.VMEM)
    anywhere = pl.BlockSpec(memory_space=pl.ANY)
    scratch = pltpu.VMEM
    return pl.pallas_call(
        functools.partial(attn_back_kernel, noise_scale, batch, clip),
        out_shape=[
            shape((length, D), low),
            shape(attn_mom.shape, jnp.float32),
            shape(mlp_mom.shape, jnp.float32),
            shape((vec.shape[0] * D // 128, 128), jnp.float32),
            shape((2, D, wide), low),
        ],
        in_specs=[anywhere, vmem]
        + [anywhere] * 6
        + [vmem]
        + [anywhere] * 10
        + [vmem, pl.BlockSpec(memory_space=pltpu.SMEM)]
        + [anywhere] * 4,
        out_specs=[anywhere] + [vmem] * 3 + [anywhere],
        scratch_shapes=[
            scratch((length, D), low),
            scratch((length, D), low),
        ]
        + [scratch((length, width), low)] * 5
        + [
            scratch((D, 2 * width), low),
            scratch((D, width), low),
            scratch((length, D), jnp.float32),
            scratch((D, wide), low),
            scratch((D, wide), low),
            scratch(attn_mom.shape, jnp.float32),
            scratch(mlp_mom.shape, jnp.float32),
            scratch(attn_mom.shape, jnp.float32),
            scratch(mlp_mom.shape, jnp.float32),
            scratch((length, D), low),
            scratch((length, 2 * width), low),
            scratch((length, width), low),
            scratch((D, 2 * width), low),
            scratch((D, 2 * width), low),
            scratch((2 * HD, length), jnp.float32),
            scratch((D, length), low),
            scratch((length, D), low),
            scratch((length, D), low),
            scratch((2, 8, D), jnp.float32),
            scratch((2, 8, 128), jnp.float32),
            scratch((4, 8, 128), jnp.float32),
        ]
        + [scratch((LINE, rows, wide), low)] * 10
        + [scratch((LINE, rows, 2 * width), low)] * 10
        + [
            scratch((4, rows, width), low),
            scratch((2, rows, wide), low),
            scratch((4, rows, wide), low),
            scratch((8,) + vec.shape, jnp.float32),
            scratch((LINE,) + vec.shape, jnp.float32),
            dma((10, LINE)),
            dma((10, LINE)),
            dma((10, LINE)),
            dma((10, LINE)),
            dma((2, 8)),
            dma((2, LINE)),
            dma((6,)),
            dma((count,)),
            dma((2, 4)),
            dma((4,)),
            dma((4,)),
            dma((2, 4)),
            dma((count,)),
            dma((count,)),
            dma((24,)),
        ],
        compiler_params=pltpu.CompilerParams(
            collective_id=collective_id, has_side_effects=True, vmem_limit_bytes=62 * MIB
        ),
        name="attn_back",
    )(
        tokens, vec, first, q, k, v, o, do, lse, qk_all, vo_all, grad_mid, ga, gb, go, x_a, x_b, y_a, y_b, sums, included,
        attn_mom, mlp_mom, attn_noise, mlp_noise,
    )


def placed(piece, start, total_size):
    return lax.dynamic_update_slice_in_dim(jnp.zeros((total_size,), jnp.float32), piece, start, 0)


def other_core(value):
    return lax.ppermute(value, "tensor", [(0, 1), (1, 0)])


SHIFTS = (0.0, 0.0, 0.0, 0.8, 0.72)


def polynomials(current):
    rows = current.shape[0]
    diagonal = lax.broadcasted_iota(jnp.int32, (rows, rows), 0) == lax.broadcasted_iota(jnp.int32, (rows, rows), 1)

    def less(matrix, shift):
        return matrix - jnp.where(diagonal, shift, 0.0) if shift else matrix

    def product(left, right):
        return contract(left.astype(jnp.bfloat16), right.astype(jnp.bfloat16), 1, 0)

    factor = None
    for iteration in range(NS_ITERS):
        shift = SHIFTS[iteration]
        moved = less(current, shift)
        square = product(moved, moved) + 2.0 * shift * moved
        lead = COEF_B * shift + COEF_C * shift * shift
        rest = lax.optimization_barrier(COEF_B * moved + COEF_C * square)
        whole = COEF_A + lead
        if factor is None:
            factor = jnp.where(diagonal, whole, 0.0) + rest
        else:
            factor = lax.optimization_barrier(whole * factor + product(rest, factor))
        if iteration < NS_ITERS - 1:
            once = lax.optimization_barrier(whole * current + shift * rest + product(rest, moved))
            second = whole * shift
            current = lax.optimization_barrier(whole * once + second * rest + product(rest, less(once, second)))
    return factor.astype(jnp.bfloat16)


def newton(owned):
    gram = contract(owned, owned, 1, 1)
    gram = gram + other_core(gram)
    scale = 1.0 / (jnp.sqrt(jnp.trace(gram)) + 1e-07)
    return (contract(polynomials(gram * (scale * scale)), owned, 1, 0) * scale).astype(jnp.bfloat16)


def body(
    fast,
    tokens,
    cotangent,
    inclusion,
    attn_weights,
    mlp_weights,
    attn_momentum,
    mlp_momentum,
    attn_noise,
    mlp_noise,
    vectors,
    vector_momentum,
    vector_noise,
):
    dp_count = lax.axis_size("dp")
    dp_index = lax.axis_index("dp")
    halves = lax.axis_size("tensor")
    tensor_index = lax.axis_index("tensor")
    head_width = D // halves
    hidden_width = FF // halves
    query_scale = 1.0 / math.sqrt(HD)
    clip = 1.5 * D * math.sqrt(LEN)
    sigma = 0.05 * math.sqrt(dp_count) / D
    batch = 0.75 * dp_count
    noise_scale = sigma * clip
    if fast:
        (
            query_key, value_out, first_low, queries, key_rows, value_rows, attended_low, result, grad_mid, grad_attended,
            grad_fc, grad_pr, grad_wo, x_fc, x_pr, y_fc, y_pr, stats, vec, sums,
        ) = forward(tokens[0], vectors.reshape(-1, 128), attn_weights, mlp_weights, cotangent[0], 0)
        grad_in, attn_moment, mlp_moment, vector_summed, owned = attn_back(
            tokens[0], vec, first_low, queries, key_rows, value_rows, attended_low, grad_attended, stats,
            query_key, value_out, grad_mid, grad_fc, grad_pr, grad_wo,
            x_fc, x_pr, y_fc, y_pr, sums,
            inclusion, attn_momentum, mlp_momentum, attn_noise, mlp_noise, noise_scale, batch, clip, 2,
        )
        vector_summed = vector_summed.reshape(-1)
    else:
        attn_shard = attn_weights.astype(jnp.bfloat16)
        mlp_shard = mlp_weights.astype(jnp.bfloat16)
        rows = attn_shard.shape[0]
        shards = (
            attn_shard[:, 0:2].reshape(rows, 2 * head_width),
            attn_shard[:, 2:4].reshape(rows, 2 * head_width),
            mlp_shard[:, 0, 0:D],
            mlp_shard[:, 0, D:],
            mlp_shard[:, 1, 0:D],
            mlp_shard[:, 1, D:],
        )
        gain_one = vectors[0:D]
        bias_one = vectors[D : 2 * D]
        gain_two = vectors[2 * D : 3 * D]
        bias_two = vectors[3 * D : 4 * D]
        query_bias = lax.dynamic_slice_in_dim(vectors, 4 * D + tensor_index * head_width, head_width)
        value_bias = lax.dynamic_slice_in_dim(vectors, 5 * D + tensor_index * head_width, head_width)
        attn_bias = vectors[6 * D : 7 * D]
        mlp_bias = vectors[7 * D : 8 * D]
        hidden_bias = lax.dynamic_slice_in_dim(
            vectors, 8 * D + tensor_index * hidden_width, hidden_width
        )
        inputs = tokens[0].astype(jnp.float32)
        length = inputs.shape[0]
        first, normed_one, inverse_one = layer_norm(inputs, gain_one, bias_one)

        def both_cores(partial):
            low = partial.astype(jnp.bfloat16)
            return low.astype(jnp.float32) + other_core(low).astype(jnp.float32)

        query_key, value_out, fc_one, fc_two, pr_one, pr_two = (
            lax.all_gather(shard, "dp", axis=0, tiled=True) for shard in shards
        )
        value_weight, out_weight = value_out[:, 0:head_width], value_out[:, head_width:]
        first_low = first.astype(jnp.bfloat16)
        qk = contract(first_low, query_key, 1, 0)
        queries = ((qk[:, 0:head_width] + query_bias) * query_scale).astype(jnp.bfloat16)
        key_rows = qk[:, head_width:].astype(jnp.bfloat16)
        value_rows = (contract(first_low, value_weight, 1, 0) + value_bias).astype(jnp.bfloat16)
        attended_low, stats = pairs_forward(queries, key_rows, value_rows)
        middle = inputs + both_cores(contract(attended_low, out_weight, 1, 1)) + attn_bias
        second_low = layer_norm(middle, gain_two, bias_two)[0].astype(jnp.bfloat16)
        pre_act = contract(second_low, jnp.concatenate([fc_one, fc_two], axis=1), 1, 0) + hidden_bias
        activation, gelu_back = jax.vjp(gelu_tanh, pre_act)
        activation_low = activation.astype(jnp.bfloat16)
        slope = gelu_back(jnp.ones_like(pre_act))[0]
        _, normed_two, inverse_two = layer_norm(middle, gain_two, bias_two)
        fc_weight = jnp.concatenate([fc_one, fc_two], axis=1)
        pr_weight = jnp.concatenate([pr_one, pr_two], axis=1)
        result = middle + both_cores(contract(activation_low, pr_weight, 1, 1)) + mlp_bias
        cot_low = cotangent[0]
        grad_out = cot_low.astype(jnp.float32)
        d_pr = contract(cot_low, activation_low, 0, 0)
        grad_pre = (contract(cot_low, pr_weight, 1, 0) * slope.astype(jnp.float32)).astype(jnp.bfloat16)
        d_fc = contract(second_low, grad_pre, 0, 0)
        d_hidden_bias = jnp.sum(grad_pre.astype(jnp.float32), axis=0)
        grad_two = both_cores(contract(grad_pre, fc_weight, 1, 1))
        grad_mid = grad_out + norm_back(grad_two, gain_two, normed_two, inverse_two)
        d_gain_two = jnp.sum(grad_two * normed_two, axis=0)
        d_bias_two = jnp.sum(grad_two, axis=0)
        d_attn_bias = jnp.sum(grad_mid, axis=0)
        d_mlp_bias = jnp.sum(grad_out, axis=0)
        mid_low = grad_mid.astype(jnp.bfloat16)
        d_out = contract(mid_low, attended_low, 0, 0)
        grad_attended = contract(mid_low, out_weight, 1, 0).astype(jnp.bfloat16)
        grad_q, grad_k, grad_v = pairs_backward(
            queries, key_rows, value_rows, attended_low, grad_attended, stats
        )
        grad_qk = jnp.concatenate([grad_q, grad_k], axis=1)
        d_query_key = contract(first_low, grad_qk, 0, 0)
        d_value = contract(first_low, grad_v, 0, 0)
        d_query_bias = jnp.sum(grad_q.astype(jnp.float32), axis=0)
        d_value_bias = jnp.sum(grad_v.astype(jnp.float32), axis=0)
        grad_one = both_cores(contract(grad_qk, query_key, 1, 1) + contract(grad_v, value_weight, 1, 1))
        grad_in = grad_mid + norm_back(grad_one, gain_one, normed_one, inverse_one)
        d_gain_one = jnp.sum(grad_one * normed_one, axis=0)
        d_bias_one = jnp.sum(grad_one, axis=0)
        split_square = sum(
            jnp.sum(value * value)
            for value in (d_query_key, d_value, d_out, d_fc, d_pr, d_query_bias, d_value_bias, d_hidden_bias)
        )
        split_tile = jnp.broadcast_to(split_square, (8, 128))
        total_square = (split_tile + other_core(split_tile))[0, 0] + sum(
            jnp.sum(value * value)
            for value in (d_gain_one, d_bias_one, d_gain_two, d_bias_two, d_attn_bias, d_mlp_bias)
        )
        factor = inclusion[0].astype(jnp.float32) * jnp.minimum(
            1.0, clip / (jnp.sqrt(total_square) + 1e-06)
        )
        leading = (tensor_index == 0).astype(jnp.float32)
        vector_grad = (
            jnp.concatenate(
                [
                    leading * d_gain_one,
                    leading * d_bias_one,
                    leading * d_gain_two,
                    leading * d_bias_two,
                    placed(d_query_bias, tensor_index * head_width, D),
                    placed(d_value_bias, tensor_index * head_width, D),
                    leading * d_attn_bias,
                    leading * d_mlp_bias,
                    placed(d_hidden_bias, tensor_index * hidden_width, FF),
                ]
            )
            * factor
        )
        result, grad_in = result.astype(jnp.bfloat16), grad_in.astype(jnp.bfloat16)
        attn_grad = jnp.concatenate([d_query_key, d_value, d_out], axis=1) * factor
        mlp_grad = jnp.stack([d_fc, d_pr], axis=1) * factor
        attn_summed = lax.psum_scatter(attn_grad, "dp", scatter_dimension=0, tiled=True)
        mlp_summed = lax.psum_scatter(mlp_grad, "dp", scatter_dimension=0, tiled=True)
        attn_summed = attn_summed.reshape(rows, 4, head_width)
        vector_summed = lax.psum(vector_grad, ("dp", "tensor"))
        attn_moment = 0.5 * attn_momentum + (attn_summed + noise_scale * attn_noise) / batch
        mlp_moment = 0.5 * mlp_momentum + (mlp_summed + noise_scale * mlp_noise) / batch
        owners = jnp.array([slot * dp_count // 6 for slot in range(6)])
        full_attn = lax.all_gather(attn_moment.astype(jnp.bfloat16), "dp", axis=0, tiled=True)
        full_mlp = lax.all_gather(mlp_moment.astype(jnp.bfloat16), "dp", axis=0, tiled=True)
        attn_pick = (owners[0:4] == dp_index)[None, :, None]
        mlp_pick = (owners[4:6] == dp_index)[None, :, None]
        mine_attn = jnp.sum(jnp.where(attn_pick, full_attn, 0), axis=1)
        mine_mlp = jnp.sum(jnp.where(mlp_pick, full_mlp, 0), axis=1)
        owned = jnp.pad(mine_attn, ((0, 0), (0, hidden_width - head_width))) + mine_mlp
    vector_moment = 0.5 * vector_momentum + (vector_summed + noise_scale * vector_noise) / batch
    vector_rate = 0.2 * math.sqrt(dp_count / LEN)
    vectors_new = vectors - vector_rate * vector_moment
    rates = (0.5, 0.5, 0.5, 0.5 * max(1.0, math.sqrt(LEN) / 8.0), 0.5 * math.sqrt(FF / D), 0.5)
    if fast:
        gram, scale, result, grad_in, attn_moment, mlp_moment = gram_of(
            owned, (result, grad_in, attn_moment, mlp_moment)
        )
        attn_new, mlp_new = scatter_rows(
            polynomials(gram), scale, owned, attn_weights, mlp_weights, rates, 3
        )
    else:
        orthogonal = newton(owned)
        attn_rows = jnp.where(attn_pick, orthogonal[:, None, 0:head_width], 0)
        mlp_rows = jnp.where(mlp_pick, orthogonal[:, None, :], 0)
        attn_orth = lax.psum_scatter(attn_rows, "dp", scatter_dimension=0, tiled=True)
        mlp_orth = lax.psum_scatter(mlp_rows, "dp", scatter_dimension=0, tiled=True)
        attn_new = attn_weights - jnp.array(rates[0:4])[None, :, None] * attn_orth
        mlp_new = mlp_weights - jnp.array(rates[4:6])[None, :, None] * mlp_orth
    return (
        result[None],
        grad_in[None],
        attn_moment,
        mlp_moment,
        attn_new,
        mlp_new,
        vector_moment,
        vectors_new,
    )


def solution(mesh):
    fast = mesh.shape["dp"] == 16 and mesh.shape["tensor"] == 2
    in_specs = (
        P("dp", None, None),
        P("dp", None, None),
        P("dp"),
        P("dp", None, "tensor"),
        P("dp", None, "tensor"),
        P("dp", None, "tensor"),
        P("dp", None, "tensor"),
        P("dp", None, "tensor"),
        P("dp", None, "tensor"),
        P(),
        P(),
        P(),
    )
    out_specs = (
        P("dp", None, None),
        P("dp", None, None),
        P("dp", None, "tensor"),
        P("dp", None, "tensor"),
        P("dp", None, "tensor"),
        P("dp", None, "tensor"),
        P(),
        P(),
    )
    return jax.shard_map(
        functools.partial(body, fast), mesh=mesh, in_specs=in_specs, out_specs=out_specs, check_vma=False
    )
```

```python
import functools
import math

import jax
import jax.numpy as jnp
from jax import lax
from jax.experimental import pallas as pl
from jax.experimental.pallas import tpu as pltpu
from jax.sharding import PartitionSpec as P

D = 768
HD = 64
FF = 3072
LEN = 960
NS_ITERS = 5


COEF_A = 3.4445
COEF_B = -4.775
COEF_C = 2.0315


def gelu_tanh(values):
    return jax.nn.gelu(values, approximate=True)


def layer_norm(values, norm_gain, norm_bias):
    centered = values - jnp.mean(values, axis=-1, keepdims=True)
    inverse = lax.rsqrt(jnp.mean(centered * centered, axis=-1, keepdims=True) + 1e-05)
    normed = centered * inverse
    return (normed * norm_gain + norm_bias, normed, inverse)


def norm_back(grad_out, norm_gain, normed, inverse):
    scaled = grad_out * norm_gain
    return inverse * (
        scaled
        - jnp.mean(scaled, axis=-1, keepdims=True)
        - normed * jnp.mean(scaled * normed, axis=-1, keepdims=True)
    )


def contract(left, right, left_dim, right_dim):
    return lax.dot_general(
        left, right, (((left_dim,), (right_dim,)), ((), ())), preferred_element_type=jnp.float32
    )


MESH = pl.DeviceIdType.MESH
MIB = 1 << 20
LINE = 4
OWNERS = (7, 8, 6, 9, 4, 11)


def place():
    dp = lax.axis_index("dp")
    core = lax.axis_index("tensor")
    z = dp // 4
    y = dp % 4 // 2
    x = dp % 2
    return dp, core, z, y, x


def remote(src, dst, send, recv, dp, core):
    return pltpu.make_async_remote_copy(
        src_ref=src, dst_ref=dst, send_sem=send, recv_sem=recv, device_id=(dp, core), device_id_type=MESH
    )


def greet(barrier, dp, core):
    pl.semaphore_signal(barrier, inc=1, device_id=(dp, core), device_id_type=MESH)


def greet_all(dp, core, count):
    barrier = pltpu.get_barrier_semaphore()
    for step in range(1, count):
        greet(barrier, (dp + step) % count, core)
    pl.semaphore_wait(barrier, count - 1)


def greet_plane(dp, core, count, z, y, x):
    barrier = pltpu.get_barrier_semaphore()
    for step in range(1, count):
        greet(barrier, (dp + step) % count, core)
    for step in range(4):
        greet(barrier, z * 4 + (dp + step) % 4, 1 - core)
    return lambda: pl.semaphore_wait(barrier, count + 3)


class Staging:
    def __init__(self, sems):
        self.sems = sems
        self.count = 0
        self.waiting = {}
        self.out = []

    def move(self, src, dst):
        copy = pltpu.make_async_copy(src, dst, self.sems.at[self.count])
        self.count += 1
        copy.start()
        return copy

    def fetch(self, name, src, dst):
        self.waiting[name] = self.move(src, dst)

    def need(self, *names):
        for name in names:
            if name in self.waiting:
                self.waiting.pop(name).wait()

    def keep(self, src, dst):
        self.out.append(self.move(src, dst))

    def finish(self):
        for copy in self.out:
            copy.wait()


def gram_kernel(noise_scale, batch, vector_rate, owned_in, *refs):
    results, vec_in, (gram, scale), kept, vec_out = refs[:4], refs[4:8], refs[8:10], refs[10:14], refs[14:16]
    held, vec, vec_new, (own, sems) = refs[16:20], refs[20:24], refs[24:26], refs[26:]
    dp = lax.axis_index("dp")
    stage = Staging(sems)
    stage.fetch("mine", owned_in.at[0], own.at[0])
    for index in range(4):
        stage.fetch(index, results[index], held[index])
    for index in range(4):
        stage.fetch(4 + index, vec_in[index], vec[index])
    stage.fetch("other", owned_in.at[1], own.at[1])
    rows = gram.shape[0]
    attn = (dp == OWNERS[0]) | (dp == OWNERS[1]) | (dp == OWNERS[2]) | (dp == OWNERS[3])
    mlp = (dp == OWNERS[4]) | (dp == OWNERS[5])

    def each(action):
        pl.when(attn)(lambda: action(own.shape[2] // 4))
        pl.when(mlp)(lambda: action(own.shape[2]))

    def first(size):
        gram[...] = contract(own[0, :, 0:size], own[0, :, 0:size], 1, 1)

    def second(size):
        total = gram[...] + contract(own[1, :, 0:size], own[1, :, 0:size], 1, 1)
        square = jnp.zeros((1, 1), jnp.float32)
        tile = 256
        here = lax.broadcasted_iota(jnp.int32, (tile, tile), 0) == lax.broadcasted_iota(jnp.int32, (tile, tile), 1)
        for start in range(0, rows, tile):
            corner = jnp.where(here, total[start : start + tile, start : start + tile], 0.0)
            square = square + jnp.sum(jnp.sum(corner, axis=0, keepdims=True), axis=1, keepdims=True)
        inverse = 1.0 / (jnp.sqrt(square) + 1e-07)
        scale[...] = jnp.broadcast_to(inverse, scale.shape)
        gram[...] = total * (inverse * inverse)

    stage.need("mine")
    each(first)
    for index in range(4):
        stage.need(index)
        stage.keep(held[index], kept[index])
    stage.need(4, 5, 6, 7)
    summed, old, moment, noise = (ref[...] for ref in vec)
    moment = 0.5 * moment + (summed + noise_scale * noise) / batch
    vec_new[0][...] = moment
    vec_new[1][...] = old - vector_rate * moment
    for index in range(2):
        stage.keep(vec_new[index], vec_out[index])
    stage.need("other")
    each(second)
    stage.finish()


def gram_of(owned, results, vectors, noise_scale, batch, vector_rate):
    rows = owned.shape[1]
    shape = jax.ShapeDtypeStruct
    vmem = pl.BlockSpec(memory_space=pltpu.VMEM)
    anywhere = pl.BlockSpec(memory_space=pl.ANY)
    return pl.pallas_call(
        functools.partial(gram_kernel, noise_scale, batch, vector_rate),
        out_shape=[shape((rows, rows), jnp.float32), shape((8, 128), jnp.float32)]
        + [shape(value.shape, value.dtype) for value in results + vectors[:2]],
        in_specs=[anywhere] * 9,
        out_specs=[vmem] * 2 + [anywhere] * 6,
        scratch_shapes=[pltpu.VMEM(value.shape, value.dtype) for value in results + vectors + vectors[:2]]
        + [pltpu.VMEM(owned.shape, owned.dtype), pltpu.SemaphoreType.DMA((16,))],
        compiler_params=pltpu.CompilerParams(vmem_limit_bytes=60 * MIB),
        name="gram",
    )(owned, *results, *vectors)


def scatter_kernel(
    rates, factor, scale, owned_in, attn_in, mlp_in, attn_new, mlp_new,
    own, attn, mlp, orth, attn_low, mlp_low, relayed, send, recv, relay_send, relay_recv, stage_sems,
):
    dp, core, z, y, x = place()
    rows = attn.shape[0]
    count = orth.shape[0] // rows
    stage = Staging(stage_sems)
    stage.fetch("own", owned_in.at[0], own)
    stage.fetch("attn", attn_in, attn)
    stage.fetch("mlp", mlp_in, mlp)
    greet_all(dp, core, count)
    stage.need("own")

    def at(ref, block):
        return ref.at[pl.ds(pl.multiple_of(block * rows, rows), rows)]

    def low_of(slot):
        return attn_low.at[slot] if slot < 4 else mlp_low.at[slot - 4]

    def size_of(slot):
        return attn.shape[2] if slot < 4 else mlp.shape[2]

    def deliver(slot, target):
        owner = OWNERS[slot]
        src = at(orth, target).at[:, 0 : size_of(slot)]
        level = target // 4
        if slot >= 4 and level in stops(owner).get(target % 4, ()):
            stop = owner // 4 * 4 + target % 4
            return remote(src, relayed.at[level], send.at[target], relay_recv.at[level], stop, core)
        return remote(src, low_of(slot), send.at[target], recv.at[slot], target, core)

    def onward(slot, action):
        owner = OWNERS[slot]
        for column, levels in stops(owner).items():

            @pl.when(dp == owner // 4 * 4 + column)
            def _():
                for level in levels:
                    action(level, level * 4 + column)

    def relay_copy(slot, level, target):
        return remote(relayed.at[level], low_of(slot), relay_send.at[level], recv.at[slot], target, core)

    def levels_of(owner):
        return (3, 2, 0) if owner // 4 == 1 else (0, 1, 3)

    def stops(owner):
        far, near, alone = levels_of(owner)
        column = owner % 4
        by_x, by_y = column + 1 - 2 * (column % 2), column + 2 - 4 * (column // 2)
        return {by_x: (far, near), by_y: (far, near, alone)}

    def queue(owner):
        far, near, alone = levels_of(owner)
        home, column = owner // 4, owner % 4
        by_x, by_y, across = column + 1 - 2 * (column % 2), column + 2 - 4 * (column // 2), 3 - column
        links = (
            [far * 4 + by_x, near * 4 + by_x, home * 4 + across, home * 4 + by_x],
            [far * 4 + by_y, near * 4 + by_y, alone * 4 + by_y, home * 4 + by_y],
            [far * 4 + across, far * 4 + column, near * 4 + across, near * 4 + column],
            [alone * 4 + across, alone * 4 + by_x, alone * 4 + column],
        )
        return [link[turn] for turn in range(4) for link in links if turn < len(link)]

    pieces = ((0, 5), (5, 11), (11, 16))
    for slot in range(6):
        owner = OWNERS[slot]
        size = size_of(slot)

        @pl.when(dp == owner)
        def _():
            waiting = queue(owner)
            ready = set()
            for first, last in (pieces[0], pieces[2], pieces[1]):
                part = pl.ds(first * rows, (last - first) * rows)
                value = contract(factor[part, :], own[:, 0:size], 1, 0) * scale[0:1, 0:1]
                orth[part, 0:size] = value.astype(orth.dtype)
                ready.update(range(first, last))
                while waiting and waiting[0] in ready:
                    deliver(slot, waiting.pop(0)).start()
            pltpu.make_async_copy(at(orth, owner).at[:, 0:size], low_of(slot), recv.at[slot]).start()

    for slot in (4, 5):

        def pass_on(level, target):
            block = relayed.at[level]
            remote(block, block, relay_send.at[level], relay_recv.at[level], dp, core).wait_recv()
            relay_copy(slot, level, target).start()

        onward(slot, pass_on)

    stage.need("attn", "mlp")
    for slot in range(6):
        owner = OWNERS[slot]
        low = low_of(slot)

        @pl.when(dp != owner)
        def _():
            remote(low, low, send.at[0], recv.at[slot], owner, core).wait_recv()

        @pl.when(dp == owner)
        def _():
            pltpu.make_async_copy(low, low, recv.at[slot]).wait()

        @pl.loop(0, rows // 16)
        def _(i):
            part = pl.ds(pl.multiple_of(i * 16, 16), 16)
            step = rates[slot] * low[part, :].astype(jnp.float32)
            if slot < 4:
                attn_new[part, slot, :] = attn[part, slot, :] - step
            else:
                mlp_new[part, slot - 4, :] = mlp[part, slot - 4, :] - step

    for slot in range(6):
        owner = OWNERS[slot]

        @pl.when(dp == owner)
        def _():
            for target in range(count):
                if target != owner:
                    deliver(slot, target).wait_send()

    for slot in (4, 5):
        onward(slot, lambda level, target: relay_copy(slot, level, target).wait_send())


def scatter_rows(factor, scale, owned, attn, mlp, rates, collective_id):
    dma = pltpu.SemaphoreType.DMA
    count = lax.axis_size("dp")
    rows = attn.shape[0]
    shape = jax.ShapeDtypeStruct
    vmem = pl.BlockSpec(memory_space=pltpu.VMEM)
    anywhere = pl.BlockSpec(memory_space=pl.ANY)
    return pl.pallas_call(
        functools.partial(scatter_kernel, rates),
        out_shape=[shape(attn.shape, jnp.float32), shape(mlp.shape, jnp.float32)],
        in_specs=[vmem] * 2 + [anywhere] * 3,
        out_specs=[vmem] * 2,
        scratch_shapes=[
            pltpu.VMEM(owned.shape[1:], owned.dtype),
            pltpu.VMEM(attn.shape, attn.dtype),
            pltpu.VMEM(mlp.shape, mlp.dtype),
            pltpu.VMEM(owned.shape[1:], owned.dtype),
            pltpu.VMEM((4, rows, attn.shape[2]), jnp.bfloat16),
            pltpu.VMEM((2, rows, mlp.shape[2]), jnp.bfloat16),
            pltpu.VMEM((LINE, rows, mlp.shape[2]), jnp.bfloat16),
            dma((count,)),
            dma((6,)),
            dma((LINE,)),
            dma((LINE,)),
            dma((3,)),
        ],
        compiler_params=pltpu.CompilerParams(
            collective_id=collective_id, has_side_effects=True, vmem_limit_bytes=32 * MIB
        ),
        name="scatter_rows",
    )(factor, scale, owned, attn, mlp)


def head_mask(shape):
    return lax.broadcasted_iota(jnp.int32, shape, 1) < HD


def spans(length):
    return [(start, min(256, length - start)) for start in range(0, length, 256)]


def attend_forward(q_ref, k_ref, v_ref, o_ref, lse_ref, turned, value_turned, after=lambda head: None):
    length = q_ref.shape[0]
    value_turned[...] = v_ref[...].astype(jnp.float32).T.astype(jnp.bfloat16)
    keys = k_ref[...]
    for head in range(2):
        mine = head_mask(keys.shape) if head == 0 else ~head_mask(keys.shape)
        head_keys = jnp.where(mine, keys, jnp.zeros_like(keys))
        for start, size in spans(length):
            stop = start + size
            scores = contract(head_keys[0:stop], q_ref[start:stop, :], 1, 1)
            key_at = lax.broadcasted_iota(jnp.int32, (stop, size), 0)
            query_at = lax.broadcasted_iota(jnp.int32, (stop, size), 1) + start
            scores = jnp.where(key_at <= query_at, scores, -1e30)
            peak = jnp.max(scores, axis=0, keepdims=True)
            weights = jnp.exp(scores - peak)
            total = jnp.sum(weights, axis=0, keepdims=True)
            mixed = contract(
                value_turned[head * HD : (head + 1) * HD, 0:stop], weights.astype(jnp.bfloat16), 1, 0
            )
            turned[head * HD : (head + 1) * HD, start:stop] = mixed / total
            lse_ref[head : head + 1, start:stop] = peak + jnp.log(total)
        after(head)
    o_ref[...] = turned[...].T.astype(jnp.bfloat16)


def attend_backward(q_ref, k_ref, v_ref, o_ref, do_ref, lse_ref, dq_ref, dk_ref, dv_ref, turned):
    length = q_ref.shape[0]
    keys, values = k_ref[...], v_ref[...]
    key_turned = keys.astype(jnp.float32).T.astype(jnp.bfloat16)
    inner = (o_ref[...].astype(jnp.float32) * do_ref[...].astype(jnp.float32)).T
    mask = head_mask(keys.shape)
    turned[...] = jnp.zeros_like(turned)
    for start, size in spans(length):
        stop = start + size
        both_k, both_v = [], []
        for head in range(2):
            mine = mask[start:stop] if head == 0 else ~mask[start:stop]
            head_keys = jnp.where(mine, keys[start:stop], 0)
            head_values = jnp.where(mine, values[start:stop], 0)
            head_inner = jnp.sum(inner[head * HD : (head + 1) * HD, start:], axis=0, keepdims=True)
            scores = contract(head_keys, q_ref[start:, :], 1, 1)
            grad_prob = contract(head_values, do_ref[start:, :], 1, 1)
            key_at = lax.broadcasted_iota(jnp.int32, scores.shape, 0)
            query_at = lax.broadcasted_iota(jnp.int32, scores.shape, 1)
            scores = jnp.where(key_at <= query_at, scores, -1e30)
            prob = jnp.exp(scores - lse_ref[head : head + 1, start:])
            grad_scores = (prob * (grad_prob - head_inner)).astype(jnp.bfloat16)
            both_v.append(contract(prob.astype(jnp.bfloat16), do_ref[start:, :], 1, 0))
            both_k.append(contract(grad_scores, q_ref[start:, :], 1, 0))
            turned[head * HD : (head + 1) * HD, start:] += contract(
                key_turned[head * HD : (head + 1) * HD, start:stop], grad_scores, 1, 0
            )
        pick = mask[start:stop]
        dk_ref[start:stop, :] = jnp.where(pick, both_k[0], both_k[1]).astype(jnp.bfloat16)
        dv_ref[start:stop, :] = jnp.where(pick, both_v[0], both_v[1]).astype(jnp.bfloat16)
    dq_ref[...] = (turned[...].T * (1.0 / math.sqrt(HD))).astype(jnp.bfloat16)


def pairs_forward(queries, keys, values):
    length, width = queries.shape
    block = pl.BlockSpec((length, 2 * HD), lambda i: (0, i))
    stat = pl.BlockSpec((None, 2, length), lambda i: (i, 0, 0))
    return pl.pallas_call(
        attend_forward,
        grid=(width // (2 * HD),),
        out_shape=[
            jax.ShapeDtypeStruct((length, width), jnp.bfloat16),
            jax.ShapeDtypeStruct((width // (2 * HD), 2, length), jnp.float32),
        ],
        in_specs=[block] * 3,
        out_specs=[block, stat],
        scratch_shapes=[pltpu.VMEM((2 * HD, length), jnp.float32), pltpu.VMEM((2 * HD, length), jnp.bfloat16)],
        compiler_params=pltpu.CompilerParams(vmem_limit_bytes=48 * MIB),
        name="attend_forward",
    )(queries, keys, values)


def pairs_backward(queries, keys, values, attended, grad_attended, stats):
    length, width = queries.shape
    block = pl.BlockSpec((length, 2 * HD), lambda i: (0, i))
    stat = pl.BlockSpec((None, 2, length), lambda i: (i, 0, 0))
    return pl.pallas_call(
        attend_backward,
        grid=(width // (2 * HD),),
        out_shape=[jax.ShapeDtypeStruct((length, width), jnp.bfloat16)] * 3,
        in_specs=[block] * 5 + [stat],
        out_specs=[block] * 3,
        scratch_shapes=[pltpu.VMEM((2 * HD, length), jnp.float32)],
        compiler_params=pltpu.CompilerParams(vmem_limit_bytes=48 * MIB),
        name="attend_backward",
    )(queries, keys, values, attended, grad_attended, stats)


NORM_ROWS = 240


class Gathering:
    def __init__(self, a_ref, b_ref, a_out, b_out, send, recv, local):
        self.own = (a_ref, b_ref)
        self.outs = (a_out, b_out)
        self.send, self.recv, self.local = send, recv, local
        self.rows = a_ref.shape[0]
        self.dp, self.core, self.z, self.y, self.x = place()
        self.x_peer = self.dp + 1 - 2 * self.x
        self.y_peer = self.dp + 2 - 4 * self.y

    def block(self, side, index):
        return self.outs[side].at[pl.ds(pl.multiple_of(index * self.rows, self.rows), self.rows)]

    def copy(self, kind, side, index, own, target):
        src = self.own[side] if own else self.block(side, index)
        return remote(
            src, self.block(side, index), self.send.at[kind, index // 4], self.recv.at[side, index], target, self.core
        )

    def arrived(self, side, index):
        block = self.block(side, index)
        remote(block, block, self.send.at[0, 0], self.recv.at[side, index], self.dp, self.core).wait_recv()

    def at(self, level, y_off, x_off):
        y = self.y + y_off * (1 - 2 * self.y)
        x = self.x + x_off * (1 - 2 * self.x)
        return level * 4 + y * 2 + x

    def line(self, level, own, action):
        index = self.at(level, 0, 0)

        @pl.when((self.z < LINE - 1) & (level <= self.z))
        def _():
            for side in range(2):
                action(self.copy(side, side, index, own, self.dp + 4))

        @pl.when((self.z > 0) & (level >= self.z))
        def _():
            for side in range(2):
                action(self.copy(2 + side, side, index, own, self.dp - 4))

        for side in range(2):
            action(self.copy(4 + side, side, index, own, self.x_peer))
            action(self.copy(6 + side, side, index, own, self.y_peer))

    def relays(self, level):
        return (
            (0, self.at(level, 0, 1), self.copy(8, 0, self.at(level, 0, 1), False, self.y_peer)),
            (1, self.at(level, 1, 0), self.copy(9, 1, self.at(level, 1, 0), False, self.x_peer)),
        )

    def by_distance(self, distance, action):
        if distance == 0:
            action(self.z)
            return

        @pl.when(self.z >= distance)
        def _():
            action(self.z - distance)

        @pl.when(self.z + distance < LINE)
        def _():
            action(self.z + distance)

    def local_copies(self):
        return [
            pltpu.make_async_copy(self.own[side], self.block(side, self.dp), self.local.at[side]) for side in range(2)
        ]

    def begin(self):
        self.line(self.z, True, lambda copy: copy.start())
        for copy in self.local_copies():
            copy.start()

    def onward(self, distance):
        def action(level):
            for side in range(2):
                self.arrived(side, self.at(level, 0, 0))
            self.line(level, False, lambda copy: copy.start())

        self.by_distance(distance, action)

    def relay(self, distance):
        def action(level):
            for side, index, copy in self.relays(level):
                self.arrived(side, index)
                copy.start()

        self.by_distance(distance, action)

    def finish(self):
        for level in range(LINE):
            self.arrived(1, self.at(level, 0, 1))
            self.arrived(0, self.at(level, 1, 0))
            for side in range(2):
                self.arrived(side, self.at(level, 1, 1))
        for copy in self.local_copies():
            copy.wait()

    def drain(self):
        for level in range(LINE):
            self.line(level, False, lambda copy: copy.wait_send())
            for _, _, copy in self.relays(level):
                copy.wait_send()


def norm_tile(values, gain, bias):
    centered = values - jnp.mean(values, axis=-1, keepdims=True)
    inverse = lax.rsqrt(jnp.mean(centered * centered, axis=-1, keepdims=True) + 1e-05)
    return centered * inverse * gain + bias


def tiles(count, rows, action):
    @pl.loop(0, count // rows)
    def _(i):
        action(pl.ds(pl.multiple_of(i * rows, rows), rows))


BACK_ROWS = 80


def fold(value):
    return jnp.sum(value.reshape(-1, 8, value.shape[1]), axis=0)


def norm_back_tile(grad, gain, values):
    centered = values - jnp.mean(values, axis=-1, keepdims=True)
    inverse = lax.rsqrt(jnp.mean(centered * centered, axis=-1, keepdims=True) + 1e-05)
    normed = centered * inverse
    scaled = grad * gain
    back = inverse * (
        scaled
        - jnp.mean(scaled, axis=-1, keepdims=True)
        - normed * jnp.mean(scaled * normed, axis=-1, keepdims=True)
    )
    return back, normed


def shifted(part, start):
    return pl.ds(pl.multiple_of(start + part.start, 16), part.size)


def column_sum(value):
    return jnp.sum(value, axis=0, keepdims=True)


def forward_kernel(
    tokens_in, vec_in, attn_in, mlp_in, cot_in,
    qk_out, vo_out, first_out, q_out, k_out, v_out, o_out, out_out, grad_mid_out, do_out, ga_out, gb_out, go_out,
    x_a, x_b, y_a, y_b, lse, vec, sums,
    tokens, qk_all, vo_all, f0, f1, p0, p1, first, q, k, v, o, middle, second, act, slope,
    turned, mixed, partial, partial_other, pre, attn, mlp, qk_shard, vo_shard, f0_shard, f1_shard, p0_shard, p1_shard,
    cot, out, grad_mid, do, ga, gb, go, du, back_partial, back_other, m_partial, m_other, low, across, acc,
    gather_send, gather_recv, local, swap_send, swap_recv, send, recv, stage_sems,
):
    dp, core, z, y, x = place()
    length = tokens.shape[0]
    width = q.shape[1]
    chunk = length // 4
    x_peer, y_peer = dp + 1 - 2 * x, dp + 2 - 4 * y
    shard_rows = x_a.shape[1]
    stage = Staging(stage_sems)
    stage.fetch("attn", attn_in, attn)
    stage.fetch("tokens", tokens_in, tokens)
    stage.fetch("mlp", mlp_in, mlp)
    stage.fetch("cot", cot_in, cot)
    for row in range(vec.shape[0]):
        for column in range(D // 128):
            at = row * (D // 128) + column
            vec[row : row + 1, column * 128 : (column + 1) * 128] = vec_in[at : at + 1, :]
    stage.need("attn")
    for slot, shard in enumerate((qk_shard, qk_shard, vo_shard, vo_shard)):
        shard[:, slot % 2 * width : (slot % 2 + 1) * width] = attn[:, slot, :].astype(jnp.bfloat16)
    barrier = pltpu.get_barrier_semaphore()
    greet(barrier, dp + 1 - 2 * x, core)
    greet(barrier, dp + 2 - 4 * y, core)
    greet(barrier, dp, 1 - core)

    @pl.when(z > 0)
    def _():
        greet(barrier, dp - 4, core)

    @pl.when(z < LINE - 1)
    def _():
        greet(barrier, dp + 4, core)

    pl.semaphore_wait(barrier, 3 + (z + 2) // 3 + (5 - z) // 3)

    rounds = [
        Gathering(a, b, a_out, b_out, gather_send.at[i], gather_recv.at[i], local.at[i])
        for i, (a, b, a_out, b_out) in enumerate(
            ((qk_shard, vo_shard, qk_all, vo_all), (f0_shard, f1_shard, f0, f1), (p0_shard, p1_shard, p0, p1))
        )
    ]
    rounds[0].begin()
    stage.need("tokens", "mlp")
    for slot, shard in enumerate((f0_shard, f1_shard, p0_shard, p1_shard)):
        shard[...] = mlp[:, slot // 2, slot % 2 * D : (slot % 2 + 1) * D].astype(jnp.bfloat16)

    def norm_one(part):
        tile = norm_tile(tokens[part, :].astype(jnp.float32), vec[0:1, :], vec[1:2, :])
        first[part, :] = tile.astype(jnp.bfloat16)

    tiles(length, NORM_ROWS, norm_one)
    stage.keep(first, first_out)
    rounds[0].onward(1)
    rounds[0].relay(0)
    rounds[0].onward(2)
    rounds[0].relay(1)
    rounds[0].onward(3)
    rounds[0].relay(2)
    rounds[0].relay(3)
    rounds[1].begin()
    rounds[0].finish()
    stage.keep(qk_all, qk_out)
    stage.keep(vo_all, vo_out)

    mine = pl.ds(pl.multiple_of(core * width, width), width)
    scale = 1.0 / math.sqrt(HD)
    q[...] = ((contract(first[...], qk_all[:, 0:width], 1, 0) + vec[4:5, mine]) * scale).astype(jnp.bfloat16)
    k[...] = contract(first[...], qk_all[:, width:], 1, 0).astype(jnp.bfloat16)
    v[...] = (contract(first[...], vo_all[:, 0:width], 1, 0) + vec[5:6, mine]).astype(jnp.bfloat16)

    for value, target in ((q, q_out), (k, k_out), (v, v_out)):
        stage.keep(value, target)

    def step(index):
        if index == 1:
            rounds[1].onward(1)
            rounds[1].relay(0)
        if index == 2:
            rounds[1].onward(2)
            rounds[1].relay(1)
        if index == 3:
            rounds[1].onward(3)
            rounds[1].relay(2)
        if index == 4:
            rounds[1].relay(3)
            rounds[2].begin()
        if index == 6:
            rounds[2].onward(1)
            rounds[2].relay(0)
        if index == 7:
            rounds[2].onward(2)
            rounds[2].relay(1)
        if index == 8:
            rounds[2].onward(3)
            rounds[2].relay(2)
        if index == 9:
            rounds[2].relay(3)

    for pair in range(width // (2 * HD)):
        lanes = pl.ds(pair * 2 * HD, 2 * HD)
        attend_forward(
            q.at[:, lanes], k.at[:, lanes], v.at[:, lanes], o.at[:, lanes], lse.at[pair], turned, mixed,
            lambda head: step(2 * pair + head),
        )

    stage.keep(o, o_out)

    def swap_copy(kind, i):
        part = pl.ds(i * chunk, chunk)
        src, dst = ((back_partial, back_other), (m_partial, m_other), (partial, partial_other))[kind]
        return remote(src.at[part], dst.at[part], swap_send.at[kind, i], swap_recv.at[kind, i], dp, 1 - core)

    for i in range(4):
        part = pl.ds(i * chunk, chunk)
        partial[part, :] = contract(o[part, :], vo_all[:, width:], 1, 1).astype(jnp.bfloat16)
        swap_copy(2, i).start()
    step(6)
    rounds[1].finish()
    for i in range(4):
        swap_copy(2, i).wait_recv()

        def norm_two(part):
            rows = pl.ds(pl.multiple_of(i * chunk + part.start, 16), part.size)
            total = partial[rows, :].astype(jnp.float32) + partial_other[rows, :].astype(jnp.float32)
            tile = tokens[rows, :].astype(jnp.float32) + total + vec[6:7, :]
            middle[rows, :] = tile
            second[rows, :] = norm_tile(tile, vec[2:3, :], vec[3:4, :]).astype(jnp.bfloat16)

        tiles(chunk, NORM_ROWS, norm_two)
        rows = pl.ds(i * chunk, chunk)
        for side, weight in enumerate((f0, f1)):
            pre[:, side * D : (side + 1) * D] = contract(second[rows, :], weight[...], 1, 0)

        def curve(part):
            rows = pl.ds(pl.multiple_of(i * chunk + part.start, 16), part.size)
            for side in range(2):
                columns = pl.ds(side * D, D)
                value = pre[part, columns] + vec[pl.ds(8 + 2 * core + side, 1), :]
                square = value * value
                root = math.sqrt(2.0 / math.pi)
                bent = jnp.tanh(value * (root + root * 0.044715 * square))
                half = 0.5 + 0.5 * bent
                act[rows, columns] = (value * half).astype(jnp.bfloat16)
                inner = root + (3.0 * root * 0.044715) * square
                slope[rows, columns] = (half + (0.5 * value) * (1.0 - bent * bent) * inner).astype(jnp.bfloat16)

        tiles(chunk, 48, curve)
        step(7 + i)

    def early(side, level):
        grad, to_x, to_y = ((ga, x_a, y_a), (gb, x_b, y_b))[side]
        x_block = level * 4 + y * 2 + 1 - x
        y_block = level * 4 + (1 - y) * 2 + x

        def part(block):
            return grad.at[pl.ds(pl.multiple_of(block * shard_rows, shard_rows), shard_rows)]

        return (
            remote(part(x_block), to_x.at[level], send.at[side, level], recv.at[side, level], x_peer, core),
            remote(part(y_block), to_y.at[level], send.at[2 + side, level], recv.at[2 + side, level], y_peer, core),
        )

    def outer(left, right, target, start):
        size = right.shape[1]
        for block in range(D // 256):
            part = pl.ds(block * 256, 256)
            value = contract(left[part, :], right[...], 1, 0)
            target[part, start : start + size] = value.astype(jnp.bfloat16)
            row = 6 if size == D else 7
            sums[row : row + 1, 0:size] += column_sum(value * value)

    stage.need("cot")
    sums[...] = jnp.zeros_like(sums)
    across[...] = cot[...].T
    for side in range(2):
        outer(across, act.at[:, side * D : (side + 1) * D], gb, side * D)
    for level in range(LINE):
        for copy in early(1, level):
            copy.start()
    rounds[2].finish()
    acc[...] = jnp.zeros_like(acc)
    for i in range(4):
        part = pl.ds(i * chunk, chunk)
        for side, weight in enumerate((p0, p1)):
            columns = pl.ds(side * D, D)
            value = contract(cot[part, :], weight[...], 1, 0) * slope[part, columns].astype(jnp.float32)
            value = value.astype(jnp.bfloat16)
            du[part, columns] = value
            sums[4 + side : 5 + side, :] += column_sum(value.astype(jnp.float32))
        back_partial[part, :] = (
            contract(du[part, 0:D], f0[...], 1, 1) + contract(du[part, D:], f1[...], 1, 1)
        ).astype(jnp.bfloat16)
        swap_copy(0, i).start()
    across[...] = second[...].T
    for side in range(2):
        outer(across, du.at[:, side * D : (side + 1) * D], ga, side * D)
    for level in range(LINE):
        for copy in early(0, level):
            copy.start()
    stage.keep(ga, ga_out)
    for i in range(4):
        part = pl.ds(i * chunk, chunk)
        m_partial[part, :] = (
            contract(act[part, 0:D], p0[...], 1, 1) + contract(act[part, D:], p1[...], 1, 1)
        ).astype(jnp.bfloat16)
        swap_copy(1, i).start()
    stage.keep(gb, gb_out)
    for i in range(4):
        swap_copy(0, i).wait_recv()

        def back(part):
            rows = shifted(part, i * chunk)
            grad = back_partial[rows, :].astype(jnp.float32) + back_other[rows, :].astype(jnp.float32)
            outgoing = cot[rows, :].astype(jnp.float32)
            value, normed = norm_back_tile(grad, vec[2:3, :], middle[rows, :])
            value = value + outgoing
            grad_mid[rows, :] = value
            low[rows, :] = value.astype(jnp.bfloat16)
            acc[0] += fold(grad * normed)
            acc[1] += fold(grad)
            acc[2] += fold(value)
            acc[3] += fold(outgoing)

        tiles(chunk, BACK_ROWS, back)
        rows = pl.ds(i * chunk, chunk)
        do[rows, :] = contract(low[rows, :], vo_all[:, width:], 1, 0).astype(jnp.bfloat16)
    for row in range(4):
        sums[row : row + 1, :] = column_sum(acc[row])
    stage.keep(grad_mid, grad_mid_out)
    stage.keep(do, do_out)
    across[...] = low[...].T
    outer(across, o, go, 0)
    stage.keep(go, go_out)
    for i in range(4):
        swap_copy(1, i).wait_recv()

        def finish(part):
            rows = shifted(part, i * chunk)
            total = m_partial[rows, :].astype(jnp.float32) + m_other[rows, :].astype(jnp.float32)
            out[rows, :] = (middle[rows, :] + total + vec[7:8, :]).astype(jnp.bfloat16)

        tiles(chunk, 48, finish)
        part = pl.ds(i * chunk, chunk)
        stage.keep(out.at[part], out_out.at[part])
    for kind in range(3):
        for i in range(4):
            swap_copy(kind, i).wait_send()
    for side in range(2):
        for level in range(LINE):
            for copy in early(side, level):
                copy.wait()
    for gathering in rounds:
        gathering.drain()
    stage.finish()


def forward(tokens, vec, attn, mlp, cot, collective_id):
    dma = pltpu.SemaphoreType.DMA
    low = jnp.bfloat16
    count = lax.axis_size("dp")
    length = tokens.shape[0]
    rows, _, width = attn.shape
    hidden = 2 * D
    shape = jax.ShapeDtypeStruct
    scratch = pltpu.VMEM
    vmem = pl.BlockSpec(memory_space=pltpu.VMEM)
    anywhere = pl.BlockSpec(memory_space=pl.ANY)
    whole, thin, wide = (length, D), (length, width), (length, hidden)
    return pl.pallas_call(
        forward_kernel,
        out_shape=[shape((D, D), low)] * 2
        + [shape(whole, low)]
        + [shape(thin, low)] * 4
        + [
            shape(whole, low),
            shape(whole, jnp.float32),
            shape(thin, low),
            shape((D, hidden), low),
            shape((D, hidden), low),
            shape((D, width), low),
        ]
        + [shape((LINE, rows, hidden), low)] * 4
        + [
            shape((width // (2 * HD), 2, length), jnp.float32),
            shape((vec.shape[0] * 128 // D, D), jnp.float32),
            shape((8, D), jnp.float32),
        ],
        in_specs=[anywhere, vmem] + [anywhere] * 3,
        out_specs=[anywhere] * 17 + [vmem] * 3,
        scratch_shapes=[scratch(whole, low)]
        + [scratch((D, D), low)] * 6
        + [scratch(whole, low)]
        + [scratch(thin, low)] * 4
        + [
            scratch(whole, jnp.float32),
            scratch(whole, low),
            scratch(wide, low),
            scratch(wide, low),
            scratch((2 * HD, length), jnp.float32),
            scratch((2 * HD, length), low),
            scratch(whole, low),
            scratch(whole, low),
            scratch((length // 4, hidden), jnp.float32),
            scratch(attn.shape, jnp.float32),
            scratch(mlp.shape, jnp.float32),
        ]
        + [scratch((rows, D), low)] * 6
        + [
            scratch(whole, low),
            scratch(whole, low),
            scratch(whole, jnp.float32),
            scratch(thin, low),
            scratch((D, hidden), low),
            scratch((D, hidden), low),
            scratch((D, width), low),
            scratch(wide, low),
        ]
        + [scratch(whole, low)] * 5
        + [
            scratch((D, length), low),
            scratch((4, 8, D), jnp.float32),
            dma((3, 10, LINE)),
            dma((3, 2, count)),
            dma((3, 2)),
            dma((3, 4)),
            dma((3, 4)),
            dma((4, LINE)),
            dma((4, LINE)),
            dma((32,)),
        ],
        compiler_params=pltpu.CompilerParams(
            collective_id=collective_id, has_side_effects=True, vmem_limit_bytes=63 * MIB
        ),
        name="forward",
    )(tokens, vec, attn, mlp, cot)


class Reducing:
    def __init__(self, grads, buffers, sources, send, recv, rows, direct):
        self.direct = direct
        self.grads, self.sources = grads, sources
        self.diag, self.from_x, self.from_y, self.up, self.down = buffers[0:2], buffers[2:4], buffers[4:6], buffers[6:8], buffers[8:10]
        self.send, self.recv, self.rows = send, recv, rows
        self.dp, self.core, self.z, self.y, self.x = place()
        self.x_peer = self.dp + 1 - 2 * self.x
        self.y_peer = self.dp + 2 - 4 * self.y
        half = self.z // 2
        self.order = (3 - 3 * half, 2 - half, 1 - self.z + 4 * half, self.z)

    def at(self, ref, block):
        return ref.at[pl.ds(pl.multiple_of(block * self.rows, self.rows), self.rows)]

    def block(self, level, y_off, x_off):
        y = self.y + y_off * (1 - 2 * self.y)
        x = self.x + x_off * (1 - 2 * self.x)
        return level * 4 + y * 2 + x

    def go(self, kind, level, src, dst, target):
        return remote(src, dst, self.send.at[kind, level], self.recv.at[kind, level], target, self.core)

    def diag_copy(self, level, side):
        block = self.at(self.sources[side], self.block(level, 1, 1))
        target = self.block(self.z, 1, 1) if self.direct else (self.y_peer, self.x_peer)[side]
        return self.go(side, level, block, self.diag[side].at[level], target)

    def own_copy(self, level, side):
        block = self.at(self.sources[side], self.block(level, 1 - side, side))
        target = (self.from_y, self.from_x)[side][side].at[level]
        return self.go(2 + side, level, block, target, (self.y_peer, self.x_peer)[side])

    def sum_copy(self, level, side):
        target = (self.from_x, self.from_y)[side][side].at[level]
        return self.go(4 + side, level, self.diag[side].at[level], target, (self.x_peer, self.y_peer)[side])

    def up_copy(self, level, side):
        return self.go(6 + side, level, self.from_x[side].at[level], self.up[side].at[level], self.dp + 4)

    def down_copy(self, level, side):
        return self.go(8 + side, level, self.from_x[side].at[level], self.down[side].at[level], self.dp - 4)

    def first(self, *indices):
        for index in indices:
            level = self.order[index]
            for side in range(2):
                self.diag_copy(level, side).start()
            for side in () if self.direct else range(2):
                self.own_copy(level, side).start()

    def scale(self, factor, factor_x, factor_y, factor_diag):
        self.factor, self.factor_x, self.factor_y, self.factor_diag = factor, factor_x, factor_y, factor_diag

    def weigh(self, side, block, dst, scale_dst, terms):
        grad = self.grads[side]

        @pl.loop(0, self.rows // 16)
        def _(i):
            part = pl.ds(pl.multiple_of(i * 16, 16), 16)
            own = grad[pl.ds(pl.multiple_of(block * self.rows + i * 16, 16), 16), :]
            total = self.factor * own.astype(jnp.float32)
            for scale, ref in ((scale_dst, dst),) + terms:
                value = ref[part, :].astype(jnp.float32)
                total = total + (value if scale is None else scale * value)
            dst[part, :] = total.astype(dst.dtype)

    def sums(self, level):
        for side in range(2):
            self.diag_copy(level, side).wait_recv()
            block = self.block(level, side, 1 - side)
            self.weigh(side, block, self.diag[side].at[level], (self.factor_y, self.factor_x)[side], ())
            self.sum_copy(level, side).start()

    def scales(self, side):
        if self.direct:
            return self.factor_x, self.factor_y
        return (None, self.factor_y) if side == 0 else (self.factor_x, None)

    def arrivals(self, level, side):
        if self.direct:
            self.diag_copy(level, side).wait_recv()
            return
        self.own_copy(level, side).wait_recv()
        self.sum_copy(level, side).wait_recv()

    def chain(self, index):
        level = self.order[index]
        block = self.block(level, 0, 0)
        for side in range(2):
            self.arrivals(level, side)
            scale_x, scale_y = self.scales(side)
            terms = ((scale_y, self.from_y[side].at[level]),)
            if self.direct:
                terms = terms + ((self.factor_diag, self.diag[side].at[level]),)

            def combine(*extra):
                self.weigh(side, block, self.from_x[side].at[level], scale_x, terms + extra)

            @pl.when(level > self.z)
            def _():
                @pl.when(self.z > 0)
                def _():
                    self.up_copy(level, side).wait_recv()
                    combine((None, self.up[side].at[level]))

                @pl.when(self.z == 0)
                def _():
                    combine()

                self.up_copy(level, side).start()

            @pl.when(level < self.z)
            def _():
                @pl.when(self.z < LINE - 1)
                def _():
                    self.down_copy(level, side).wait_recv()
                    combine((None, self.down[side].at[level]))

                @pl.when(self.z == LINE - 1)
                def _():
                    combine()

                self.down_copy(level, side).start()

    def last(self, side):
        self.arrivals(self.z, side)

        @pl.when(self.z > 0)
        def _():
            self.up_copy(self.z, side).wait_recv()

        @pl.when(self.z == 0)
        def _():
            self.up[side][0] = jnp.zeros(self.up[side].shape[1:], self.up[side].dtype)

        @pl.when(self.z < LINE - 1)
        def _():
            self.down_copy(self.z, side).wait_recv()

        @pl.when(self.z == LINE - 1)
        def _():
            self.down[side][LINE - 1] = jnp.zeros(self.down[side].shape[1:], self.down[side].dtype)

    def total(self, side, part, columns):
        here = pl.ds(pl.multiple_of(self.dp * self.rows + part.start, 16), part.size)
        total = self.factor * self.grads[side][here, columns].astype(jnp.float32)
        terms = list(zip(self.scales(side) + (None, None), (self.from_x, self.from_y, self.up, self.down)))
        if self.direct:
            terms.append((self.factor_diag, self.diag))
        for scale, ref in terms:
            value = ref[side][self.z, part, columns].astype(jnp.float32)
            total = total + (value if scale is None else scale * value)
        return total

    def drain(self):
        for level in range(LINE):
            for side in range(2):
                self.diag_copy(level, side).wait_send()
                if not self.direct:
                    self.own_copy(level, side).wait_send()
                    self.sum_copy(level, side).wait_send()

            @pl.when(level > self.z)
            def _():
                for side in range(2):
                    self.up_copy(level, side).wait_send()

            @pl.when(level < self.z)
            def _():
                for side in range(2):
                    self.down_copy(level, side).wait_send()


def owner_at(slot):
    return OWNERS[slot] // 4, OWNERS[slot] % 4 // 2, OWNERS[slot] % 2


def attn_back_kernel(
    noise_scale, batch, clip,
    tokens_in, vec, first_in, q_in, k_in, v_in, o_in, do_in, lse, qk_in, vo_in, grad_mid_in, ga_in, gb_in, go_in,
    x_a_in, x_b_in, y_a_in, y_b_in, sums, included, attn_mom_in, mlp_mom_in, attn_noise_in, mlp_noise_in,
    grad_in_out, attn_out, mlp_out, vec_out, owned,
    tokens, first, q, k, v, o, do, qk_all, wv, grad_mid, ga, gb, attn_mom, mlp_mom, attn_noise, mlp_noise, grad_in,
    dqk, dv, ga_late, gb_late, head_turned, turned, partial, other, acc, square, factors,
    diag_a, diag_b, x_a, x_b, y_a, y_b, up_a, up_b, down_a, down_b,
    late_diag_a, late_diag_b, late_x_a, late_x_b, late_y_a, late_y_b, late_up_a, late_up_b, late_down_a, late_down_b,
    attn_low, mlp_low, relayed, vec_plane, vec_line,
    send, recv, late_send, late_recv, vec_sems, line_sems, gather_send, gather_recv, relay_sems, swap_send, swap_recv, small, pass_send, pass_recv,
    stage_sems,
):
    dp, core, z, y, x = place()
    rows, _, width = attn_mom.shape
    wide = mlp_mom.shape[2]
    length = tokens.shape[0]
    chunk = length // 4
    x_peer, y_peer = dp + 1 - 2 * x, dp + 2 - 4 * y
    count = ga.shape[0] // rows
    stage = Staging(stage_sems)
    for name, src, dst in (
        ("q", q_in, q), ("k", k_in, k), ("v", v_in, v), ("o", o_in, o), ("do", do_in, do), ("qk_all", qk_in, qk_all),
        ("wv", vo_in.at[:, pl.ds(0, width)], wv), ("first", first_in, first), ("go", go_in, gb_late.at[:, pl.ds(width, width)]),
        ("tokens", tokens_in, tokens), ("grad_mid", grad_mid_in, grad_mid), ("ga", ga_in, ga), ("gb", gb_in, gb),
        ("x_a", x_a_in, x_a), ("x_b", x_b_in, x_b), ("y_a", y_a_in, y_a), ("y_b", y_b_in, y_b),
        ("mlp_mom", mlp_mom_in, mlp_mom), ("mlp_noise", mlp_noise_in, mlp_noise), ("attn_mom", attn_mom_in, attn_mom),
        ("attn_noise", attn_noise_in, attn_noise),
    ):
        stage.fetch(name, src, dst)
    greeted = greet_plane(dp, core, count, z, y, x)

    main = Reducing(
        (ga, gb), (diag_a, diag_b, x_a, x_b, y_a, y_b, up_a, up_b, down_a, down_b), (ga_in, gb_in), send, recv, rows, True
    )
    late = Reducing(
        (ga_late, gb_late),
        (late_diag_a, late_diag_b, late_x_a, late_x_b, late_y_a, late_y_b, late_up_a, late_up_b, late_down_a, late_down_b),
        (ga_late, gb_late),
        late_send,
        late_recv,
        rows,
        False,
    )

    def small_copy(index):
        src, dst, target = (
            (square.at[0], square.at[1], (dp, 1 - core)),
            (factors.at[0], factors.at[1], (x_peer, core)),
            (factors.at[0], factors.at[2], (y_peer, core)),
            (factors.at[0], factors.at[3], (main.block(z, 1, 1), core)),
        )[index]
        return remote(src, dst, small.at[0, index], small.at[1, index], *target)

    mine_in_plane = (y * 2 + x) * 2 + core

    def plane_copies():
        copies = []
        for y_off, x_off, core_off in [(i // 4, i // 2 % 2, i % 2) for i in range(1, 8)]:
            target = main.block(z, y_off, x_off)
            target_core = core + core_off * (1 - 2 * core)
            place_there = target % 4 * 2 + target_core
            copies.append(
                remote(
                    vec_plane.at[mine_in_plane], vec_plane.at[mine_in_plane], vec_sems.at[0, place_there],
                    vec_sems.at[1, mine_in_plane], target, target_core,
                )
            )
        return copies

    def plane_arrivals():
        for i in range(1, 8):
            index = (mine_in_plane + i) % 8
            block = vec_plane.at[index]
            remote(block, block, vec_sems.at[0, index], vec_sems.at[1, index], dp, core).wait_recv()

    def line_copies():
        return [
            remote(vec_line.at[z], vec_line.at[z], line_sems.at[0, (z + i) % LINE], line_sems.at[1, z], (dp + 4 * i) % count, core)
            for i in range(1, LINE)
        ]

    def vec_turn():
        plane_arrivals()
        total = vec_plane[0]
        for index in range(1, 8):
            total = total + vec_plane[index]
        vec_line[z] = total
        for copy in line_copies():
            copy.start()

    def vec_finish():
        for i in range(1, LINE):
            index = (z + i) % LINE
            block = vec_line.at[index]
            remote(block, block, line_sems.at[0, index], line_sems.at[1, index], dp, core).wait_recv()
        total = vec_line[0]
        for index in range(1, LINE):
            total = total + vec_line[index]
        per_row = D // 128
        for row in range(vec_out.shape[0]):
            at = row % per_row * 128
            vec_out[row : row + 1, :] = total[row // per_row : row // per_row + 1, at : at + 128]
        for copy in plane_copies() + line_copies():
            copy.wait_send()

    def swap_copy(i):
        part = pl.ds(i * chunk, chunk)
        return remote(partial.at[part], other.at[part], swap_send.at[i], swap_recv.at[i], dp, 1 - core)

    acc[...] = jnp.zeros_like(acc)
    stage.need("q", "k", "v", "o", "do")
    for pair in range(width // (2 * HD)):
        lanes = pl.ds(pair * 2 * HD, 2 * HD)
        attend_backward(
            q.at[:, lanes], k.at[:, lanes], v.at[:, lanes], o.at[:, lanes], do.at[:, lanes], lse.at[pair],
            dqk.at[:, lanes], dqk.at[:, pl.ds(width + pair * 2 * HD, 2 * HD)], dv.at[:, lanes], head_turned,
        )
        if pair == 0:
            greeted()
            main.first(0, 1, 2, 3)
    stage.need("qk_all", "wv")
    for i in range(4):
        part = pl.ds(i * chunk, chunk)
        partial[part, :] = (contract(dqk[part, :], qk_all[...], 1, 1) + contract(dv[part, :], wv[...], 1, 1)).astype(
            jnp.bfloat16
        )
        swap_copy(i).start()
    stage.need("first", "go")
    turned[...] = first[...].T
    squares = jnp.zeros((1, 1), jnp.float32)
    for right, target in ((dqk, ga_late), (dv, gb_late)):
        for block in range(D // 256):
            part = pl.ds(block * 256, 256)
            value = contract(turned[part, :], right[...], 1, 0)
            target[part, 0 : right.shape[1]] = value.astype(jnp.bfloat16)
            squares = squares + jnp.sum(column_sum(value * value), axis=1, keepdims=True)
    late.first(0, 1)
    bias_q = column_sum(dqk[:, 0:width].astype(jnp.float32))
    bias_v = column_sum(dv[...].astype(jnp.float32))
    for value in (sums[6:7, :], sums[7:8, :]):
        squares = squares + jnp.sum(value, axis=1, keepdims=True)
    for value in (bias_q, bias_v, sums[4:5, :], sums[5:6, :]):
        squares = squares + jnp.sum(value * value, axis=1, keepdims=True)
    square[0] = jnp.broadcast_to(squares, square.shape[1:])
    small_copy(0).start()

    stage.need("tokens", "grad_mid")
    for i in range(4):
        swap_copy(i).wait_recv()

        def back(part):
            here = shifted(part, i * chunk)
            grad = partial[here, :].astype(jnp.float32) + other[here, :].astype(jnp.float32)
            value, normed = norm_back_tile(grad, vec[0:1, :], tokens[here, :].astype(jnp.float32))
            grad_in[here, :] = (grad_mid[here, :] + value).astype(jnp.bfloat16)
            acc[0] += fold(grad * normed)
            acc[1] += fold(grad)

        tiles(chunk, BACK_ROWS, back)
    stage.keep(grad_in, grad_in_out)
    gain_one, bias_one = column_sum(acc[0]), column_sum(acc[1])
    shared = jnp.zeros((1, 1), jnp.float32)
    for value in (gain_one, bias_one, sums[0:1, :], sums[1:2, :], sums[2:3, :], sums[3:4, :]):
        shared = shared + jnp.sum(value * value, axis=1, keepdims=True)
    small_copy(0).wait_recv()
    norm = jnp.sqrt(square[0, 0:1, 0:1] + square[1, 0:1, 0:1] + shared)
    factor = included[0].astype(jnp.float32) * jnp.minimum(1.0, clip / (norm + 1e-06))
    factors[0] = jnp.broadcast_to(factor, factors.shape[1:])
    for index in (1, 2, 3):
        small_copy(index).start()
    leading = factor * (1 - core).astype(jnp.float32)
    vec_plane[mine_in_plane] = jnp.zeros(vec_plane.shape[1:], jnp.float32)
    mine = pl.ds(pl.multiple_of(core * width, width), width)
    for row, value in ((0, gain_one), (1, bias_one), (2, sums[0:1, :]), (3, sums[1:2, :]), (6, sums[2:3, :]), (7, sums[3:4, :])):
        vec_plane[mine_in_plane, row : row + 1, :] = leading * value
    vec_plane[mine_in_plane, 4:5, mine] = factor * bias_q
    vec_plane[mine_in_plane, 5:6, mine] = factor * bias_v
    vec_plane[mine_in_plane, pl.ds(8 + 2 * core, 1), :] = factor * sums[4:5, :]
    vec_plane[mine_in_plane, pl.ds(9 + 2 * core, 1), :] = factor * sums[5:6, :]
    stage.need("ga", "gb", "x_a", "x_b", "y_a", "y_b", "mlp_mom", "mlp_noise", "attn_mom", "attn_noise")
    for index in (1, 2, 3):
        small_copy(index).wait_recv()
    for part in (main, late):
        part.scale(factor, factors[1, 0:1, 0:1], factors[2, 0:1, 0:1], factors[3, 0:1, 0:1])

    def moment(slot, reducing, side, column):
        size = width if slot < 4 else wide
        low = attn_low.at[slot] if slot < 4 else mlp_low.at[slot - 4]
        old, noise, new = (attn_mom, attn_noise, attn_out) if slot < 4 else (mlp_mom, mlp_noise, mlp_out)
        index = slot if slot < 4 else slot - 4

        @pl.loop(0, rows // 16)
        def _(i):
            part = pl.ds(pl.multiple_of(i * 16, 16), 16)
            total = reducing.total(side, part, pl.ds(column, size))
            value = 0.5 * old[part, index, :] + (total + noise_scale * noise[part, index, :]) / batch
            new[part, index, :] = value
            low[part, :] = value.astype(low.dtype)

        for action in sends(slot):
            action(lambda copy: copy.start())

    def landing(slot, source):
        size = width if slot < 4 else wide
        return main.at(owned.at[0], source).at[:, 0:size]

    def sends(slot):
        owner = OWNERS[slot]
        owner_z, owner_y, owner_x = owner_at(slot)
        low = attn_low.at[slot] if slot < 4 else mlp_low.at[slot - 4]
        alone = 0 if owner_z == 1 else LINE - 1
        far = (y != owner_y) & (x != owner_x)
        near = (y != owner_y) | (x != owner_x)
        across = (z != owner_z) & (far | ((z == alone) & near))

        def keep(action):
            @pl.when(dp == owner)
            def _():
                action(pltpu.make_async_copy(low, landing(slot, dp), gather_send.at[slot]))

        def direct(action):
            away = (dp != owner) & jnp.logical_not(across) if slot >= 4 else dp != owner

            @pl.when(away)
            def _():
                action(remote(low, landing(slot, dp), gather_send.at[slot], gather_recv.at[dp], owner, core))

        def turn(action):
            if slot >= 4:

                @pl.when(across)
                def _():
                    stop = z * 4 + owner_y * 2 + owner_x
                    action(remote(low, relayed.at[dp % 4], gather_send.at[slot], relay_sems.at[0, dp % 4], stop, core))

        return keep, direct, turn

    def relays(slot, action):
        owner_z, owner_y, owner_x = owner_at(slot)
        alone = 0 if owner_z == 1 else LINE - 1
        column = owner_y * 2 + owner_x
        here = (y == owner_y) & (x == owner_x) & (z != owner_z)

        @pl.when(here)
        def _():
            action(3 - column)

        @pl.when(here & (z == alone))
        def _():
            action(column + 1 - 2 * owner_x)
            action(column + 2 - 4 * owner_y)

    def relay_copy(slot, column):
        source = z * 4 + column
        return remote(
            relayed.at[column], landing(slot, source), relay_sems.at[1, column], gather_recv.at[source], OWNERS[slot], core
        )

    def forward(slot, column):
        block = relayed.at[column]
        remote(block, block, relay_sems.at[1, column], relay_sems.at[0, column], dp, core).wait_recv()
        relay_copy(slot, column).start()

    def pass_on(slot, source):
        size = width if slot < 4 else wide
        block = landing(slot, source)
        other_half = main.at(owned.at[1], source).at[:, 0:size]
        return remote(block, other_half, pass_send.at[source], pass_recv.at[source], dp, 1 - core)

    def turned_off(slot, source):
        owner_z, owner_y, owner_x = owner_at(slot)
        off_x, off_y = source % 2 != owner_x, source % 4 // 2 != owner_y
        alone = 0 if owner_z == 1 else LINE - 1
        return slot >= 4 and source // 4 != owner_z and ((off_x and off_y) or (source // 4 == alone and (off_x or off_y)))

    def collect(slot, late_ones):
        @pl.when(dp == OWNERS[slot])
        def _():
            for step in range(1, count):
                source = (OWNERS[slot] + step) % count
                if turned_off(slot, source) == late_ones:
                    block = landing(slot, source)
                    remote(block, block, gather_send.at[slot], gather_recv.at[source], source, core).wait_recv()
                    pass_on(slot, source).start()

    main.chain(0)
    late.first(2)
    late.sums(late.order[0])
    main.chain(1)
    late.first(3)
    late.sums(late.order[1])
    main.chain(2)
    late.sums(late.order[2])
    late.sums(late.order[3])
    main.last(0)
    moment(4, main, 0, 0)
    main.last(1)
    moment(5, main, 1, 0)
    late.chain(0)
    for copy in plane_copies():
        copy.start()
    late.chain(1)
    for slot in (4, 5):
        relays(slot, functools.partial(forward, slot))
    late.chain(2)
    vec_turn()
    for slot in (4, 5):
        collect(slot, False)
    late.last(0)
    moment(0, late, 0, 0)
    moment(1, late, 0, width)
    late.last(1)
    moment(2, late, 1, 0)
    moment(3, late, 1, width)

    for slot in range(6):
        low = attn_low.at[slot] if slot < 4 else mlp_low.at[slot - 4]

        @pl.when(dp == OWNERS[slot])
        def _():
            pltpu.make_async_copy(low, landing(slot, dp), gather_send.at[slot]).wait()
            pass_on(slot, dp).start()

    for slot in (4, 5):
        collect(slot, True)
    for slot in range(4):
        collect(slot, False)
    for slot in range(6):
        owner = OWNERS[slot]
        low = attn_low.at[slot] if slot < 4 else mlp_low.at[slot - 4]

        @pl.when(dp != owner)
        def _():
            remote(low, low, gather_send.at[slot], gather_recv.at[dp], owner, core).wait_send()

        @pl.when(dp == owner)
        def _():
            @pl.loop(0, count)
            def _(source):
                pass_on(slot, source).wait()

    vec_finish()
    for slot in (4, 5):
        relays(slot, lambda column: relay_copy(slot, column).wait_send())
    for index in range(4):
        small_copy(index).wait_send()
    for i in range(4):
        swap_copy(i).wait_send()
    main.drain()
    late.drain()
    stage.finish()


def attn_back(
    tokens, vec, first, q, k, v, o, do, lse, qk_all, vo_all, grad_mid, ga, gb, go, x_a, x_b, y_a, y_b, sums, included,
    attn_mom, mlp_mom, attn_noise, mlp_noise, noise_scale, batch, clip, collective_id,
):
    dma = pltpu.SemaphoreType.DMA
    low = jnp.bfloat16
    count = lax.axis_size("dp")
    length = tokens.shape[0]
    rows, _, width = attn_mom.shape
    wide = mlp_mom.shape[2]
    shape = jax.ShapeDtypeStruct
    vmem = pl.BlockSpec(memory_space=pltpu.VMEM)
    anywhere = pl.BlockSpec(memory_space=pl.ANY)
    scratch = pltpu.VMEM
    return pl.pallas_call(
        functools.partial(attn_back_kernel, noise_scale, batch, clip),
        out_shape=[
            shape((length, D), low),
            shape(attn_mom.shape, jnp.float32),
            shape(mlp_mom.shape, jnp.float32),
            shape((vec.shape[0] * D // 128, 128), jnp.float32),
            shape((2, D, wide), low),
        ],
        in_specs=[anywhere, vmem]
        + [anywhere] * 6
        + [vmem]
        + [anywhere] * 10
        + [vmem, pl.BlockSpec(memory_space=pltpu.SMEM)]
        + [anywhere] * 4,
        out_specs=[anywhere] + [vmem] * 3 + [anywhere],
        scratch_shapes=[
            scratch((length, D), low),
            scratch((length, D), low),
        ]
        + [scratch((length, width), low)] * 5
        + [
            scratch((D, 2 * width), low),
            scratch((D, width), low),
            scratch((length, D), jnp.float32),
            scratch((D, wide), low),
            scratch((D, wide), low),
            scratch(attn_mom.shape, jnp.float32),
            scratch(mlp_mom.shape, jnp.float32),
            scratch(attn_mom.shape, jnp.float32),
            scratch(mlp_mom.shape, jnp.float32),
            scratch((length, D), low),
            scratch((length, 2 * width), low),
            scratch((length, width), low),
            scratch((D, 2 * width), low),
            scratch((D, 2 * width), low),
            scratch((2 * HD, length), jnp.float32),
            scratch((D, length), low),
            scratch((length, D), low),
            scratch((length, D), low),
            scratch((2, 8, D), jnp.float32),
            scratch((2, 8, 128), jnp.float32),
            scratch((4, 8, 128), jnp.float32),
        ]
        + [scratch((LINE, rows, wide), low)] * 10
        + [scratch((LINE, rows, 2 * width), low)] * 10
        + [
            scratch((4, rows, width), low),
            scratch((2, rows, wide), low),
            scratch((4, rows, wide), low),
            scratch((8,) + vec.shape, jnp.float32),
            scratch((LINE,) + vec.shape, jnp.float32),
            dma((10, LINE)),
            dma((10, LINE)),
            dma((10, LINE)),
            dma((10, LINE)),
            dma((2, 8)),
            dma((2, LINE)),
            dma((6,)),
            dma((count,)),
            dma((2, 4)),
            dma((4,)),
            dma((4,)),
            dma((2, 4)),
            dma((count,)),
            dma((count,)),
            dma((24,)),
        ],
        compiler_params=pltpu.CompilerParams(
            collective_id=collective_id, has_side_effects=True, vmem_limit_bytes=62 * MIB
        ),
        name="attn_back",
    )(
        tokens, vec, first, q, k, v, o, do, lse, qk_all, vo_all, grad_mid, ga, gb, go, x_a, x_b, y_a, y_b, sums, included,
        attn_mom, mlp_mom, attn_noise, mlp_noise,
    )


def placed(piece, start, total_size):
    return lax.dynamic_update_slice_in_dim(jnp.zeros((total_size,), jnp.float32), piece, start, 0)


def other_core(value):
    return lax.ppermute(value, "tensor", [(0, 1), (1, 0)])


SHIFTS = (0.0, 0.0, 0.0, 0.8, 0.72)


def polynomials(current):
    rows = current.shape[0]
    diagonal = lax.broadcasted_iota(jnp.int32, (rows, rows), 0) == lax.broadcasted_iota(jnp.int32, (rows, rows), 1)

    def less(matrix, shift):
        return matrix - jnp.where(diagonal, shift, 0.0) if shift else matrix

    def product(left, right):
        return contract(left.astype(jnp.bfloat16), right.astype(jnp.bfloat16), 1, 0)

    factor = None
    for iteration in range(NS_ITERS):
        shift = SHIFTS[iteration]
        moved = less(current, shift)
        square = product(moved, moved) + 2.0 * shift * moved
        lead = COEF_B * shift + COEF_C * shift * shift
        rest = lax.optimization_barrier(COEF_B * moved + COEF_C * square)
        whole = COEF_A + lead
        if factor is None:
            factor = jnp.where(diagonal, whole, 0.0) + rest
        else:
            factor = lax.optimization_barrier(whole * factor + product(rest, factor))
        if iteration < NS_ITERS - 1:
            once = lax.optimization_barrier(whole * current + shift * rest + product(rest, moved))
            second = whole * shift
            current = lax.optimization_barrier(whole * once + second * rest + product(rest, less(once, second)))
    return factor.astype(jnp.bfloat16)


def newton(owned):
    gram = contract(owned, owned, 1, 1)
    gram = gram + other_core(gram)
    scale = 1.0 / (jnp.sqrt(jnp.trace(gram)) + 1e-07)
    return (contract(polynomials(gram * (scale * scale)), owned, 1, 0) * scale).astype(jnp.bfloat16)


def body(
    fast,
    tokens,
    cotangent,
    inclusion,
    attn_weights,
    mlp_weights,
    attn_momentum,
    mlp_momentum,
    attn_noise,
    mlp_noise,
    vectors,
    vector_momentum,
    vector_noise,
):
    dp_count = lax.axis_size("dp")
    dp_index = lax.axis_index("dp")
    halves = lax.axis_size("tensor")
    tensor_index = lax.axis_index("tensor")
    head_width = D // halves
    hidden_width = FF // halves
    query_scale = 1.0 / math.sqrt(HD)
    clip = 1.5 * D * math.sqrt(LEN)
    sigma = 0.05 * math.sqrt(dp_count) / D
    batch = 0.75 * dp_count
    noise_scale = sigma * clip
    if fast:
        (
            query_key, value_out, first_low, queries, key_rows, value_rows, attended_low, result, grad_mid, grad_attended,
            grad_fc, grad_pr, grad_wo, x_fc, x_pr, y_fc, y_pr, stats, vec, sums,
        ) = forward(tokens[0], vectors.reshape(-1, 128), attn_weights, mlp_weights, cotangent[0], 0)
        grad_in, attn_moment, mlp_moment, vector_summed, owned = attn_back(
            tokens[0], vec, first_low, queries, key_rows, value_rows, attended_low, grad_attended, stats,
            query_key, value_out, grad_mid, grad_fc, grad_pr, grad_wo,
            x_fc, x_pr, y_fc, y_pr, sums,
            inclusion, attn_momentum, mlp_momentum, attn_noise, mlp_noise, noise_scale, batch, clip, 2,
        )
    else:
        attn_shard = attn_weights.astype(jnp.bfloat16)
        mlp_shard = mlp_weights.astype(jnp.bfloat16)
        rows = attn_shard.shape[0]
        shards = (
            attn_shard[:, 0:2].reshape(rows, 2 * head_width),
            attn_shard[:, 2:4].reshape(rows, 2 * head_width),
            mlp_shard[:, 0, 0:D],
            mlp_shard[:, 0, D:],
            mlp_shard[:, 1, 0:D],
            mlp_shard[:, 1, D:],
        )
        gain_one = vectors[0:D]
        bias_one = vectors[D : 2 * D]
        gain_two = vectors[2 * D : 3 * D]
        bias_two = vectors[3 * D : 4 * D]
        query_bias = lax.dynamic_slice_in_dim(vectors, 4 * D + tensor_index * head_width, head_width)
        value_bias = lax.dynamic_slice_in_dim(vectors, 5 * D + tensor_index * head_width, head_width)
        attn_bias = vectors[6 * D : 7 * D]
        mlp_bias = vectors[7 * D : 8 * D]
        hidden_bias = lax.dynamic_slice_in_dim(
            vectors, 8 * D + tensor_index * hidden_width, hidden_width
        )
        inputs = tokens[0].astype(jnp.float32)
        length = inputs.shape[0]
        first, normed_one, inverse_one = layer_norm(inputs, gain_one, bias_one)

        def both_cores(partial):
            low = partial.astype(jnp.bfloat16)
            return low.astype(jnp.float32) + other_core(low).astype(jnp.float32)

        query_key, value_out, fc_one, fc_two, pr_one, pr_two = (
            lax.all_gather(shard, "dp", axis=0, tiled=True) for shard in shards
        )
        value_weight, out_weight = value_out[:, 0:head_width], value_out[:, head_width:]
        first_low = first.astype(jnp.bfloat16)
        qk = contract(first_low, query_key, 1, 0)
        queries = ((qk[:, 0:head_width] + query_bias) * query_scale).astype(jnp.bfloat16)
        key_rows = qk[:, head_width:].astype(jnp.bfloat16)
        value_rows = (contract(first_low, value_weight, 1, 0) + value_bias).astype(jnp.bfloat16)
        attended_low, stats = pairs_forward(queries, key_rows, value_rows)
        middle = inputs + both_cores(contract(attended_low, out_weight, 1, 1)) + attn_bias
        second_low = layer_norm(middle, gain_two, bias_two)[0].astype(jnp.bfloat16)
        pre_act = contract(second_low, jnp.concatenate([fc_one, fc_two], axis=1), 1, 0) + hidden_bias
        activation, gelu_back = jax.vjp(gelu_tanh, pre_act)
        activation_low = activation.astype(jnp.bfloat16)
        slope = gelu_back(jnp.ones_like(pre_act))[0]
        _, normed_two, inverse_two = layer_norm(middle, gain_two, bias_two)
        fc_weight = jnp.concatenate([fc_one, fc_two], axis=1)
        pr_weight = jnp.concatenate([pr_one, pr_two], axis=1)
        result = middle + both_cores(contract(activation_low, pr_weight, 1, 1)) + mlp_bias
        cot_low = cotangent[0]
        grad_out = cot_low.astype(jnp.float32)
        d_pr = contract(cot_low, activation_low, 0, 0)
        grad_pre = (contract(cot_low, pr_weight, 1, 0) * slope.astype(jnp.float32)).astype(jnp.bfloat16)
        d_fc = contract(second_low, grad_pre, 0, 0)
        d_hidden_bias = jnp.sum(grad_pre.astype(jnp.float32), axis=0)
        grad_two = both_cores(contract(grad_pre, fc_weight, 1, 1))
        grad_mid = grad_out + norm_back(grad_two, gain_two, normed_two, inverse_two)
        d_gain_two = jnp.sum(grad_two * normed_two, axis=0)
        d_bias_two = jnp.sum(grad_two, axis=0)
        d_attn_bias = jnp.sum(grad_mid, axis=0)
        d_mlp_bias = jnp.sum(grad_out, axis=0)
        mid_low = grad_mid.astype(jnp.bfloat16)
        d_out = contract(mid_low, attended_low, 0, 0)
        grad_attended = contract(mid_low, out_weight, 1, 0).astype(jnp.bfloat16)
        grad_q, grad_k, grad_v = pairs_backward(
            queries, key_rows, value_rows, attended_low, grad_attended, stats
        )
        grad_qk = jnp.concatenate([grad_q, grad_k], axis=1)
        d_query_key = contract(first_low, grad_qk, 0, 0)
        d_value = contract(first_low, grad_v, 0, 0)
        d_query_bias = jnp.sum(grad_q.astype(jnp.float32), axis=0)
        d_value_bias = jnp.sum(grad_v.astype(jnp.float32), axis=0)
        grad_one = both_cores(contract(grad_qk, query_key, 1, 1) + contract(grad_v, value_weight, 1, 1))
        grad_in = grad_mid + norm_back(grad_one, gain_one, normed_one, inverse_one)
        d_gain_one = jnp.sum(grad_one * normed_one, axis=0)
        d_bias_one = jnp.sum(grad_one, axis=0)
        split_square = sum(
            jnp.sum(value * value)
            for value in (d_query_key, d_value, d_out, d_fc, d_pr, d_query_bias, d_value_bias, d_hidden_bias)
        )
        split_tile = jnp.broadcast_to(split_square, (8, 128))
        total_square = (split_tile + other_core(split_tile))[0, 0] + sum(
            jnp.sum(value * value)
            for value in (d_gain_one, d_bias_one, d_gain_two, d_bias_two, d_attn_bias, d_mlp_bias)
        )
        factor = inclusion[0].astype(jnp.float32) * jnp.minimum(
            1.0, clip / (jnp.sqrt(total_square) + 1e-06)
        )
        leading = (tensor_index == 0).astype(jnp.float32)
        vector_grad = (
            jnp.concatenate(
                [
                    leading * d_gain_one,
                    leading * d_bias_one,
                    leading * d_gain_two,
                    leading * d_bias_two,
                    placed(d_query_bias, tensor_index * head_width, D),
                    placed(d_value_bias, tensor_index * head_width, D),
                    leading * d_attn_bias,
                    leading * d_mlp_bias,
                    placed(d_hidden_bias, tensor_index * hidden_width, FF),
                ]
            )
            * factor
        )
        result, grad_in = result.astype(jnp.bfloat16), grad_in.astype(jnp.bfloat16)
        attn_grad = jnp.concatenate([d_query_key, d_value, d_out], axis=1) * factor
        mlp_grad = jnp.stack([d_fc, d_pr], axis=1) * factor
        attn_summed = lax.psum_scatter(attn_grad, "dp", scatter_dimension=0, tiled=True)
        mlp_summed = lax.psum_scatter(mlp_grad, "dp", scatter_dimension=0, tiled=True)
        attn_summed = attn_summed.reshape(rows, 4, head_width)
        vector_summed = lax.psum(vector_grad, ("dp", "tensor"))
        attn_moment = 0.5 * attn_momentum + (attn_summed + noise_scale * attn_noise) / batch
        mlp_moment = 0.5 * mlp_momentum + (mlp_summed + noise_scale * mlp_noise) / batch
        owners = jnp.array([slot * dp_count // 6 for slot in range(6)])
        full_attn = lax.all_gather(attn_moment.astype(jnp.bfloat16), "dp", axis=0, tiled=True)
        full_mlp = lax.all_gather(mlp_moment.astype(jnp.bfloat16), "dp", axis=0, tiled=True)
        attn_pick = (owners[0:4] == dp_index)[None, :, None]
        mlp_pick = (owners[4:6] == dp_index)[None, :, None]
        mine_attn = jnp.sum(jnp.where(attn_pick, full_attn, 0), axis=1)
        mine_mlp = jnp.sum(jnp.where(mlp_pick, full_mlp, 0), axis=1)
        owned = jnp.pad(mine_attn, ((0, 0), (0, hidden_width - head_width))) + mine_mlp
    vector_rate = 0.2 * math.sqrt(dp_count / LEN)
    rates = (0.5, 0.5, 0.5, 0.5 * max(1.0, math.sqrt(LEN) / 8.0), 0.5 * math.sqrt(FF / D), 0.5)
    if fast:
        tiled = tuple(value.reshape(-1, 128) for value in (vector_summed, vectors, vector_momentum, vector_noise))
        gram, scale, result, grad_in, attn_moment, mlp_moment, vector_moment, vectors_new = gram_of(
            owned, (result, grad_in, attn_moment, mlp_moment), tiled, noise_scale, batch, vector_rate
        )
        vector_moment, vectors_new = vector_moment.reshape(-1), vectors_new.reshape(-1)
        attn_new, mlp_new = scatter_rows(
            polynomials(gram), scale, owned, attn_weights, mlp_weights, rates, 3
        )
    else:
        vector_moment = 0.5 * vector_momentum + (vector_summed + noise_scale * vector_noise) / batch
        vectors_new = vectors - vector_rate * vector_moment
        orthogonal = newton(owned)
        attn_rows = jnp.where(attn_pick, orthogonal[:, None, 0:head_width], 0)
        mlp_rows = jnp.where(mlp_pick, orthogonal[:, None, :], 0)
        attn_orth = lax.psum_scatter(attn_rows, "dp", scatter_dimension=0, tiled=True)
        mlp_orth = lax.psum_scatter(mlp_rows, "dp", scatter_dimension=0, tiled=True)
        attn_new = attn_weights - jnp.array(rates[0:4])[None, :, None] * attn_orth
        mlp_new = mlp_weights - jnp.array(rates[4:6])[None, :, None] * mlp_orth
    return (
        result[None],
        grad_in[None],
        attn_moment,
        mlp_moment,
        attn_new,
        mlp_new,
        vector_moment,
        vectors_new,
    )


def solution(mesh):
    fast = mesh.shape["dp"] == 16 and mesh.shape["tensor"] == 2
    in_specs = (
        P("dp", None, None),
        P("dp", None, None),
        P("dp"),
        P("dp", None, "tensor"),
        P("dp", None, "tensor"),
        P("dp", None, "tensor"),
        P("dp", None, "tensor"),
        P("dp", None, "tensor"),
        P("dp", None, "tensor"),
        P(),
        P(),
        P(),
    )
    out_specs = (
        P("dp", None, None),
        P("dp", None, None),
        P("dp", None, "tensor"),
        P("dp", None, "tensor"),
        P("dp", None, "tensor"),
        P("dp", None, "tensor"),
        P(),
        P(),
    )
    return jax.shard_map(
        functools.partial(body, fast), mesh=mesh, in_specs=in_specs, out_specs=out_specs, check_vma=False
    )
```

```python
import functools
import math

import jax
import jax.numpy as jnp
from jax import lax
from jax.experimental import pallas as pl
from jax.experimental.pallas import tpu as pltpu
from jax.sharding import PartitionSpec as P

D = 768
HD = 64
FF = 3072
LEN = 960
NS_ITERS = 5


COEF_A = 3.4445
COEF_B = -4.775
COEF_C = 2.0315


def gelu_tanh(values):
    return jax.nn.gelu(values, approximate=True)


def layer_norm(values, norm_gain, norm_bias):
    centered = values - jnp.mean(values, axis=-1, keepdims=True)
    inverse = lax.rsqrt(jnp.mean(centered * centered, axis=-1, keepdims=True) + 1e-05)
    normed = centered * inverse
    return (normed * norm_gain + norm_bias, normed, inverse)


def norm_back(grad_out, norm_gain, normed, inverse):
    scaled = grad_out * norm_gain
    return inverse * (
        scaled
        - jnp.mean(scaled, axis=-1, keepdims=True)
        - normed * jnp.mean(scaled * normed, axis=-1, keepdims=True)
    )


def contract(left, right, left_dim, right_dim):
    return lax.dot_general(
        left, right, (((left_dim,), (right_dim,)), ((), ())), preferred_element_type=jnp.float32
    )


MESH = pl.DeviceIdType.MESH
MIB = 1 << 20
LINE = 4
OWNERS = (7, 8, 6, 9, 4, 11)


def place():
    dp = lax.axis_index("dp")
    core = lax.axis_index("tensor")
    z = dp // 4
    y = dp % 4 // 2
    x = dp % 2
    return dp, core, z, y, x


def remote(src, dst, send, recv, dp, core):
    return pltpu.make_async_remote_copy(
        src_ref=src, dst_ref=dst, send_sem=send, recv_sem=recv, device_id=(dp, core), device_id_type=MESH
    )


def greet(barrier, dp, core):
    pl.semaphore_signal(barrier, inc=1, device_id=(dp, core), device_id_type=MESH)


def greet_all(dp, core, count):
    barrier = pltpu.get_barrier_semaphore()
    for step in range(1, count):
        greet(barrier, (dp + step) % count, core)
    pl.semaphore_wait(barrier, count - 1)


def greet_plane(dp, core, count, z, y, x):
    barrier = pltpu.get_barrier_semaphore()
    for step in range(1, count):
        greet(barrier, (dp + step) % count, core)
    for step in range(4):
        greet(barrier, z * 4 + (dp + step) % 4, 1 - core)
    return lambda: pl.semaphore_wait(barrier, count + 3)


class Staging:
    def __init__(self, sems):
        self.sems = sems
        self.count = 0
        self.waiting = {}
        self.out = []

    def move(self, src, dst):
        copy = pltpu.make_async_copy(src, dst, self.sems.at[self.count])
        self.count += 1
        copy.start()
        return copy

    def fetch(self, name, src, dst):
        self.waiting[name] = self.move(src, dst)

    def need(self, *names):
        for name in names:
            if name in self.waiting:
                self.waiting.pop(name).wait()

    def keep(self, src, dst):
        self.out.append(self.move(src, dst))

    def finish(self):
        for copy in self.out:
            copy.wait()


def gram_kernel(noise_scale, batch, vector_rate, owned_in, *refs):
    results, vec_in, (gram, low, scale), kept, vec_out = refs[:4], refs[4:8], refs[8:11], refs[11:15], refs[15:17]
    held, vec, vec_new, (own, sems) = refs[17:21], refs[21:25], refs[25:27], refs[27:]
    dp = lax.axis_index("dp")
    stage = Staging(sems)
    stage.fetch("mine", owned_in.at[0], own.at[0])
    for index in range(4):
        stage.fetch(index, results[index], held[index])
    for index in range(4):
        stage.fetch(4 + index, vec_in[index], vec[index])
    stage.fetch("other", owned_in.at[1], own.at[1])
    rows = gram.shape[0]
    attn = (dp == OWNERS[0]) | (dp == OWNERS[1]) | (dp == OWNERS[2]) | (dp == OWNERS[3])
    mlp = (dp == OWNERS[4]) | (dp == OWNERS[5])

    def each(action):
        pl.when(attn)(lambda: action(own.shape[2] // 4))
        pl.when(mlp)(lambda: action(own.shape[2]))

    def first(size):
        gram[...] = contract(own[0, :, 0:size], own[0, :, 0:size], 1, 1)

    def second(size):
        total = gram[...] + contract(own[1, :, 0:size], own[1, :, 0:size], 1, 1)
        square = jnp.zeros((1, 1), jnp.float32)
        tile = 256
        here = lax.broadcasted_iota(jnp.int32, (tile, tile), 0) == lax.broadcasted_iota(jnp.int32, (tile, tile), 1)
        for start in range(0, rows, tile):
            corner = jnp.where(here, total[start : start + tile, start : start + tile], 0.0)
            square = square + jnp.sum(jnp.sum(corner, axis=0, keepdims=True), axis=1, keepdims=True)
        inverse = 1.0 / (jnp.sqrt(square) + 1e-07)
        scale[...] = jnp.broadcast_to(inverse, scale.shape)
        total = total * (inverse * inverse)
        gram[...] = total
        low[...] = total.astype(low.dtype)

    stage.need("mine")
    each(first)
    for index in range(4):
        stage.need(index)
        stage.keep(held[index], kept[index])
    stage.need(4, 5, 6, 7)
    summed, old, moment, noise = (ref[...] for ref in vec)
    moment = 0.5 * moment + (summed + noise_scale * noise) / batch
    vec_new[0][...] = moment
    vec_new[1][...] = old - vector_rate * moment
    for index in range(2):
        stage.keep(vec_new[index], vec_out[index])
    stage.need("other")
    each(second)
    stage.finish()


def gram_of(owned, results, vectors, noise_scale, batch, vector_rate):
    rows = owned.shape[1]
    shape = jax.ShapeDtypeStruct
    vmem = pl.BlockSpec(memory_space=pltpu.VMEM)
    anywhere = pl.BlockSpec(memory_space=pl.ANY)
    return pl.pallas_call(
        functools.partial(gram_kernel, noise_scale, batch, vector_rate),
        out_shape=[
            shape((rows, rows), jnp.float32),
            shape((rows, rows), jnp.bfloat16),
            shape((8, 128), jnp.float32),
        ]
        + [shape(value.shape, value.dtype) for value in results + vectors[:2]],
        in_specs=[anywhere] * 9,
        out_specs=[vmem] * 3 + [anywhere] * 6,
        scratch_shapes=[pltpu.VMEM(value.shape, value.dtype) for value in results + vectors + vectors[:2]]
        + [pltpu.VMEM(owned.shape, owned.dtype), pltpu.SemaphoreType.DMA((16,))],
        compiler_params=pltpu.CompilerParams(vmem_limit_bytes=60 * MIB),
        name="gram",
    )(owned, *results, *vectors)


def scatter_kernel(
    rates, factor, scale, owned_in, attn_in, mlp_in, attn_new, mlp_new,
    own, attn, mlp, orth, attn_low, mlp_low, relayed, send, recv, relay_send, relay_recv, stage_sems,
):
    dp, core, z, y, x = place()
    rows = attn.shape[0]
    count = orth.shape[0] // rows
    stage = Staging(stage_sems)
    stage.fetch("own", owned_in.at[0], own)
    stage.fetch("attn", attn_in, attn)
    stage.fetch("mlp", mlp_in, mlp)
    greet_all(dp, core, count)
    stage.need("own")

    def at(ref, block):
        return ref.at[pl.ds(pl.multiple_of(block * rows, rows), rows)]

    def low_of(slot):
        return attn_low.at[slot] if slot < 4 else mlp_low.at[slot - 4]

    def size_of(slot):
        return attn.shape[2] if slot < 4 else mlp.shape[2]

    def deliver(slot, target):
        owner = OWNERS[slot]
        src = at(orth, target).at[:, 0 : size_of(slot)]
        level = target // 4
        if slot >= 4 and level in stops(owner).get(target % 4, ()):
            stop = owner // 4 * 4 + target % 4
            return remote(src, relayed.at[level], send.at[target], relay_recv.at[level], stop, core)
        return remote(src, low_of(slot), send.at[target], recv.at[slot], target, core)

    def onward(slot, action):
        owner = OWNERS[slot]
        for column, levels in stops(owner).items():

            @pl.when(dp == owner // 4 * 4 + column)
            def _():
                for level in levels:
                    action(level, level * 4 + column)

    def relay_copy(slot, level, target):
        return remote(relayed.at[level], low_of(slot), relay_send.at[level], recv.at[slot], target, core)

    def levels_of(owner):
        return (3, 2, 0) if owner // 4 == 1 else (0, 1, 3)

    def stops(owner):
        far, near, alone = levels_of(owner)
        column = owner % 4
        by_x, by_y = column + 1 - 2 * (column % 2), column + 2 - 4 * (column // 2)
        return {by_x: (far, near), by_y: (far, near, alone)}

    def queue(owner):
        far, near, alone = levels_of(owner)
        home, column = owner // 4, owner % 4
        by_x, by_y, across = column + 1 - 2 * (column % 2), column + 2 - 4 * (column // 2), 3 - column
        links = (
            [far * 4 + by_x, near * 4 + by_x, home * 4 + across, home * 4 + by_x],
            [far * 4 + by_y, near * 4 + by_y, alone * 4 + by_y, home * 4 + by_y],
            [far * 4 + across, far * 4 + column, near * 4 + across, near * 4 + column],
            [alone * 4 + across, alone * 4 + by_x, alone * 4 + column],
        )
        return [link[turn] for turn in range(4) for link in links if turn < len(link)]

    pieces = ((0, 5), (5, 11), (11, 16))
    for slot in range(6):
        owner = OWNERS[slot]
        size = size_of(slot)

        @pl.when(dp == owner)
        def _():
            waiting = queue(owner)
            ready = set()
            for first, last in (pieces[0], pieces[2], pieces[1]):
                part = pl.ds(first * rows, (last - first) * rows)
                value = contract(factor[part, :], own[:, 0:size], 1, 0) * scale[0:1, 0:1]
                orth[part, 0:size] = value.astype(orth.dtype)
                ready.update(range(first, last))
                while waiting and waiting[0] in ready:
                    deliver(slot, waiting.pop(0)).start()
            pltpu.make_async_copy(at(orth, owner).at[:, 0:size], low_of(slot), recv.at[slot]).start()

    for slot in (4, 5):

        def pass_on(level, target):
            block = relayed.at[level]
            remote(block, block, relay_send.at[level], relay_recv.at[level], dp, core).wait_recv()
            relay_copy(slot, level, target).start()

        onward(slot, pass_on)

    stage.need("attn", "mlp")
    for slot in range(6):
        owner = OWNERS[slot]
        low = low_of(slot)

        @pl.when(dp != owner)
        def _():
            remote(low, low, send.at[0], recv.at[slot], owner, core).wait_recv()

        @pl.when(dp == owner)
        def _():
            pltpu.make_async_copy(low, low, recv.at[slot]).wait()

        @pl.loop(0, rows // 16)
        def _(i):
            part = pl.ds(pl.multiple_of(i * 16, 16), 16)
            step = rates[slot] * low[part, :].astype(jnp.float32)
            if slot < 4:
                attn_new[part, slot, :] = attn[part, slot, :] - step
            else:
                mlp_new[part, slot - 4, :] = mlp[part, slot - 4, :] - step

    for slot in range(6):
        owner = OWNERS[slot]

        @pl.when(dp == owner)
        def _():
            for target in range(count):
                if target != owner:
                    deliver(slot, target).wait_send()

    for slot in (4, 5):
        onward(slot, lambda level, target: relay_copy(slot, level, target).wait_send())


def scatter_rows(factor, scale, owned, attn, mlp, rates, collective_id):
    dma = pltpu.SemaphoreType.DMA
    count = lax.axis_size("dp")
    rows = attn.shape[0]
    shape = jax.ShapeDtypeStruct
    vmem = pl.BlockSpec(memory_space=pltpu.VMEM)
    anywhere = pl.BlockSpec(memory_space=pl.ANY)
    return pl.pallas_call(
        functools.partial(scatter_kernel, rates),
        out_shape=[shape(attn.shape, jnp.float32), shape(mlp.shape, jnp.float32)],
        in_specs=[vmem] * 2 + [anywhere] * 3,
        out_specs=[vmem] * 2,
        scratch_shapes=[
            pltpu.VMEM(owned.shape[1:], owned.dtype),
            pltpu.VMEM(attn.shape, attn.dtype),
            pltpu.VMEM(mlp.shape, mlp.dtype),
            pltpu.VMEM(owned.shape[1:], owned.dtype),
            pltpu.VMEM((4, rows, attn.shape[2]), jnp.bfloat16),
            pltpu.VMEM((2, rows, mlp.shape[2]), jnp.bfloat16),
            pltpu.VMEM((LINE, rows, mlp.shape[2]), jnp.bfloat16),
            dma((count,)),
            dma((6,)),
            dma((LINE,)),
            dma((LINE,)),
            dma((3,)),
        ],
        compiler_params=pltpu.CompilerParams(
            collective_id=collective_id, has_side_effects=True, vmem_limit_bytes=32 * MIB
        ),
        name="scatter_rows",
    )(factor, scale, owned, attn, mlp)


def head_mask(shape):
    return lax.broadcasted_iota(jnp.int32, shape, 1) < HD


def spans(length):
    return [(start, min(256, length - start)) for start in range(0, length, 256)]


def attend_forward(q_ref, k_ref, v_ref, o_ref, lse_ref, turned, value_turned, after=lambda head: None):
    length = q_ref.shape[0]
    value_turned[...] = v_ref[...].astype(jnp.float32).T.astype(jnp.bfloat16)
    keys = k_ref[...]
    for head in range(2):
        mine = head_mask(keys.shape) if head == 0 else ~head_mask(keys.shape)
        head_keys = jnp.where(mine, keys, jnp.zeros_like(keys))
        for start, size in spans(length):
            stop = start + size
            scores = contract(head_keys[0:stop], q_ref[start:stop, :], 1, 1)
            key_at = lax.broadcasted_iota(jnp.int32, (stop, size), 0)
            query_at = lax.broadcasted_iota(jnp.int32, (stop, size), 1) + start
            scores = jnp.where(key_at <= query_at, scores, -1e30)
            peak = jnp.max(scores, axis=0, keepdims=True)
            weights = jnp.exp(scores - peak)
            total = jnp.sum(weights, axis=0, keepdims=True)
            mixed = contract(
                value_turned[head * HD : (head + 1) * HD, 0:stop], weights.astype(jnp.bfloat16), 1, 0
            )
            turned[head * HD : (head + 1) * HD, start:stop] = mixed / total
            lse_ref[head : head + 1, start:stop] = peak + jnp.log(total)
        after(head)
    o_ref[...] = turned[...].T.astype(jnp.bfloat16)


def attend_backward(q_ref, k_ref, v_ref, o_ref, do_ref, lse_ref, dq_ref, dk_ref, dv_ref, turned):
    length = q_ref.shape[0]
    keys, values = k_ref[...], v_ref[...]
    key_turned = keys.astype(jnp.float32).T.astype(jnp.bfloat16)
    inner = (o_ref[...].astype(jnp.float32) * do_ref[...].astype(jnp.float32)).T
    mask = head_mask(keys.shape)
    turned[...] = jnp.zeros_like(turned)
    for start, size in spans(length):
        stop = start + size
        both_k, both_v = [], []
        for head in range(2):
            mine = mask[start:stop] if head == 0 else ~mask[start:stop]
            head_keys = jnp.where(mine, keys[start:stop], 0)
            head_values = jnp.where(mine, values[start:stop], 0)
            head_inner = jnp.sum(inner[head * HD : (head + 1) * HD, start:], axis=0, keepdims=True)
            scores = contract(head_keys, q_ref[start:, :], 1, 1)
            grad_prob = contract(head_values, do_ref[start:, :], 1, 1)
            key_at = lax.broadcasted_iota(jnp.int32, scores.shape, 0)
            query_at = lax.broadcasted_iota(jnp.int32, scores.shape, 1)
            scores = jnp.where(key_at <= query_at, scores, -1e30)
            prob = jnp.exp(scores - lse_ref[head : head + 1, start:])
            grad_scores = (prob * (grad_prob - head_inner)).astype(jnp.bfloat16)
            both_v.append(contract(prob.astype(jnp.bfloat16), do_ref[start:, :], 1, 0))
            both_k.append(contract(grad_scores, q_ref[start:, :], 1, 0))
            turned[head * HD : (head + 1) * HD, start:] += contract(
                key_turned[head * HD : (head + 1) * HD, start:stop], grad_scores, 1, 0
            )
        pick = mask[start:stop]
        dk_ref[start:stop, :] = jnp.where(pick, both_k[0], both_k[1]).astype(jnp.bfloat16)
        dv_ref[start:stop, :] = jnp.where(pick, both_v[0], both_v[1]).astype(jnp.bfloat16)
    dq_ref[...] = (turned[...].T * (1.0 / math.sqrt(HD))).astype(jnp.bfloat16)


def pairs_forward(queries, keys, values):
    length, width = queries.shape
    block = pl.BlockSpec((length, 2 * HD), lambda i: (0, i))
    stat = pl.BlockSpec((None, 2, length), lambda i: (i, 0, 0))
    return pl.pallas_call(
        attend_forward,
        grid=(width // (2 * HD),),
        out_shape=[
            jax.ShapeDtypeStruct((length, width), jnp.bfloat16),
            jax.ShapeDtypeStruct((width // (2 * HD), 2, length), jnp.float32),
        ],
        in_specs=[block] * 3,
        out_specs=[block, stat],
        scratch_shapes=[pltpu.VMEM((2 * HD, length), jnp.float32), pltpu.VMEM((2 * HD, length), jnp.bfloat16)],
        compiler_params=pltpu.CompilerParams(vmem_limit_bytes=48 * MIB),
        name="attend_forward",
    )(queries, keys, values)


def pairs_backward(queries, keys, values, attended, grad_attended, stats):
    length, width = queries.shape
    block = pl.BlockSpec((length, 2 * HD), lambda i: (0, i))
    stat = pl.BlockSpec((None, 2, length), lambda i: (i, 0, 0))
    return pl.pallas_call(
        attend_backward,
        grid=(width // (2 * HD),),
        out_shape=[jax.ShapeDtypeStruct((length, width), jnp.bfloat16)] * 3,
        in_specs=[block] * 5 + [stat],
        out_specs=[block] * 3,
        scratch_shapes=[pltpu.VMEM((2 * HD, length), jnp.float32)],
        compiler_params=pltpu.CompilerParams(vmem_limit_bytes=48 * MIB),
        name="attend_backward",
    )(queries, keys, values, attended, grad_attended, stats)


NORM_ROWS = 240


class Gathering:
    def __init__(self, a_ref, b_ref, a_out, b_out, send, recv, local):
        self.own = (a_ref, b_ref)
        self.outs = (a_out, b_out)
        self.send, self.recv, self.local = send, recv, local
        self.rows = a_ref.shape[0]
        self.dp, self.core, self.z, self.y, self.x = place()
        self.x_peer = self.dp + 1 - 2 * self.x
        self.y_peer = self.dp + 2 - 4 * self.y

    def block(self, side, index):
        return self.outs[side].at[pl.ds(pl.multiple_of(index * self.rows, self.rows), self.rows)]

    def copy(self, kind, side, index, own, target):
        src = self.own[side] if own else self.block(side, index)
        return remote(
            src, self.block(side, index), self.send.at[kind, index // 4], self.recv.at[side, index], target, self.core
        )

    def arrived(self, side, index):
        block = self.block(side, index)
        remote(block, block, self.send.at[0, 0], self.recv.at[side, index], self.dp, self.core).wait_recv()

    def at(self, level, y_off, x_off):
        y = self.y + y_off * (1 - 2 * self.y)
        x = self.x + x_off * (1 - 2 * self.x)
        return level * 4 + y * 2 + x

    def line(self, level, own, action):
        index = self.at(level, 0, 0)

        @pl.when((self.z < LINE - 1) & (level <= self.z))
        def _():
            for side in range(2):
                action(self.copy(side, side, index, own, self.dp + 4))

        @pl.when((self.z > 0) & (level >= self.z))
        def _():
            for side in range(2):
                action(self.copy(2 + side, side, index, own, self.dp - 4))

        for side in range(2):
            action(self.copy(4 + side, side, index, own, self.x_peer))
            action(self.copy(6 + side, side, index, own, self.y_peer))

    def relays(self, level):
        return (
            (0, self.at(level, 0, 1), self.copy(8, 0, self.at(level, 0, 1), False, self.y_peer)),
            (1, self.at(level, 1, 0), self.copy(9, 1, self.at(level, 1, 0), False, self.x_peer)),
        )

    def by_distance(self, distance, action):
        if distance == 0:
            action(self.z)
            return

        @pl.when(self.z >= distance)
        def _():
            action(self.z - distance)

        @pl.when(self.z + distance < LINE)
        def _():
            action(self.z + distance)

    def local_copies(self):
        return [
            pltpu.make_async_copy(self.own[side], self.block(side, self.dp), self.local.at[side]) for side in range(2)
        ]

    def begin(self):
        self.line(self.z, True, lambda copy: copy.start())
        for copy in self.local_copies():
            copy.start()

    def onward(self, distance):
        def action(level):
            for side in range(2):
                self.arrived(side, self.at(level, 0, 0))
            self.line(level, False, lambda copy: copy.start())

        self.by_distance(distance, action)

    def relay(self, distance):
        def action(level):
            for side, index, copy in self.relays(level):
                self.arrived(side, index)
                copy.start()

        self.by_distance(distance, action)

    def finish(self):
        for level in range(LINE):
            self.arrived(1, self.at(level, 0, 1))
            self.arrived(0, self.at(level, 1, 0))
            for side in range(2):
                self.arrived(side, self.at(level, 1, 1))
        for copy in self.local_copies():
            copy.wait()

    def drain(self):
        for level in range(LINE):
            self.line(level, False, lambda copy: copy.wait_send())
            for _, _, copy in self.relays(level):
                copy.wait_send()


def norm_tile(values, gain, bias):
    centered = values - jnp.mean(values, axis=-1, keepdims=True)
    inverse = lax.rsqrt(jnp.mean(centered * centered, axis=-1, keepdims=True) + 1e-05)
    return centered * inverse * gain + bias


def tiles(count, rows, action):
    @pl.loop(0, count // rows)
    def _(i):
        action(pl.ds(pl.multiple_of(i * rows, rows), rows))


BACK_ROWS = 80


def fold(value):
    return jnp.sum(value.reshape(-1, 8, value.shape[1]), axis=0)


def norm_back_tile(grad, gain, values):
    centered = values - jnp.mean(values, axis=-1, keepdims=True)
    inverse = lax.rsqrt(jnp.mean(centered * centered, axis=-1, keepdims=True) + 1e-05)
    normed = centered * inverse
    scaled = grad * gain
    back = inverse * (
        scaled
        - jnp.mean(scaled, axis=-1, keepdims=True)
        - normed * jnp.mean(scaled * normed, axis=-1, keepdims=True)
    )
    return back, normed


def shifted(part, start):
    return pl.ds(pl.multiple_of(start + part.start, 16), part.size)


def column_sum(value):
    return jnp.sum(value, axis=0, keepdims=True)


def forward_kernel(
    tokens_in, vec_in, attn_in, mlp_in, cot_in,
    qk_out, vo_out, first_out, q_out, k_out, v_out, o_out, out_out, grad_mid_out, do_out, ga_out, gb_out, go_out,
    x_a, x_b, y_a, y_b, lse, vec, sums,
    tokens, qk_all, vo_all, f0, f1, p0, p1, first, q, k, v, o, middle, second, act, slope,
    turned, mixed, partial, partial_other, pre, attn, mlp, qk_shard, vo_shard, f0_shard, f1_shard, p0_shard, p1_shard,
    cot, out, grad_mid, do, ga, gb, go, du, back_partial, back_other, m_partial, m_other, low, across, acc,
    gather_send, gather_recv, local, swap_send, swap_recv, send, recv, stage_sems,
):
    dp, core, z, y, x = place()
    length = tokens.shape[0]
    width = q.shape[1]
    chunk = length // 4
    x_peer, y_peer = dp + 1 - 2 * x, dp + 2 - 4 * y
    shard_rows = x_a.shape[1]
    stage = Staging(stage_sems)
    stage.fetch("attn", attn_in, attn)
    stage.fetch("tokens", tokens_in, tokens)
    stage.fetch("mlp", mlp_in, mlp)
    stage.fetch("cot", cot_in, cot)
    for row in range(vec.shape[0]):
        for column in range(D // 128):
            at = row * (D // 128) + column
            vec[row : row + 1, column * 128 : (column + 1) * 128] = vec_in[at : at + 1, :]
    stage.need("attn")
    for slot, shard in enumerate((qk_shard, qk_shard, vo_shard, vo_shard)):
        shard[:, slot % 2 * width : (slot % 2 + 1) * width] = attn[:, slot, :].astype(jnp.bfloat16)
    barrier = pltpu.get_barrier_semaphore()
    greet(barrier, dp + 1 - 2 * x, core)
    greet(barrier, dp + 2 - 4 * y, core)
    greet(barrier, dp, 1 - core)

    @pl.when(z > 0)
    def _():
        greet(barrier, dp - 4, core)

    @pl.when(z < LINE - 1)
    def _():
        greet(barrier, dp + 4, core)

    pl.semaphore_wait(barrier, 3 + (z + 2) // 3 + (5 - z) // 3)

    rounds = [
        Gathering(a, b, a_out, b_out, gather_send.at[i], gather_recv.at[i], local.at[i])
        for i, (a, b, a_out, b_out) in enumerate(
            ((qk_shard, vo_shard, qk_all, vo_all), (f0_shard, f1_shard, f0, f1), (p0_shard, p1_shard, p0, p1))
        )
    ]
    rounds[0].begin()
    stage.need("tokens", "mlp")
    for slot, shard in enumerate((f0_shard, f1_shard, p0_shard, p1_shard)):
        shard[...] = mlp[:, slot // 2, slot % 2 * D : (slot % 2 + 1) * D].astype(jnp.bfloat16)

    def norm_one(part):
        tile = norm_tile(tokens[part, :].astype(jnp.float32), vec[0:1, :], vec[1:2, :])
        first[part, :] = tile.astype(jnp.bfloat16)

    tiles(length, NORM_ROWS, norm_one)
    stage.keep(first, first_out)
    rounds[0].onward(1)
    rounds[0].relay(0)
    rounds[0].onward(2)
    rounds[0].relay(1)
    rounds[0].onward(3)
    rounds[0].relay(2)
    rounds[0].relay(3)
    rounds[1].begin()
    rounds[0].finish()
    stage.keep(qk_all, qk_out)
    stage.keep(vo_all, vo_out)

    mine = pl.ds(pl.multiple_of(core * width, width), width)
    scale = 1.0 / math.sqrt(HD)
    q[...] = ((contract(first[...], qk_all[:, 0:width], 1, 0) + vec[4:5, mine]) * scale).astype(jnp.bfloat16)
    k[...] = contract(first[...], qk_all[:, width:], 1, 0).astype(jnp.bfloat16)
    v[...] = (contract(first[...], vo_all[:, 0:width], 1, 0) + vec[5:6, mine]).astype(jnp.bfloat16)

    for value, target in ((q, q_out), (k, k_out), (v, v_out)):
        stage.keep(value, target)

    def step(index):
        if index == 1:
            rounds[1].onward(1)
            rounds[1].relay(0)
        if index == 2:
            rounds[1].onward(2)
            rounds[1].relay(1)
        if index == 3:
            rounds[1].onward(3)
            rounds[1].relay(2)
        if index == 4:
            rounds[1].relay(3)
            rounds[2].begin()
        if index == 6:
            rounds[2].onward(1)
            rounds[2].relay(0)
        if index == 7:
            rounds[2].onward(2)
            rounds[2].relay(1)
        if index == 8:
            rounds[2].onward(3)
            rounds[2].relay(2)
        if index == 9:
            rounds[2].relay(3)

    for pair in range(width // (2 * HD)):
        lanes = pl.ds(pair * 2 * HD, 2 * HD)
        attend_forward(
            q.at[:, lanes], k.at[:, lanes], v.at[:, lanes], o.at[:, lanes], lse.at[pair], turned, mixed,
            lambda head: step(2 * pair + head),
        )

    stage.keep(o, o_out)

    def swap_copy(kind, i):
        part = pl.ds(i * chunk, chunk)
        src, dst = ((back_partial, back_other), (m_partial, m_other), (partial, partial_other))[kind]
        return remote(src.at[part], dst.at[part], swap_send.at[kind, i], swap_recv.at[kind, i], dp, 1 - core)

    for i in range(4):
        part = pl.ds(i * chunk, chunk)
        partial[part, :] = contract(o[part, :], vo_all[:, width:], 1, 1).astype(jnp.bfloat16)
        swap_copy(2, i).start()
    step(6)
    rounds[1].finish()
    for i in range(4):
        swap_copy(2, i).wait_recv()

        def norm_two(part):
            rows = pl.ds(pl.multiple_of(i * chunk + part.start, 16), part.size)
            total = partial[rows, :].astype(jnp.float32) + partial_other[rows, :].astype(jnp.float32)
            tile = tokens[rows, :].astype(jnp.float32) + total + vec[6:7, :]
            middle[rows, :] = tile
            second[rows, :] = norm_tile(tile, vec[2:3, :], vec[3:4, :]).astype(jnp.bfloat16)

        tiles(chunk, NORM_ROWS, norm_two)
        rows = pl.ds(i * chunk, chunk)
        for side, weight in enumerate((f0, f1)):
            pre[:, side * D : (side + 1) * D] = contract(second[rows, :], weight[...], 1, 0)

        def curve(part):
            rows = pl.ds(pl.multiple_of(i * chunk + part.start, 16), part.size)
            for side in range(2):
                columns = pl.ds(side * D, D)
                value = pre[part, columns] + vec[pl.ds(8 + 2 * core + side, 1), :]
                square = value * value
                root = math.sqrt(2.0 / math.pi)
                bent = jnp.tanh(value * (root + root * 0.044715 * square))
                half = 0.5 + 0.5 * bent
                act[rows, columns] = (value * half).astype(jnp.bfloat16)
                inner = root + (3.0 * root * 0.044715) * square
                slope[rows, columns] = (half + (0.5 * value) * (1.0 - bent * bent) * inner).astype(jnp.bfloat16)

        tiles(chunk, 48, curve)
        step(7 + i)

    def early(side, level):
        grad, to_x, to_y = ((ga, x_a, y_a), (gb, x_b, y_b))[side]
        x_block = level * 4 + y * 2 + 1 - x
        y_block = level * 4 + (1 - y) * 2 + x

        def part(block):
            return grad.at[pl.ds(pl.multiple_of(block * shard_rows, shard_rows), shard_rows)]

        return (
            remote(part(x_block), to_x.at[level], send.at[side, level], recv.at[side, level], x_peer, core),
            remote(part(y_block), to_y.at[level], send.at[2 + side, level], recv.at[2 + side, level], y_peer, core),
        )

    def outer(left, right, target, start):
        size = right.shape[1]
        for block in range(D // 256):
            part = pl.ds(block * 256, 256)
            value = contract(left[part, :], right[...], 1, 0)
            target[part, start : start + size] = value.astype(jnp.bfloat16)
            row = 6 if size == D else 7
            sums[row : row + 1, 0:size] += column_sum(value * value)

    stage.need("cot")
    sums[...] = jnp.zeros_like(sums)
    across[...] = cot[...].T
    for side in range(2):
        outer(across, act.at[:, side * D : (side + 1) * D], gb, side * D)
    for level in range(LINE):
        for copy in early(1, level):
            copy.start()
    rounds[2].finish()
    acc[...] = jnp.zeros_like(acc)
    for i in range(4):
        part = pl.ds(i * chunk, chunk)
        for side, weight in enumerate((p0, p1)):
            columns = pl.ds(side * D, D)
            value = contract(cot[part, :], weight[...], 1, 0) * slope[part, columns].astype(jnp.float32)
            value = value.astype(jnp.bfloat16)
            du[part, columns] = value
            sums[4 + side : 5 + side, :] += column_sum(value.astype(jnp.float32))
        back_partial[part, :] = (
            contract(du[part, 0:D], f0[...], 1, 1) + contract(du[part, D:], f1[...], 1, 1)
        ).astype(jnp.bfloat16)
        swap_copy(0, i).start()
    across[...] = second[...].T
    for side in range(2):
        outer(across, du.at[:, side * D : (side + 1) * D], ga, side * D)
    for level in range(LINE):
        for copy in early(0, level):
            copy.start()
    stage.keep(ga, ga_out)
    for i in range(4):
        part = pl.ds(i * chunk, chunk)
        m_partial[part, :] = (
            contract(act[part, 0:D], p0[...], 1, 1) + contract(act[part, D:], p1[...], 1, 1)
        ).astype(jnp.bfloat16)
        swap_copy(1, i).start()
    stage.keep(gb, gb_out)
    for i in range(4):
        swap_copy(0, i).wait_recv()

        def back(part):
            rows = shifted(part, i * chunk)
            grad = back_partial[rows, :].astype(jnp.float32) + back_other[rows, :].astype(jnp.float32)
            outgoing = cot[rows, :].astype(jnp.float32)
            value, normed = norm_back_tile(grad, vec[2:3, :], middle[rows, :])
            value = value + outgoing
            grad_mid[rows, :] = value
            low[rows, :] = value.astype(jnp.bfloat16)
            acc[0] += fold(grad * normed)
            acc[1] += fold(grad)
            acc[2] += fold(value)
            acc[3] += fold(outgoing)

        tiles(chunk, BACK_ROWS, back)
        rows = pl.ds(i * chunk, chunk)
        do[rows, :] = contract(low[rows, :], vo_all[:, width:], 1, 0).astype(jnp.bfloat16)
    for row in range(4):
        sums[row : row + 1, :] = column_sum(acc[row])
    stage.keep(grad_mid, grad_mid_out)
    stage.keep(do, do_out)
    across[...] = low[...].T
    outer(across, o, go, 0)
    stage.keep(go, go_out)
    for i in range(4):
        swap_copy(1, i).wait_recv()

        def finish(part):
            rows = shifted(part, i * chunk)
            total = m_partial[rows, :].astype(jnp.float32) + m_other[rows, :].astype(jnp.float32)
            out[rows, :] = (middle[rows, :] + total + vec[7:8, :]).astype(jnp.bfloat16)

        tiles(chunk, 48, finish)
        part = pl.ds(i * chunk, chunk)
        stage.keep(out.at[part], out_out.at[part])
    for kind in range(3):
        for i in range(4):
            swap_copy(kind, i).wait_send()
    for side in range(2):
        for level in range(LINE):
            for copy in early(side, level):
                copy.wait()
    for gathering in rounds:
        gathering.drain()
    stage.finish()


def forward(tokens, vec, attn, mlp, cot, collective_id):
    dma = pltpu.SemaphoreType.DMA
    low = jnp.bfloat16
    count = lax.axis_size("dp")
    length = tokens.shape[0]
    rows, _, width = attn.shape
    hidden = 2 * D
    shape = jax.ShapeDtypeStruct
    scratch = pltpu.VMEM
    vmem = pl.BlockSpec(memory_space=pltpu.VMEM)
    anywhere = pl.BlockSpec(memory_space=pl.ANY)
    whole, thin, wide = (length, D), (length, width), (length, hidden)
    return pl.pallas_call(
        forward_kernel,
        out_shape=[shape((D, D), low)] * 2
        + [shape(whole, low)]
        + [shape(thin, low)] * 4
        + [
            shape(whole, low),
            shape(whole, jnp.float32),
            shape(thin, low),
            shape((D, hidden), low),
            shape((D, hidden), low),
            shape((D, width), low),
        ]
        + [shape((LINE, rows, hidden), low)] * 4
        + [
            shape((width // (2 * HD), 2, length), jnp.float32),
            shape((vec.shape[0] * 128 // D, D), jnp.float32),
            shape((8, D), jnp.float32),
        ],
        in_specs=[anywhere, vmem] + [anywhere] * 3,
        out_specs=[anywhere] * 17 + [vmem] * 3,
        scratch_shapes=[scratch(whole, low)]
        + [scratch((D, D), low)] * 6
        + [scratch(whole, low)]
        + [scratch(thin, low)] * 4
        + [
            scratch(whole, jnp.float32),
            scratch(whole, low),
            scratch(wide, low),
            scratch(wide, low),
            scratch((2 * HD, length), jnp.float32),
            scratch((2 * HD, length), low),
            scratch(whole, low),
            scratch(whole, low),
            scratch((length // 4, hidden), jnp.float32),
            scratch(attn.shape, jnp.float32),
            scratch(mlp.shape, jnp.float32),
        ]
        + [scratch((rows, D), low)] * 6
        + [
            scratch(whole, low),
            scratch(whole, low),
            scratch(whole, jnp.float32),
            scratch(thin, low),
            scratch((D, hidden), low),
            scratch((D, hidden), low),
            scratch((D, width), low),
            scratch(wide, low),
        ]
        + [scratch(whole, low)] * 5
        + [
            scratch((D, length), low),
            scratch((4, 8, D), jnp.float32),
            dma((3, 10, LINE)),
            dma((3, 2, count)),
            dma((3, 2)),
            dma((3, 4)),
            dma((3, 4)),
            dma((4, LINE)),
            dma((4, LINE)),
            dma((32,)),
        ],
        compiler_params=pltpu.CompilerParams(
            collective_id=collective_id, has_side_effects=True, vmem_limit_bytes=63 * MIB
        ),
        name="forward",
    )(tokens, vec, attn, mlp, cot)


class Reducing:
    def __init__(self, grads, buffers, sources, send, recv, rows, direct):
        self.direct = direct
        self.grads, self.sources = grads, sources
        self.diag, self.from_x, self.from_y, self.up, self.down = buffers[0:2], buffers[2:4], buffers[4:6], buffers[6:8], buffers[8:10]
        self.send, self.recv, self.rows = send, recv, rows
        self.dp, self.core, self.z, self.y, self.x = place()
        self.x_peer = self.dp + 1 - 2 * self.x
        self.y_peer = self.dp + 2 - 4 * self.y
        half = self.z // 2
        self.order = (3 - 3 * half, 2 - half, 1 - self.z + 4 * half, self.z)

    def at(self, ref, block):
        return ref.at[pl.ds(pl.multiple_of(block * self.rows, self.rows), self.rows)]

    def block(self, level, y_off, x_off):
        y = self.y + y_off * (1 - 2 * self.y)
        x = self.x + x_off * (1 - 2 * self.x)
        return level * 4 + y * 2 + x

    def go(self, kind, level, src, dst, target):
        return remote(src, dst, self.send.at[kind, level], self.recv.at[kind, level], target, self.core)

    def diag_copy(self, level, side):
        block = self.at(self.sources[side], self.block(level, 1, 1))
        target = self.block(self.z, 1, 1) if self.direct else (self.y_peer, self.x_peer)[side]
        return self.go(side, level, block, self.diag[side].at[level], target)

    def own_copy(self, level, side):
        block = self.at(self.sources[side], self.block(level, 1 - side, side))
        target = (self.from_y, self.from_x)[side][side].at[level]
        return self.go(2 + side, level, block, target, (self.y_peer, self.x_peer)[side])

    def sum_copy(self, level, side):
        target = (self.from_x, self.from_y)[side][side].at[level]
        return self.go(4 + side, level, self.diag[side].at[level], target, (self.x_peer, self.y_peer)[side])

    def up_copy(self, level, side):
        return self.go(6 + side, level, self.from_x[side].at[level], self.up[side].at[level], self.dp + 4)

    def down_copy(self, level, side):
        return self.go(8 + side, level, self.from_x[side].at[level], self.down[side].at[level], self.dp - 4)

    def first(self, *indices):
        for index in indices:
            level = self.order[index]
            for side in range(2):
                self.diag_copy(level, side).start()
            for side in () if self.direct else range(2):
                self.own_copy(level, side).start()

    def scale(self, factor, factor_x, factor_y, factor_diag):
        self.factor, self.factor_x, self.factor_y, self.factor_diag = factor, factor_x, factor_y, factor_diag

    def weigh(self, side, block, dst, scale_dst, terms):
        grad = self.grads[side]

        @pl.loop(0, self.rows // 16)
        def _(i):
            part = pl.ds(pl.multiple_of(i * 16, 16), 16)
            own = grad[pl.ds(pl.multiple_of(block * self.rows + i * 16, 16), 16), :]
            total = self.factor * own.astype(jnp.float32)
            for scale, ref in ((scale_dst, dst),) + terms:
                value = ref[part, :].astype(jnp.float32)
                total = total + (value if scale is None else scale * value)
            dst[part, :] = total.astype(dst.dtype)

    def sums(self, level):
        for side in range(2):
            self.diag_copy(level, side).wait_recv()
            block = self.block(level, side, 1 - side)
            self.weigh(side, block, self.diag[side].at[level], (self.factor_y, self.factor_x)[side], ())
            self.sum_copy(level, side).start()

    def scales(self, side):
        if self.direct:
            return self.factor_x, self.factor_y
        return (None, self.factor_y) if side == 0 else (self.factor_x, None)

    def arrivals(self, level, side):
        if self.direct:
            self.diag_copy(level, side).wait_recv()
            return
        self.own_copy(level, side).wait_recv()
        self.sum_copy(level, side).wait_recv()

    def chain(self, index):
        level = self.order[index]
        block = self.block(level, 0, 0)
        for side in range(2):
            self.arrivals(level, side)
            scale_x, scale_y = self.scales(side)
            terms = ((scale_y, self.from_y[side].at[level]),)
            if self.direct:
                terms = terms + ((self.factor_diag, self.diag[side].at[level]),)

            def combine(*extra):
                self.weigh(side, block, self.from_x[side].at[level], scale_x, terms + extra)

            @pl.when(level > self.z)
            def _():
                @pl.when(self.z > 0)
                def _():
                    self.up_copy(level, side).wait_recv()
                    combine((None, self.up[side].at[level]))

                @pl.when(self.z == 0)
                def _():
                    combine()

                self.up_copy(level, side).start()

            @pl.when(level < self.z)
            def _():
                @pl.when(self.z < LINE - 1)
                def _():
                    self.down_copy(level, side).wait_recv()
                    combine((None, self.down[side].at[level]))

                @pl.when(self.z == LINE - 1)
                def _():
                    combine()

                self.down_copy(level, side).start()

    def last(self, side):
        self.arrivals(self.z, side)

        @pl.when(self.z > 0)
        def _():
            self.up_copy(self.z, side).wait_recv()

        @pl.when(self.z == 0)
        def _():
            self.up[side][0] = jnp.zeros(self.up[side].shape[1:], self.up[side].dtype)

        @pl.when(self.z < LINE - 1)
        def _():
            self.down_copy(self.z, side).wait_recv()

        @pl.when(self.z == LINE - 1)
        def _():
            self.down[side][LINE - 1] = jnp.zeros(self.down[side].shape[1:], self.down[side].dtype)

    def total(self, side, part, columns):
        here = pl.ds(pl.multiple_of(self.dp * self.rows + part.start, 16), part.size)
        total = self.factor * self.grads[side][here, columns].astype(jnp.float32)
        terms = list(zip(self.scales(side) + (None, None), (self.from_x, self.from_y, self.up, self.down)))
        if self.direct:
            terms.append((self.factor_diag, self.diag))
        for scale, ref in terms:
            value = ref[side][self.z, part, columns].astype(jnp.float32)
            total = total + (value if scale is None else scale * value)
        return total

    def drain(self):
        for level in range(LINE):
            for side in range(2):
                self.diag_copy(level, side).wait_send()
                if not self.direct:
                    self.own_copy(level, side).wait_send()
                    self.sum_copy(level, side).wait_send()

            @pl.when(level > self.z)
            def _():
                for side in range(2):
                    self.up_copy(level, side).wait_send()

            @pl.when(level < self.z)
            def _():
                for side in range(2):
                    self.down_copy(level, side).wait_send()


def owner_at(slot):
    return OWNERS[slot] // 4, OWNERS[slot] % 4 // 2, OWNERS[slot] % 2


def attn_back_kernel(
    noise_scale, batch, clip,
    tokens_in, vec, first_in, q_in, k_in, v_in, o_in, do_in, lse, qk_in, vo_in, grad_mid_in, ga_in, gb_in, go_in,
    x_a_in, x_b_in, y_a_in, y_b_in, sums, included, attn_mom_in, mlp_mom_in, attn_noise_in, mlp_noise_in,
    grad_in_out, attn_out, mlp_out, vec_out, owned,
    tokens, first, q, k, v, o, do, qk_all, wv, grad_mid, ga, gb, attn_mom, mlp_mom, attn_noise, mlp_noise, grad_in,
    dqk, dv, ga_late, gb_late, head_turned, turned, partial, other, acc, square, factors,
    diag_a, diag_b, x_a, x_b, y_a, y_b, up_a, up_b, down_a, down_b,
    late_diag_a, late_diag_b, late_x_a, late_x_b, late_y_a, late_y_b, late_up_a, late_up_b, late_down_a, late_down_b,
    attn_low, mlp_low, relayed, vec_plane, vec_line,
    send, recv, late_send, late_recv, vec_sems, line_sems, gather_send, gather_recv, relay_sems, swap_send, swap_recv, small, pass_send, pass_recv,
    stage_sems,
):
    dp, core, z, y, x = place()
    rows, _, width = attn_mom.shape
    wide = mlp_mom.shape[2]
    length = tokens.shape[0]
    chunk = length // 4
    x_peer, y_peer = dp + 1 - 2 * x, dp + 2 - 4 * y
    count = ga.shape[0] // rows
    stage = Staging(stage_sems)
    for name, src, dst in (
        ("q", q_in, q), ("k", k_in, k), ("v", v_in, v), ("o", o_in, o), ("do", do_in, do), ("qk_all", qk_in, qk_all),
        ("wv", vo_in.at[:, pl.ds(0, width)], wv), ("first", first_in, first), ("go", go_in, gb_late.at[:, pl.ds(width, width)]),
        ("tokens", tokens_in, tokens), ("grad_mid", grad_mid_in, grad_mid), ("ga", ga_in, ga), ("gb", gb_in, gb),
        ("x_a", x_a_in, x_a), ("x_b", x_b_in, x_b), ("y_a", y_a_in, y_a), ("y_b", y_b_in, y_b),
        ("mlp_mom", mlp_mom_in, mlp_mom), ("mlp_noise", mlp_noise_in, mlp_noise), ("attn_mom", attn_mom_in, attn_mom),
        ("attn_noise", attn_noise_in, attn_noise),
    ):
        stage.fetch(name, src, dst)
    greeted = greet_plane(dp, core, count, z, y, x)

    main = Reducing(
        (ga, gb), (diag_a, diag_b, x_a, x_b, y_a, y_b, up_a, up_b, down_a, down_b), (ga_in, gb_in), send, recv, rows, True
    )
    late = Reducing(
        (ga_late, gb_late),
        (late_diag_a, late_diag_b, late_x_a, late_x_b, late_y_a, late_y_b, late_up_a, late_up_b, late_down_a, late_down_b),
        (ga_late, gb_late),
        late_send,
        late_recv,
        rows,
        False,
    )

    def small_copy(index):
        src, dst, target = (
            (square.at[0], square.at[1], (dp, 1 - core)),
            (factors.at[0], factors.at[1], (x_peer, core)),
            (factors.at[0], factors.at[2], (y_peer, core)),
            (factors.at[0], factors.at[3], (main.block(z, 1, 1), core)),
        )[index]
        return remote(src, dst, small.at[0, index], small.at[1, index], *target)

    mine_in_plane = (y * 2 + x) * 2 + core

    def plane_copies():
        copies = []
        for y_off, x_off, core_off in [(i // 4, i // 2 % 2, i % 2) for i in range(1, 8)]:
            target = main.block(z, y_off, x_off)
            target_core = core + core_off * (1 - 2 * core)
            place_there = target % 4 * 2 + target_core
            copies.append(
                remote(
                    vec_plane.at[mine_in_plane], vec_plane.at[mine_in_plane], vec_sems.at[0, place_there],
                    vec_sems.at[1, mine_in_plane], target, target_core,
                )
            )
        return copies

    def plane_arrivals():
        for i in range(1, 8):
            index = (mine_in_plane + i) % 8
            block = vec_plane.at[index]
            remote(block, block, vec_sems.at[0, index], vec_sems.at[1, index], dp, core).wait_recv()

    def line_copies():
        return [
            remote(vec_line.at[z], vec_line.at[z], line_sems.at[0, (z + i) % LINE], line_sems.at[1, z], (dp + 4 * i) % count, core)
            for i in range(1, LINE)
        ]

    def vec_turn():
        plane_arrivals()
        total = vec_plane[0]
        for index in range(1, 8):
            total = total + vec_plane[index]
        vec_line[z] = total
        for copy in line_copies():
            copy.start()

    def vec_finish():
        for i in range(1, LINE):
            index = (z + i) % LINE
            block = vec_line.at[index]
            remote(block, block, line_sems.at[0, index], line_sems.at[1, index], dp, core).wait_recv()
        total = vec_line[0]
        for index in range(1, LINE):
            total = total + vec_line[index]
        per_row = D // 128
        for row in range(vec_out.shape[0]):
            at = row % per_row * 128
            vec_out[row : row + 1, :] = total[row // per_row : row // per_row + 1, at : at + 128]
        for copy in plane_copies() + line_copies():
            copy.wait_send()

    def swap_copy(i):
        part = pl.ds(i * chunk, chunk)
        return remote(partial.at[part], other.at[part], swap_send.at[i], swap_recv.at[i], dp, 1 - core)

    acc[...] = jnp.zeros_like(acc)
    stage.need("q", "k", "v", "o", "do")
    for pair in range(width // (2 * HD)):
        lanes = pl.ds(pair * 2 * HD, 2 * HD)
        attend_backward(
            q.at[:, lanes], k.at[:, lanes], v.at[:, lanes], o.at[:, lanes], do.at[:, lanes], lse.at[pair],
            dqk.at[:, lanes], dqk.at[:, pl.ds(width + pair * 2 * HD, 2 * HD)], dv.at[:, lanes], head_turned,
        )
        if pair == 0:
            greeted()
            main.first(0, 1, 2, 3)
    stage.need("qk_all", "wv")
    for i in range(4):
        part = pl.ds(i * chunk, chunk)
        partial[part, :] = (contract(dqk[part, :], qk_all[...], 1, 1) + contract(dv[part, :], wv[...], 1, 1)).astype(
            jnp.bfloat16
        )
        swap_copy(i).start()
    stage.need("first", "go")
    turned[...] = first[...].T
    squares = jnp.zeros((1, 1), jnp.float32)
    for right, target in ((dqk, ga_late), (dv, gb_late)):
        for block in range(D // 256):
            part = pl.ds(block * 256, 256)
            value = contract(turned[part, :], right[...], 1, 0)
            target[part, 0 : right.shape[1]] = value.astype(jnp.bfloat16)
            squares = squares + jnp.sum(column_sum(value * value), axis=1, keepdims=True)
    late.first(0, 1)
    bias_q = column_sum(dqk[:, 0:width].astype(jnp.float32))
    bias_v = column_sum(dv[...].astype(jnp.float32))
    for value in (sums[6:7, :], sums[7:8, :]):
        squares = squares + jnp.sum(value, axis=1, keepdims=True)
    for value in (bias_q, bias_v, sums[4:5, :], sums[5:6, :]):
        squares = squares + jnp.sum(value * value, axis=1, keepdims=True)
    square[0] = jnp.broadcast_to(squares, square.shape[1:])
    small_copy(0).start()

    stage.need("tokens", "grad_mid")
    for i in range(4):
        swap_copy(i).wait_recv()

        def back(part):
            here = shifted(part, i * chunk)
            grad = partial[here, :].astype(jnp.float32) + other[here, :].astype(jnp.float32)
            value, normed = norm_back_tile(grad, vec[0:1, :], tokens[here, :].astype(jnp.float32))
            grad_in[here, :] = (grad_mid[here, :] + value).astype(jnp.bfloat16)
            acc[0] += fold(grad * normed)
            acc[1] += fold(grad)

        tiles(chunk, BACK_ROWS, back)
    stage.keep(grad_in, grad_in_out)
    gain_one, bias_one = column_sum(acc[0]), column_sum(acc[1])
    shared = jnp.zeros((1, 1), jnp.float32)
    for value in (gain_one, bias_one, sums[0:1, :], sums[1:2, :], sums[2:3, :], sums[3:4, :]):
        shared = shared + jnp.sum(value * value, axis=1, keepdims=True)
    small_copy(0).wait_recv()
    norm = jnp.sqrt(square[0, 0:1, 0:1] + square[1, 0:1, 0:1] + shared)
    factor = included[0].astype(jnp.float32) * jnp.minimum(1.0, clip / (norm + 1e-06))
    factors[0] = jnp.broadcast_to(factor, factors.shape[1:])
    for index in (1, 2, 3):
        small_copy(index).start()
    leading = factor * (1 - core).astype(jnp.float32)
    vec_plane[mine_in_plane] = jnp.zeros(vec_plane.shape[1:], jnp.float32)
    mine = pl.ds(pl.multiple_of(core * width, width), width)
    for row, value in ((0, gain_one), (1, bias_one), (2, sums[0:1, :]), (3, sums[1:2, :]), (6, sums[2:3, :]), (7, sums[3:4, :])):
        vec_plane[mine_in_plane, row : row + 1, :] = leading * value
    vec_plane[mine_in_plane, 4:5, mine] = factor * bias_q
    vec_plane[mine_in_plane, 5:6, mine] = factor * bias_v
    vec_plane[mine_in_plane, pl.ds(8 + 2 * core, 1), :] = factor * sums[4:5, :]
    vec_plane[mine_in_plane, pl.ds(9 + 2 * core, 1), :] = factor * sums[5:6, :]
    stage.need("ga", "gb", "x_a", "x_b", "y_a", "y_b", "mlp_mom", "mlp_noise", "attn_mom", "attn_noise")
    for index in (1, 2, 3):
        small_copy(index).wait_recv()
    for part in (main, late):
        part.scale(factor, factors[1, 0:1, 0:1], factors[2, 0:1, 0:1], factors[3, 0:1, 0:1])

    def moment(slot, reducing, side, column):
        size = width if slot < 4 else wide
        low = attn_low.at[slot] if slot < 4 else mlp_low.at[slot - 4]
        old, noise, new = (attn_mom, attn_noise, attn_out) if slot < 4 else (mlp_mom, mlp_noise, mlp_out)
        index = slot if slot < 4 else slot - 4

        @pl.loop(0, rows // 16)
        def _(i):
            part = pl.ds(pl.multiple_of(i * 16, 16), 16)
            total = reducing.total(side, part, pl.ds(column, size))
            value = 0.5 * old[part, index, :] + (total + noise_scale * noise[part, index, :]) / batch
            new[part, index, :] = value
            low[part, :] = value.astype(low.dtype)

        for action in sends(slot):
            action(lambda copy: copy.start())

    def landing(slot, source):
        size = width if slot < 4 else wide
        return main.at(owned.at[0], source).at[:, 0:size]

    def sends(slot):
        owner = OWNERS[slot]
        owner_z, owner_y, owner_x = owner_at(slot)
        low = attn_low.at[slot] if slot < 4 else mlp_low.at[slot - 4]
        alone = 0 if owner_z == 1 else LINE - 1
        far = (y != owner_y) & (x != owner_x)
        near = (y != owner_y) | (x != owner_x)
        across = (z != owner_z) & (far | ((z == alone) & near))

        def keep(action):
            @pl.when(dp == owner)
            def _():
                action(pltpu.make_async_copy(low, landing(slot, dp), gather_send.at[slot]))

        def direct(action):
            away = (dp != owner) & jnp.logical_not(across) if slot >= 4 else dp != owner

            @pl.when(away)
            def _():
                action(remote(low, landing(slot, dp), gather_send.at[slot], gather_recv.at[dp], owner, core))

        def turn(action):
            if slot >= 4:

                @pl.when(across)
                def _():
                    stop = z * 4 + owner_y * 2 + owner_x
                    action(remote(low, relayed.at[dp % 4], gather_send.at[slot], relay_sems.at[0, dp % 4], stop, core))

        return keep, direct, turn

    def relays(slot, action):
        owner_z, owner_y, owner_x = owner_at(slot)
        alone = 0 if owner_z == 1 else LINE - 1
        column = owner_y * 2 + owner_x
        here = (y == owner_y) & (x == owner_x) & (z != owner_z)

        @pl.when(here)
        def _():
            action(3 - column)

        @pl.when(here & (z == alone))
        def _():
            action(column + 1 - 2 * owner_x)
            action(column + 2 - 4 * owner_y)

    def relay_copy(slot, column):
        source = z * 4 + column
        return remote(
            relayed.at[column], landing(slot, source), relay_sems.at[1, column], gather_recv.at[source], OWNERS[slot], core
        )

    def forward(slot, column):
        block = relayed.at[column]
        remote(block, block, relay_sems.at[1, column], relay_sems.at[0, column], dp, core).wait_recv()
        relay_copy(slot, column).start()

    def pass_on(slot, source):
        size = width if slot < 4 else wide
        block = landing(slot, source)
        other_half = main.at(owned.at[1], source).at[:, 0:size]
        return remote(block, other_half, pass_send.at[source], pass_recv.at[source], dp, 1 - core)

    def turned_off(slot, source):
        owner_z, owner_y, owner_x = owner_at(slot)
        off_x, off_y = source % 2 != owner_x, source % 4 // 2 != owner_y
        alone = 0 if owner_z == 1 else LINE - 1
        return slot >= 4 and source // 4 != owner_z and ((off_x and off_y) or (source // 4 == alone and (off_x or off_y)))

    def collect(slot, late_ones):
        @pl.when(dp == OWNERS[slot])
        def _():
            for step in range(1, count):
                source = (OWNERS[slot] + step) % count
                if turned_off(slot, source) == late_ones:
                    block = landing(slot, source)
                    remote(block, block, gather_send.at[slot], gather_recv.at[source], source, core).wait_recv()
                    pass_on(slot, source).start()

    main.chain(0)
    late.first(2)
    late.sums(late.order[0])
    main.chain(1)
    late.first(3)
    late.sums(late.order[1])
    main.chain(2)
    late.sums(late.order[2])
    late.sums(late.order[3])
    main.last(0)
    moment(4, main, 0, 0)
    main.last(1)
    moment(5, main, 1, 0)
    late.chain(0)
    for copy in plane_copies():
        copy.start()
    late.chain(1)
    for slot in (4, 5):
        relays(slot, functools.partial(forward, slot))
    late.chain(2)
    vec_turn()
    for slot in (4, 5):
        collect(slot, False)
    late.last(0)
    moment(0, late, 0, 0)
    moment(1, late, 0, width)
    late.last(1)
    moment(2, late, 1, 0)
    moment(3, late, 1, width)

    for slot in range(6):
        low = attn_low.at[slot] if slot < 4 else mlp_low.at[slot - 4]

        @pl.when(dp == OWNERS[slot])
        def _():
            pltpu.make_async_copy(low, landing(slot, dp), gather_send.at[slot]).wait()
            pass_on(slot, dp).start()

    for slot in (4, 5):
        collect(slot, True)
    for slot in range(4):
        collect(slot, False)
    for slot in range(6):
        owner = OWNERS[slot]
        low = attn_low.at[slot] if slot < 4 else mlp_low.at[slot - 4]

        @pl.when(dp != owner)
        def _():
            remote(low, low, gather_send.at[slot], gather_recv.at[dp], owner, core).wait_send()

        @pl.when(dp == owner)
        def _():
            @pl.loop(0, count)
            def _(source):
                pass_on(slot, source).wait()

    vec_finish()
    for slot in (4, 5):
        relays(slot, lambda column: relay_copy(slot, column).wait_send())
    for index in range(4):
        small_copy(index).wait_send()
    for i in range(4):
        swap_copy(i).wait_send()
    main.drain()
    late.drain()
    stage.finish()


def attn_back(
    tokens, vec, first, q, k, v, o, do, lse, qk_all, vo_all, grad_mid, ga, gb, go, x_a, x_b, y_a, y_b, sums, included,
    attn_mom, mlp_mom, attn_noise, mlp_noise, noise_scale, batch, clip, collective_id,
):
    dma = pltpu.SemaphoreType.DMA
    low = jnp.bfloat16
    count = lax.axis_size("dp")
    length = tokens.shape[0]
    rows, _, width = attn_mom.shape
    wide = mlp_mom.shape[2]
    shape = jax.ShapeDtypeStruct
    vmem = pl.BlockSpec(memory_space=pltpu.VMEM)
    anywhere = pl.BlockSpec(memory_space=pl.ANY)
    scratch = pltpu.VMEM
    return pl.pallas_call(
        functools.partial(attn_back_kernel, noise_scale, batch, clip),
        out_shape=[
            shape((length, D), low),
            shape(attn_mom.shape, jnp.float32),
            shape(mlp_mom.shape, jnp.float32),
            shape((vec.shape[0] * D // 128, 128), jnp.float32),
            shape((2, D, wide), low),
        ],
        in_specs=[anywhere, vmem]
        + [anywhere] * 6
        + [vmem]
        + [anywhere] * 10
        + [vmem, pl.BlockSpec(memory_space=pltpu.SMEM)]
        + [anywhere] * 4,
        out_specs=[anywhere] + [vmem] * 3 + [anywhere],
        scratch_shapes=[
            scratch((length, D), low),
            scratch((length, D), low),
        ]
        + [scratch((length, width), low)] * 5
        + [
            scratch((D, 2 * width), low),
            scratch((D, width), low),
            scratch((length, D), jnp.float32),
            scratch((D, wide), low),
            scratch((D, wide), low),
            scratch(attn_mom.shape, jnp.float32),
            scratch(mlp_mom.shape, jnp.float32),
            scratch(attn_mom.shape, jnp.float32),
            scratch(mlp_mom.shape, jnp.float32),
            scratch((length, D), low),
            scratch((length, 2 * width), low),
            scratch((length, width), low),
            scratch((D, 2 * width), low),
            scratch((D, 2 * width), low),
            scratch((2 * HD, length), jnp.float32),
            scratch((D, length), low),
            scratch((length, D), low),
            scratch((length, D), low),
            scratch((2, 8, D), jnp.float32),
            scratch((2, 8, 128), jnp.float32),
            scratch((4, 8, 128), jnp.float32),
        ]
        + [scratch((LINE, rows, wide), low)] * 10
        + [scratch((LINE, rows, 2 * width), low)] * 10
        + [
            scratch((4, rows, width), low),
            scratch((2, rows, wide), low),
            scratch((4, rows, wide), low),
            scratch((8,) + vec.shape, jnp.float32),
            scratch((LINE,) + vec.shape, jnp.float32),
            dma((10, LINE)),
            dma((10, LINE)),
            dma((10, LINE)),
            dma((10, LINE)),
            dma((2, 8)),
            dma((2, LINE)),
            dma((6,)),
            dma((count,)),
            dma((2, 4)),
            dma((4,)),
            dma((4,)),
            dma((2, 4)),
            dma((count,)),
            dma((count,)),
            dma((24,)),
        ],
        compiler_params=pltpu.CompilerParams(
            collective_id=collective_id, has_side_effects=True, vmem_limit_bytes=62 * MIB
        ),
        name="attn_back",
    )(
        tokens, vec, first, q, k, v, o, do, lse, qk_all, vo_all, grad_mid, ga, gb, go, x_a, x_b, y_a, y_b, sums, included,
        attn_mom, mlp_mom, attn_noise, mlp_noise,
    )


def placed(piece, start, total_size):
    return lax.dynamic_update_slice_in_dim(jnp.zeros((total_size,), jnp.float32), piece, start, 0)


def other_core(value):
    return lax.ppermute(value, "tensor", [(0, 1), (1, 0)])


SHIFTS = (0.0, 0.0, 0.0, 0.8, 0.72)


def polynomials(current, low):
    rows = current.shape[0]
    diagonal = lax.broadcasted_iota(jnp.int32, (rows, rows), 0) == lax.broadcasted_iota(jnp.int32, (rows, rows), 1)

    def less(matrix, shift):
        return matrix - jnp.where(diagonal, shift, 0.0) if shift else matrix

    def product(left, right):
        return contract(left.astype(jnp.bfloat16), right.astype(jnp.bfloat16), 1, 0)

    factor = None
    for iteration in range(NS_ITERS):
        shift = SHIFTS[iteration]
        moved = less(current, shift)
        operand = moved if iteration else low
        square = product(operand, operand) + 2.0 * shift * moved
        lead = COEF_B * shift + COEF_C * shift * shift
        rest = lax.optimization_barrier(COEF_B * moved + COEF_C * square)
        whole = COEF_A + lead
        if factor is None:
            factor = jnp.where(diagonal, whole, 0.0) + rest
        else:
            factor = lax.optimization_barrier(whole * factor + product(rest, factor))
        if iteration < NS_ITERS - 1:
            once = lax.optimization_barrier(whole * current + shift * rest + product(rest, operand))
            second = whole * shift
            current = lax.optimization_barrier(whole * once + second * rest + product(rest, less(once, second)))
    return factor.astype(jnp.bfloat16)


def newton(owned):
    gram = contract(owned, owned, 1, 1)
    gram = gram + other_core(gram)
    scale = 1.0 / (jnp.sqrt(jnp.trace(gram)) + 1e-07)
    return (contract(polynomials(gram * (scale * scale), gram * (scale * scale)), owned, 1, 0) * scale).astype(jnp.bfloat16)


def body(
    fast,
    tokens,
    cotangent,
    inclusion,
    attn_weights,
    mlp_weights,
    attn_momentum,
    mlp_momentum,
    attn_noise,
    mlp_noise,
    vectors,
    vector_momentum,
    vector_noise,
):
    dp_count = lax.axis_size("dp")
    dp_index = lax.axis_index("dp")
    halves = lax.axis_size("tensor")
    tensor_index = lax.axis_index("tensor")
    head_width = D // halves
    hidden_width = FF // halves
    query_scale = 1.0 / math.sqrt(HD)
    clip = 1.5 * D * math.sqrt(LEN)
    sigma = 0.05 * math.sqrt(dp_count) / D
    batch = 0.75 * dp_count
    noise_scale = sigma * clip
    if fast:
        (
            query_key, value_out, first_low, queries, key_rows, value_rows, attended_low, result, grad_mid, grad_attended,
            grad_fc, grad_pr, grad_wo, x_fc, x_pr, y_fc, y_pr, stats, vec, sums,
        ) = forward(tokens[0], vectors.reshape(-1, 128), attn_weights, mlp_weights, cotangent[0], 0)
        grad_in, attn_moment, mlp_moment, vector_summed, owned = attn_back(
            tokens[0], vec, first_low, queries, key_rows, value_rows, attended_low, grad_attended, stats,
            query_key, value_out, grad_mid, grad_fc, grad_pr, grad_wo,
            x_fc, x_pr, y_fc, y_pr, sums,
            inclusion, attn_momentum, mlp_momentum, attn_noise, mlp_noise, noise_scale, batch, clip, 2,
        )
    else:
        attn_shard = attn_weights.astype(jnp.bfloat16)
        mlp_shard = mlp_weights.astype(jnp.bfloat16)
        rows = attn_shard.shape[0]
        shards = (
            attn_shard[:, 0:2].reshape(rows, 2 * head_width),
            attn_shard[:, 2:4].reshape(rows, 2 * head_width),
            mlp_shard[:, 0, 0:D],
            mlp_shard[:, 0, D:],
            mlp_shard[:, 1, 0:D],
            mlp_shard[:, 1, D:],
        )
        gain_one = vectors[0:D]
        bias_one = vectors[D : 2 * D]
        gain_two = vectors[2 * D : 3 * D]
        bias_two = vectors[3 * D : 4 * D]
        query_bias = lax.dynamic_slice_in_dim(vectors, 4 * D + tensor_index * head_width, head_width)
        value_bias = lax.dynamic_slice_in_dim(vectors, 5 * D + tensor_index * head_width, head_width)
        attn_bias = vectors[6 * D : 7 * D]
        mlp_bias = vectors[7 * D : 8 * D]
        hidden_bias = lax.dynamic_slice_in_dim(
            vectors, 8 * D + tensor_index * hidden_width, hidden_width
        )
        inputs = tokens[0].astype(jnp.float32)
        length = inputs.shape[0]
        first, normed_one, inverse_one = layer_norm(inputs, gain_one, bias_one)

        def both_cores(partial):
            low = partial.astype(jnp.bfloat16)
            return low.astype(jnp.float32) + other_core(low).astype(jnp.float32)

        query_key, value_out, fc_one, fc_two, pr_one, pr_two = (
            lax.all_gather(shard, "dp", axis=0, tiled=True) for shard in shards
        )
        value_weight, out_weight = value_out[:, 0:head_width], value_out[:, head_width:]
        first_low = first.astype(jnp.bfloat16)
        qk = contract(first_low, query_key, 1, 0)
        queries = ((qk[:, 0:head_width] + query_bias) * query_scale).astype(jnp.bfloat16)
        key_rows = qk[:, head_width:].astype(jnp.bfloat16)
        value_rows = (contract(first_low, value_weight, 1, 0) + value_bias).astype(jnp.bfloat16)
        attended_low, stats = pairs_forward(queries, key_rows, value_rows)
        middle = inputs + both_cores(contract(attended_low, out_weight, 1, 1)) + attn_bias
        second_low = layer_norm(middle, gain_two, bias_two)[0].astype(jnp.bfloat16)
        pre_act = contract(second_low, jnp.concatenate([fc_one, fc_two], axis=1), 1, 0) + hidden_bias
        activation, gelu_back = jax.vjp(gelu_tanh, pre_act)
        activation_low = activation.astype(jnp.bfloat16)
        slope = gelu_back(jnp.ones_like(pre_act))[0]
        _, normed_two, inverse_two = layer_norm(middle, gain_two, bias_two)
        fc_weight = jnp.concatenate([fc_one, fc_two], axis=1)
        pr_weight = jnp.concatenate([pr_one, pr_two], axis=1)
        result = middle + both_cores(contract(activation_low, pr_weight, 1, 1)) + mlp_bias
        cot_low = cotangent[0]
        grad_out = cot_low.astype(jnp.float32)
        d_pr = contract(cot_low, activation_low, 0, 0)
        grad_pre = (contract(cot_low, pr_weight, 1, 0) * slope.astype(jnp.float32)).astype(jnp.bfloat16)
        d_fc = contract(second_low, grad_pre, 0, 0)
        d_hidden_bias = jnp.sum(grad_pre.astype(jnp.float32), axis=0)
        grad_two = both_cores(contract(grad_pre, fc_weight, 1, 1))
        grad_mid = grad_out + norm_back(grad_two, gain_two, normed_two, inverse_two)
        d_gain_two = jnp.sum(grad_two * normed_two, axis=0)
        d_bias_two = jnp.sum(grad_two, axis=0)
        d_attn_bias = jnp.sum(grad_mid, axis=0)
        d_mlp_bias = jnp.sum(grad_out, axis=0)
        mid_low = grad_mid.astype(jnp.bfloat16)
        d_out = contract(mid_low, attended_low, 0, 0)
        grad_attended = contract(mid_low, out_weight, 1, 0).astype(jnp.bfloat16)
        grad_q, grad_k, grad_v = pairs_backward(
            queries, key_rows, value_rows, attended_low, grad_attended, stats
        )
        grad_qk = jnp.concatenate([grad_q, grad_k], axis=1)
        d_query_key = contract(first_low, grad_qk, 0, 0)
        d_value = contract(first_low, grad_v, 0, 0)
        d_query_bias = jnp.sum(grad_q.astype(jnp.float32), axis=0)
        d_value_bias = jnp.sum(grad_v.astype(jnp.float32), axis=0)
        grad_one = both_cores(contract(grad_qk, query_key, 1, 1) + contract(grad_v, value_weight, 1, 1))
        grad_in = grad_mid + norm_back(grad_one, gain_one, normed_one, inverse_one)
        d_gain_one = jnp.sum(grad_one * normed_one, axis=0)
        d_bias_one = jnp.sum(grad_one, axis=0)
        split_square = sum(
            jnp.sum(value * value)
            for value in (d_query_key, d_value, d_out, d_fc, d_pr, d_query_bias, d_value_bias, d_hidden_bias)
        )
        split_tile = jnp.broadcast_to(split_square, (8, 128))
        total_square = (split_tile + other_core(split_tile))[0, 0] + sum(
            jnp.sum(value * value)
            for value in (d_gain_one, d_bias_one, d_gain_two, d_bias_two, d_attn_bias, d_mlp_bias)
        )
        factor = inclusion[0].astype(jnp.float32) * jnp.minimum(
            1.0, clip / (jnp.sqrt(total_square) + 1e-06)
        )
        leading = (tensor_index == 0).astype(jnp.float32)
        vector_grad = (
            jnp.concatenate(
                [
                    leading * d_gain_one,
                    leading * d_bias_one,
                    leading * d_gain_two,
                    leading * d_bias_two,
                    placed(d_query_bias, tensor_index * head_width, D),
                    placed(d_value_bias, tensor_index * head_width, D),
                    leading * d_attn_bias,
                    leading * d_mlp_bias,
                    placed(d_hidden_bias, tensor_index * hidden_width, FF),
                ]
            )
            * factor
        )
        result, grad_in = result.astype(jnp.bfloat16), grad_in.astype(jnp.bfloat16)
        attn_grad = jnp.concatenate([d_query_key, d_value, d_out], axis=1) * factor
        mlp_grad = jnp.stack([d_fc, d_pr], axis=1) * factor
        attn_summed = lax.psum_scatter(attn_grad, "dp", scatter_dimension=0, tiled=True)
        mlp_summed = lax.psum_scatter(mlp_grad, "dp", scatter_dimension=0, tiled=True)
        attn_summed = attn_summed.reshape(rows, 4, head_width)
        vector_summed = lax.psum(vector_grad, ("dp", "tensor"))
        attn_moment = 0.5 * attn_momentum + (attn_summed + noise_scale * attn_noise) / batch
        mlp_moment = 0.5 * mlp_momentum + (mlp_summed + noise_scale * mlp_noise) / batch
        owners = jnp.array([slot * dp_count // 6 for slot in range(6)])
        full_attn = lax.all_gather(attn_moment.astype(jnp.bfloat16), "dp", axis=0, tiled=True)
        full_mlp = lax.all_gather(mlp_moment.astype(jnp.bfloat16), "dp", axis=0, tiled=True)
        attn_pick = (owners[0:4] == dp_index)[None, :, None]
        mlp_pick = (owners[4:6] == dp_index)[None, :, None]
        mine_attn = jnp.sum(jnp.where(attn_pick, full_attn, 0), axis=1)
        mine_mlp = jnp.sum(jnp.where(mlp_pick, full_mlp, 0), axis=1)
        owned = jnp.pad(mine_attn, ((0, 0), (0, hidden_width - head_width))) + mine_mlp
    vector_rate = 0.2 * math.sqrt(dp_count / LEN)
    rates = (0.5, 0.5, 0.5, 0.5 * max(1.0, math.sqrt(LEN) / 8.0), 0.5 * math.sqrt(FF / D), 0.5)
    if fast:
        tiled = tuple(value.reshape(-1, 128) for value in (vector_summed, vectors, vector_momentum, vector_noise))
        gram, gram_low, scale, result, grad_in, attn_moment, mlp_moment, vector_moment, vectors_new = gram_of(
            owned, (result, grad_in, attn_moment, mlp_moment), tiled, noise_scale, batch, vector_rate
        )
        vector_moment, vectors_new = vector_moment.reshape(-1), vectors_new.reshape(-1)
        attn_new, mlp_new = scatter_rows(
            polynomials(gram, gram_low), scale, owned, attn_weights, mlp_weights, rates, 3
        )
    else:
        vector_moment = 0.5 * vector_momentum + (vector_summed + noise_scale * vector_noise) / batch
        vectors_new = vectors - vector_rate * vector_moment
        orthogonal = newton(owned)
        attn_rows = jnp.where(attn_pick, orthogonal[:, None, 0:head_width], 0)
        mlp_rows = jnp.where(mlp_pick, orthogonal[:, None, :], 0)
        attn_orth = lax.psum_scatter(attn_rows, "dp", scatter_dimension=0, tiled=True)
        mlp_orth = lax.psum_scatter(mlp_rows, "dp", scatter_dimension=0, tiled=True)
        attn_new = attn_weights - jnp.array(rates[0:4])[None, :, None] * attn_orth
        mlp_new = mlp_weights - jnp.array(rates[4:6])[None, :, None] * mlp_orth
    return (
        result[None],
        grad_in[None],
        attn_moment,
        mlp_moment,
        attn_new,
        mlp_new,
        vector_moment,
        vectors_new,
    )


def solution(mesh):
    fast = mesh.shape["dp"] == 16 and mesh.shape["tensor"] == 2
    in_specs = (
        P("dp", None, None),
        P("dp", None, None),
        P("dp"),
        P("dp", None, "tensor"),
        P("dp", None, "tensor"),
        P("dp", None, "tensor"),
        P("dp", None, "tensor"),
        P("dp", None, "tensor"),
        P("dp", None, "tensor"),
        P(),
        P(),
        P(),
    )
    out_specs = (
        P("dp", None, None),
        P("dp", None, None),
        P("dp", None, "tensor"),
        P("dp", None, "tensor"),
        P("dp", None, "tensor"),
        P("dp", None, "tensor"),
        P(),
        P(),
    )
    return jax.shard_map(
        functools.partial(body, fast), mesh=mesh, in_specs=in_specs, out_specs=out_specs, check_vma=False
    )
```

```python
import functools
import math

import jax
import jax.numpy as jnp
from jax import lax
from jax.experimental import pallas as pl
from jax.experimental.pallas import tpu as pltpu
from jax.sharding import PartitionSpec as P

D = 768
HD = 64
FF = 3072
LEN = 960
NS_ITERS = 5


COEF_A = 3.4445
COEF_B = -4.775
COEF_C = 2.0315


def gelu_tanh(values):
    return jax.nn.gelu(values, approximate=True)


def layer_norm(values, norm_gain, norm_bias):
    centered = values - jnp.mean(values, axis=-1, keepdims=True)
    inverse = lax.rsqrt(jnp.mean(centered * centered, axis=-1, keepdims=True) + 1e-05)
    normed = centered * inverse
    return (normed * norm_gain + norm_bias, normed, inverse)


def norm_back(grad_out, norm_gain, normed, inverse):
    scaled = grad_out * norm_gain
    return inverse * (
        scaled
        - jnp.mean(scaled, axis=-1, keepdims=True)
        - normed * jnp.mean(scaled * normed, axis=-1, keepdims=True)
    )


def contract(left, right, left_dim, right_dim):
    return lax.dot_general(
        left, right, (((left_dim,), (right_dim,)), ((), ())), preferred_element_type=jnp.float32
    )


MESH = pl.DeviceIdType.MESH
MIB = 1 << 20
LINE = 4
OWNERS = (7, 8, 6, 9, 4, 11)


def place():
    dp = lax.axis_index("dp")
    core = lax.axis_index("tensor")
    z = dp // 4
    y = dp % 4 // 2
    x = dp % 2
    return dp, core, z, y, x


def remote(src, dst, send, recv, dp, core):
    return pltpu.make_async_remote_copy(
        src_ref=src, dst_ref=dst, send_sem=send, recv_sem=recv, device_id=(dp, core), device_id_type=MESH
    )


def greet(barrier, dp, core):
    pl.semaphore_signal(barrier, inc=1, device_id=(dp, core), device_id_type=MESH)


def greet_all(dp, core, count):
    barrier = pltpu.get_barrier_semaphore()
    for step in range(1, count):
        greet(barrier, (dp + step) % count, core)
    pl.semaphore_wait(barrier, count - 1)


def greet_plane(dp, core, count, z, y, x):
    barrier = pltpu.get_barrier_semaphore()
    for step in range(1, count):
        greet(barrier, (dp + step) % count, core)
    for step in range(4):
        greet(barrier, z * 4 + (dp + step) % 4, 1 - core)
    return lambda: pl.semaphore_wait(barrier, count + 3)


class Staging:
    def __init__(self, sems):
        self.sems = sems
        self.count = 0
        self.waiting = {}
        self.out = []

    def move(self, src, dst):
        copy = pltpu.make_async_copy(src, dst, self.sems.at[self.count])
        self.count += 1
        copy.start()
        return copy

    def fetch(self, name, src, dst):
        self.waiting[name] = self.move(src, dst)

    def need(self, *names):
        for name in names:
            if name in self.waiting:
                self.waiting.pop(name).wait()

    def keep(self, src, dst):
        self.out.append(self.move(src, dst))

    def finish(self):
        for copy in self.out:
            copy.wait()


def gram_kernel(noise_scale, batch, vector_rate, owned_in, *refs):
    results, vec_in, (gram, low, scale), kept, vec_out = refs[:4], refs[4:8], refs[8:11], refs[11:15], refs[15:17]
    held, vec, vec_new, (own, sems) = refs[17:21], refs[21:25], refs[25:27], refs[27:]
    dp = lax.axis_index("dp")
    stage = Staging(sems)
    stage.fetch("mine", owned_in.at[0], own.at[0])
    for index in range(4):
        stage.fetch(index, results[index], held[index])
    for index in range(4):
        stage.fetch(4 + index, vec_in[index], vec[index])
    stage.fetch("other", owned_in.at[1], own.at[1])
    rows = gram.shape[0]
    attn = (dp == OWNERS[0]) | (dp == OWNERS[1]) | (dp == OWNERS[2]) | (dp == OWNERS[3])
    mlp = (dp == OWNERS[4]) | (dp == OWNERS[5])

    def each(action):
        pl.when(attn)(lambda: action(own.shape[2] // 4))
        pl.when(mlp)(lambda: action(own.shape[2]))

    def first(size):
        gram[...] = contract(own[0, :, 0:size], own[0, :, 0:size], 1, 1)

    def second(size):
        total = gram[...] + contract(own[1, :, 0:size], own[1, :, 0:size], 1, 1)
        square = jnp.zeros((1, 1), jnp.float32)
        tile = 256
        here = lax.broadcasted_iota(jnp.int32, (tile, tile), 0) == lax.broadcasted_iota(jnp.int32, (tile, tile), 1)
        for start in range(0, rows, tile):
            corner = jnp.where(here, total[start : start + tile, start : start + tile], 0.0)
            square = square + jnp.sum(jnp.sum(corner, axis=0, keepdims=True), axis=1, keepdims=True)
        inverse = 1.0 / (jnp.sqrt(square) + 1e-07)
        scale[...] = jnp.broadcast_to(inverse, scale.shape)
        total = total * (inverse * inverse)
        gram[...] = total
        low[...] = total.astype(low.dtype)

    stage.need("mine")
    each(first)
    for index in range(4):
        stage.need(index)
        stage.keep(held[index], kept[index])
    stage.need(4, 5, 6, 7)
    summed, old, moment, noise = (ref[...] for ref in vec)
    moment = 0.5 * moment + (summed + noise_scale * noise) / batch
    vec_new[0][...] = moment
    vec_new[1][...] = old - vector_rate * moment
    for index in range(2):
        stage.keep(vec_new[index], vec_out[index])
    stage.need("other")
    each(second)
    stage.finish()


def gram_of(owned, results, vectors, noise_scale, batch, vector_rate):
    rows = owned.shape[1]
    shape = jax.ShapeDtypeStruct
    vmem = pl.BlockSpec(memory_space=pltpu.VMEM)
    anywhere = pl.BlockSpec(memory_space=pl.ANY)
    return pl.pallas_call(
        functools.partial(gram_kernel, noise_scale, batch, vector_rate),
        out_shape=[
            shape((rows, rows), jnp.float32),
            shape((rows, rows), jnp.bfloat16),
            shape((8, 128), jnp.float32),
        ]
        + [shape(value.shape, value.dtype) for value in results + vectors[:2]],
        in_specs=[anywhere] * 9,
        out_specs=[vmem] * 3 + [anywhere] * 6,
        scratch_shapes=[pltpu.VMEM(value.shape, value.dtype) for value in results + vectors + vectors[:2]]
        + [pltpu.VMEM(owned.shape, owned.dtype), pltpu.SemaphoreType.DMA((16,))],
        compiler_params=pltpu.CompilerParams(vmem_limit_bytes=60 * MIB),
        name="gram",
    )(owned, *results, *vectors)


def scatter_kernel(
    rates, factor, scale, owned_in, attn_in, mlp_in, attn_new, mlp_new,
    own, attn, mlp, orth, attn_low, mlp_low, relayed, send, recv, relay_send, relay_recv, stage_sems,
):
    dp, core, z, y, x = place()
    rows = attn.shape[0]
    count = orth.shape[0] // rows
    stage = Staging(stage_sems)
    stage.fetch("own", owned_in.at[0], own)
    stage.fetch("attn", attn_in, attn)
    stage.fetch("mlp", mlp_in, mlp)
    greet_all(dp, core, count)
    stage.need("own")

    def at(ref, block):
        return ref.at[pl.ds(pl.multiple_of(block * rows, rows), rows)]

    def low_of(slot):
        return attn_low.at[slot] if slot < 4 else mlp_low.at[slot - 4]

    def size_of(slot):
        return attn.shape[2] if slot < 4 else mlp.shape[2]

    def deliver(slot, target):
        owner = OWNERS[slot]
        src = at(orth, target).at[:, 0 : size_of(slot)]
        level = target // 4
        if slot >= 4 and level in stops(owner).get(target % 4, ()):
            stop = owner // 4 * 4 + target % 4
            return remote(src, relayed.at[level], send.at[target], relay_recv.at[level], stop, core)
        return remote(src, low_of(slot), send.at[target], recv.at[slot], target, core)

    def onward(slot, action):
        owner = OWNERS[slot]
        for column, levels in stops(owner).items():

            @pl.when(dp == owner // 4 * 4 + column)
            def _():
                for level in levels:
                    action(level, level * 4 + column)

    def relay_copy(slot, level, target):
        return remote(relayed.at[level], low_of(slot), relay_send.at[level], recv.at[slot], target, core)

    def levels_of(owner):
        return (3, 2, 0) if owner // 4 == 1 else (0, 1, 3)

    def stops(owner):
        far, near, alone = levels_of(owner)
        column = owner % 4
        by_x, by_y = column + 1 - 2 * (column % 2), column + 2 - 4 * (column // 2)
        return {by_x: (far, near), by_y: (far, near, alone)}

    def queue(owner):
        far, near, alone = levels_of(owner)
        home, column = owner // 4, owner % 4
        by_x, by_y, across = column + 1 - 2 * (column % 2), column + 2 - 4 * (column // 2), 3 - column
        links = (
            [far * 4 + by_x, near * 4 + by_x, home * 4 + across, home * 4 + by_x],
            [far * 4 + by_y, near * 4 + by_y, alone * 4 + by_y, home * 4 + by_y],
            [far * 4 + across, far * 4 + column, near * 4 + across, near * 4 + column],
            [alone * 4 + across, alone * 4 + by_x, alone * 4 + column],
        )
        return [link[turn] for turn in range(4) for link in links if turn < len(link)]

    pieces = ((0, 5), (5, 11), (11, 16))
    for slot in range(6):
        owner = OWNERS[slot]
        size = size_of(slot)

        @pl.when(dp == owner)
        def _():
            waiting = queue(owner)
            ready = set()
            for first, last in (pieces[0], pieces[2], pieces[1]):
                part = pl.ds(first * rows, (last - first) * rows)
                value = contract(factor[part, :], own[:, 0:size], 1, 0) * scale[0:1, 0:1]
                orth[part, 0:size] = value.astype(orth.dtype)
                ready.update(range(first, last))
                while waiting and waiting[0] in ready:
                    deliver(slot, waiting.pop(0)).start()
            pltpu.make_async_copy(at(orth, owner).at[:, 0:size], low_of(slot), recv.at[slot]).start()

    for slot in (4, 5):

        def pass_on(level, target):
            block = relayed.at[level]
            remote(block, block, relay_send.at[level], relay_recv.at[level], dp, core).wait_recv()
            relay_copy(slot, level, target).start()

        onward(slot, pass_on)

    stage.need("attn", "mlp")
    for slot in range(6):
        owner = OWNERS[slot]
        low = low_of(slot)

        @pl.when(dp != owner)
        def _():
            remote(low, low, send.at[0], recv.at[slot], owner, core).wait_recv()

        @pl.when(dp == owner)
        def _():
            pltpu.make_async_copy(low, low, recv.at[slot]).wait()

        @pl.loop(0, rows // 16)
        def _(i):
            part = pl.ds(pl.multiple_of(i * 16, 16), 16)
            step = rates[slot] * low[part, :].astype(jnp.float32)
            if slot < 4:
                attn_new[part, slot, :] = attn[part, slot, :] - step
            else:
                mlp_new[part, slot - 4, :] = mlp[part, slot - 4, :] - step

    for slot in range(6):
        owner = OWNERS[slot]

        @pl.when(dp == owner)
        def _():
            for target in range(count):
                if target != owner:
                    deliver(slot, target).wait_send()

    for slot in (4, 5):
        onward(slot, lambda level, target: relay_copy(slot, level, target).wait_send())


def scatter_rows(factor, scale, owned, attn, mlp, rates, collective_id):
    dma = pltpu.SemaphoreType.DMA
    count = lax.axis_size("dp")
    rows = attn.shape[0]
    shape = jax.ShapeDtypeStruct
    vmem = pl.BlockSpec(memory_space=pltpu.VMEM)
    anywhere = pl.BlockSpec(memory_space=pl.ANY)
    return pl.pallas_call(
        functools.partial(scatter_kernel, rates),
        out_shape=[shape(attn.shape, jnp.float32), shape(mlp.shape, jnp.float32)],
        in_specs=[vmem] * 2 + [anywhere] * 3,
        out_specs=[vmem] * 2,
        scratch_shapes=[
            pltpu.VMEM(owned.shape[1:], owned.dtype),
            pltpu.VMEM(attn.shape, attn.dtype),
            pltpu.VMEM(mlp.shape, mlp.dtype),
            pltpu.VMEM(owned.shape[1:], owned.dtype),
            pltpu.VMEM((4, rows, attn.shape[2]), jnp.bfloat16),
            pltpu.VMEM((2, rows, mlp.shape[2]), jnp.bfloat16),
            pltpu.VMEM((LINE, rows, mlp.shape[2]), jnp.bfloat16),
            dma((count,)),
            dma((6,)),
            dma((LINE,)),
            dma((LINE,)),
            dma((3,)),
        ],
        compiler_params=pltpu.CompilerParams(
            collective_id=collective_id, has_side_effects=True, vmem_limit_bytes=32 * MIB
        ),
        name="scatter_rows",
    )(factor, scale, owned, attn, mlp)


def head_mask(shape):
    return lax.broadcasted_iota(jnp.int32, shape, 1) < HD


def spans(length):
    return [(start, min(256, length - start)) for start in range(0, length, 256)]


def attend_forward(q_ref, k_ref, v_ref, o_ref, lse_ref, turned, value_turned, after=lambda head: None):
    length = q_ref.shape[0]
    value_turned[...] = v_ref[...].astype(jnp.float32).T.astype(jnp.bfloat16)
    keys = k_ref[...]
    for head in range(2):
        mine = head_mask(keys.shape) if head == 0 else ~head_mask(keys.shape)
        head_keys = jnp.where(mine, keys, jnp.zeros_like(keys))
        for start, size in spans(length):
            stop = start + size
            scores = contract(head_keys[0:stop], q_ref[start:stop, :], 1, 1)
            key_at = lax.broadcasted_iota(jnp.int32, (stop, size), 0)
            query_at = lax.broadcasted_iota(jnp.int32, (stop, size), 1) + start
            scores = jnp.where(key_at <= query_at, scores, -1e30)
            peak = jnp.max(scores, axis=0, keepdims=True)
            weights = jnp.exp(scores - peak)
            total = jnp.sum(weights, axis=0, keepdims=True)
            mixed = contract(
                value_turned[head * HD : (head + 1) * HD, 0:stop], weights.astype(jnp.bfloat16), 1, 0
            )
            turned[head * HD : (head + 1) * HD, start:stop] = mixed / total
            lse_ref[head : head + 1, start:stop] = peak + jnp.log(total)
        after(head)
    o_ref[...] = turned[...].T.astype(jnp.bfloat16)


def attend_backward(q_ref, k_ref, v_ref, o_ref, do_ref, lse_ref, dq_ref, dk_ref, dv_ref, turned):
    length = q_ref.shape[0]
    keys, values = k_ref[...], v_ref[...]
    key_turned = keys.astype(jnp.float32).T.astype(jnp.bfloat16)
    inner = (o_ref[...].astype(jnp.float32) * do_ref[...].astype(jnp.float32)).T
    mask = head_mask(keys.shape)
    turned[...] = jnp.zeros_like(turned)
    for start, size in spans(length):
        stop = start + size
        both_k, both_v = [], []
        for head in range(2):
            mine = mask[start:stop] if head == 0 else ~mask[start:stop]
            head_keys = jnp.where(mine, keys[start:stop], 0)
            head_values = jnp.where(mine, values[start:stop], 0)
            head_inner = jnp.sum(inner[head * HD : (head + 1) * HD, start:], axis=0, keepdims=True)
            scores = contract(head_keys, q_ref[start:, :], 1, 1)
            grad_prob = contract(head_values, do_ref[start:, :], 1, 1)
            key_at = lax.broadcasted_iota(jnp.int32, scores.shape, 0)
            query_at = lax.broadcasted_iota(jnp.int32, scores.shape, 1)
            scores = jnp.where(key_at <= query_at, scores, -1e30)
            prob = jnp.exp(scores - lse_ref[head : head + 1, start:])
            grad_scores = (prob * (grad_prob - head_inner)).astype(jnp.bfloat16)
            both_v.append(contract(prob.astype(jnp.bfloat16), do_ref[start:, :], 1, 0))
            both_k.append(contract(grad_scores, q_ref[start:, :], 1, 0))
            turned[head * HD : (head + 1) * HD, start:] += contract(
                key_turned[head * HD : (head + 1) * HD, start:stop], grad_scores, 1, 0
            )
        pick = mask[start:stop]
        dk_ref[start:stop, :] = jnp.where(pick, both_k[0], both_k[1]).astype(jnp.bfloat16)
        dv_ref[start:stop, :] = jnp.where(pick, both_v[0], both_v[1]).astype(jnp.bfloat16)
    dq_ref[...] = (turned[...].T * (1.0 / math.sqrt(HD))).astype(jnp.bfloat16)


def pairs_forward(queries, keys, values):
    length, width = queries.shape
    block = pl.BlockSpec((length, 2 * HD), lambda i: (0, i))
    stat = pl.BlockSpec((None, 2, length), lambda i: (i, 0, 0))
    return pl.pallas_call(
        attend_forward,
        grid=(width // (2 * HD),),
        out_shape=[
            jax.ShapeDtypeStruct((length, width), jnp.bfloat16),
            jax.ShapeDtypeStruct((width // (2 * HD), 2, length), jnp.float32),
        ],
        in_specs=[block] * 3,
        out_specs=[block, stat],
        scratch_shapes=[pltpu.VMEM((2 * HD, length), jnp.float32), pltpu.VMEM((2 * HD, length), jnp.bfloat16)],
        compiler_params=pltpu.CompilerParams(vmem_limit_bytes=48 * MIB),
        name="attend_forward",
    )(queries, keys, values)


def pairs_backward(queries, keys, values, attended, grad_attended, stats):
    length, width = queries.shape
    block = pl.BlockSpec((length, 2 * HD), lambda i: (0, i))
    stat = pl.BlockSpec((None, 2, length), lambda i: (i, 0, 0))
    return pl.pallas_call(
        attend_backward,
        grid=(width // (2 * HD),),
        out_shape=[jax.ShapeDtypeStruct((length, width), jnp.bfloat16)] * 3,
        in_specs=[block] * 5 + [stat],
        out_specs=[block] * 3,
        scratch_shapes=[pltpu.VMEM((2 * HD, length), jnp.float32)],
        compiler_params=pltpu.CompilerParams(vmem_limit_bytes=48 * MIB),
        name="attend_backward",
    )(queries, keys, values, attended, grad_attended, stats)


NORM_ROWS = 240


class Gathering:
    def __init__(self, a_ref, b_ref, a_out, b_out, send, recv, local):
        self.own = (a_ref, b_ref)
        self.outs = (a_out, b_out)
        self.send, self.recv, self.local = send, recv, local
        self.rows = a_ref.shape[0]
        self.dp, self.core, self.z, self.y, self.x = place()
        self.x_peer = self.dp + 1 - 2 * self.x
        self.y_peer = self.dp + 2 - 4 * self.y

    def block(self, side, index):
        return self.outs[side].at[pl.ds(pl.multiple_of(index * self.rows, self.rows), self.rows)]

    def copy(self, kind, side, index, own, target):
        src = self.own[side] if own else self.block(side, index)
        return remote(
            src, self.block(side, index), self.send.at[kind, index // 4], self.recv.at[side, index], target, self.core
        )

    def arrived(self, side, index):
        block = self.block(side, index)
        remote(block, block, self.send.at[0, 0], self.recv.at[side, index], self.dp, self.core).wait_recv()

    def at(self, level, y_off, x_off):
        y = self.y + y_off * (1 - 2 * self.y)
        x = self.x + x_off * (1 - 2 * self.x)
        return level * 4 + y * 2 + x

    def line(self, level, own, action):
        index = self.at(level, 0, 0)

        @pl.when((self.z < LINE - 1) & (level <= self.z))
        def _():
            for side in range(2):
                action(self.copy(side, side, index, own, self.dp + 4))

        @pl.when((self.z > 0) & (level >= self.z))
        def _():
            for side in range(2):
                action(self.copy(2 + side, side, index, own, self.dp - 4))

        for side in range(2):
            action(self.copy(4 + side, side, index, own, self.x_peer))
            action(self.copy(6 + side, side, index, own, self.y_peer))

    def relays(self, level):
        return (
            (0, self.at(level, 0, 1), self.copy(8, 0, self.at(level, 0, 1), False, self.y_peer)),
            (1, self.at(level, 1, 0), self.copy(9, 1, self.at(level, 1, 0), False, self.x_peer)),
        )

    def by_distance(self, distance, action):
        if distance == 0:
            action(self.z)
            return

        @pl.when(self.z >= distance)
        def _():
            action(self.z - distance)

        @pl.when(self.z + distance < LINE)
        def _():
            action(self.z + distance)

    def local_copies(self):
        return [
            pltpu.make_async_copy(self.own[side], self.block(side, self.dp), self.local.at[side]) for side in range(2)
        ]

    def begin(self):
        self.line(self.z, True, lambda copy: copy.start())
        for copy in self.local_copies():
            copy.start()

    def onward(self, distance):
        def action(level):
            for side in range(2):
                self.arrived(side, self.at(level, 0, 0))
            self.line(level, False, lambda copy: copy.start())

        self.by_distance(distance, action)

    def relay(self, distance):
        def action(level):
            for side, index, copy in self.relays(level):
                self.arrived(side, index)
                copy.start()

        self.by_distance(distance, action)

    def finish(self):
        for level in range(LINE):
            self.arrived(1, self.at(level, 0, 1))
            self.arrived(0, self.at(level, 1, 0))
            for side in range(2):
                self.arrived(side, self.at(level, 1, 1))
        for copy in self.local_copies():
            copy.wait()

    def drain(self):
        for level in range(LINE):
            self.line(level, False, lambda copy: copy.wait_send())
            for _, _, copy in self.relays(level):
                copy.wait_send()


def norm_tile(values, gain, bias):
    centered = values - jnp.mean(values, axis=-1, keepdims=True)
    inverse = lax.rsqrt(jnp.mean(centered * centered, axis=-1, keepdims=True) + 1e-05)
    return centered * inverse * gain + bias


def tiles(count, rows, action):
    @pl.loop(0, count // rows)
    def _(i):
        action(pl.ds(pl.multiple_of(i * rows, rows), rows))


BACK_ROWS = 80


def fold(value):
    return jnp.sum(value.reshape(-1, 8, value.shape[1]), axis=0)


def norm_back_tile(grad, gain, values):
    centered = values - jnp.mean(values, axis=-1, keepdims=True)
    inverse = lax.rsqrt(jnp.mean(centered * centered, axis=-1, keepdims=True) + 1e-05)
    normed = centered * inverse
    scaled = grad * gain
    back = inverse * (
        scaled
        - jnp.mean(scaled, axis=-1, keepdims=True)
        - normed * jnp.mean(scaled * normed, axis=-1, keepdims=True)
    )
    return back, normed


def shifted(part, start):
    return pl.ds(pl.multiple_of(start + part.start, 16), part.size)


def column_sum(value):
    return jnp.sum(value, axis=0, keepdims=True)


def forward_kernel(
    tokens_in, vec_in, attn_in, mlp_in, cot_in,
    qk_out, vo_out, first_out, q_out, k_out, v_out, o_out, out_out, grad_mid_out, do_out, ga_out, gb_out, go_out,
    x_a, x_b, y_a, y_b, lse, vec, sums,
    tokens, qk_all, vo_all, f0, f1, p0, p1, first, q, k, v, o, middle, second, act, slope,
    turned, mixed, partial, partial_other, pre, attn, mlp, qk_shard, vo_shard, f0_shard, f1_shard, p0_shard, p1_shard,
    cot, out, grad_mid, do, ga, gb, go, du, back_partial, back_other, m_partial, m_other, low, across, acc,
    gather_send, gather_recv, local, swap_send, swap_recv, send, recv, stage_sems,
):
    dp, core, z, y, x = place()
    length = tokens.shape[0]
    width = q.shape[1]
    chunk = length // 4
    x_peer, y_peer = dp + 1 - 2 * x, dp + 2 - 4 * y
    shard_rows = x_a.shape[1]
    stage = Staging(stage_sems)
    stage.fetch("attn", attn_in, attn)
    stage.fetch("tokens", tokens_in, tokens)
    stage.fetch("mlp", mlp_in, mlp)
    stage.fetch("cot", cot_in, cot)
    for row in range(vec.shape[0]):
        for column in range(D // 128):
            at = row * (D // 128) + column
            vec[row : row + 1, column * 128 : (column + 1) * 128] = vec_in[at : at + 1, :]
    stage.need("attn")
    for slot, shard in enumerate((qk_shard, qk_shard, vo_shard, vo_shard)):
        shard[:, slot % 2 * width : (slot % 2 + 1) * width] = attn[:, slot, :].astype(jnp.bfloat16)
    barrier = pltpu.get_barrier_semaphore()
    greet(barrier, dp + 1 - 2 * x, core)
    greet(barrier, dp + 2 - 4 * y, core)
    greet(barrier, dp, 1 - core)

    @pl.when(z > 0)
    def _():
        greet(barrier, dp - 4, core)

    @pl.when(z < LINE - 1)
    def _():
        greet(barrier, dp + 4, core)

    pl.semaphore_wait(barrier, 3 + (z + 2) // 3 + (5 - z) // 3)

    rounds = [
        Gathering(a, b, a_out, b_out, gather_send.at[i], gather_recv.at[i], local.at[i])
        for i, (a, b, a_out, b_out) in enumerate(
            ((qk_shard, vo_shard, qk_all, vo_all), (f0_shard, f1_shard, f0, f1), (p0_shard, p1_shard, p0, p1))
        )
    ]
    rounds[0].begin()
    stage.need("tokens", "mlp")
    for slot, shard in enumerate((f0_shard, f1_shard, p0_shard, p1_shard)):
        shard[...] = mlp[:, slot // 2, slot % 2 * D : (slot % 2 + 1) * D].astype(jnp.bfloat16)

    def norm_one(part):
        tile = norm_tile(tokens[part, :].astype(jnp.float32), vec[0:1, :], vec[1:2, :])
        first[part, :] = tile.astype(jnp.bfloat16)

    tiles(length, NORM_ROWS, norm_one)
    stage.keep(first, first_out)
    rounds[0].onward(1)
    rounds[0].relay(0)
    rounds[0].onward(2)
    rounds[0].relay(1)
    rounds[0].onward(3)
    rounds[0].relay(2)
    rounds[0].relay(3)
    rounds[1].begin()
    rounds[0].finish()
    stage.keep(qk_all, qk_out)
    stage.keep(vo_all, vo_out)

    mine = pl.ds(pl.multiple_of(core * width, width), width)
    scale = 1.0 / math.sqrt(HD)
    q[...] = ((contract(first[...], qk_all[:, 0:width], 1, 0) + vec[4:5, mine]) * scale).astype(jnp.bfloat16)
    k[...] = contract(first[...], qk_all[:, width:], 1, 0).astype(jnp.bfloat16)
    v[...] = (contract(first[...], vo_all[:, 0:width], 1, 0) + vec[5:6, mine]).astype(jnp.bfloat16)

    for value, target in ((q, q_out), (k, k_out), (v, v_out)):
        stage.keep(value, target)

    def step(index):
        if index == 1:
            rounds[1].onward(1)
            rounds[1].relay(0)
        if index == 2:
            rounds[1].onward(2)
            rounds[1].relay(1)
        if index == 3:
            rounds[1].onward(3)
            rounds[1].relay(2)
        if index == 4:
            rounds[1].relay(3)
            rounds[2].begin()
        if index == 6:
            rounds[2].onward(1)
            rounds[2].relay(0)
        if index == 7:
            rounds[2].onward(2)
            rounds[2].relay(1)
        if index == 8:
            rounds[2].onward(3)
            rounds[2].relay(2)
        if index == 9:
            rounds[2].relay(3)

    for pair in range(width // (2 * HD)):
        lanes = pl.ds(pair * 2 * HD, 2 * HD)
        attend_forward(
            q.at[:, lanes], k.at[:, lanes], v.at[:, lanes], o.at[:, lanes], lse.at[pair], turned, mixed,
            lambda head: step(2 * pair + head),
        )

    stage.keep(o, o_out)

    def swap_copy(kind, i):
        part = pl.ds(i * chunk, chunk)
        src, dst = ((back_partial, back_other), (m_partial, m_other), (partial, partial_other))[kind]
        return remote(src.at[part], dst.at[part], swap_send.at[kind, i], swap_recv.at[kind, i], dp, 1 - core)

    for i in range(4):
        part = pl.ds(i * chunk, chunk)
        partial[part, :] = contract(o[part, :], vo_all[:, width:], 1, 1).astype(jnp.bfloat16)
        swap_copy(2, i).start()
    step(6)
    rounds[1].finish()
    for i in range(4):
        swap_copy(2, i).wait_recv()

        def norm_two(part):
            rows = pl.ds(pl.multiple_of(i * chunk + part.start, 16), part.size)
            total = partial[rows, :].astype(jnp.float32) + partial_other[rows, :].astype(jnp.float32)
            tile = tokens[rows, :].astype(jnp.float32) + total + vec[6:7, :]
            middle[rows, :] = tile
            second[rows, :] = norm_tile(tile, vec[2:3, :], vec[3:4, :]).astype(jnp.bfloat16)

        tiles(chunk, NORM_ROWS, norm_two)
        rows = pl.ds(i * chunk, chunk)
        for side, weight in enumerate((f0, f1)):
            pre[:, side * D : (side + 1) * D] = contract(second[rows, :], weight[...], 1, 0)

        def curve(part):
            rows = pl.ds(pl.multiple_of(i * chunk + part.start, 16), part.size)
            for side in range(2):
                columns = pl.ds(side * D, D)
                value = pre[part, columns] + vec[pl.ds(8 + 2 * core + side, 1), :]
                square = value * value
                root = math.sqrt(2.0 / math.pi)
                bent = jnp.tanh(value * (root + root * 0.044715 * square))
                half = 0.5 + 0.5 * bent
                act[rows, columns] = (value * half).astype(jnp.bfloat16)
                inner = root + (3.0 * root * 0.044715) * square
                slope[rows, columns] = (half + (0.5 * value) * (1.0 - bent * bent) * inner).astype(jnp.bfloat16)

        tiles(chunk, 48, curve)
        step(7 + i)

    def early(side, level):
        grad, to_x, to_y = ((ga, x_a, y_a), (gb, x_b, y_b))[side]
        x_block = level * 4 + y * 2 + 1 - x
        y_block = level * 4 + (1 - y) * 2 + x

        def part(block):
            return grad.at[pl.ds(pl.multiple_of(block * shard_rows, shard_rows), shard_rows)]

        return (
            remote(part(x_block), to_x.at[level], send.at[side, level], recv.at[side, level], x_peer, core),
            remote(part(y_block), to_y.at[level], send.at[2 + side, level], recv.at[2 + side, level], y_peer, core),
        )

    def outer(left, right, target, start):
        size = right.shape[1]
        for block in range(D // 256):
            part = pl.ds(block * 256, 256)
            value = contract(left[part, :], right[...], 1, 0)
            target[part, start : start + size] = value.astype(jnp.bfloat16)
            row = 6 if size == D else 7
            sums[row : row + 1, 0:size] += column_sum(value * value)

    stage.need("cot")
    sums[...] = jnp.zeros_like(sums)
    across[...] = cot[...].T
    for side in range(2):
        outer(across, act.at[:, side * D : (side + 1) * D], gb, side * D)
    for level in range(LINE):
        for copy in early(1, level):
            copy.start()
    rounds[2].finish()
    acc[...] = jnp.zeros_like(acc)
    for i in range(4):
        part = pl.ds(i * chunk, chunk)
        for side, weight in enumerate((p0, p1)):
            columns = pl.ds(side * D, D)
            value = contract(cot[part, :], weight[...], 1, 0) * slope[part, columns].astype(jnp.float32)
            value = value.astype(jnp.bfloat16)
            du[part, columns] = value
            sums[4 + side : 5 + side, :] += column_sum(value.astype(jnp.float32))
        back_partial[part, :] = (
            contract(du[part, 0:D], f0[...], 1, 1) + contract(du[part, D:], f1[...], 1, 1)
        ).astype(jnp.bfloat16)
        swap_copy(0, i).start()
    across[...] = second[...].T
    for side in range(2):
        outer(across, du.at[:, side * D : (side + 1) * D], ga, side * D)
    for level in range(LINE):
        for copy in early(0, level):
            copy.start()
    stage.keep(ga, ga_out)
    for i in range(4):
        part = pl.ds(i * chunk, chunk)
        m_partial[part, :] = (
            contract(act[part, 0:D], p0[...], 1, 1) + contract(act[part, D:], p1[...], 1, 1)
        ).astype(jnp.bfloat16)
        swap_copy(1, i).start()
    stage.keep(gb, gb_out)
    for i in range(4):
        swap_copy(0, i).wait_recv()

        def back(part):
            rows = shifted(part, i * chunk)
            grad = back_partial[rows, :].astype(jnp.float32) + back_other[rows, :].astype(jnp.float32)
            outgoing = cot[rows, :].astype(jnp.float32)
            value, normed = norm_back_tile(grad, vec[2:3, :], middle[rows, :])
            value = value + outgoing
            grad_mid[rows, :] = value
            low[rows, :] = value.astype(jnp.bfloat16)
            acc[0] += fold(grad * normed)
            acc[1] += fold(grad)
            acc[2] += fold(value)
            acc[3] += fold(outgoing)

        tiles(chunk, BACK_ROWS, back)
        rows = pl.ds(i * chunk, chunk)
        do[rows, :] = contract(low[rows, :], vo_all[:, width:], 1, 0).astype(jnp.bfloat16)
    for row in range(4):
        sums[row : row + 1, :] = column_sum(acc[row])
    stage.keep(grad_mid, grad_mid_out)
    stage.keep(do, do_out)
    across[...] = low[...].T
    outer(across, o, go, 0)
    stage.keep(go, go_out)
    for i in range(4):
        swap_copy(1, i).wait_recv()

        def finish(part):
            rows = shifted(part, i * chunk)
            total = m_partial[rows, :].astype(jnp.float32) + m_other[rows, :].astype(jnp.float32)
            out[rows, :] = (middle[rows, :] + total + vec[7:8, :]).astype(jnp.bfloat16)

        tiles(chunk, 48, finish)
        part = pl.ds(i * chunk, chunk)
        stage.keep(out.at[part], out_out.at[part])
    for kind in range(3):
        for i in range(4):
            swap_copy(kind, i).wait_send()
    for side in range(2):
        for level in range(LINE):
            for copy in early(side, level):
                copy.wait()
    for gathering in rounds:
        gathering.drain()
    stage.finish()


def forward(tokens, vec, attn, mlp, cot, collective_id):
    dma = pltpu.SemaphoreType.DMA
    low = jnp.bfloat16
    count = lax.axis_size("dp")
    length = tokens.shape[0]
    rows, _, width = attn.shape
    hidden = 2 * D
    shape = jax.ShapeDtypeStruct
    scratch = pltpu.VMEM
    vmem = pl.BlockSpec(memory_space=pltpu.VMEM)
    anywhere = pl.BlockSpec(memory_space=pl.ANY)
    whole, thin, wide = (length, D), (length, width), (length, hidden)
    return pl.pallas_call(
        forward_kernel,
        out_shape=[shape((D, D), low)] * 2
        + [shape(whole, low)]
        + [shape(thin, low)] * 4
        + [
            shape(whole, low),
            shape(whole, jnp.float32),
            shape(thin, low),
            shape((D, hidden), low),
            shape((D, hidden), low),
            shape((D, width), low),
        ]
        + [shape((LINE, rows, hidden), low)] * 4
        + [
            shape((width // (2 * HD), 2, length), jnp.float32),
            shape((vec.shape[0] * 128 // D, D), jnp.float32),
            shape((8, D), jnp.float32),
        ],
        in_specs=[anywhere, vmem] + [anywhere] * 3,
        out_specs=[anywhere] * 17 + [vmem] * 3,
        scratch_shapes=[scratch(whole, low)]
        + [scratch((D, D), low)] * 6
        + [scratch(whole, low)]
        + [scratch(thin, low)] * 4
        + [
            scratch(whole, jnp.float32),
            scratch(whole, low),
            scratch(wide, low),
            scratch(wide, low),
            scratch((2 * HD, length), jnp.float32),
            scratch((2 * HD, length), low),
            scratch(whole, low),
            scratch(whole, low),
            scratch((length // 4, hidden), jnp.float32),
            scratch(attn.shape, jnp.float32),
            scratch(mlp.shape, jnp.float32),
        ]
        + [scratch((rows, D), low)] * 6
        + [
            scratch(whole, low),
            scratch(whole, low),
            scratch(whole, jnp.float32),
            scratch(thin, low),
            scratch((D, hidden), low),
            scratch((D, hidden), low),
            scratch((D, width), low),
            scratch(wide, low),
        ]
        + [scratch(whole, low)] * 5
        + [
            scratch((D, length), low),
            scratch((4, 8, D), jnp.float32),
            dma((3, 10, LINE)),
            dma((3, 2, count)),
            dma((3, 2)),
            dma((3, 4)),
            dma((3, 4)),
            dma((4, LINE)),
            dma((4, LINE)),
            dma((32,)),
        ],
        compiler_params=pltpu.CompilerParams(
            collective_id=collective_id, has_side_effects=True, vmem_limit_bytes=63 * MIB
        ),
        name="forward",
    )(tokens, vec, attn, mlp, cot)


class Reducing:
    def __init__(self, grads, buffers, sources, send, recv, rows, direct):
        self.direct = direct
        self.grads, self.sources = grads, sources
        self.diag, self.from_x, self.from_y, self.up, self.down = buffers[0:2], buffers[2:4], buffers[4:6], buffers[6:8], buffers[8:10]
        self.send, self.recv, self.rows = send, recv, rows
        self.dp, self.core, self.z, self.y, self.x = place()
        self.x_peer = self.dp + 1 - 2 * self.x
        self.y_peer = self.dp + 2 - 4 * self.y
        half = self.z // 2
        self.order = (3 - 3 * half, 2 - half, 1 - self.z + 4 * half, self.z)

    def at(self, ref, block):
        return ref.at[pl.ds(pl.multiple_of(block * self.rows, self.rows), self.rows)]

    def block(self, level, y_off, x_off):
        y = self.y + y_off * (1 - 2 * self.y)
        x = self.x + x_off * (1 - 2 * self.x)
        return level * 4 + y * 2 + x

    def go(self, kind, level, src, dst, target):
        return remote(src, dst, self.send.at[kind, level], self.recv.at[kind, level], target, self.core)

    def diag_copy(self, level, side):
        block = self.at(self.sources[side], self.block(level, 1, 1))
        target = self.block(self.z, 1, 1) if self.direct else (self.y_peer, self.x_peer)[side]
        return self.go(side, level, block, self.diag[side].at[level], target)

    def own_copy(self, level, side):
        block = self.at(self.sources[side], self.block(level, 1 - side, side))
        target = (self.from_y, self.from_x)[side][side].at[level]
        return self.go(2 + side, level, block, target, (self.y_peer, self.x_peer)[side])

    def sum_copy(self, level, side):
        target = (self.from_x, self.from_y)[side][side].at[level]
        return self.go(4 + side, level, self.diag[side].at[level], target, (self.x_peer, self.y_peer)[side])

    def up_copy(self, level, side):
        return self.go(6 + side, level, self.from_x[side].at[level], self.up[side].at[level], self.dp + 4)

    def down_copy(self, level, side):
        return self.go(8 + side, level, self.from_x[side].at[level], self.down[side].at[level], self.dp - 4)

    def first(self, *indices):
        for index in indices:
            level = self.order[index]
            for side in range(2):
                self.diag_copy(level, side).start()
            for side in () if self.direct else range(2):
                self.own_copy(level, side).start()

    def scale(self, factor, factor_x, factor_y, factor_diag):
        self.factor, self.factor_x, self.factor_y, self.factor_diag = factor, factor_x, factor_y, factor_diag

    def weigh(self, side, block, dst, scale_dst, terms):
        grad = self.grads[side]

        @pl.loop(0, self.rows // 16)
        def _(i):
            part = pl.ds(pl.multiple_of(i * 16, 16), 16)
            own = grad[pl.ds(pl.multiple_of(block * self.rows + i * 16, 16), 16), :]
            total = self.factor * own.astype(jnp.float32)
            for scale, ref in ((scale_dst, dst),) + terms:
                value = ref[part, :].astype(jnp.float32)
                total = total + (value if scale is None else scale * value)
            dst[part, :] = total.astype(dst.dtype)

    def sums(self, level):
        for side in range(2):
            self.diag_copy(level, side).wait_recv()
            block = self.block(level, side, 1 - side)
            self.weigh(side, block, self.diag[side].at[level], (self.factor_y, self.factor_x)[side], ())
            self.sum_copy(level, side).start()

    def scales(self, side):
        if self.direct:
            return self.factor_x, self.factor_y
        return (None, self.factor_y) if side == 0 else (self.factor_x, None)

    def arrivals(self, level, side):
        if self.direct:
            self.diag_copy(level, side).wait_recv()
            return
        self.own_copy(level, side).wait_recv()
        self.sum_copy(level, side).wait_recv()

    def chain(self, index):
        level = self.order[index]
        block = self.block(level, 0, 0)
        for side in range(2):
            self.arrivals(level, side)
            scale_x, scale_y = self.scales(side)
            terms = ((scale_y, self.from_y[side].at[level]),)
            if self.direct:
                terms = terms + ((self.factor_diag, self.diag[side].at[level]),)

            def combine(*extra):
                self.weigh(side, block, self.from_x[side].at[level], scale_x, terms + extra)

            @pl.when(level > self.z)
            def _():
                @pl.when(self.z > 0)
                def _():
                    self.up_copy(level, side).wait_recv()
                    combine((None, self.up[side].at[level]))

                @pl.when(self.z == 0)
                def _():
                    combine()

                self.up_copy(level, side).start()

            @pl.when(level < self.z)
            def _():
                @pl.when(self.z < LINE - 1)
                def _():
                    self.down_copy(level, side).wait_recv()
                    combine((None, self.down[side].at[level]))

                @pl.when(self.z == LINE - 1)
                def _():
                    combine()

                self.down_copy(level, side).start()

    def last(self, side):
        self.arrivals(self.z, side)

        @pl.when(self.z > 0)
        def _():
            self.up_copy(self.z, side).wait_recv()

        @pl.when(self.z == 0)
        def _():
            self.up[side][0] = jnp.zeros(self.up[side].shape[1:], self.up[side].dtype)

        @pl.when(self.z < LINE - 1)
        def _():
            self.down_copy(self.z, side).wait_recv()

        @pl.when(self.z == LINE - 1)
        def _():
            self.down[side][LINE - 1] = jnp.zeros(self.down[side].shape[1:], self.down[side].dtype)

    def total(self, side, part, columns):
        here = pl.ds(pl.multiple_of(self.dp * self.rows + part.start, 16), part.size)
        total = self.factor * self.grads[side][here, columns].astype(jnp.float32)
        terms = list(zip(self.scales(side) + (None, None), (self.from_x, self.from_y, self.up, self.down)))
        if self.direct:
            terms.append((self.factor_diag, self.diag))
        for scale, ref in terms:
            value = ref[side][self.z, part, columns].astype(jnp.float32)
            total = total + (value if scale is None else scale * value)
        return total

    def drain(self):
        for level in range(LINE):
            for side in range(2):
                self.diag_copy(level, side).wait_send()
                if not self.direct:
                    self.own_copy(level, side).wait_send()
                    self.sum_copy(level, side).wait_send()

            @pl.when(level > self.z)
            def _():
                for side in range(2):
                    self.up_copy(level, side).wait_send()

            @pl.when(level < self.z)
            def _():
                for side in range(2):
                    self.down_copy(level, side).wait_send()


def owner_at(slot):
    return OWNERS[slot] // 4, OWNERS[slot] % 4 // 2, OWNERS[slot] % 2


def attn_back_kernel(
    noise_scale, batch, clip,
    tokens_in, vec, first_in, q_in, k_in, v_in, o_in, do_in, lse, qk_in, vo_in, grad_mid_in, ga_in, gb_in, go_in,
    x_a_in, x_b_in, y_a_in, y_b_in, sums, included, attn_mom_in, mlp_mom_in, attn_noise_in, mlp_noise_in,
    grad_in_out, attn_out, mlp_out, vec_out, owned,
    tokens, first, q, k, v, o, do, qk_all, wv, grad_mid, ga, gb, attn_mom, mlp_mom, attn_noise, mlp_noise, grad_in,
    dqk, dv, ga_late, gb_late, head_turned, turned, partial, other, acc, square, factors,
    diag_a, diag_b, x_a, x_b, y_a, y_b, up_a, up_b, down_a, down_b,
    late_diag_a, late_diag_b, late_x_a, late_x_b, late_y_a, late_y_b, late_up_a, late_up_b, late_down_a, late_down_b,
    attn_low, mlp_low, relayed, vec_plane, vec_line,
    send, recv, late_send, late_recv, vec_sems, line_sems, gather_send, gather_recv, relay_sems, swap_send, swap_recv, small, pass_send, pass_recv,
    stage_sems,
):
    dp, core, z, y, x = place()
    rows, _, width = attn_mom.shape
    wide = mlp_mom.shape[2]
    length = tokens.shape[0]
    chunk = length // 4
    x_peer, y_peer = dp + 1 - 2 * x, dp + 2 - 4 * y
    count = ga.shape[0] // rows
    stage = Staging(stage_sems)
    for name, src, dst in (
        ("q", q_in, q), ("k", k_in, k), ("v", v_in, v), ("o", o_in, o), ("do", do_in, do), ("qk_all", qk_in, qk_all),
        ("wv", vo_in.at[:, pl.ds(0, width)], wv), ("first", first_in, first), ("go", go_in, gb_late.at[:, pl.ds(width, width)]),
        ("tokens", tokens_in, tokens), ("grad_mid", grad_mid_in, grad_mid), ("ga", ga_in, ga), ("gb", gb_in, gb),
        ("x_a", x_a_in, x_a), ("x_b", x_b_in, x_b), ("y_a", y_a_in, y_a), ("y_b", y_b_in, y_b),
        ("mlp_mom", mlp_mom_in, mlp_mom), ("mlp_noise", mlp_noise_in, mlp_noise), ("attn_mom", attn_mom_in, attn_mom),
        ("attn_noise", attn_noise_in, attn_noise),
    ):
        stage.fetch(name, src, dst)
    greeted = greet_plane(dp, core, count, z, y, x)

    main = Reducing(
        (ga, gb), (diag_a, diag_b, x_a, x_b, y_a, y_b, up_a, up_b, down_a, down_b), (ga_in, gb_in), send, recv, rows, True
    )
    late = Reducing(
        (ga_late, gb_late),
        (late_diag_a, late_diag_b, late_x_a, late_x_b, late_y_a, late_y_b, late_up_a, late_up_b, late_down_a, late_down_b),
        (ga_late, gb_late),
        late_send,
        late_recv,
        rows,
        False,
    )

    def small_copy(index):
        src, dst, target = (
            (square.at[0], square.at[1], (dp, 1 - core)),
            (factors.at[0], factors.at[1], (x_peer, core)),
            (factors.at[0], factors.at[2], (y_peer, core)),
            (factors.at[0], factors.at[3], (main.block(z, 1, 1), core)),
        )[index]
        return remote(src, dst, small.at[0, index], small.at[1, index], *target)

    mine_in_plane = (y * 2 + x) * 2 + core

    def plane_copies():
        copies = []
        for y_off, x_off, core_off in [(i // 4, i // 2 % 2, i % 2) for i in range(1, 8)]:
            target = main.block(z, y_off, x_off)
            target_core = core + core_off * (1 - 2 * core)
            place_there = target % 4 * 2 + target_core
            copies.append(
                remote(
                    vec_plane.at[mine_in_plane], vec_plane.at[mine_in_plane], vec_sems.at[0, place_there],
                    vec_sems.at[1, mine_in_plane], target, target_core,
                )
            )
        return copies

    def plane_arrivals():
        for i in range(1, 8):
            index = (mine_in_plane + i) % 8
            block = vec_plane.at[index]
            remote(block, block, vec_sems.at[0, index], vec_sems.at[1, index], dp, core).wait_recv()

    def line_copies():
        return [
            remote(vec_line.at[z], vec_line.at[z], line_sems.at[0, (z + i) % LINE], line_sems.at[1, z], (dp + 4 * i) % count, core)
            for i in range(1, LINE)
        ]

    def vec_turn():
        plane_arrivals()
        total = vec_plane[0]
        for index in range(1, 8):
            total = total + vec_plane[index]
        vec_line[z] = total
        for copy in line_copies():
            copy.start()

    def vec_finish():
        for i in range(1, LINE):
            index = (z + i) % LINE
            block = vec_line.at[index]
            remote(block, block, line_sems.at[0, index], line_sems.at[1, index], dp, core).wait_recv()
        total = vec_line[0]
        for index in range(1, LINE):
            total = total + vec_line[index]
        per_row = D // 128
        for row in range(vec_out.shape[0]):
            at = row % per_row * 128
            vec_out[row : row + 1, :] = total[row // per_row : row // per_row + 1, at : at + 128]
        for copy in plane_copies() + line_copies():
            copy.wait_send()

    def swap_copy(i):
        part = pl.ds(i * chunk, chunk)
        return remote(partial.at[part], other.at[part], swap_send.at[i], swap_recv.at[i], dp, 1 - core)

    acc[...] = jnp.zeros_like(acc)
    stage.need("q", "k", "v", "o", "do")
    for pair in range(width // (2 * HD)):
        lanes = pl.ds(pair * 2 * HD, 2 * HD)
        attend_backward(
            q.at[:, lanes], k.at[:, lanes], v.at[:, lanes], o.at[:, lanes], do.at[:, lanes], lse.at[pair],
            dqk.at[:, lanes], dqk.at[:, pl.ds(width + pair * 2 * HD, 2 * HD)], dv.at[:, lanes], head_turned,
        )
        if pair == 0:
            greeted()
            main.first(0, 1, 2, 3)
    stage.need("qk_all", "wv")
    for i in range(4):
        part = pl.ds(i * chunk, chunk)
        partial[part, :] = (contract(dqk[part, :], qk_all[...], 1, 1) + contract(dv[part, :], wv[...], 1, 1)).astype(
            jnp.bfloat16
        )
        swap_copy(i).start()
    stage.need("first", "go")
    turned[...] = first[...].T
    squares = jnp.zeros((1, 1), jnp.float32)
    for right, target in ((dqk, ga_late), (dv, gb_late)):
        for block in range(D // 256):
            part = pl.ds(block * 256, 256)
            value = contract(turned[part, :], right[...], 1, 0)
            target[part, 0 : right.shape[1]] = value.astype(jnp.bfloat16)
            squares = squares + jnp.sum(column_sum(value * value), axis=1, keepdims=True)
    late.first(0, 1)
    bias_q = column_sum(dqk[:, 0:width].astype(jnp.float32))
    bias_v = column_sum(dv[...].astype(jnp.float32))
    for value in (sums[6:7, :], sums[7:8, :]):
        squares = squares + jnp.sum(value, axis=1, keepdims=True)
    for value in (bias_q, bias_v, sums[4:5, :], sums[5:6, :]):
        squares = squares + jnp.sum(value * value, axis=1, keepdims=True)
    square[0] = jnp.broadcast_to(squares, square.shape[1:])
    small_copy(0).start()

    stage.need("tokens", "grad_mid")
    for i in range(4):
        swap_copy(i).wait_recv()

        def back(part):
            here = shifted(part, i * chunk)
            grad = partial[here, :].astype(jnp.float32) + other[here, :].astype(jnp.float32)
            value, normed = norm_back_tile(grad, vec[0:1, :], tokens[here, :].astype(jnp.float32))
            grad_in[here, :] = (grad_mid[here, :] + value).astype(jnp.bfloat16)
            acc[0] += fold(grad * normed)
            acc[1] += fold(grad)

        tiles(chunk, BACK_ROWS, back)
    stage.keep(grad_in, grad_in_out)
    gain_one, bias_one = column_sum(acc[0]), column_sum(acc[1])
    shared = jnp.zeros((1, 1), jnp.float32)
    for value in (gain_one, bias_one, sums[0:1, :], sums[1:2, :], sums[2:3, :], sums[3:4, :]):
        shared = shared + jnp.sum(value * value, axis=1, keepdims=True)
    small_copy(0).wait_recv()
    norm = jnp.sqrt(square[0, 0:1, 0:1] + square[1, 0:1, 0:1] + shared)
    factor = included[0].astype(jnp.float32) * jnp.minimum(1.0, clip / (norm + 1e-06))
    factors[0] = jnp.broadcast_to(factor, factors.shape[1:])
    for index in (1, 2, 3):
        small_copy(index).start()
    leading = factor * (1 - core).astype(jnp.float32)
    vec_plane[mine_in_plane] = jnp.zeros(vec_plane.shape[1:], jnp.float32)
    mine = pl.ds(pl.multiple_of(core * width, width), width)
    for row, value in ((0, gain_one), (1, bias_one), (2, sums[0:1, :]), (3, sums[1:2, :]), (6, sums[2:3, :]), (7, sums[3:4, :])):
        vec_plane[mine_in_plane, row : row + 1, :] = leading * value
    vec_plane[mine_in_plane, 4:5, mine] = factor * bias_q
    vec_plane[mine_in_plane, 5:6, mine] = factor * bias_v
    vec_plane[mine_in_plane, pl.ds(8 + 2 * core, 1), :] = factor * sums[4:5, :]
    vec_plane[mine_in_plane, pl.ds(9 + 2 * core, 1), :] = factor * sums[5:6, :]
    stage.need("ga", "gb", "x_a", "x_b", "y_a", "y_b", "mlp_mom", "mlp_noise", "attn_mom", "attn_noise")
    for index in (1, 2, 3):
        small_copy(index).wait_recv()
    for part in (main, late):
        part.scale(factor, factors[1, 0:1, 0:1], factors[2, 0:1, 0:1], factors[3, 0:1, 0:1])

    def moment(slot, reducing, side, column):
        size = width if slot < 4 else wide
        low = attn_low.at[slot] if slot < 4 else mlp_low.at[slot - 4]
        old, noise, new = (attn_mom, attn_noise, attn_out) if slot < 4 else (mlp_mom, mlp_noise, mlp_out)
        index = slot if slot < 4 else slot - 4

        @pl.loop(0, rows // 16)
        def _(i):
            part = pl.ds(pl.multiple_of(i * 16, 16), 16)
            total = reducing.total(side, part, pl.ds(column, size))
            value = 0.5 * old[part, index, :] + (total + noise_scale * noise[part, index, :]) / batch
            new[part, index, :] = value
            low[part, :] = value.astype(low.dtype)

        for action in sends(slot):
            action(lambda copy: copy.start())

    def landing(slot, source):
        size = width if slot < 4 else wide
        return main.at(owned.at[0], source).at[:, 0:size]

    def sends(slot):
        owner = OWNERS[slot]
        owner_z, owner_y, owner_x = owner_at(slot)
        low = attn_low.at[slot] if slot < 4 else mlp_low.at[slot - 4]
        alone = 0 if owner_z == 1 else LINE - 1
        far = (y != owner_y) & (x != owner_x)
        near = (y != owner_y) | (x != owner_x)
        across = (z != owner_z) & (far | ((z == alone) & near))

        def keep(action):
            @pl.when(dp == owner)
            def _():
                action(pltpu.make_async_copy(low, landing(slot, dp), gather_send.at[slot]))

        def direct(action):
            away = (dp != owner) & jnp.logical_not(across) if slot >= 4 else dp != owner

            @pl.when(away)
            def _():
                action(remote(low, landing(slot, dp), gather_send.at[slot], gather_recv.at[dp], owner, core))

        def turn(action):
            if slot >= 4:

                @pl.when(across)
                def _():
                    stop = z * 4 + owner_y * 2 + owner_x
                    action(remote(low, relayed.at[dp % 4], gather_send.at[slot], relay_sems.at[0, dp % 4], stop, core))

        return keep, direct, turn

    def relays(slot, action):
        owner_z, owner_y, owner_x = owner_at(slot)
        alone = 0 if owner_z == 1 else LINE - 1
        column = owner_y * 2 + owner_x
        here = (y == owner_y) & (x == owner_x) & (z != owner_z)

        @pl.when(here)
        def _():
            action(3 - column)

        @pl.when(here & (z == alone))
        def _():
            action(column + 1 - 2 * owner_x)
            action(column + 2 - 4 * owner_y)

    def relay_copy(slot, column):
        source = z * 4 + column
        return remote(
            relayed.at[column], landing(slot, source), relay_sems.at[1, column], gather_recv.at[source], OWNERS[slot], core
        )

    def forward(slot, column):
        block = relayed.at[column]
        remote(block, block, relay_sems.at[1, column], relay_sems.at[0, column], dp, core).wait_recv()
        relay_copy(slot, column).start()

    def pass_on(slot, source):
        size = width if slot < 4 else wide
        block = landing(slot, source)
        other_half = main.at(owned.at[1], source).at[:, 0:size]
        return remote(block, other_half, pass_send.at[source], pass_recv.at[source], dp, 1 - core)

    def turned_off(slot, source):
        owner_z, owner_y, owner_x = owner_at(slot)
        off_x, off_y = source % 2 != owner_x, source % 4 // 2 != owner_y
        alone = 0 if owner_z == 1 else LINE - 1
        return slot >= 4 and source // 4 != owner_z and ((off_x and off_y) or (source // 4 == alone and (off_x or off_y)))

    def collect(slot, late_ones):
        @pl.when(dp == OWNERS[slot])
        def _():
            for step in range(1, count):
                source = (OWNERS[slot] + step) % count
                if turned_off(slot, source) == late_ones:
                    block = landing(slot, source)
                    remote(block, block, gather_send.at[slot], gather_recv.at[source], source, core).wait_recv()
                    pass_on(slot, source).start()

    main.chain(0)
    late.first(2)
    late.sums(late.order[0])
    main.chain(1)
    late.first(3)
    late.sums(late.order[1])
    main.chain(2)
    late.sums(late.order[2])
    late.sums(late.order[3])
    late.chain(0)
    main.last(0)
    moment(4, main, 0, 0)
    main.last(1)
    moment(5, main, 1, 0)
    for copy in plane_copies():
        copy.start()
    late.chain(1)
    for slot in (4, 5):
        relays(slot, functools.partial(forward, slot))
    late.chain(2)
    vec_turn()
    for slot in (4, 5):
        collect(slot, False)
    late.last(0)
    moment(0, late, 0, 0)
    moment(1, late, 0, width)
    late.last(1)
    moment(2, late, 1, 0)
    moment(3, late, 1, width)

    for slot in range(6):
        low = attn_low.at[slot] if slot < 4 else mlp_low.at[slot - 4]

        @pl.when(dp == OWNERS[slot])
        def _():
            pltpu.make_async_copy(low, landing(slot, dp), gather_send.at[slot]).wait()
            pass_on(slot, dp).start()

    for slot in (4, 5):
        collect(slot, True)
    for slot in range(4):
        collect(slot, False)
    for slot in range(6):
        owner = OWNERS[slot]
        low = attn_low.at[slot] if slot < 4 else mlp_low.at[slot - 4]

        @pl.when(dp != owner)
        def _():
            remote(low, low, gather_send.at[slot], gather_recv.at[dp], owner, core).wait_send()

        @pl.when(dp == owner)
        def _():
            @pl.loop(0, count)
            def _(source):
                pass_on(slot, source).wait()

    vec_finish()
    for slot in (4, 5):
        relays(slot, lambda column: relay_copy(slot, column).wait_send())
    for index in range(4):
        small_copy(index).wait_send()
    for i in range(4):
        swap_copy(i).wait_send()
    main.drain()
    late.drain()
    stage.finish()


def attn_back(
    tokens, vec, first, q, k, v, o, do, lse, qk_all, vo_all, grad_mid, ga, gb, go, x_a, x_b, y_a, y_b, sums, included,
    attn_mom, mlp_mom, attn_noise, mlp_noise, noise_scale, batch, clip, collective_id,
):
    dma = pltpu.SemaphoreType.DMA
    low = jnp.bfloat16
    count = lax.axis_size("dp")
    length = tokens.shape[0]
    rows, _, width = attn_mom.shape
    wide = mlp_mom.shape[2]
    shape = jax.ShapeDtypeStruct
    vmem = pl.BlockSpec(memory_space=pltpu.VMEM)
    anywhere = pl.BlockSpec(memory_space=pl.ANY)
    scratch = pltpu.VMEM
    return pl.pallas_call(
        functools.partial(attn_back_kernel, noise_scale, batch, clip),
        out_shape=[
            shape((length, D), low),
            shape(attn_mom.shape, jnp.float32),
            shape(mlp_mom.shape, jnp.float32),
            shape((vec.shape[0] * D // 128, 128), jnp.float32),
            shape((2, D, wide), low),
        ],
        in_specs=[anywhere, vmem]
        + [anywhere] * 6
        + [vmem]
        + [anywhere] * 10
        + [vmem, pl.BlockSpec(memory_space=pltpu.SMEM)]
        + [anywhere] * 4,
        out_specs=[anywhere] + [vmem] * 3 + [anywhere],
        scratch_shapes=[
            scratch((length, D), low),
            scratch((length, D), low),
        ]
        + [scratch((length, width), low)] * 5
        + [
            scratch((D, 2 * width), low),
            scratch((D, width), low),
            scratch((length, D), jnp.float32),
            scratch((D, wide), low),
            scratch((D, wide), low),
            scratch(attn_mom.shape, jnp.float32),
            scratch(mlp_mom.shape, jnp.float32),
            scratch(attn_mom.shape, jnp.float32),
            scratch(mlp_mom.shape, jnp.float32),
            scratch((length, D), low),
            scratch((length, 2 * width), low),
            scratch((length, width), low),
            scratch((D, 2 * width), low),
            scratch((D, 2 * width), low),
            scratch((2 * HD, length), jnp.float32),
            scratch((D, length), low),
            scratch((length, D), low),
            scratch((length, D), low),
            scratch((2, 8, D), jnp.float32),
            scratch((2, 8, 128), jnp.float32),
            scratch((4, 8, 128), jnp.float32),
        ]
        + [scratch((LINE, rows, wide), low)] * 10
        + [scratch((LINE, rows, 2 * width), low)] * 10
        + [
            scratch((4, rows, width), low),
            scratch((2, rows, wide), low),
            scratch((4, rows, wide), low),
            scratch((8,) + vec.shape, jnp.float32),
            scratch((LINE,) + vec.shape, jnp.float32),
            dma((10, LINE)),
            dma((10, LINE)),
            dma((10, LINE)),
            dma((10, LINE)),
            dma((2, 8)),
            dma((2, LINE)),
            dma((6,)),
            dma((count,)),
            dma((2, 4)),
            dma((4,)),
            dma((4,)),
            dma((2, 4)),
            dma((count,)),
            dma((count,)),
            dma((24,)),
        ],
        compiler_params=pltpu.CompilerParams(
            collective_id=collective_id, has_side_effects=True, vmem_limit_bytes=62 * MIB
        ),
        name="attn_back",
    )(
        tokens, vec, first, q, k, v, o, do, lse, qk_all, vo_all, grad_mid, ga, gb, go, x_a, x_b, y_a, y_b, sums, included,
        attn_mom, mlp_mom, attn_noise, mlp_noise,
    )


def placed(piece, start, total_size):
    return lax.dynamic_update_slice_in_dim(jnp.zeros((total_size,), jnp.float32), piece, start, 0)


def other_core(value):
    return lax.ppermute(value, "tensor", [(0, 1), (1, 0)])


SHIFTS = (0.0, 0.0, 0.0, 0.8, 0.72)


def polynomials(current, low):
    rows = current.shape[0]
    diagonal = lax.broadcasted_iota(jnp.int32, (rows, rows), 0) == lax.broadcasted_iota(jnp.int32, (rows, rows), 1)

    def less(matrix, shift):
        return matrix - jnp.where(diagonal, shift, 0.0) if shift else matrix

    def product(left, right):
        return contract(left.astype(jnp.bfloat16), right.astype(jnp.bfloat16), 1, 0)

    factor = None
    for iteration in range(NS_ITERS):
        shift = SHIFTS[iteration]
        moved = less(current, shift)
        operand = moved if iteration else low
        square = product(operand, operand) + 2.0 * shift * moved
        lead = COEF_B * shift + COEF_C * shift * shift
        rest = lax.optimization_barrier(COEF_B * moved + COEF_C * square)
        whole = COEF_A + lead
        if factor is None:
            factor = jnp.where(diagonal, whole, 0.0) + rest
        else:
            factor = lax.optimization_barrier(whole * factor + product(rest, factor))
        if iteration < NS_ITERS - 1:
            once = lax.optimization_barrier(whole * current + shift * rest + product(rest, operand))
            second = whole * shift
            current = lax.optimization_barrier(whole * once + second * rest + product(rest, less(once, second)))
    return factor.astype(jnp.bfloat16)


def newton(owned):
    gram = contract(owned, owned, 1, 1)
    gram = gram + other_core(gram)
    scale = 1.0 / (jnp.sqrt(jnp.trace(gram)) + 1e-07)
    return (contract(polynomials(gram * (scale * scale), gram * (scale * scale)), owned, 1, 0) * scale).astype(jnp.bfloat16)


def body(
    fast,
    tokens,
    cotangent,
    inclusion,
    attn_weights,
    mlp_weights,
    attn_momentum,
    mlp_momentum,
    attn_noise,
    mlp_noise,
    vectors,
    vector_momentum,
    vector_noise,
):
    dp_count = lax.axis_size("dp")
    dp_index = lax.axis_index("dp")
    halves = lax.axis_size("tensor")
    tensor_index = lax.axis_index("tensor")
    head_width = D // halves
    hidden_width = FF // halves
    query_scale = 1.0 / math.sqrt(HD)
    clip = 1.5 * D * math.sqrt(LEN)
    sigma = 0.05 * math.sqrt(dp_count) / D
    batch = 0.75 * dp_count
    noise_scale = sigma * clip
    if fast:
        (
            query_key, value_out, first_low, queries, key_rows, value_rows, attended_low, result, grad_mid, grad_attended,
            grad_fc, grad_pr, grad_wo, x_fc, x_pr, y_fc, y_pr, stats, vec, sums,
        ) = forward(tokens[0], vectors.reshape(-1, 128), attn_weights, mlp_weights, cotangent[0], 0)
        grad_in, attn_moment, mlp_moment, vector_summed, owned = attn_back(
            tokens[0], vec, first_low, queries, key_rows, value_rows, attended_low, grad_attended, stats,
            query_key, value_out, grad_mid, grad_fc, grad_pr, grad_wo,
            x_fc, x_pr, y_fc, y_pr, sums,
            inclusion, attn_momentum, mlp_momentum, attn_noise, mlp_noise, noise_scale, batch, clip, 2,
        )
    else:
        attn_shard = attn_weights.astype(jnp.bfloat16)
        mlp_shard = mlp_weights.astype(jnp.bfloat16)
        rows = attn_shard.shape[0]
        shards = (
            attn_shard[:, 0:2].reshape(rows, 2 * head_width),
            attn_shard[:, 2:4].reshape(rows, 2 * head_width),
            mlp_shard[:, 0, 0:D],
            mlp_shard[:, 0, D:],
            mlp_shard[:, 1, 0:D],
            mlp_shard[:, 1, D:],
        )
        gain_one = vectors[0:D]
        bias_one = vectors[D : 2 * D]
        gain_two = vectors[2 * D : 3 * D]
        bias_two = vectors[3 * D : 4 * D]
        query_bias = lax.dynamic_slice_in_dim(vectors, 4 * D + tensor_index * head_width, head_width)
        value_bias = lax.dynamic_slice_in_dim(vectors, 5 * D + tensor_index * head_width, head_width)
        attn_bias = vectors[6 * D : 7 * D]
        mlp_bias = vectors[7 * D : 8 * D]
        hidden_bias = lax.dynamic_slice_in_dim(
            vectors, 8 * D + tensor_index * hidden_width, hidden_width
        )
        inputs = tokens[0].astype(jnp.float32)
        length = inputs.shape[0]
        first, normed_one, inverse_one = layer_norm(inputs, gain_one, bias_one)

        def both_cores(partial):
            low = partial.astype(jnp.bfloat16)
            return low.astype(jnp.float32) + other_core(low).astype(jnp.float32)

        query_key, value_out, fc_one, fc_two, pr_one, pr_two = (
            lax.all_gather(shard, "dp", axis=0, tiled=True) for shard in shards
        )
        value_weight, out_weight = value_out[:, 0:head_width], value_out[:, head_width:]
        first_low = first.astype(jnp.bfloat16)
        qk = contract(first_low, query_key, 1, 0)
        queries = ((qk[:, 0:head_width] + query_bias) * query_scale).astype(jnp.bfloat16)
        key_rows = qk[:, head_width:].astype(jnp.bfloat16)
        value_rows = (contract(first_low, value_weight, 1, 0) + value_bias).astype(jnp.bfloat16)
        attended_low, stats = pairs_forward(queries, key_rows, value_rows)
        middle = inputs + both_cores(contract(attended_low, out_weight, 1, 1)) + attn_bias
        second_low = layer_norm(middle, gain_two, bias_two)[0].astype(jnp.bfloat16)
        pre_act = contract(second_low, jnp.concatenate([fc_one, fc_two], axis=1), 1, 0) + hidden_bias
        activation, gelu_back = jax.vjp(gelu_tanh, pre_act)
        activation_low = activation.astype(jnp.bfloat16)
        slope = gelu_back(jnp.ones_like(pre_act))[0]
        _, normed_two, inverse_two = layer_norm(middle, gain_two, bias_two)
        fc_weight = jnp.concatenate([fc_one, fc_two], axis=1)
        pr_weight = jnp.concatenate([pr_one, pr_two], axis=1)
        result = middle + both_cores(contract(activation_low, pr_weight, 1, 1)) + mlp_bias
        cot_low = cotangent[0]
        grad_out = cot_low.astype(jnp.float32)
        d_pr = contract(cot_low, activation_low, 0, 0)
        grad_pre = (contract(cot_low, pr_weight, 1, 0) * slope.astype(jnp.float32)).astype(jnp.bfloat16)
        d_fc = contract(second_low, grad_pre, 0, 0)
        d_hidden_bias = jnp.sum(grad_pre.astype(jnp.float32), axis=0)
        grad_two = both_cores(contract(grad_pre, fc_weight, 1, 1))
        grad_mid = grad_out + norm_back(grad_two, gain_two, normed_two, inverse_two)
        d_gain_two = jnp.sum(grad_two * normed_two, axis=0)
        d_bias_two = jnp.sum(grad_two, axis=0)
        d_attn_bias = jnp.sum(grad_mid, axis=0)
        d_mlp_bias = jnp.sum(grad_out, axis=0)
        mid_low = grad_mid.astype(jnp.bfloat16)
        d_out = contract(mid_low, attended_low, 0, 0)
        grad_attended = contract(mid_low, out_weight, 1, 0).astype(jnp.bfloat16)
        grad_q, grad_k, grad_v = pairs_backward(
            queries, key_rows, value_rows, attended_low, grad_attended, stats
        )
        grad_qk = jnp.concatenate([grad_q, grad_k], axis=1)
        d_query_key = contract(first_low, grad_qk, 0, 0)
        d_value = contract(first_low, grad_v, 0, 0)
        d_query_bias = jnp.sum(grad_q.astype(jnp.float32), axis=0)
        d_value_bias = jnp.sum(grad_v.astype(jnp.float32), axis=0)
        grad_one = both_cores(contract(grad_qk, query_key, 1, 1) + contract(grad_v, value_weight, 1, 1))
        grad_in = grad_mid + norm_back(grad_one, gain_one, normed_one, inverse_one)
        d_gain_one = jnp.sum(grad_one * normed_one, axis=0)
        d_bias_one = jnp.sum(grad_one, axis=0)
        split_square = sum(
            jnp.sum(value * value)
            for value in (d_query_key, d_value, d_out, d_fc, d_pr, d_query_bias, d_value_bias, d_hidden_bias)
        )
        split_tile = jnp.broadcast_to(split_square, (8, 128))
        total_square = (split_tile + other_core(split_tile))[0, 0] + sum(
            jnp.sum(value * value)
            for value in (d_gain_one, d_bias_one, d_gain_two, d_bias_two, d_attn_bias, d_mlp_bias)
        )
        factor = inclusion[0].astype(jnp.float32) * jnp.minimum(
            1.0, clip / (jnp.sqrt(total_square) + 1e-06)
        )
        leading = (tensor_index == 0).astype(jnp.float32)
        vector_grad = (
            jnp.concatenate(
                [
                    leading * d_gain_one,
                    leading * d_bias_one,
                    leading * d_gain_two,
                    leading * d_bias_two,
                    placed(d_query_bias, tensor_index * head_width, D),
                    placed(d_value_bias, tensor_index * head_width, D),
                    leading * d_attn_bias,
                    leading * d_mlp_bias,
                    placed(d_hidden_bias, tensor_index * hidden_width, FF),
                ]
            )
            * factor
        )
        result, grad_in = result.astype(jnp.bfloat16), grad_in.astype(jnp.bfloat16)
        attn_grad = jnp.concatenate([d_query_key, d_value, d_out], axis=1) * factor
        mlp_grad = jnp.stack([d_fc, d_pr], axis=1) * factor
        attn_summed = lax.psum_scatter(attn_grad, "dp", scatter_dimension=0, tiled=True)
        mlp_summed = lax.psum_scatter(mlp_grad, "dp", scatter_dimension=0, tiled=True)
        attn_summed = attn_summed.reshape(rows, 4, head_width)
        vector_summed = lax.psum(vector_grad, ("dp", "tensor"))
        attn_moment = 0.5 * attn_momentum + (attn_summed + noise_scale * attn_noise) / batch
        mlp_moment = 0.5 * mlp_momentum + (mlp_summed + noise_scale * mlp_noise) / batch
        owners = jnp.array([slot * dp_count // 6 for slot in range(6)])
        full_attn = lax.all_gather(attn_moment.astype(jnp.bfloat16), "dp", axis=0, tiled=True)
        full_mlp = lax.all_gather(mlp_moment.astype(jnp.bfloat16), "dp", axis=0, tiled=True)
        attn_pick = (owners[0:4] == dp_index)[None, :, None]
        mlp_pick = (owners[4:6] == dp_index)[None, :, None]
        mine_attn = jnp.sum(jnp.where(attn_pick, full_attn, 0), axis=1)
        mine_mlp = jnp.sum(jnp.where(mlp_pick, full_mlp, 0), axis=1)
        owned = jnp.pad(mine_attn, ((0, 0), (0, hidden_width - head_width))) + mine_mlp
    vector_rate = 0.2 * math.sqrt(dp_count / LEN)
    rates = (0.5, 0.5, 0.5, 0.5 * max(1.0, math.sqrt(LEN) / 8.0), 0.5 * math.sqrt(FF / D), 0.5)
    if fast:
        tiled = tuple(value.reshape(-1, 128) for value in (vector_summed, vectors, vector_momentum, vector_noise))
        gram, gram_low, scale, result, grad_in, attn_moment, mlp_moment, vector_moment, vectors_new = gram_of(
            owned, (result, grad_in, attn_moment, mlp_moment), tiled, noise_scale, batch, vector_rate
        )
        vector_moment, vectors_new = vector_moment.reshape(-1), vectors_new.reshape(-1)
        attn_new, mlp_new = scatter_rows(
            polynomials(gram, gram_low), scale, owned, attn_weights, mlp_weights, rates, 3
        )
    else:
        vector_moment = 0.5 * vector_momentum + (vector_summed + noise_scale * vector_noise) / batch
        vectors_new = vectors - vector_rate * vector_moment
        orthogonal = newton(owned)
        attn_rows = jnp.where(attn_pick, orthogonal[:, None, 0:head_width], 0)
        mlp_rows = jnp.where(mlp_pick, orthogonal[:, None, :], 0)
        attn_orth = lax.psum_scatter(attn_rows, "dp", scatter_dimension=0, tiled=True)
        mlp_orth = lax.psum_scatter(mlp_rows, "dp", scatter_dimension=0, tiled=True)
        attn_new = attn_weights - jnp.array(rates[0:4])[None, :, None] * attn_orth
        mlp_new = mlp_weights - jnp.array(rates[4:6])[None, :, None] * mlp_orth
    return (
        result[None],
        grad_in[None],
        attn_moment,
        mlp_moment,
        attn_new,
        mlp_new,
        vector_moment,
        vectors_new,
    )


def solution(mesh):
    fast = mesh.shape["dp"] == 16 and mesh.shape["tensor"] == 2
    in_specs = (
        P("dp", None, None),
        P("dp", None, None),
        P("dp"),
        P("dp", None, "tensor"),
        P("dp", None, "tensor"),
        P("dp", None, "tensor"),
        P("dp", None, "tensor"),
        P("dp", None, "tensor"),
        P("dp", None, "tensor"),
        P(),
        P(),
        P(),
    )
    out_specs = (
        P("dp", None, None),
        P("dp", None, None),
        P("dp", None, "tensor"),
        P("dp", None, "tensor"),
        P("dp", None, "tensor"),
        P("dp", None, "tensor"),
        P(),
        P(),
    )
    return jax.shard_map(
        functools.partial(body, fast), mesh=mesh, in_specs=in_specs, out_specs=out_specs, check_vma=False
    )
```
